32 devices in a mesh: groups: 2 (over y), seq: 8 (over z, x), wt: 2 (over core).
Axes of the slice: x: 2, y: 2, z: 4, core: 2. Of those that a mesh axis runs over, the one named last changes fastest.
Arguments:
- query_input: bfloat16 [8192, 4096], P(('groups', 'seq'), 'wt'), parts along dimension 0, may hold values from -6 to 6
- key_input: bfloat16 [8192, 4096], P(('groups', 'seq'), 'wt'), parts along dimension 0, may hold values from -6 to 6
- value_input: bfloat16 [8192, 4096], P(('groups', 'seq'), 'wt'), parts along dimension 0, may hold values from -6 to 6
- gate_input: bfloat16 [8192, 4096], P(('groups', 'seq'), 'wt'), parts along dimension 0, may hold values from -6 to 6
- segment: int32 [8192], P(('groups', 'seq')), parts along dimension 0, may hold values from 0 to 7, never falling along the last dimension, each value on 1 to 1024 neighbouring positions
- decay_exponent: int32 [32], P('wt'), may hold values from 5 to 21
- retention: float32 [32, 8192], P('wt', ('groups', 'seq')), parts along dimension 1, may hold values from 0.5 to 1
- norm_gain: float32 [4096], P('wt'), may hold values from 0.5 to 1.5
Outputs:
- gated: bfloat16 [8192, 4096], P(('groups', 'seq'), 'wt'), parts along dimension 0
- snapshots: float32 [16, 32, 128, 128], P(('groups', 'seq'), 'wt'), parts along dimension 0
The draws below stay inside these ranges and needn't reach their ends.
There are 2 independent parts, one for each index of `groups`. The reference program is written for one: setup_inputs(seed, part) draws one part's arguments, and reference() takes and returns one part's arrays. A program takes and returns all parts, laid end to end along the dimension named above; an argument that names none is the same for every part. Nothing has to cross between parts.
Inputs may be any that keep to these rules, and one draw needn't show every extreme that they name: `segment`: never falls along the slab and starts at 0.
All inputs are finite; a program needn't handle non-finite values.
Results may differ from the reference program's by a relative error of at most 0.0047.
Values sent between devices are 32-bit elements; how exact they have to be, the bound alone decides.
No kernel may reach another device: no remote copies, remote signals or barrier semaphores. Data moves between devices by JAX's collectives and lax.ppermute only.
A program may use at most 192 MiB of HBM per device.

```python
import math
import jax
import jax.numpy as jnp
import numpy as np
from jax import lax

H = 32
DH = 128
CH = 512
DOCS = 8
NT = 4096
HF = 4096
N_SEQ = 8


def draw_retention(key, part):
    key = jax.random.fold_in(key, 7)
    first_key, second_key = jax.random.split(key)
    chance = 4.0 / NT
    samples = jax.random.uniform(first_key, (H, NT), jnp.float32)
    losses = jax.random.uniform(second_key, (H, NT), jnp.float32, 0.5, 0.8)
    return jnp.where(samples < chance, losses, 1.0).astype(jnp.float32)


def place_ends(values, rng, smallest, top_value):
    longest = values.shape.index(max(values.shape))
    spots = []
    for shift in (0, 1):
        where = [jax.random.randint(jax.random.fold_in(rng, axis), (), 0, length) for axis, length in enumerate(values.shape)]
        where[longest] = (where[longest] + shift) % values.shape[longest]
        spots.append(tuple(where))
    return values.at[spots[0]].set(smallest).at[spots[1]].set(top_value)


def block_scale(own_key, shape, cuts, smallest, top_value):
    factor_of = 1.0
    for position, blocks in cuts:
        heights = jax.random.uniform(jax.random.fold_in(jax.random.fold_in(own_key, 6), position), (blocks,), jnp.float32, smallest / len(cuts), top_value / len(cuts))
        factor_of = factor_of * jnp.repeat(jnp.exp(heights), shape[position] // blocks).reshape((-1,) + (1,) * (len(shape) - 1 - position))
    return factor_of


def split_up(number_of, total, bound, skew):
    loads = [(1 << 20) // math.isqrt(grade ** skew) + 1 for grade in range(2, number_of + 1)]
    surplus, given = total - bound - (number_of - 1), [1] * (number_of - 1)
    while surplus > 0:
        candidates = [i for i in range(number_of - 1) if given[i] < bound]
        whole, left = sum([loads[i] for i in candidates]), surplus
        for i in candidates:
            addition = min(bound - given[i], max(1, left * loads[i] // whole), surplus)
            given[i] = given[i] + addition
            surplus = surplus - addition
    return np.array([bound] + given)


def uneven_parts(rng, amount, total, limit, slope):
    if amount == 2:
        one = jax.random.randint(rng, (), max(1, total - limit), min(limit, total - 1) + 1)
        return jnp.stack([one, total - one])
    sizes = jnp.asarray(split_up(amount, total, limit, slope), jnp.int32)
    pairs = (amount - 1) // 2
    giver, receiver = sizes[1:1 + 2 * pairs:2], sizes[2:2 + 2 * pairs:2]
    slack = jnp.minimum(giver - 1, limit - receiver)
    passed = jax.random.randint(jax.random.fold_in(rng, 1), (pairs,), 0, 1 << 20) % (slack + 1)
    sizes = sizes.at[1:1 + 2 * pairs:2].set(giver - passed).at[2:2 + 2 * pairs:2].set(receiver + passed)
    return sizes[jax.random.permutation(jax.random.fold_in(rng, 2), amount)]


def noise(own_key, shape, scale, bound, pieces=(), dtype=jnp.bfloat16):
    result = jax.random.normal(own_key, shape, jnp.float32) * scale
    if len(pieces) > 0:
        result = block_scale(own_key, shape, pieces, -0.22, 0.18) * result
    return jnp.clip(result, min=-bound, max=bound).astype(dtype)


def setup_inputs(seed: int = 0, part: int = 0) -> dict:
    splits = jax.random.split(jax.random.key(seed), 9)
    part_keys = jax.random.split(jax.random.fold_in(splits[8], part), 9)
    query_input = noise(part_keys[0], (NT, HF), 1.0, 6.0, ((0, 8), (1, 2)))
    key_input = noise(part_keys[1], (NT, HF), 1.0, 6.0, ((0, 8), (1, 2)))
    value_input = noise(part_keys[2], (NT, HF), 1.0, 6.0, ((0, 8), (1, 2)))
    gate_input = noise(part_keys[3], (NT, HF), 1.0, 6.0, ((0, 8), (1, 2)))
    segment = jnp.searchsorted(jnp.cumsum(uneven_parts(part_keys[4], DOCS, NT, NT // 4, 1)), jnp.arange(NT), side="right").astype(jnp.int32)
    decay_exponent = place_ends(jax.random.randint(splits[5], (H,), 5, 22), jax.random.fold_in(splits[5], 1), 5, 21).astype(jnp.int32)
    retention = draw_retention(jax.random.fold_in(jax.random.fold_in(splits[8], part), 71), part)
    norm_gain = jnp.clip(1.0 + 0.1 * jax.random.normal(splits[7], (HF,), jnp.float32), 0.5, 1.5)
    return dict(query_input=query_input, key_input=key_input, value_input=value_input, gate_input=gate_input, segment=segment, decay_exponent=decay_exponent, retention=retention, norm_gain=norm_gain)


def reference(query_input, key_input, value_input, gate_input, segment, decay_exponent, retention, norm_gain):
    highest = lax.Precision.HIGHEST
    rate = jnp.exp2(-decay_exponent.astype(jnp.float32))
    log_keep = jnp.log(retention).reshape(H, N_SEQ, CH).transpose(1, 0, 2)
    span_inputs = (query_input.reshape(N_SEQ, CH, H, DH), key_input.reshape(N_SEQ, CH, H, DH), value_input.reshape(N_SEQ, CH, H, DH), gate_input.reshape(N_SEQ, CH, H, DH), segment.reshape(N_SEQ, CH), log_keep)
    causal = jnp.arange(CH)[:, None] >= jnp.arange(CH)[None, :]
    gain = norm_gain.reshape(H, DH)

    def span_step(carried, inputs):
        state_in, previous = carried
        queries, key_rows, value_rows, gate_rows, seg_rows, keep_rows = inputs
        decay_log = -rate[:, None] + keep_rows
        cumulative = jnp.cumsum(decay_log, axis=1)
        final_log = cumulative[:, -1]
        same_doc = seg_rows[:, None] == seg_rows[None, :]
        difference = cumulative[:, :, None] - cumulative[:, None, :]
        weight_mask = jnp.where(causal & same_doc, jnp.exp(jnp.minimum(difference, 0.0)), 0.0)
        query_f = queries.astype(jnp.float32)
        key_f = key_rows.astype(jnp.float32)
        value_f = value_rows.astype(jnp.float32)
        scores = jnp.einsum('thd,shd->hts', query_f, key_f, precision=highest) * weight_mask
        probabilities = lax.optimization_barrier(scores.astype(jnp.bfloat16)).astype(jnp.float32)
        intra_term = jnp.einsum('hts,shd->thd', probabilities, value_f, precision=highest)
        valid = (seg_rows == previous).astype(jnp.float32)
        inter_term = jnp.einsum('thd,hde->the', query_f, state_in, precision=highest)
        inter_term = inter_term * (jnp.exp(cumulative).T * valid[:, None])[:, :, None]
        mixed_out = intra_term + inter_term
        mean_square = lax.optimization_barrier(jnp.mean(mixed_out * mixed_out, axis=-1, keepdims=True))
        gated = mixed_out * lax.rsqrt(mean_square + 1e-06) * gain * jax.nn.sigmoid(gate_rows.astype(jnp.float32))
        gated = gated.astype(jnp.bfloat16).reshape(CH, H * DH)
        key_weight = jnp.where(seg_rows[None, :] == seg_rows[-1], jnp.exp(final_log[:, None] - cumulative), 0.0)
        keyed = lax.optimization_barrier((key_f * key_weight.T[:, :, None]).astype(jnp.bfloat16)).astype(jnp.float32)
        local_state = jnp.einsum('shd,she->hde', keyed, value_f, precision=highest)
        carry_factor = jnp.exp(final_log) * (seg_rows[-1] == previous).astype(jnp.float32)
        snapshot = carry_factor[:, None, None] * state_in + local_state
        return ((snapshot, seg_rows[-1]), (gated, snapshot))
    initial = (jnp.zeros((H, DH, DH), jnp.float32), segment[0])
    _, (gated_all, snapshots) = lax.scan(span_step, initial, span_inputs)
    return (gated_all.reshape(NT, H * DH), snapshots)
```

```python
import functools

import jax
import jax.numpy as jnp
from jax import lax
from jax.experimental import pallas as pl
from jax.experimental.pallas import tpu as pltpu
from jax.sharding import PartitionSpec as P

F32 = jnp.float32
BF16 = jnp.bfloat16
NN = (((1,), (0,)), ((), ()))
NT = (((1,), (1,)), ((), ()))
MIB = 1 << 20


def vmem_spec(shape, index_map):
    return pl.BlockSpec(shape, index_map)


def as_column(row, lanes):
    return jnp.broadcast_to(row, (lanes, row.shape[1])).T


def state_kernel(heads, seg_ref, exponent_ref, keep_ref, k_ref, v_ref, msg_ref, a_ref, w_ref):
    tokens = seg_ref.shape[1]
    size = msg_ref.shape[1]
    group = k_ref.shape[1] // size
    step = pl.program_id(0)

    @pl.when(step == 0)
    def _():
        across = lax.broadcasted_iota(jnp.int32, (heads, heads), 1)
        down = lax.broadcasted_iota(jnp.int32, (heads, heads), 0)
        spread = jnp.broadcast_to(exponent_ref[...], (heads, heads))
        exponent = jnp.sum(jnp.where(across == down, spread, 0).astype(F32), axis=1, keepdims=True)
        a = -jnp.exp2(-exponent) + jnp.log(keep_ref[...])
        high = a.astype(BF16)
        rest = a - high.astype(F32)
        middle = rest.astype(BF16)
        low = (rest - middle.astype(F32)).astype(BF16)
        parts = jnp.concatenate([high, middle, low], axis=0)
        earlier = lax.broadcasted_iota(jnp.int32, (tokens, tokens), 0)
        later = lax.broadcasted_iota(jnp.int32, (tokens, tokens), 1)
        upper = jnp.where(earlier <= later, 1.0, 0.0).astype(BF16)
        sums = lax.dot_general(parts, upper, NN, preferred_element_type=F32)
        cumulative = sums[:heads] + (sums[heads : 2 * heads] + sums[2 * heads :])
        a_ref[...] = cumulative
        final = cumulative[:, tokens - 1 :]
        seg = seg_ref[...]
        last = seg[:, tokens - 1 :]
        w_ref[...] = jnp.where(seg == last, jnp.exp(final - cumulative), 0.0)
        msg_ref[heads * size : heads * size + heads, :] = jnp.broadcast_to(final, (heads, size))
        msg_ref[heads * size + heads :, :] = jnp.broadcast_to(last.astype(F32), (8, size))

    for j in range(group):
        head = step * group + j
        columns = slice(j * size, (j + 1) * size)
        keyed = (k_ref[:, columns].astype(F32).T * w_ref[pl.ds(head, 1), :]).astype(BF16)
        local = lax.dot_general(keyed, v_ref[:, columns], NN, preferred_element_type=F32)
        msg_ref[pl.ds(pl.multiple_of(head * size, size), size), :] = local


def local_states(seg, exponent, keep, k, v, heads, group):
    tokens, size = k.shape[0], k.shape[1] // heads
    rows = heads * size + heads + 8
    wide = pl.BlockSpec((tokens, group * size), lambda i: (0, i))
    whole = lambda shape: pl.BlockSpec(shape, lambda i: (0, 0))
    return pl.pallas_call(
        functools.partial(state_kernel, heads),
        grid=(heads // group,),
        in_specs=[whole((1, tokens)), whole((1, heads)), whole((heads, tokens)), wide, wide],
        out_specs=[whole((rows, size)), whole((heads, tokens))],
        out_shape=[
            jax.ShapeDtypeStruct((rows, size), F32),
            jax.ShapeDtypeStruct((heads, tokens), F32),
        ],
        scratch_shapes=[pltpu.VMEM((heads, tokens), F32)],
        compiler_params=pltpu.CompilerParams(vmem_limit_bytes=16 * MIB),
        cost_estimate=pl.CostEstimate(
            flops=2 * tokens * heads * size * size, bytes_accessed=5 * MIB, transcendentals=0
        ),
        name="local_states",
    )(seg, exponent, keep, k, v)


def join_kernel(heads, order_ref, mine_ref, other_ref, out_ref):
    size = mine_ref.shape[1]
    top = heads * size
    mine_later = order_ref[0] == 1
    final_mine, final_other = mine_ref[top : top + heads, :], other_ref[top : top + heads, :]
    end_mine, end_other = mine_ref[top + heads :, :], other_ref[top + heads :, :]
    same = jnp.where(end_mine[:1] == end_other[:1], 1.0, 0.0)
    scale_mine = jnp.where(mine_later, 1.0, jnp.exp(final_other) * same)
    scale_other = jnp.where(mine_later, jnp.exp(final_mine) * same, 1.0)
    for head in range(heads):
        rows = slice(head * size, (head + 1) * size)
        out_ref[rows, :] = (
            scale_mine[head : head + 1] * mine_ref[rows, :]
            + scale_other[head : head + 1] * other_ref[rows, :]
        )
    out_ref[top : top + heads, :] = final_mine + final_other
    out_ref[top + heads :, :] = jnp.where(mine_later, end_mine, end_other)


def joined(order, mine, other, heads):
    rows, size = mine.shape
    return pl.pallas_call(
        functools.partial(join_kernel, heads),
        in_specs=[pl.BlockSpec(memory_space=pltpu.SMEM)]
        + [pl.BlockSpec(memory_space=pltpu.VMEM)] * 2,
        out_specs=pl.BlockSpec(memory_space=pltpu.VMEM),
        out_shape=jax.ShapeDtypeStruct((rows, size), F32),
        compiler_params=pltpu.CompilerParams(vmem_limit_bytes=16 * MIB),
        cost_estimate=pl.CostEstimate(
            flops=3 * rows * size, bytes_accessed=12 * rows * size, transcendentals=0
        ),
        name="join_windows",
    )(order, mine, other)


def intra_kernel(seg_ref, a_ref, q_ref, k_ref, v_ref, o_ref, mask_ref):
    tokens = seg_ref.shape[1]
    size = 128
    group = q_ref.shape[1] // size
    step = pl.program_id(0)
    block = min(tokens, 256)

    @pl.when(step == 0)
    def _():
        seg = seg_ref[...].astype(F32)
        column = as_column(seg, 128)
        for start in range(0, tokens, 128):
            across = lax.broadcasted_iota(jnp.int32, (tokens, 128), 1) + start
            down = lax.broadcasted_iota(jnp.int32, (tokens, 128), 0)
            seen = (column == seg[:, start : start + 128]) & (across <= down)
            mask_ref[:, start : start + 128] = jnp.where(seen, 0.0, -1e30)

    for j in range(group):
        head = step * group + j
        columns = slice(j * size, (j + 1) * size)
        a_row = a_ref[pl.ds(head, 1), :] * 1.4426950408889634
        a_column = as_column(a_row, 128)
        for start in range(0, tokens, block):
            here, upto = slice(start, start + block), slice(0, start + block)
            scores = lax.dot_general(
                q_ref[here, columns], k_ref[upto, columns], NT, preferred_element_type=F32
            )
            spread = jnp.concatenate([a_column[here]] * ((start + block) // 128), axis=1)
            weight = jnp.exp2(spread - a_row[:, upto] + mask_ref[here, upto])
            probs = (scores * weight).astype(BF16)
            o_ref[here, columns] = lax.dot_general(
                probs, v_ref[upto, columns], NN, preferred_element_type=F32
            )


def intra(seg, a, q, k, v, heads, group):
    tokens, size = k.shape[0], k.shape[1] // heads
    wide = pl.BlockSpec((tokens, group * size), lambda i: (0, i))
    whole = lambda shape: pl.BlockSpec(shape, lambda i: (0, 0))
    return pl.pallas_call(
        intra_kernel,
        grid=(heads // group,),
        in_specs=[whole((1, tokens)), whole((heads, tokens)), wide, wide, wide],
        out_specs=wide,
        out_shape=jax.ShapeDtypeStruct((tokens, heads * size), F32),
        scratch_shapes=[pltpu.VMEM((tokens, tokens), F32)],
        compiler_params=pltpu.CompilerParams(vmem_limit_bytes=24 * MIB),
        cost_estimate=pl.CostEstimate(
            flops=3 * tokens * tokens * heads * size,
            bytes_accessed=10 * MIB,
            transcendentals=tokens * tokens * heads,
        ),
        name="intra_span",
    )(seg, a, q, k, v)


def final_kernel(
    order_ref,
    seg_ref,
    a_ref,
    gain_ref,
    own_final_ref,
    own_end_ref,
    pair_final_ref,
    pair_end_ref,
    before_end_ref,
    own_ref,
    pair_ref,
    before_ref,
    o_ref,
    q_ref,
    g_ref,
    gated_ref,
    snap_ref,
):
    size = own_ref.shape[1]
    group = q_ref.shape[1] // size
    step = pl.program_id(0)
    second = order_ref[0] == 1
    own_end, pair_end, before_end = own_end_ref[:1], pair_end_ref[:1], before_end_ref[:1]
    previous = jnp.where(second, pair_end, before_end)
    kept = jnp.where(own_end == previous, 1.0, 0.0)
    bridged = jnp.where(pair_end == before_end, 1.0, 0.0)
    valid = seg_ref[...].astype(F32) == previous[:, :1]
    for j in range(group):
        head = step * group + j
        columns = slice(j * size, (j + 1) * size)
        rows = slice(j * size, (j + 1) * size)
        pair_decay = jnp.exp(pair_final_ref[pl.ds(head, 1), :])
        own_decay = jnp.exp(own_final_ref[pl.ds(head, 1), :])
        from_before = jnp.where(second, bridged * pair_decay, 1.0)
        from_pair = jnp.where(second, 1.0, 0.0)
        state = from_before * before_ref[rows, :] + from_pair * pair_ref[rows, :]
        snap_ref[0, j] = (kept * own_decay) * state + own_ref[rows, :]
        high = state.astype(BF16)
        low = (state - high.astype(F32)).astype(BF16)
        q = q_ref[:, columns]
        inter = lax.dot_general(
            jnp.concatenate([q, q], axis=1),
            jnp.concatenate([high, low], axis=0),
            NN,
            preferred_element_type=F32,
        )
        decay = jnp.where(valid, jnp.exp(a_ref[pl.ds(head, 1), :]), 0.0)
        mixed = o_ref[:, columns] + inter * as_column(decay, size)
        mean_square = jnp.mean(mixed * mixed, axis=1, keepdims=True)
        g = g_ref[:, columns].astype(F32)
        gain = gain_ref[:, columns]
        gated = mixed * lax.rsqrt(mean_square + 1e-06) * gain / (1.0 + jnp.exp(-g))
        gated_ref[:, columns] = gated.astype(BF16)


def finish(order, seg, a, gain, own, pair, before, o, q, g, heads, group):
    tokens, size = q.shape[0], q.shape[1] // heads
    wide = pl.BlockSpec((tokens, group * size), lambda i: (0, i))
    whole = lambda shape: pl.BlockSpec(shape, lambda i: (0, 0))
    finals = pl.BlockSpec((heads, size), lambda i: (size, 0))
    ends = pl.BlockSpec((8, size), lambda i: ((heads * size + heads) // 8, 0))
    states = pl.BlockSpec((group * size, size), lambda i: (i, 0))
    return pl.pallas_call(
        final_kernel,
        grid=(heads // group,),
        in_specs=[
            pl.BlockSpec(memory_space=pltpu.SMEM),
            whole((1, tokens)),
            whole((heads, tokens)),
            pl.BlockSpec((1, group * size), lambda i: (0, i)),
            finals,
            ends,
            finals,
            ends,
            ends,
            states,
            states,
            states,
            wide,
            wide,
            wide,
        ],
        out_specs=[wide, pl.BlockSpec((1, group, size, size), lambda i: (0, i, 0, 0))],
        out_shape=[
            jax.ShapeDtypeStruct((tokens, heads * size), BF16),
            jax.ShapeDtypeStruct((1, heads, size, size), F32),
        ],
        compiler_params=pltpu.CompilerParams(vmem_limit_bytes=24 * MIB),
        cost_estimate=pl.CostEstimate(
            flops=4 * tokens * heads * size * size,
            bytes_accessed=14 * MIB,
            transcendentals=2 * tokens * heads * size,
        ),
        name="finish",
    )(order, seg, a, gain, own, own, pair, pair, before, own, pair, before, o, q, g)


def shards(q, k, v, g, segment, decay_exponent, retention, norm_gain):
    heads = decay_exponent.shape[0]
    tokens = q.shape[0]
    count = lax.axis_size("seq")
    place = lax.axis_index("seq")
    reach = max(1, count // 4)
    seg = segment.reshape(1, tokens)
    gain = norm_gain.reshape(1, -1)
    order = lax.rem(place, 2).astype(jnp.int32).reshape(1)

    own, a = local_states(seg, decay_exponent.reshape(1, heads), retention, k, v, heads, 4)
    swap = [(c, c ^ 1) for c in range(count)]
    pair = lax.ppermute(own, "seq", swap)
    both = joined(order, own, pair, heads)
    before = lax.ppermute(both, "seq", [(c, c + 2) for c in range(count - 2)])
    window = 2
    while window < reach:
        far = lax.ppermute(before, "seq", [(c, c + window) for c in range(count - window)])
        before = joined(jnp.ones((1,), jnp.int32), before, far, heads)
        window *= 2
    o = intra(seg, a, q, k, v, heads, 4)
    gated, snapshots = finish(order, seg, a, gain, own, pair, before, o, q, g, heads, 4)
    return gated, snapshots


def solution(mesh):
    placed = (
        P(("groups", "seq"), "wt"),
        P(("groups", "seq"), "wt"),
        P(("groups", "seq"), "wt"),
        P(("groups", "seq"), "wt"),
        P(("groups", "seq")),
        P("wt"),
        P("wt", ("groups", "seq")),
        P("wt"),
    )
    return jax.shard_map(
        shards,
        mesh=mesh,
        in_specs=placed,
        out_specs=(P(("groups", "seq"), "wt"), P(("groups", "seq"), "wt", None, None)),
        check_vma=False,
    )
```

```python
import functools

import jax
import jax.numpy as jnp
from jax import lax
from jax.experimental import pallas as pl
from jax.experimental.pallas import tpu as pltpu
from jax.sharding import PartitionSpec as P

F32 = jnp.float32
BF16 = jnp.bfloat16
NN = (((1,), (0,)), ((), ()))
NT = (((1,), (1,)), ((), ()))
MIB = 1 << 20
FIRST_LIMIT = 62 * MIB


def vmem_spec(shape, index_map):
    return pl.BlockSpec(shape, index_map)


def as_column(row, lanes):
    return jnp.broadcast_to(row, (lanes, row.shape[1])).T


def meta_rows(heads):
    return -(-(heads + 1) // 8) * 8


def put_message(msg_ref, first, heads, size, w_ref, finals, end, k_ref, v_ref):
    top = heads * size
    for j in range(heads):
        columns = slice(j * size, (j + 1) * size)
        weight = w_ref[first + j : first + j + 1, :]
        keyed = (k_ref[:, columns].astype(F32).T * weight).astype(BF16)
        msg_ref[columns, :] = lax.dot_general(
            keyed, v_ref[:, columns], NN, preferred_element_type=F32
        )
    msg_ref[top : top + heads, :] = jnp.broadcast_to(finals, (heads, size))
    below = meta_rows(heads) - heads
    msg_ref[top + heads :, :] = jnp.broadcast_to(end.astype(F32), (below, size))


def first_kernel(
    heads,
    chunk,
    seg_hbm,
    exponent_hbm,
    keep_hbm,
    k_hbm,
    v_hbm,
    msg_ref,
    a_ref,
    w_ref,
    seg_ref,
    exponent_ref,
    keep_ref,
    k_ref,
    v_ref,
    sems,
):
    tokens = seg_ref.shape[1]
    size = msg_ref.shape[1]
    wide = pl.ds(0, chunk * size)
    copies = [
        pltpu.make_async_copy(source, target, sems.at[i])
        for i, (source, target) in enumerate(
            [
                (keep_hbm, keep_ref),
                (exponent_hbm, exponent_ref),
                (seg_hbm, seg_ref),
                (k_hbm.at[:, wide], k_ref),
                (v_hbm.at[:, wide], v_ref),
            ]
        )
    ]
    for copy in copies:
        copy.start()
    earlier = lax.broadcasted_iota(jnp.int32, (tokens, tokens), 0)
    later = lax.broadcasted_iota(jnp.int32, (tokens, tokens), 1)
    upper = jnp.where(earlier <= later, 1.0, 0.0).astype(BF16)
    across = lax.broadcasted_iota(jnp.int32, (heads, heads), 1)
    down = lax.broadcasted_iota(jnp.int32, (heads, heads), 0)
    for copy in copies[:3]:
        copy.wait()
    spread = jnp.broadcast_to(exponent_ref[...], (heads, heads))
    exponent = jnp.sum(jnp.where(across == down, spread, 0).astype(F32), axis=1, keepdims=True)
    a = -jnp.exp2(-exponent) + jnp.log(keep_ref[...])
    high = a.astype(BF16)
    rest = a - high.astype(F32)
    middle = rest.astype(BF16)
    low = (rest - middle.astype(F32)).astype(BF16)
    parts = jnp.concatenate([high, middle, low], axis=0)
    sums = lax.dot_general(parts, upper, NN, preferred_element_type=F32)
    cumulative = sums[:heads] + (sums[heads : 2 * heads] + sums[2 * heads :])
    a_ref[...] = cumulative
    final = cumulative[:, tokens - 1 :]
    seg = seg_ref[...]
    last = seg[:, tokens - 1 :]
    w_ref[...] = jnp.where(seg == last, jnp.exp(final - cumulative), 0.0)
    for copy in copies[3:]:
        copy.wait()
    put_message(msg_ref, 0, chunk, size, w_ref, final[:chunk], last, k_ref, v_ref)


def first_message(seg, exponent, keep, k, v, heads, chunk):
    tokens, size = k.shape[0], k.shape[1] // heads
    rows = chunk * size + meta_rows(chunk)
    return pl.pallas_call(
        functools.partial(first_kernel, heads, chunk),
        in_specs=[pl.BlockSpec(memory_space=pltpu.HBM)] * 5,
        out_specs=[pl.BlockSpec(memory_space=pltpu.VMEM)] * 3,
        out_shape=[
            jax.ShapeDtypeStruct((rows, size), F32),
            jax.ShapeDtypeStruct((heads, tokens), F32),
            jax.ShapeDtypeStruct((heads, tokens), F32),
        ],
        scratch_shapes=[
            pltpu.VMEM((1, tokens), jnp.int32),
            pltpu.VMEM((1, heads), jnp.int32),
            pltpu.VMEM((heads, tokens), F32),
            pltpu.VMEM((tokens, chunk * size), BF16),
            pltpu.VMEM((tokens, chunk * size), BF16),
            pltpu.SemaphoreType.DMA((5,)),
        ],
        compiler_params=pltpu.CompilerParams(vmem_limit_bytes=FIRST_LIMIT),
        cost_estimate=pl.CostEstimate(
            flops=2 * tokens * chunk * size * size, bytes_accessed=2 * MIB, transcendentals=0
        ),
        name="first_message",
    )(seg, exponent, keep, k, v)


def next_kernel(
    first, heads, k_hbm, v_hbm, seg_ref, a_ref, w_ref, gate_ref, msg_ref, k_ref, v_ref, sems
):
    tokens = seg_ref.shape[1]
    size = msg_ref.shape[1]
    wide = pl.ds(first * size, heads * size)
    k_copy = pltpu.make_async_copy(k_hbm.at[:, wide], k_ref, sems.at[0])
    v_copy = pltpu.make_async_copy(v_hbm.at[:, wide], v_ref, sems.at[1])
    k_copy.start()
    v_copy.start()
    final = a_ref[first : first + heads, tokens - 1 :]
    last = seg_ref[:, tokens - 1 :]
    k_copy.wait()
    v_copy.wait()
    put_message(msg_ref, first, heads, size, w_ref, final, last, k_ref, v_ref)


def next_message(k, v, seg, a, w, gate, first, heads):
    tokens, size = k.shape[0], k.shape[1] // a.shape[0]
    rows = heads * size + meta_rows(heads)
    return pl.pallas_call(
        functools.partial(next_kernel, first, heads),
        in_specs=[pl.BlockSpec(memory_space=pltpu.HBM)] * 2
        + [pl.BlockSpec(memory_space=pltpu.VMEM)] * 3
        + [pl.BlockSpec(memory_space=pl.ANY)],
        out_specs=pl.BlockSpec(memory_space=pltpu.VMEM),
        out_shape=jax.ShapeDtypeStruct((rows, size), F32),
        scratch_shapes=[
            pltpu.VMEM((tokens, heads * size), BF16),
            pltpu.VMEM((tokens, heads * size), BF16),
            pltpu.SemaphoreType.DMA((2,)),
        ],
        compiler_params=pltpu.CompilerParams(vmem_limit_bytes=16 * MIB),
        cost_estimate=pl.CostEstimate(
            flops=2 * tokens * heads * size * size, bytes_accessed=2 * MIB, transcendentals=0
        ),
        name="next_message",
    )(k, v, seg, a, w, gate)


def join_kernel(heads, order_ref, mine_ref, other_ref, *rest):
    out_ref = rest[-1]
    size = mine_ref.shape[1]
    top = heads * size
    mine_later = order_ref[0] == 1
    final_mine, final_other = mine_ref[top : top + heads, :], other_ref[top : top + heads, :]
    end_mine, end_other = mine_ref[top + heads :, :], other_ref[top + heads :, :]
    same = jnp.where(end_mine[:1] == end_other[:1], 1.0, 0.0)
    scale_mine = jnp.where(mine_later, 1.0, jnp.exp(final_other) * same)
    scale_other = jnp.where(mine_later, jnp.exp(final_mine) * same, 1.0)
    for head in range(heads):
        rows = slice(head * size, (head + 1) * size)
        out_ref[rows, :] = (
            scale_mine[head : head + 1] * mine_ref[rows, :]
            + scale_other[head : head + 1] * other_ref[rows, :]
        )
    out_ref[top : top + heads, :] = final_mine + final_other
    out_ref[top + heads :, :] = jnp.where(mine_later, end_mine, end_other)


def joined(order, mine, other, heads, after=()):
    rows, size = mine.shape
    return pl.pallas_call(
        functools.partial(join_kernel, heads),
        in_specs=[pl.BlockSpec(memory_space=pltpu.SMEM)]
        + [pl.BlockSpec(memory_space=pltpu.VMEM)] * 2
        + [pl.BlockSpec(memory_space=pl.ANY)] * len(after),
        out_specs=pl.BlockSpec(memory_space=pltpu.VMEM),
        out_shape=jax.ShapeDtypeStruct((rows, size), F32),
        compiler_params=pltpu.CompilerParams(vmem_limit_bytes=16 * MIB),
        cost_estimate=pl.CostEstimate(
            flops=3 * rows * size, bytes_accessed=12 * rows * size, transcendentals=0
        ),
        name="join_windows",
    )(order, mine, other, *after)


def make_mask(seg_ref, mask_ref):
    tokens = seg_ref.shape[1]
    seg = seg_ref[...].astype(F32)
    column = as_column(seg, 128)
    for start in range(0, tokens, 128):
        across = lax.broadcasted_iota(jnp.int32, (tokens, 128), 1) + start
        down = lax.broadcasted_iota(jnp.int32, (tokens, 128), 0)
        seen = (column == seg[:, start : start + 128]) & (across <= down)
        mask_ref[:, start : start + 128] = jnp.where(seen, 0.0, -1e30)


def intra_kernel(
    first, heads, seg_ref, a_ref, q_hbm, k_hbm, v_hbm, o_ref, mask_ref, q_ref, k_ref, v_ref, sems
):
    tokens = seg_ref.shape[1]
    size = q_ref.shape[1] // heads
    block = min(tokens, 256)
    wide = pl.ds(first * size, heads * size)
    copies = [
        pltpu.make_async_copy(source.at[:, wide], target, sems.at[i])
        for i, (source, target) in enumerate([(q_hbm, q_ref), (k_hbm, k_ref), (v_hbm, v_ref)])
    ]
    for copy in copies:
        copy.start()
    make_mask(seg_ref, mask_ref)
    for copy in copies:
        copy.wait()
    for j in range(heads):
        columns = slice(j * size, (j + 1) * size)
        a_row = a_ref[first + j : first + j + 1, :] * 1.4426950408889634
        a_column = as_column(a_row, 128)
        for start in range(0, tokens, block):
            here, upto = slice(start, start + block), slice(0, start + block)
            scores = lax.dot_general(
                q_ref[here, columns], k_ref[upto, columns], NT, preferred_element_type=F32
            )
            spread = jnp.concatenate([a_column[here]] * ((start + block) // 128), axis=1)
            weight = jnp.exp2(spread - a_row[:, upto] + mask_ref[here, upto])
            probs = (scores * weight).astype(BF16)
            o_ref[here, columns] = lax.dot_general(
                probs, v_ref[upto, columns], NN, preferred_element_type=F32
            )


def intra(seg, a, q, k, v, first, heads):
    tokens, size = k.shape[0], k.shape[1] // a.shape[0]
    return pl.pallas_call(
        functools.partial(intra_kernel, first, heads),
        in_specs=[pl.BlockSpec(memory_space=pltpu.VMEM)] * 2
        + [pl.BlockSpec(memory_space=pltpu.HBM)] * 3,
        out_specs=pl.BlockSpec(memory_space=pltpu.VMEM),
        out_shape=jax.ShapeDtypeStruct((tokens, heads * size), F32),
        scratch_shapes=[pltpu.VMEM((tokens, tokens), F32)]
        + [pltpu.VMEM((tokens, heads * size), BF16)] * 3
        + [pltpu.SemaphoreType.DMA((3,))],
        compiler_params=pltpu.CompilerParams(vmem_limit_bytes=24 * MIB),
        cost_estimate=pl.CostEstimate(
            flops=3 * tokens * tokens * heads * size,
            bytes_accessed=3 * MIB,
            transcendentals=tokens * tokens * heads,
        ),
        name="intra_span",
    )(seg, a, q, k, v)


def final_kernel(
    first,
    heads,
    order_ref,
    seg_ref,
    a_ref,
    own_ref,
    pair_ref,
    before_ref,
    o_ref,
    gain_ref,
    q_ref,
    g_ref,
    *rest,
):
    gated_ref, snap_ref, token_ref = rest[-3:]
    token_ref[...] = jnp.zeros_like(token_ref)
    size = own_ref.shape[1]
    top = heads * size
    second = order_ref[0] == 1
    ends = slice(top + heads, top + heads + 1)
    finals = slice(top, top + heads)
    own_end, pair_end, before_end = own_ref[ends, :], pair_ref[ends, :], before_ref[ends, :]
    previous = jnp.where(second, pair_end, before_end)
    kept = jnp.where(own_end == previous, 1.0, 0.0)
    bridged = jnp.where(pair_end == before_end, 1.0, 0.0)
    own_decay = jnp.exp(own_ref[finals, :]) * kept
    from_before = jnp.where(second, jnp.exp(pair_ref[finals, :]) * bridged, 1.0)
    from_pair = jnp.where(second, 1.0, 0.0)
    valid = seg_ref[...].astype(F32) == previous[:, :1]
    for j in range(heads):
        rows = columns = slice(j * size, (j + 1) * size)
        state = from_before[j : j + 1] * before_ref[rows, :] + from_pair * pair_ref[rows, :]
        snap_ref[0, j] = own_decay[j : j + 1] * state + own_ref[rows, :]
        high = state.astype(BF16)
        low = (state - high.astype(F32)).astype(BF16)
        q = q_ref[:, columns]
        inter = lax.dot_general(
            jnp.concatenate([q, q], axis=1),
            jnp.concatenate([high, low], axis=0),
            NN,
            preferred_element_type=F32,
        )
        decay = jnp.where(valid, jnp.exp(a_ref[first + j : first + j + 1, :]), 0.0)
        mixed = o_ref[:, columns] + inter * as_column(decay, size)
        mean_square = jnp.mean(mixed * mixed, axis=1, keepdims=True)
        g = g_ref[:, columns].astype(F32)
        gain = gain_ref[:, columns]
        gated = mixed * lax.rsqrt(mean_square + 1e-06) * gain / (1.0 + jnp.exp(-g))
        gated_ref[:, columns] = gated.astype(BF16)


def finish(order, seg, a, own, pair, before, o, gain, q, g, so_far, first, heads):
    tokens, total = q.shape[0], a.shape[0]
    size = q.shape[1] // total
    place = first // heads
    wide = lambda rows: pl.BlockSpec((rows, heads * size), lambda i: (0, place))
    vmem = pl.BlockSpec(memory_space=pltpu.VMEM)
    return pl.pallas_call(
        functools.partial(final_kernel, first, heads),
        grid=(1,),
        in_specs=[pl.BlockSpec(memory_space=pltpu.SMEM)]
        + [vmem] * 6
        + [wide(1), wide(tokens), wide(tokens)]
        + [pl.BlockSpec(memory_space=pl.ANY)] * len(so_far),
        out_specs=[
            wide(tokens),
            pl.BlockSpec((1, heads, size, size), lambda i: (0, place, 0, 0)),
            vmem,
        ],
        out_shape=[
            jax.ShapeDtypeStruct((tokens, total * size), BF16),
            jax.ShapeDtypeStruct((1, total, size, size), F32),
            jax.ShapeDtypeStruct((8, 128), F32),
        ],
        input_output_aliases={10 + i: i for i in range(len(so_far))},
        compiler_params=pltpu.CompilerParams(vmem_limit_bytes=24 * MIB),
        cost_estimate=pl.CostEstimate(
            flops=4 * tokens * heads * size * size,
            bytes_accessed=4 * MIB,
            transcendentals=2 * tokens * heads * size,
        ),
        name="finish",
    )(order, seg, a, own, pair, before, o, gain, q, g, *so_far)


def shards(q, k, v, g, segment, decay_exponent, retention, norm_gain):
    heads = decay_exponent.shape[0]
    tokens = q.shape[0]
    count = lax.axis_size("seq")
    place = lax.axis_index("seq")
    reach = max(1, count // 4)
    chunk = 4
    firsts = list(range(0, heads, chunk))
    seg = segment.reshape(1, tokens)
    gain = norm_gain.reshape(1, -1)
    order = lax.rem(place, 2).astype(jnp.int32).reshape(1)
    swap = [(c, c ^ 1) for c in range(count)]

    own, pair, both, before, o = {}, {}, {}, {}, {}
    tokens_of, so_far = {}, ()
    own[0], a, w = first_message(seg, decay_exponent.reshape(1, heads), retention, k, v, heads, chunk)
    pair[0] = lax.ppermute(own[0], "seq", swap)
    own[1] = next_message(k, v, seg, a, w, w, firsts[1], chunk)
    pair[1] = lax.ppermute(own[1], "seq", swap)
    for i, first in enumerate(firsts):
        o[i] = intra(seg, a, q, k, v, first, chunk)
        after = (o[i],) + ((tokens_of[i - 2],) if i > 1 else ())
        both[i] = joined(order, own[i], pair[i], chunk, after)
        before[i] = lax.ppermute(both[i], "seq", [(c, c + 2) for c in range(count - 2)])
        window = 2
        while window < reach:
            far = lax.ppermute(before[i], "seq", [(c, c + window) for c in range(count - window)])
            before[i] = joined(jnp.ones((1,), jnp.int32), before[i], far, chunk)
            window *= 2
        if i + 2 < len(firsts):
            own[i + 2] = next_message(k, v, seg, a, w, both[i], firsts[i + 2], chunk)
            pair[i + 2] = lax.ppermute(own[i + 2], "seq", swap)
        *so_far, tokens_of[i] = finish(
            order, seg, a, own[i], pair[i], before[i], o[i], gain, q, g, so_far, first, chunk
        )
    return tuple(so_far)


def solution(mesh):
    placed = (
        P(("groups", "seq"), "wt"),
        P(("groups", "seq"), "wt"),
        P(("groups", "seq"), "wt"),
        P(("groups", "seq"), "wt"),
        P(("groups", "seq")),
        P("wt"),
        P("wt", ("groups", "seq")),
        P("wt"),
    )
    return jax.shard_map(
        shards,
        mesh=mesh,
        in_specs=placed,
        out_specs=(P(("groups", "seq"), "wt"), P(("groups", "seq"), "wt", None, None)),
        check_vma=False,
    )
```

```python
import functools

import jax
import jax.numpy as jnp
from jax import lax
from jax.experimental import pallas as pl
from jax.experimental.pallas import tpu as pltpu
from jax.sharding import PartitionSpec as P

F32 = jnp.float32
BF16 = jnp.bfloat16
NN = (((1,), (0,)), ((), ()))
NT = (((1,), (1,)), ((), ()))
MIB = 1 << 20


def vmem_spec(shape, index_map):
    return pl.BlockSpec(shape, index_map)


def as_column(row, lanes):
    return jnp.broadcast_to(row, (lanes, row.shape[1])).T


def meta_rows(heads):
    return -(-(heads + 1) // 8) * 8


def put_message(msg_ref, first, heads, size, w_ref, finals, end, k_ref, v_ref):
    top = heads * size
    for j in range(heads):
        columns = slice(j * size, (j + 1) * size)
        weight = w_ref[first + j : first + j + 1, :]
        keyed = (k_ref[:, columns].astype(F32).T * weight).astype(BF16)
        msg_ref[columns, :] = lax.dot_general(
            keyed, v_ref[:, columns], NN, preferred_element_type=F32
        )
    msg_ref[top : top + heads, :] = jnp.broadcast_to(finals, (heads, size))
    below = meta_rows(heads) - heads
    msg_ref[top + heads :, :] = jnp.broadcast_to(end.astype(F32), (below, size))


def first_kernel(
    heads,
    chunk,
    seg_hbm,
    exponent_hbm,
    keep_hbm,
    k_hbm,
    v_hbm,
    msg_ref,
    a_ref,
    w_ref,
    seg_ref,
    exponent_ref,
    keep_ref,
    k_ref,
    v_ref,
    sems,
):
    tokens = seg_ref.shape[1]
    size = msg_ref.shape[1]
    wide = pl.ds(0, chunk * size)
    copies = [
        pltpu.make_async_copy(source, target, sems.at[i])
        for i, (source, target) in enumerate(
            [
                (keep_hbm, keep_ref),
                (exponent_hbm, exponent_ref),
                (seg_hbm, seg_ref),
                (k_hbm.at[:, wide], k_ref),
                (v_hbm.at[:, wide], v_ref),
            ]
        )
    ]
    for copy in copies:
        copy.start()
    earlier = lax.broadcasted_iota(jnp.int32, (tokens, tokens), 0)
    later = lax.broadcasted_iota(jnp.int32, (tokens, tokens), 1)
    upper = jnp.where(earlier <= later, 1.0, 0.0).astype(BF16)
    across = lax.broadcasted_iota(jnp.int32, (heads, heads), 1)
    down = lax.broadcasted_iota(jnp.int32, (heads, heads), 0)
    for copy in copies[:3]:
        copy.wait()
    spread = jnp.broadcast_to(exponent_ref[...], (heads, heads))
    exponent = jnp.sum(jnp.where(across == down, spread, 0).astype(F32), axis=1, keepdims=True)
    a = -jnp.exp2(-exponent) + jnp.log(keep_ref[...])
    high = a.astype(BF16)
    rest = a - high.astype(F32)
    middle = rest.astype(BF16)
    low = (rest - middle.astype(F32)).astype(BF16)
    parts = jnp.concatenate([high, middle, low], axis=0)
    sums = lax.dot_general(parts, upper, NN, preferred_element_type=F32)
    cumulative = sums[:heads] + (sums[heads : 2 * heads] + sums[2 * heads :])
    a_ref[...] = cumulative
    final = cumulative[:, tokens - 1 :]
    seg = seg_ref[...]
    last = seg[:, tokens - 1 :]
    w_ref[...] = jnp.where(seg == last, jnp.exp(final - cumulative), 0.0)
    for copy in copies[3:]:
        copy.wait()
    put_message(msg_ref, 0, chunk, size, w_ref, final[:chunk], last, k_ref, v_ref)


def first_message(seg, exponent, keep, k, v, heads, chunk):
    tokens, size = k.shape[0], k.shape[1] // heads
    rows = chunk * size + meta_rows(chunk)
    return pl.pallas_call(
        functools.partial(first_kernel, heads, chunk),
        in_specs=[pl.BlockSpec(memory_space=pltpu.HBM)] * 5,
        out_specs=[pl.BlockSpec(memory_space=pltpu.VMEM)] * 4,
        out_shape=[
            pltpu.VMEM((rows, size), F32),
            pltpu.VMEM((heads, tokens), F32),
            pltpu.VMEM((heads, tokens), F32),
            pltpu.VMEM((1, tokens), jnp.int32),
        ],
        scratch_shapes=[
            pltpu.VMEM((1, heads), jnp.int32),
            pltpu.VMEM((heads, tokens), F32),
            pltpu.VMEM((tokens, chunk * size), BF16),
            pltpu.VMEM((tokens, chunk * size), BF16),
            pltpu.SemaphoreType.DMA((5,)),
        ],
        compiler_params=pltpu.CompilerParams(vmem_limit_bytes=16 * MIB),
        cost_estimate=pl.CostEstimate(
            flops=2 * tokens * chunk * size * size, bytes_accessed=2 * MIB, transcendentals=0
        ),
        name="first_message",
    )(seg, exponent, keep, k, v)


def next_kernel(
    first, heads, k_hbm, v_hbm, seg_ref, a_ref, w_ref, gate_ref, msg_ref, k_ref, v_ref, sems
):
    tokens = seg_ref.shape[1]
    size = msg_ref.shape[1]
    wide = pl.ds(first * size, heads * size)
    k_copy = pltpu.make_async_copy(k_hbm.at[:, wide], k_ref, sems.at[0])
    v_copy = pltpu.make_async_copy(v_hbm.at[:, wide], v_ref, sems.at[1])
    k_copy.start()
    v_copy.start()
    final = a_ref[first : first + heads, tokens - 1 :]
    last = seg_ref[:, tokens - 1 :]
    k_copy.wait()
    v_copy.wait()
    put_message(msg_ref, first, heads, size, w_ref, final, last, k_ref, v_ref)


def next_message(k, v, seg, a, w, gate, first, heads):
    tokens, size = k.shape[0], k.shape[1] // a.shape[0]
    rows = heads * size + meta_rows(heads)
    return pl.pallas_call(
        functools.partial(next_kernel, first, heads),
        in_specs=[pl.BlockSpec(memory_space=pltpu.HBM)] * 2
        + [pl.BlockSpec(memory_space=pltpu.VMEM)] * 3
        + [pl.BlockSpec(memory_space=pl.ANY)],
        out_specs=pl.BlockSpec(memory_space=pltpu.VMEM),
        out_shape=pltpu.VMEM((rows, size), F32),
        scratch_shapes=[
            pltpu.VMEM((tokens, heads * size), BF16),
            pltpu.VMEM((tokens, heads * size), BF16),
            pltpu.SemaphoreType.DMA((2,)),
        ],
        compiler_params=pltpu.CompilerParams(vmem_limit_bytes=16 * MIB),
        cost_estimate=pl.CostEstimate(
            flops=2 * tokens * heads * size * size, bytes_accessed=2 * MIB, transcendentals=0
        ),
        name="next_message",
    )(k, v, seg, a, w, gate)


def join_kernel(heads, order_ref, mine_ref, other_ref, *rest):
    out_ref = rest[-1]
    size = mine_ref.shape[1]
    top = heads * size
    mine_later = order_ref[0] == 1
    final_mine, final_other = mine_ref[top : top + heads, :], other_ref[top : top + heads, :]
    end_mine, end_other = mine_ref[top + heads :, :], other_ref[top + heads :, :]
    same = jnp.where(end_mine[:1] == end_other[:1], 1.0, 0.0)
    scale_mine = jnp.where(mine_later, 1.0, jnp.exp(final_other) * same)
    scale_other = jnp.where(mine_later, jnp.exp(final_mine) * same, 1.0)
    for head in range(heads):
        rows = slice(head * size, (head + 1) * size)
        out_ref[rows, :] = (
            scale_mine[head : head + 1] * mine_ref[rows, :]
            + scale_other[head : head + 1] * other_ref[rows, :]
        )
    out_ref[top : top + heads, :] = final_mine + final_other
    out_ref[top + heads :, :] = jnp.where(mine_later, end_mine, end_other)


def joined(order, mine, other, heads, after=()):
    rows, size = mine.shape
    return pl.pallas_call(
        functools.partial(join_kernel, heads),
        in_specs=[pl.BlockSpec(memory_space=pltpu.SMEM)]
        + [pl.BlockSpec(memory_space=pltpu.VMEM)] * 2
        + [pl.BlockSpec(memory_space=pl.ANY)] * len(after),
        out_specs=pl.BlockSpec(memory_space=pltpu.VMEM),
        out_shape=pltpu.VMEM((rows, size), F32),
        compiler_params=pltpu.CompilerParams(vmem_limit_bytes=16 * MIB),
        cost_estimate=pl.CostEstimate(
            flops=3 * rows * size, bytes_accessed=12 * rows * size, transcendentals=0
        ),
        name="join_windows",
    )(order, mine, other, *after)


def make_mask(seg_ref, mask_ref):
    tokens = seg_ref.shape[1]
    seg = seg_ref[...].astype(F32)
    column = as_column(seg, 128)
    for start in range(0, tokens, 128):
        across = lax.broadcasted_iota(jnp.int32, (tokens, 128), 1) + start
        down = lax.broadcasted_iota(jnp.int32, (tokens, 128), 0)
        seen = (column == seg[:, start : start + 128]) & (across <= down)
        mask_ref[:, start : start + 128] = jnp.where(seen, 0.0, -1e30)


def intra_kernel(
    first, heads, seg_ref, a_ref, q_hbm, k_hbm, v_hbm, o_ref, mask_ref, q_ref, k_ref, v_ref, sems
):
    tokens = seg_ref.shape[1]
    size = q_ref.shape[1] // heads
    block = min(tokens, 256)
    wide = pl.ds(first * size, heads * size)
    copies = [
        pltpu.make_async_copy(source.at[:, wide], target, sems.at[i])
        for i, (source, target) in enumerate([(q_hbm, q_ref), (k_hbm, k_ref), (v_hbm, v_ref)])
    ]
    for copy in copies:
        copy.start()
    make_mask(seg_ref, mask_ref)
    for copy in copies:
        copy.wait()
    for j in range(heads):
        columns = slice(j * size, (j + 1) * size)
        a_row = a_ref[first + j : first + j + 1, :] * 1.4426950408889634
        a_column = as_column(a_row, 128)
        for start in range(0, tokens, block):
            here, upto = slice(start, start + block), slice(0, start + block)
            scores = lax.dot_general(
                q_ref[here, columns], k_ref[upto, columns], NT, preferred_element_type=F32
            )
            spread = jnp.concatenate([a_column[here]] * ((start + block) // 128), axis=1)
            weight = jnp.exp2(spread - a_row[:, upto] + mask_ref[here, upto])
            probs = (scores * weight).astype(BF16)
            o_ref[here, columns] = lax.dot_general(
                probs, v_ref[upto, columns], NN, preferred_element_type=F32
            )


def intra(seg, a, q, k, v, first, heads):
    tokens, size = k.shape[0], k.shape[1] // a.shape[0]
    return pl.pallas_call(
        functools.partial(intra_kernel, first, heads),
        in_specs=[pl.BlockSpec(memory_space=pltpu.VMEM)] * 2
        + [pl.BlockSpec(memory_space=pltpu.HBM)] * 3,
        out_specs=pl.BlockSpec(memory_space=pltpu.VMEM),
        out_shape=pltpu.VMEM((tokens, heads * size), F32),
        scratch_shapes=[pltpu.VMEM((tokens, tokens), F32)]
        + [pltpu.VMEM((tokens, heads * size), BF16)] * 3
        + [pltpu.SemaphoreType.DMA((3,))],
        compiler_params=pltpu.CompilerParams(vmem_limit_bytes=24 * MIB),
        cost_estimate=pl.CostEstimate(
            flops=3 * tokens * tokens * heads * size,
            bytes_accessed=3 * MIB,
            transcendentals=tokens * tokens * heads,
        ),
        name="intra_span",
    )(seg, a, q, k, v)


def final_kernel(
    first,
    heads,
    order_ref,
    seg_ref,
    a_ref,
    own_ref,
    pair_ref,
    before_ref,
    o_ref,
    gain_ref,
    q_ref,
    g_ref,
    *rest,
):
    gated_ref, snap_ref, token_ref = rest[-3:]
    token_ref[...] = jnp.zeros_like(token_ref)
    size = own_ref.shape[1]
    top = heads * size
    second = order_ref[0] == 1
    ends = slice(top + heads, top + heads + 1)
    finals = slice(top, top + heads)
    own_end, pair_end, before_end = own_ref[ends, :], pair_ref[ends, :], before_ref[ends, :]
    previous = jnp.where(second, pair_end, before_end)
    kept = jnp.where(own_end == previous, 1.0, 0.0)
    bridged = jnp.where(pair_end == before_end, 1.0, 0.0)
    own_decay = jnp.exp(own_ref[finals, :]) * kept
    from_before = jnp.where(second, jnp.exp(pair_ref[finals, :]) * bridged, 1.0)
    from_pair = jnp.where(second, 1.0, 0.0)
    valid = seg_ref[...].astype(F32) == previous[:, :1]
    for j in range(heads):
        rows = columns = slice(j * size, (j + 1) * size)
        state = from_before[j : j + 1] * before_ref[rows, :] + from_pair * pair_ref[rows, :]
        snap_ref[0, j] = own_decay[j : j + 1] * state + own_ref[rows, :]
        high = state.astype(BF16)
        low = (state - high.astype(F32)).astype(BF16)
        q = q_ref[:, columns]
        inter = lax.dot_general(
            jnp.concatenate([q, q], axis=1),
            jnp.concatenate([high, low], axis=0),
            NN,
            preferred_element_type=F32,
        )
        decay = jnp.where(valid, jnp.exp(a_ref[first + j : first + j + 1, :]), 0.0)
        mixed = o_ref[:, columns] + inter * as_column(decay, size)
        mean_square = jnp.mean(mixed * mixed, axis=1, keepdims=True)
        g = g_ref[:, columns].astype(F32)
        gain = gain_ref[:, columns]
        gated = mixed * lax.rsqrt(mean_square + 1e-06) * gain / (1.0 + jnp.exp(-g))
        gated_ref[:, columns] = gated.astype(BF16)


def finish(order, seg, a, own, pair, before, o, gain, q, g, so_far, first, heads):
    tokens, total = q.shape[0], a.shape[0]
    size = q.shape[1] // total
    place = first // heads
    wide = lambda rows: pl.BlockSpec((rows, heads * size), lambda i: (0, place))
    vmem = pl.BlockSpec(memory_space=pltpu.VMEM)
    return pl.pallas_call(
        functools.partial(final_kernel, first, heads),
        grid=(1,),
        in_specs=[pl.BlockSpec(memory_space=pltpu.SMEM)]
        + [vmem] * 6
        + [wide(1), wide(tokens), wide(tokens)]
        + [pl.BlockSpec(memory_space=pl.ANY)] * len(so_far),
        out_specs=[
            wide(tokens),
            pl.BlockSpec((1, heads, size, size), lambda i: (0, place, 0, 0)),
            vmem,
        ],
        out_shape=[
            jax.ShapeDtypeStruct((tokens, total * size), BF16),
            jax.ShapeDtypeStruct((1, total, size, size), F32),
            jax.ShapeDtypeStruct((8, 128), F32),
        ],
        input_output_aliases={10 + i: i for i in range(len(so_far))},
        compiler_params=pltpu.CompilerParams(vmem_limit_bytes=24 * MIB),
        cost_estimate=pl.CostEstimate(
            flops=4 * tokens * heads * size * size,
            bytes_accessed=4 * MIB,
            transcendentals=2 * tokens * heads * size,
        ),
        name="finish",
    )(order, seg, a, own, pair, before, o, gain, q, g, *so_far)


def shards(q, k, v, g, segment, decay_exponent, retention, norm_gain):
    heads = decay_exponent.shape[0]
    tokens = q.shape[0]
    count = lax.axis_size("seq")
    place = lax.axis_index("seq")
    reach = max(1, count // 4)
    chunk = 4
    firsts = list(range(0, heads, chunk))
    seg = segment.reshape(1, tokens)
    gain = norm_gain.reshape(1, -1)
    far = lambda x: pltpu.with_memory_space_constraint(x, pltpu.HBM)
    q_far, k, v, seg, retention = far(q), far(k), far(v), far(seg), far(retention)
    exponent = far(decay_exponent.reshape(1, heads))
    order = lax.rem(place, 2).astype(jnp.int32).reshape(1)
    swap = [(c, c ^ 1) for c in range(count)]

    own, pair, both, before, o, done = {}, {}, {}, {}, {}, {}
    result = ()
    last = len(firsts) - 1

    def exchange(i):
        pair[i] = lax.ppermute(own[i], "seq", swap)

    def inside(i):
        o[i] = intra(seg, a, q_far, k, v, firsts[i], chunk)

    def pass_on(i, after):
        both[i] = joined(order, own[i], pair[i], chunk, after)
        before[i] = lax.ppermute(both[i], "seq", [(c, c + 2) for c in range(count - 2)])
        window = 2
        while window < reach:
            past = lax.ppermute(before[i], "seq", [(c, c + window) for c in range(count - window)])
            before[i] = joined(jnp.ones((1,), jnp.int32), before[i], past, chunk)
            window *= 2

    own[0], a, w, seg = first_message(seg, exponent, retention, k, v, heads, chunk)
    exchange(0)
    own[1] = next_message(k, v, seg, a, w, w, firsts[1], chunk)
    exchange(1)
    inside(0)
    for i, first in enumerate(firsts):
        if i < last:
            inside(i + 1)
        pass_on(i, (o[0], o[min(i + 1, last)]) + ((done[0],) if i == last else ()))
        if i + 2 <= last:
            own[i + 2] = next_message(k, v, seg, a, w, both[i], firsts[i + 2], chunk)
            exchange(i + 2)
        for j in {last - 1: (0,), last: range(1, last + 1)}.get(i, ()):
            *result, done[j] = finish(
                order, seg, a, own[j], pair[j], before[j], o[j], gain, q, g, result, firsts[j], chunk
            )
    return tuple(result)


def solution(mesh):
    placed = (
        P(("groups", "seq"), "wt"),
        P(("groups", "seq"), "wt"),
        P(("groups", "seq"), "wt"),
        P(("groups", "seq"), "wt"),
        P(("groups", "seq")),
        P("wt"),
        P("wt", ("groups", "seq")),
        P("wt"),
    )
    return jax.shard_map(
        shards,
        mesh=mesh,
        in_specs=placed,
        out_specs=(P(("groups", "seq"), "wt"), P(("groups", "seq"), "wt", None, None)),
        check_vma=False,
    )
```

```python
import functools

import jax
import jax.numpy as jnp
from jax import lax
from jax.experimental import pallas as pl
from jax.experimental.pallas import tpu as pltpu
from jax.sharding import PartitionSpec as P

F32 = jnp.float32
BF16 = jnp.bfloat16
NN = (((1,), (0,)), ((), ()))
NT = (((1,), (1,)), ((), ()))
MIB = 1 << 20


def vmem_spec(shape, index_map):
    return pl.BlockSpec(shape, index_map)


def as_column(row, lanes):
    return jnp.broadcast_to(row, (lanes, row.shape[1])).T


def meta_rows(heads):
    return -(-(heads + 1) // 8) * 8


def put_message(msg_ref, first, heads, size, w_ref, finals, end, k_ref, v_ref):
    top = heads * size
    for j in range(heads):
        columns = slice(j * size, (j + 1) * size)
        weight = w_ref[first + j : first + j + 1, :]
        keyed = (k_ref[:, columns].astype(F32).T * weight).astype(BF16)
        msg_ref[columns, :] = lax.dot_general(
            keyed, v_ref[:, columns], NN, preferred_element_type=F32
        )
    msg_ref[top : top + heads, :] = jnp.broadcast_to(finals, (heads, size))
    below = meta_rows(heads) - heads
    msg_ref[top + heads :, :] = jnp.broadcast_to(end.astype(F32), (below, size))


def first_kernel(
    heads,
    chunk,
    seg_hbm,
    exponent_hbm,
    keep_hbm,
    k_hbm,
    v_hbm,
    msg_ref,
    a_ref,
    w_ref,
    seg_ref,
    k_ref,
    v_ref,
    exponent_ref,
    keep_ref,
    sems,
):
    tokens = seg_ref.shape[1]
    size = msg_ref.shape[1]
    wide = pl.ds(0, chunk * size)
    copies = [
        pltpu.make_async_copy(source, target, sems.at[i])
        for i, (source, target) in enumerate(
            [
                (keep_hbm, keep_ref),
                (exponent_hbm, exponent_ref),
                (seg_hbm, seg_ref),
                (k_hbm.at[:, wide], k_ref),
                (v_hbm.at[:, wide], v_ref),
            ]
        )
    ]
    for copy in copies:
        copy.start()
    earlier = lax.broadcasted_iota(jnp.int32, (tokens, tokens), 0)
    later = lax.broadcasted_iota(jnp.int32, (tokens, tokens), 1)
    upper = jnp.where(earlier <= later, 1.0, 0.0).astype(BF16)
    across = lax.broadcasted_iota(jnp.int32, (heads, heads), 1)
    down = lax.broadcasted_iota(jnp.int32, (heads, heads), 0)
    for copy in copies[:3]:
        copy.wait()
    spread = jnp.broadcast_to(exponent_ref[...], (heads, heads))
    exponent = jnp.sum(jnp.where(across == down, spread, 0).astype(F32), axis=1, keepdims=True)
    a = -jnp.exp2(-exponent) + jnp.log(keep_ref[...])
    high = a.astype(BF16)
    rest = a - high.astype(F32)
    middle = rest.astype(BF16)
    low = (rest - middle.astype(F32)).astype(BF16)
    parts = jnp.concatenate([high, middle, low], axis=0)
    sums = lax.dot_general(parts, upper, NN, preferred_element_type=F32)
    cumulative = sums[:heads] + (sums[heads : 2 * heads] + sums[2 * heads :])
    a_ref[...] = cumulative
    final = cumulative[:, tokens - 1 :]
    seg = seg_ref[...]
    last = seg[:, tokens - 1 :]
    w_ref[...] = jnp.where(seg == last, jnp.exp(final - cumulative), 0.0)
    for copy in copies[3:]:
        copy.wait()
    put_message(msg_ref, 0, chunk, size, w_ref, final[:chunk], last, k_ref, v_ref)


def first_message(seg, exponent, keep, k, v, heads, chunk):
    tokens, size = k.shape[0], k.shape[1] // heads
    rows = chunk * size + meta_rows(chunk)
    return pl.pallas_call(
        functools.partial(first_kernel, heads, chunk),
        in_specs=[pl.BlockSpec(memory_space=pltpu.HBM)] * 5,
        out_specs=[pl.BlockSpec(memory_space=pltpu.VMEM)] * 6,
        out_shape=[
            pltpu.VMEM((rows, size), F32),
            pltpu.VMEM((heads, tokens), F32),
            pltpu.VMEM((heads, tokens), F32),
            pltpu.VMEM((1, tokens), jnp.int32),
            pltpu.VMEM((tokens, chunk * size), BF16),
            pltpu.VMEM((tokens, chunk * size), BF16),
        ],
        scratch_shapes=[
            pltpu.VMEM((1, heads), jnp.int32),
            pltpu.VMEM((heads, tokens), F32),
            pltpu.SemaphoreType.DMA((5,)),
        ],
        compiler_params=pltpu.CompilerParams(vmem_limit_bytes=16 * MIB),
        cost_estimate=pl.CostEstimate(
            flops=2 * tokens * chunk * size * size, bytes_accessed=2 * MIB, transcendentals=0
        ),
        name="first_message",
    )(seg, exponent, keep, k, v)


def prepare_kernel(
    chunk, seg_ref, a_ref, w_ref, q_hbm, k_hbm, v_hbm, mask_ref, *refs
):
    tokens = seg_ref.shape[1]
    heads = a_ref.shape[0]
    count = heads // chunk
    messages, refs = refs[: count - 1], refs[count - 1 :]
    k_refs, refs = refs[: count - 1], refs[count - 1 :]
    v_refs, refs = refs[: count - 1], refs[count - 1 :]
    q_refs, sems = refs[:count], refs[count]
    size = messages[0].shape[1]
    wide = lambda i: pl.ds(i * chunk * size, chunk * size)
    copies = []
    for i in range(1, count):
        for source, target in ((k_hbm, k_refs[i - 1]), (v_hbm, v_refs[i - 1])):
            copies.append((source.at[:, wide(i)], target))
    for i in range(count):
        copies.append((q_hbm.at[:, wide(i)], q_refs[i]))
    copies = [pltpu.make_async_copy(*pair, sems.at[i]) for i, pair in enumerate(copies)]
    for copy in copies:
        copy.start()
    make_mask(seg_ref, mask_ref)
    last = seg_ref[:, tokens - 1 :]
    for i in range(1, count):
        copies[2 * i - 2].wait()
        copies[2 * i - 1].wait()
        first = i * chunk
        final = a_ref[first : first + chunk, tokens - 1 :]
        put_message(
            messages[i - 1], first, chunk, size, w_ref, final, last, k_refs[i - 1], v_refs[i - 1]
        )
    for copy in copies[2 * count - 2 :]:
        copy.wait()


def prepare(seg, a, w, q, k, v, chunk):
    heads = a.shape[0]
    tokens, size = k.shape[0], k.shape[1] // heads
    count = heads // chunk
    rows = chunk * size + meta_rows(chunk)
    near = pltpu.VMEM((tokens, chunk * size), BF16)
    mask, *rest = pl.pallas_call(
        functools.partial(prepare_kernel, chunk),
        in_specs=[pl.BlockSpec(memory_space=pltpu.VMEM)] * 3
        + [pl.BlockSpec(memory_space=pltpu.HBM)] * 3,
        out_specs=[pl.BlockSpec(memory_space=pltpu.VMEM)] * (4 * count - 2),
        out_shape=[pltpu.VMEM((tokens, tokens), F32)]
        + [pltpu.VMEM((rows, size), F32)] * (count - 1)
        + [near] * (3 * count - 2),
        scratch_shapes=[pltpu.SemaphoreType.DMA((3 * count - 2,))],
        compiler_params=pltpu.CompilerParams(vmem_limit_bytes=16 * MIB),
        cost_estimate=pl.CostEstimate(
            flops=2 * tokens * heads * size * size, bytes_accessed=6 * MIB, transcendentals=0
        ),
        name="prepare",
    )(seg, a, w, q, k, v)
    messages, rest = rest[: count - 1], rest[count - 1 :]
    return mask, messages, rest[: count - 1], rest[count - 1 : 2 * count - 2], rest[2 * count - 2 :]


def join_kernel(heads, order_ref, mine_ref, other_ref, *rest):
    out_ref = rest[-1]
    size = mine_ref.shape[1]
    top = heads * size
    mine_later = order_ref[0] == 1
    final_mine, final_other = mine_ref[top : top + heads, :], other_ref[top : top + heads, :]
    end_mine, end_other = mine_ref[top + heads :, :], other_ref[top + heads :, :]
    same = jnp.where(end_mine[:1] == end_other[:1], 1.0, 0.0)
    scale_mine = jnp.where(mine_later, 1.0, jnp.exp(final_other) * same)
    scale_other = jnp.where(mine_later, jnp.exp(final_mine) * same, 1.0)
    for head in range(heads):
        rows = slice(head * size, (head + 1) * size)
        out_ref[rows, :] = (
            scale_mine[head : head + 1] * mine_ref[rows, :]
            + scale_other[head : head + 1] * other_ref[rows, :]
        )
    out_ref[top : top + heads, :] = final_mine + final_other
    out_ref[top + heads :, :] = jnp.where(mine_later, end_mine, end_other)


def joined(order, mine, other, heads, after=(), through=()):
    rows, size = mine.shape
    message = pltpu.VMEM((rows, size), F32)
    vmem, anywhere = pl.BlockSpec(memory_space=pltpu.VMEM), pl.BlockSpec(memory_space=pl.ANY)
    return pl.pallas_call(
        functools.partial(join_kernel, heads),
        in_specs=[pl.BlockSpec(memory_space=pltpu.SMEM), vmem, vmem]
        + [anywhere] * (len(through) + len(after)),
        out_specs=[anywhere] * len(through) + [vmem],
        out_shape=[message] * (len(through) + 1),
        input_output_aliases={3 + i: i for i in range(len(through))},
        compiler_params=pltpu.CompilerParams(vmem_limit_bytes=16 * MIB),
        cost_estimate=pl.CostEstimate(
            flops=3 * rows * size, bytes_accessed=12 * rows * size, transcendentals=0
        ),
        name="join_windows",
    )(order, mine, other, *through, *after)


def make_mask(seg_ref, mask_ref):
    tokens = seg_ref.shape[1]
    seg = seg_ref[...].astype(F32)
    column = as_column(seg, 128)
    for start in range(0, tokens, 128):
        across = lax.broadcasted_iota(jnp.int32, (tokens, 128), 1) + start
        down = lax.broadcasted_iota(jnp.int32, (tokens, 128), 0)
        seen = (column == seg[:, start : start + 128]) & (across <= down)
        mask_ref[:, start : start + 128] = jnp.where(seen, 0.0, -1e30)


def intra_kernel(
    first,
    heads,
    mask_ref,
    a_ref,
    gain_ref,
    q_ref,
    k_ref,
    v_ref,
    g_hbm,
    o_ref,
    decay_ref,
    gate_ref,
    g_ref,
    sems,
):
    tokens = mask_ref.shape[0]
    size = q_ref.shape[1] // heads
    block = min(tokens, 256)
    wide = pl.ds(first * size, heads * size)
    copy = pltpu.make_async_copy(g_hbm.at[:, wide], g_ref, sems.at[0])
    copy.start()
    for j in range(heads):
        columns = slice(j * size, (j + 1) * size)
        a_row = a_ref[first + j : first + j + 1, :] * 1.4426950408889634
        a_column = as_column(a_row, 128)
        decay_ref[:, columns] = jnp.exp2(a_column)
        for start in range(0, tokens, block):
            here, upto = slice(start, start + block), slice(0, start + block)
            scores = lax.dot_general(
                q_ref[here, columns], k_ref[upto, columns], NT, preferred_element_type=F32
            )
            spread = jnp.concatenate([a_column[here]] * ((start + block) // 128), axis=1)
            weight = jnp.exp2(spread - a_row[:, upto] + mask_ref[here, upto])
            probs = (scores * weight).astype(BF16)
            o_ref[here, columns] = lax.dot_general(
                probs, v_ref[upto, columns], NN, preferred_element_type=F32
            )
    copy.wait()
    for j in range(heads):
        columns = slice(j * size, (j + 1) * size)
        half = 0.5 * gain_ref[:, (first + j) * size : (first + j + 1) * size]
        gate_ref[:, columns] = half + half * jnp.tanh(0.5 * g_ref[:, columns].astype(F32))


def intra(mask, a, gain, q, k, v, g, first, heads):
    tokens, size = k.shape[0], k.shape[1] // heads
    vmem = pl.BlockSpec(memory_space=pltpu.VMEM)
    return pl.pallas_call(
        functools.partial(intra_kernel, first, heads),
        in_specs=[vmem] * 6 + [pl.BlockSpec(memory_space=pltpu.HBM)],
        out_specs=[vmem] * 3,
        out_shape=[pltpu.VMEM((tokens, heads * size), F32)] * 3,
        scratch_shapes=[
            pltpu.VMEM((tokens, heads * size), BF16),
            pltpu.SemaphoreType.DMA((1,)),
        ],
        compiler_params=pltpu.CompilerParams(vmem_limit_bytes=16 * MIB),
        cost_estimate=pl.CostEstimate(
            flops=3 * tokens * tokens * heads * size,
            bytes_accessed=3 * MIB,
            transcendentals=tokens * tokens * heads,
        ),
        name="intra_span",
    )(mask, a, gain, q, k, v, g)


def final_kernel(
    first,
    heads,
    order_ref,
    seg_ref,
    own_ref,
    pair_ref,
    before_ref,
    o_ref,
    decay_ref,
    gate_ref,
    q_ref,
    *rest,
):
    gated_hbm, snap_hbm, token_ref, gated_ref, snap_ref, sems = rest[-6:]
    token_ref[...] = jnp.zeros_like(token_ref)
    tokens, size = q_ref.shape[0], own_ref.shape[1]
    top = heads * size
    second = order_ref[0] == 1
    ends = slice(top + heads, top + heads + 1)
    finals = slice(top, top + heads)
    own_end, pair_end, before_end = own_ref[ends, :], pair_ref[ends, :], before_ref[ends, :]
    previous = jnp.where(second, pair_end, before_end)
    kept = jnp.where(own_end == previous, 1.0, 0.0)
    bridged = jnp.where(pair_end == before_end, 1.0, 0.0)
    own_decay = jnp.exp(own_ref[finals, :]) * kept
    from_before = jnp.where(second, jnp.exp(pair_ref[finals, :]) * bridged, 1.0)
    from_pair = jnp.where(second, 1.0, 0.0)
    valid = as_column(jnp.where(seg_ref[...].astype(F32) == previous[:, :1], 1.0, 0.0), size)
    copies = []
    for j in range(heads):
        rows = columns = slice(j * size, (j + 1) * size)
        state = from_before[j : j + 1] * before_ref[rows, :] + from_pair * pair_ref[rows, :]
        snap_ref[j] = own_decay[j : j + 1] * state + own_ref[rows, :]
        high = state.astype(BF16)
        low = (state - high.astype(F32)).astype(BF16)
        q = q_ref[:, columns]
        inter = lax.dot_general(
            jnp.concatenate([q, q], axis=1),
            jnp.concatenate([high, low], axis=0),
            NN,
            preferred_element_type=F32,
        )
        mixed = o_ref[:, columns] + inter * (decay_ref[:, columns] * valid)
        mean_square = jnp.mean(mixed * mixed, axis=1, keepdims=True)
        gated = mixed * lax.rsqrt(mean_square + 1e-06) * gate_ref[:, columns]
        gated_ref[:, columns] = gated.astype(BF16)
        if j % 2 == 1 or j == heads - 1:
            begin = j - j % 2
            width = (j + 1 - begin) * size
            heads_here = pl.ds(first + begin, j + 1 - begin)
            place = pl.ds((first + begin) * size, width)
            for source, target in (
                (gated_ref.at[:, pl.ds(begin * size, width)], gated_hbm.at[:, place]),
                (snap_ref.at[pl.ds(begin, j + 1 - begin)], snap_hbm.at[0, heads_here]),
            ):
                copies.append(pltpu.make_async_copy(source, target, sems.at[len(copies)]))
                copies[-1].start()
    for copy in copies:
        copy.wait()


def finish(order, seg, own, pair, before, o, decay, gate, q, so_far, first, heads, total):
    tokens, size = q.shape[0], q.shape[1] // heads
    vmem, hbm = pl.BlockSpec(memory_space=pltpu.VMEM), pl.BlockSpec(memory_space=pltpu.HBM)
    return pl.pallas_call(
        functools.partial(final_kernel, first, heads),
        in_specs=[pl.BlockSpec(memory_space=pltpu.SMEM)] + [vmem] * 8 + [hbm] * len(so_far),
        out_specs=[hbm, hbm, vmem],
        out_shape=[
            pltpu.HBM((tokens, total * size), BF16),
            pltpu.HBM((1, total, size, size), F32),
            pltpu.VMEM((8, 128), F32),
        ],
        scratch_shapes=[
            pltpu.VMEM((tokens, heads * size), BF16),
            pltpu.VMEM((heads, size, size), F32),
            pltpu.SemaphoreType.DMA((2 * heads,)),
        ],
        input_output_aliases={9 + i: i for i in range(len(so_far))},
        compiler_params=pltpu.CompilerParams(vmem_limit_bytes=16 * MIB),
        cost_estimate=pl.CostEstimate(
            flops=4 * tokens * heads * size * size,
            bytes_accessed=4 * MIB,
            transcendentals=2 * tokens * heads * size,
        ),
        name="finish",
    )(order, seg, own, pair, before, o, decay, gate, q, *so_far)


def shards(q, k, v, g, segment, decay_exponent, retention, norm_gain):
    heads = decay_exponent.shape[0]
    tokens = q.shape[0]
    count = lax.axis_size("seq")
    place = lax.axis_index("seq")
    reach = max(1, count // 4)
    chunk = 4
    firsts = list(range(0, heads, chunk))
    last = len(firsts) - 1
    far = lambda x: pltpu.with_memory_space_constraint(x, pltpu.HBM)
    q, k, v, g = far(q), far(k), far(v), far(g)
    gain = norm_gain.reshape(1, -1)
    order = lax.rem(place, 2).astype(jnp.int32).reshape(1)
    swap = [(c, c ^ 1) for c in range(count)]

    pair, before, inside, done = {}, {}, {}, {}
    result = ()

    own0, a, w, seg, k0, v0 = first_message(
        far(segment.reshape(1, tokens)),
        far(decay_exponent.reshape(1, heads)),
        far(retention),
        k,
        v,
        heads,
        chunk,
    )
    own = [own0]
    pair[0] = lax.ppermute(own[0], "seq", swap)
    mask, messages, k_near, v_near, q_near = prepare(seg, a, w, q, k, v, chunk)
    k_near, v_near = [k0, *k_near], [v0, *v_near]
    own += messages
    pair[1] = lax.ppermute(own[1], "seq", swap)

    def look_inside(i):
        inside[i] = intra(mask, a, gain, q_near[i], k_near[i], v_near[i], g, firsts[i], chunk)

    look_inside(0)
    for i in range(last + 1):
        if i < last:
            look_inside(i + 1)
        after = (inside[0][0], inside[min(i + 1, last)][0]) + ((done[0],) if i == last else ())
        through = (own[i + 2],) if i + 2 <= last else ()
        *through, both = joined(order, own[i], pair[i], chunk, after, through)
        if through:
            own[i + 2] = through[0]
            pair[i + 2] = lax.ppermute(own[i + 2], "seq", swap)
        before[i] = lax.ppermute(both, "seq", [(c, c + 2) for c in range(count - 2)])
        window = 2
        while window < reach:
            past = lax.ppermute(before[i], "seq", [(c, c + window) for c in range(count - window)])
            (before[i],) = joined(jnp.ones((1,), jnp.int32), before[i], past, chunk)
            window *= 2
        for j in {last - 1: (0,), last: range(1, last + 1)}.get(i, ()):
            *result, done[j] = finish(
                order, seg, own[j], pair[j], before[j], *inside[j], q_near[j], result, firsts[j],
                chunk, heads,
            )
    return tuple(result)


def solution(mesh):
    placed = (
        P(("groups", "seq"), "wt"),
        P(("groups", "seq"), "wt"),
        P(("groups", "seq"), "wt"),
        P(("groups", "seq"), "wt"),
        P(("groups", "seq")),
        P("wt"),
        P("wt", ("groups", "seq")),
        P("wt"),
    )
    return jax.shard_map(
        shards,
        mesh=mesh,
        in_specs=placed,
        out_specs=(P(("groups", "seq"), "wt"), P(("groups", "seq"), "wt", None, None)),
        check_vma=False,
    )
```

```python
import functools

import jax
import jax.numpy as jnp
from jax import lax
from jax.experimental import pallas as pl
from jax.experimental.pallas import tpu as pltpu
from jax.sharding import PartitionSpec as P

F32 = jnp.float32
BF16 = jnp.bfloat16
NN = (((1,), (0,)), ((), ()))
NT = (((1,), (1,)), ((), ()))
MIB = 1 << 20


def vmem_spec(shape, index_map):
    return pl.BlockSpec(shape, index_map)


def as_column(row, lanes):
    return jnp.broadcast_to(row, (lanes, row.shape[1])).T


def meta_rows(heads):
    return -(-(heads + 1) // 8) * 8


def put_message(msg_ref, first, heads, size, w_ref, finals, end, k_ref, v_ref):
    top = heads * size
    for j in range(heads):
        columns = slice(j * size, (j + 1) * size)
        weight = w_ref[first + j : first + j + 1, :]
        keyed = (k_ref[:, columns].astype(F32).T * weight).astype(BF16)
        msg_ref[columns, :] = lax.dot_general(
            keyed, v_ref[:, columns], NN, preferred_element_type=F32
        )
    msg_ref[top : top + heads, :] = jnp.broadcast_to(finals, (heads, size))
    below = meta_rows(heads) - heads
    msg_ref[top + heads :, :] = jnp.broadcast_to(end.astype(F32), (below, size))


def first_kernel(
    heads,
    chunk,
    seg_hbm,
    exponent_hbm,
    keep_hbm,
    k_hbm,
    v_hbm,
    msg_ref,
    a_ref,
    w_ref,
    seg_ref,
    exponent_ref,
    keep_ref,
    k_ref,
    v_ref,
    sems,
):
    tokens = seg_ref.shape[1]
    size = msg_ref.shape[1]
    wide = pl.ds(0, chunk * size)
    copies = [
        pltpu.make_async_copy(source, target, sems.at[i])
        for i, (source, target) in enumerate(
            [
                (keep_hbm, keep_ref),
                (exponent_hbm, exponent_ref),
                (seg_hbm, seg_ref),
                (k_hbm.at[:, wide], k_ref),
                (v_hbm.at[:, wide], v_ref),
            ]
        )
    ]
    for copy in copies:
        copy.start()
    earlier = lax.broadcasted_iota(jnp.int32, (tokens, tokens), 0)
    later = lax.broadcasted_iota(jnp.int32, (tokens, tokens), 1)
    upper = jnp.where(earlier <= later, 1.0, 0.0).astype(BF16)
    across = lax.broadcasted_iota(jnp.int32, (heads, heads), 1)
    down = lax.broadcasted_iota(jnp.int32, (heads, heads), 0)
    for copy in copies[:3]:
        copy.wait()
    spread = jnp.broadcast_to(exponent_ref[...], (heads, heads))
    exponent = jnp.sum(jnp.where(across == down, spread, 0).astype(F32), axis=1, keepdims=True)
    a = -jnp.exp2(-exponent) + jnp.log(keep_ref[...])
    high = a.astype(BF16)
    rest = a - high.astype(F32)
    middle = rest.astype(BF16)
    low = (rest - middle.astype(F32)).astype(BF16)
    parts = jnp.concatenate([high, middle, low], axis=0)
    sums = lax.dot_general(parts, upper, NN, preferred_element_type=F32)
    cumulative = sums[:heads] + (sums[heads : 2 * heads] + sums[2 * heads :])
    a_ref[...] = cumulative
    final = cumulative[:, tokens - 1 :]
    seg = seg_ref[...]
    last = seg[:, tokens - 1 :]
    w_ref[...] = jnp.where(seg == last, jnp.exp(final - cumulative), 0.0)
    for copy in copies[3:]:
        copy.wait()
    put_message(msg_ref, 0, chunk, size, w_ref, final[:chunk], last, k_ref, v_ref)


def first_message(seg, exponent, keep, k, v, heads, chunk):
    tokens, size = k.shape[0], k.shape[1] // heads
    rows = chunk * size + meta_rows(chunk)
    return pl.pallas_call(
        functools.partial(first_kernel, heads, chunk),
        in_specs=[pl.BlockSpec(memory_space=pltpu.HBM)] * 5,
        out_specs=[pl.BlockSpec(memory_space=pltpu.VMEM)] * 4,
        out_shape=[
            pltpu.VMEM((rows, size), F32),
            pltpu.VMEM((heads, tokens), F32),
            pltpu.VMEM((heads, tokens), F32),
            pltpu.VMEM((1, tokens), jnp.int32),
        ],
        scratch_shapes=[
            pltpu.VMEM((1, heads), jnp.int32),
            pltpu.VMEM((heads, tokens), F32),
            pltpu.VMEM((tokens, chunk * size), BF16),
            pltpu.VMEM((tokens, chunk * size), BF16),
            pltpu.SemaphoreType.DMA((5,)),
        ],
        compiler_params=pltpu.CompilerParams(vmem_limit_bytes=8 * MIB),
        cost_estimate=pl.CostEstimate(
            flops=2 * tokens * chunk * size * size, bytes_accessed=2 * MIB, transcendentals=0
        ),
        name="first_message",
    )(seg, exponent, keep, k, v)


def rest_kernel(chunk, seg_ref, a_ref, w_ref, k_hbm, v_hbm, *refs):
    messages, (k_ref, v_ref, sems) = refs[:-3], refs[-3:]
    tokens, size = seg_ref.shape[1], messages[0].shape[1]
    copies = []
    for i in range(len(messages)):
        wide = pl.ds((i + 1) * chunk * size, chunk * size)
        copies += [
            pltpu.make_async_copy(k_hbm.at[:, wide], k_ref.at[i], sems.at[0, i]),
            pltpu.make_async_copy(v_hbm.at[:, wide], v_ref.at[i], sems.at[1, i]),
        ]
    for copy in copies:
        copy.start()
    last = seg_ref[:, tokens - 1 :]
    for i, msg_ref in enumerate(messages):
        copies[2 * i].wait()
        copies[2 * i + 1].wait()
        first = (i + 1) * chunk
        final = a_ref[first : first + chunk, tokens - 1 :]
        put_message(msg_ref, first, chunk, size, w_ref, final, last, k_ref.at[i], v_ref.at[i])


def rest_messages(seg, a, w, k, v, chunk):
    heads = a.shape[0]
    tokens, size = k.shape[0], k.shape[1] // heads
    count = heads // chunk - 1
    rows = chunk * size + meta_rows(chunk)
    return pl.pallas_call(
        functools.partial(rest_kernel, chunk),
        in_specs=[pl.BlockSpec(memory_space=pltpu.VMEM)] * 3
        + [pl.BlockSpec(memory_space=pltpu.HBM)] * 2,
        out_specs=[pl.BlockSpec(memory_space=pltpu.VMEM)] * count,
        out_shape=[pltpu.VMEM((rows, size), F32)] * count,
        scratch_shapes=[pltpu.VMEM((count, tokens, chunk * size), BF16)] * 2
        + [pltpu.SemaphoreType.DMA((2, count))],
        compiler_params=pltpu.CompilerParams(vmem_limit_bytes=8 * MIB),
        cost_estimate=pl.CostEstimate(
            flops=2 * tokens * heads * size * size, bytes_accessed=4 * MIB, transcendentals=0
        ),
        name="rest_messages",
    )(seg, a, w, k, v)


def join_kernel(heads, order_ref, mine_ref, other_ref, *rest):
    *copied, out_ref = rest
    if copied:
        copied[-1][...] = copied[0][...]
    size = mine_ref.shape[1]
    top = heads * size
    mine_later = (order_ref[0] & 1) == 1
    final_mine, final_other = mine_ref[top : top + heads, :], other_ref[top : top + heads, :]
    end_mine, end_other = mine_ref[top + heads :, :], other_ref[top + heads :, :]
    same = jnp.where(end_mine[:1] == end_other[:1], 1.0, 0.0)
    scale_mine = jnp.where(mine_later, 1.0, jnp.exp(final_other) * same)
    scale_other = jnp.where(mine_later, jnp.exp(final_mine) * same, 1.0)
    for head in range(heads):
        rows = slice(head * size, (head + 1) * size)
        out_ref[rows, :] = (
            scale_mine[head : head + 1] * mine_ref[rows, :]
            + scale_other[head : head + 1] * other_ref[rows, :]
        )
    out_ref[top : top + heads, :] = final_mine + final_other
    out_ref[top + heads :, :] = jnp.where(mine_later, end_mine, end_other)


def joined(order, mine, other, heads, after=(), through=()):
    rows, size = mine.shape
    message = pltpu.VMEM((rows, size), F32)
    vmem, anywhere = pl.BlockSpec(memory_space=pltpu.VMEM), pl.BlockSpec(memory_space=pl.ANY)

    def kernel(order_ref, mine_ref, other_ref, *rest):
        rest = rest[: len(through)] + rest[len(through) + len(after) :]
        join_kernel(heads, order_ref, mine_ref, other_ref, *rest)

    return pl.pallas_call(
        kernel,
        in_specs=[pl.BlockSpec(memory_space=pltpu.SMEM), vmem, vmem]
        + [vmem] * len(through)
        + [anywhere] * len(after),
        out_specs=[vmem] * (len(through) + 1),
        out_shape=[message] * (len(through) + 1),
        compiler_params=pltpu.CompilerParams(vmem_limit_bytes=8 * MIB),
        cost_estimate=pl.CostEstimate(
            flops=3 * rows * size, bytes_accessed=12 * rows * size, transcendentals=0
        ),
        name="join_windows",
    )(order, mine, other, *through, *after)


def make_mask(seg_ref, mask_ref):
    tokens = seg_ref.shape[1]
    seg = seg_ref[...].astype(F32)
    column = as_column(seg, 128)
    for start in range(0, tokens, 128):
        across = lax.broadcasted_iota(jnp.int32, (tokens, 128), 1) + start
        down = lax.broadcasted_iota(jnp.int32, (tokens, 128), 0)
        seen = (column == seg[:, start : start + 128]) & (across <= down)
        mask_ref[:, start : start + 128] = jnp.where(seen, 0.0, -1e30)


def intra_kernel(
    first,
    heads,
    seg_ref,
    a_ref,
    gain_ref,
    q_hbm,
    k_hbm,
    v_hbm,
    g_hbm,
    o_ref,
    gate_ref,
    q_ref,
    mask_ref,
    k_ref,
    v_ref,
    g_ref,
    sems,
):
    tokens = seg_ref.shape[1]
    size = q_ref.shape[1] // heads
    block = min(tokens, 128)
    copies = []
    for p in range(0, heads, 2):
        there, here = pl.ds((first + p) * size, 2 * size), pl.ds(p * size, 2 * size)
        for i, (source, target) in enumerate(((q_hbm, q_ref), (k_hbm, k_ref), (v_hbm, v_ref))):
            copies.append(
                pltpu.make_async_copy(source.at[:, there], target.at[:, here], sems.at[i, p // 2])
            )
    wide = pl.ds(first * size, heads * size)
    copies.append(pltpu.make_async_copy(g_hbm.at[:, wide], g_ref, sems.at[3, 0]))
    for copy in copies:
        copy.start()
    make_mask(seg_ref, mask_ref)
    for j in range(heads):
        if j % 2 == 0:
            for copy in copies[3 * (j // 2) : 3 * (j // 2) + 3]:
                copy.wait()
        columns = slice(j * size, (j + 1) * size)
        a_row = a_ref[first + j : first + j + 1, :] * 1.4426950408889634
        a_column = as_column(a_row, 128)
        for start in range(0, tokens, block):
            here, upto = slice(start, start + block), slice(0, start + block)
            scores = lax.dot_general(
                q_ref[here, columns], k_ref[upto, columns], NT, preferred_element_type=F32
            )
            spread = jnp.concatenate([a_column[here]] * ((start + block) // 128), axis=1)
            weight = jnp.exp2(spread - a_row[:, upto] + mask_ref[here, upto])
            probs = (scores * weight).astype(BF16)
            o_ref[here, columns] = lax.dot_general(
                probs, v_ref[upto, columns], NN, preferred_element_type=F32
            )
    copies[-1].wait()
    for j in range(heads):
        columns = slice(j * size, (j + 1) * size)
        half = 0.5 * gain_ref[:, (first + j) * size : (first + j + 1) * size]
        for start in range(0, tokens, block):
            here = slice(start, start + block)
            gate_ref[here, columns] = half + half * jnp.tanh(
                0.5 * g_ref[here, columns].astype(F32)
            )


def intra(seg, a, gain, q, k, v, g, first, heads):
    tokens, size = k.shape[0], k.shape[1] // a.shape[0]
    vmem = pl.BlockSpec(memory_space=pltpu.VMEM)
    return pl.pallas_call(
        functools.partial(intra_kernel, first, heads),
        in_specs=[vmem] * 3 + [pl.BlockSpec(memory_space=pltpu.HBM)] * 4,
        out_specs=[vmem] * 3,
        out_shape=[pltpu.VMEM((tokens, heads * size), dtype) for dtype in (F32, F32, BF16)],
        scratch_shapes=[pltpu.VMEM((tokens, tokens), F32)]
        + [pltpu.VMEM((tokens, heads * size), BF16)] * 3
        + [pltpu.SemaphoreType.DMA((4, heads // 2))],
        compiler_params=pltpu.CompilerParams(vmem_limit_bytes=8 * MIB),
        cost_estimate=pl.CostEstimate(
            flops=3 * tokens * tokens * heads * size,
            bytes_accessed=3 * MIB,
            transcendentals=tokens * tokens * heads,
        ),
        name="intra_span",
    )(seg, a, gain, q, k, v, g)


def final_kernel(
    first,
    heads,
    order_ref,
    seg_ref,
    own_ref,
    pair_ref,
    before_ref,
    o_ref,
    gate_ref,
    q_ref,
    a_ref,
    *rest,
):
    gated_hbm, snap_hbm, token_ref, gated_ref, snap_ref, sems = rest[-6:]
    token_ref[...] = jnp.zeros_like(token_ref)
    tokens, size = q_ref.shape[0], own_ref.shape[1]
    block = min(tokens, 128)
    top = heads * size
    second = (order_ref[0] & 1) == 1
    ends = slice(top + heads, top + heads + 1)
    finals = slice(top, top + heads)
    own_end, pair_end, before_end = own_ref[ends, :], pair_ref[ends, :], before_ref[ends, :]
    previous = jnp.where(second, pair_end, before_end)
    kept = jnp.where(own_end == previous, 1.0, 0.0)
    bridged = jnp.where(pair_end == before_end, 1.0, 0.0)
    own_decay = jnp.exp(own_ref[finals, :]) * kept
    from_before = jnp.where(second, jnp.exp(pair_ref[finals, :]) * bridged, 1.0)
    from_before = jnp.where(order_ref[0] >= 2, from_before, 0.0)
    from_pair = jnp.where(second, 1.0, 0.0)
    valid = seg_ref[...].astype(F32) == previous[:, :1]
    copies = []
    for j in range(heads):
        rows = columns = slice(j * size, (j + 1) * size)
        state = from_before[j : j + 1] * before_ref[rows, :] + from_pair * pair_ref[rows, :]
        snap_ref[j] = own_decay[j : j + 1] * state + own_ref[rows, :]
        high = state.astype(BF16)
        low = (state - high.astype(F32)).astype(BF16)
        q = q_ref[:, columns]
        both = jnp.concatenate([high, low], axis=0)
        decay = jnp.where(valid, jnp.exp(a_ref[first + j : first + j + 1, :]), 0.0)
        decay = as_column(decay, size)
        for start in range(0, tokens, block):
            here = slice(start, start + block)
            inter = lax.dot_general(
                jnp.concatenate([q[here], q[here]], axis=1), both, NN, preferred_element_type=F32
            )
            mixed = o_ref[here, columns] + inter * decay[here]
            mean_square = jnp.mean(mixed * mixed, axis=1, keepdims=True)
            gated = mixed * lax.rsqrt(mean_square + 1e-06) * gate_ref[here, columns]
            gated_ref[here, columns] = gated.astype(BF16)
        if j % 2 == 1 or j == heads - 1:
            begin = j - j % 2
            width = (j + 1 - begin) * size
            heads_here = pl.ds(first + begin, j + 1 - begin)
            place = pl.ds((first + begin) * size, width)
            for source, target in (
                (gated_ref.at[:, pl.ds(begin * size, width)], gated_hbm.at[:, place]),
                (snap_ref.at[pl.ds(begin, j + 1 - begin)], snap_hbm.at[0, heads_here]),
            ):
                copies.append(pltpu.make_async_copy(source, target, sems.at[len(copies)]))
                copies[-1].start()
    for copy in copies:
        copy.wait()


def finish(order, seg, own, pair, before, o, gate, q, a, so_far, first, heads):
    tokens, size = q.shape[0], q.shape[1] // heads
    total = a.shape[0]
    vmem, hbm = pl.BlockSpec(memory_space=pltpu.VMEM), pl.BlockSpec(memory_space=pltpu.HBM)
    return pl.pallas_call(
        functools.partial(final_kernel, first, heads),
        in_specs=[pl.BlockSpec(memory_space=pltpu.SMEM)] + [vmem] * 8 + [hbm] * len(so_far),
        out_specs=[hbm, hbm, vmem],
        out_shape=[
            pltpu.HBM((tokens, total * size), BF16),
            pltpu.HBM((1, total, size, size), F32),
            pltpu.VMEM((8, 128), F32),
        ],
        scratch_shapes=[
            pltpu.VMEM((tokens, heads * size), BF16),
            pltpu.VMEM((heads, size, size), F32),
            pltpu.SemaphoreType.DMA((2 * heads,)),
        ],
        input_output_aliases={9 + i: i for i in range(len(so_far))},
        compiler_params=pltpu.CompilerParams(vmem_limit_bytes=8 * MIB),
        cost_estimate=pl.CostEstimate(
            flops=4 * tokens * heads * size * size,
            bytes_accessed=4 * MIB,
            transcendentals=2 * tokens * heads * size,
        ),
        name="finish",
    )(order, seg, own, pair, before, o, gate, q, a, *so_far)


def shards(q, k, v, g, segment, decay_exponent, retention, norm_gain):
    heads = decay_exponent.shape[0]
    tokens = q.shape[0]
    count = lax.axis_size("seq")
    place = lax.axis_index("seq")
    reach = max(1, count // 4)
    chunk = 4
    firsts = list(range(0, heads, chunk))
    last = len(firsts) - 1
    far = lambda x: pltpu.with_memory_space_constraint(x, pltpu.HBM)
    q, k, v, g = far(q), far(k), far(v), far(g)
    gain = norm_gain.reshape(1, -1)
    order = jnp.where(place >= 2, 2 + (place & 1), place & 1).astype(jnp.int32).reshape(1)
    swap = [(c, c ^ 1) for c in range(count)]
    turn = [(c, (c + 2) % count) for c in range(count)]

    pair, before, inside, done = {}, {}, {}, {}
    result = ()

    own0, a, w, seg = first_message(
        far(segment.reshape(1, tokens)),
        far(decay_exponent.reshape(1, heads)),
        far(retention),
        k,
        v,
        heads,
        chunk,
    )
    own = [own0]
    pair[0] = lax.ppermute(own[0], "seq", swap)
    own += rest_messages(seg, a, w, k, v, chunk)
    pair[1] = lax.ppermute(own[1], "seq", swap)

    def look_inside(i):
        inside[i] = intra(seg, a, gain, q, k, v, g, firsts[i], chunk)

    look_inside(0)
    for i in range(last + 1):
        if i < last:
            look_inside(i + 1)
        after = (inside[0][0], inside[min(i + 1, last)][0]) + ((done[0],) if i == last else ())
        through = (own[i + 2],) if i + 2 <= last else ()
        *through, both = joined(order, own[i], pair[i], chunk, after, through)
        if through:
            own[i + 2] = through[0]
            pair[i + 2] = lax.ppermute(own[i + 2], "seq", swap)
        before[i] = lax.ppermute(both, "seq", turn)
        window = 2
        if window < reach:
            before[i] = jnp.where(place >= 2, before[i], 0.0)
        while window < reach:
            past = lax.ppermute(before[i], "seq", [(c, c + window) for c in range(count - window)])
            (before[i],) = joined(jnp.ones((1,), jnp.int32), before[i], past, chunk)
            window *= 2
        for j in {last - 1: (0,), last: range(1, last + 1)}.get(i, ()):
            *result, done[j] = finish(
                order, seg, own[j], pair[j], before[j], *inside[j], a, result, firsts[j], chunk
            )
    return tuple(result)


def solution(mesh):
    placed = (
        P(("groups", "seq"), "wt"),
        P(("groups", "seq"), "wt"),
        P(("groups", "seq"), "wt"),
        P(("groups", "seq"), "wt"),
        P(("groups", "seq")),
        P("wt"),
        P("wt", ("groups", "seq")),
        P("wt"),
    )
    return jax.shard_map(
        shards,
        mesh=mesh,
        in_specs=placed,
        out_specs=(P(("groups", "seq"), "wt"), P(("groups", "seq"), "wt", None, None)),
        check_vma=False,
    )
```

```python
import functools

import jax
import jax.numpy as jnp
from jax import lax
from jax.experimental import pallas as pl
from jax.experimental.pallas import tpu as pltpu
from jax.sharding import PartitionSpec as P

F32 = jnp.float32
BF16 = jnp.bfloat16
NN = (((1,), (0,)), ((), ()))
NT = (((1,), (1,)), ((), ()))
MIB = 1 << 20


def vmem_spec(shape, index_map):
    return pl.BlockSpec(shape, index_map)


def as_column(row, lanes):
    return jnp.broadcast_to(row, (lanes, row.shape[1])).T


def meta_rows(heads):
    return -(-(heads + 1) // 8) * 8


def put_message(msg_ref, first, heads, size, w_ref, finals, end, k_ref, v_ref):
    top = heads * size
    for j in range(heads):
        columns = slice(j * size, (j + 1) * size)
        weight = w_ref[first + j : first + j + 1, :]
        keyed = (k_ref[:, columns].astype(F32).T * weight).astype(BF16)
        msg_ref[columns, :] = lax.dot_general(
            keyed, v_ref[:, columns], NN, preferred_element_type=F32
        )
    msg_ref[top : top + heads, :] = jnp.broadcast_to(finals, (heads, size))
    below = meta_rows(heads) - heads
    msg_ref[top + heads :, :] = jnp.broadcast_to(end.astype(F32), (below, size))


def first_kernel(
    heads,
    chunk,
    seg_hbm,
    exponent_hbm,
    keep_hbm,
    k_hbm,
    v_hbm,
    msg_ref,
    a_ref,
    w_ref,
    seg_ref,
    k_ref,
    v_ref,
    exponent_ref,
    keep_ref,
    sems,
):
    tokens = seg_ref.shape[1]
    size = msg_ref.shape[1]
    wide = pl.ds(0, chunk * size)
    copies = [
        pltpu.make_async_copy(source, target, sems.at[i])
        for i, (source, target) in enumerate(
            [
                (keep_hbm, keep_ref),
                (exponent_hbm, exponent_ref),
                (seg_hbm, seg_ref),
                (k_hbm.at[:, wide], k_ref),
                (v_hbm.at[:, wide], v_ref),
            ]
        )
    ]
    for copy in copies:
        copy.start()
    earlier = lax.broadcasted_iota(jnp.int32, (tokens, tokens), 0)
    later = lax.broadcasted_iota(jnp.int32, (tokens, tokens), 1)
    upper = jnp.where(earlier <= later, 1.0, 0.0).astype(BF16)
    across = lax.broadcasted_iota(jnp.int32, (heads, heads), 1)
    down = lax.broadcasted_iota(jnp.int32, (heads, heads), 0)
    for copy in copies[:3]:
        copy.wait()
    spread = jnp.broadcast_to(exponent_ref[...], (heads, heads))
    exponent = jnp.sum(jnp.where(across == down, spread, 0).astype(F32), axis=1, keepdims=True)
    a = -jnp.exp2(-exponent) + jnp.log(keep_ref[...])
    high = a.astype(BF16)
    rest = a - high.astype(F32)
    middle = rest.astype(BF16)
    low = (rest - middle.astype(F32)).astype(BF16)
    parts = jnp.concatenate([high, middle, low], axis=0)
    sums = lax.dot_general(parts, upper, NN, preferred_element_type=F32)
    cumulative = sums[:heads] + (sums[heads : 2 * heads] + sums[2 * heads :])
    a_ref[...] = cumulative
    final = cumulative[:, tokens - 1 :]
    seg = seg_ref[...]
    last = seg[:, tokens - 1 :]
    w_ref[...] = jnp.where(seg == last, jnp.exp(final - cumulative), 0.0)
    for copy in copies[3:]:
        copy.wait()
    put_message(msg_ref, 0, chunk, size, w_ref, final[:chunk], last, k_ref, v_ref)


def first_message(seg, exponent, keep, k, v, heads, chunk):
    tokens, size = k.shape[0], k.shape[1] // heads
    rows = chunk * size + meta_rows(chunk)
    return pl.pallas_call(
        functools.partial(first_kernel, heads, chunk),
        in_specs=[pl.BlockSpec(memory_space=pltpu.HBM)] * 5,
        out_specs=[pl.BlockSpec(memory_space=pltpu.VMEM)] * 6,
        out_shape=[
            pltpu.VMEM((rows, size), F32),
            pltpu.VMEM((heads, tokens), F32),
            pltpu.VMEM((heads, tokens), F32),
            pltpu.VMEM((1, tokens), jnp.int32),
            pltpu.VMEM((tokens, chunk * size), BF16),
            pltpu.VMEM((tokens, chunk * size), BF16),
        ],
        scratch_shapes=[
            pltpu.VMEM((1, heads), jnp.int32),
            pltpu.VMEM((heads, tokens), F32),
            pltpu.SemaphoreType.DMA((5,)),
        ],
        compiler_params=pltpu.CompilerParams(vmem_limit_bytes=8 * MIB),
        cost_estimate=pl.CostEstimate(
            flops=2 * tokens * chunk * size * size, bytes_accessed=2 * MIB, transcendentals=0
        ),
        name="first_message",
    )(seg, exponent, keep, k, v)


def rest_kernel(chunk, seg_ref, a_ref, w_ref, q_hbm, k_hbm, v_hbm, g_hbm, *refs):
    messages, (mask_ref, q_ref, g_ref, k_ref, v_ref, sems) = refs[:-6], refs[-6:]
    tokens, size = seg_ref.shape[1], messages[0].shape[1]
    copies = []
    for i in range(len(messages)):
        wide = pl.ds((i + 1) * chunk * size, chunk * size)
        copies += [
            pltpu.make_async_copy(k_hbm.at[:, wide], k_ref.at[i], sems.at[0, i]),
            pltpu.make_async_copy(v_hbm.at[:, wide], v_ref.at[i], sems.at[1, i]),
        ]
    wide = pl.ds(0, chunk * size)
    copies += [
        pltpu.make_async_copy(q_hbm.at[:, wide], q_ref, sems.at[2, 0]),
        pltpu.make_async_copy(g_hbm.at[:, wide], g_ref, sems.at[2, 1]),
    ]
    for copy in copies:
        copy.start()
    make_mask(seg_ref, mask_ref)
    last = seg_ref[:, tokens - 1 :]
    for i, msg_ref in enumerate(messages):
        copies[2 * i].wait()
        copies[2 * i + 1].wait()
        first = (i + 1) * chunk
        final = a_ref[first : first + chunk, tokens - 1 :]
        put_message(msg_ref, first, chunk, size, w_ref, final, last, k_ref.at[i], v_ref.at[i])
    copies[-2].wait()
    copies[-1].wait()


def rest_messages(seg, a, w, q, k, v, g, chunk):
    heads = a.shape[0]
    tokens, size = k.shape[0], k.shape[1] // heads
    count = heads // chunk - 1
    rows = chunk * size + meta_rows(chunk)
    *messages, mask, q0, g0 = pl.pallas_call(
        functools.partial(rest_kernel, chunk),
        in_specs=[pl.BlockSpec(memory_space=pltpu.VMEM)] * 3
        + [pl.BlockSpec(memory_space=pltpu.HBM)] * 4,
        out_specs=[pl.BlockSpec(memory_space=pltpu.VMEM)] * (count + 3),
        out_shape=[pltpu.VMEM((rows, size), F32)] * count
        + [pltpu.VMEM((tokens, tokens), F32)]
        + [pltpu.VMEM((tokens, chunk * size), BF16)] * 2,
        scratch_shapes=[pltpu.VMEM((count, tokens, chunk * size), BF16)] * 2
        + [pltpu.SemaphoreType.DMA((3, max(count, 2)))],
        compiler_params=pltpu.CompilerParams(vmem_limit_bytes=8 * MIB),
        cost_estimate=pl.CostEstimate(
            flops=2 * tokens * heads * size * size, bytes_accessed=4 * MIB, transcendentals=0
        ),
        name="rest_messages",
    )(seg, a, w, q, k, v, g)
    return messages, mask, q0, g0


def join_kernel(heads, order_ref, mine_ref, other_ref, *rest):
    *copied, out_ref = rest
    if copied:
        copied[-1][...] = copied[0][...]
    size = mine_ref.shape[1]
    top = heads * size
    mine_later = (order_ref[0] & 1) == 1
    final_mine, final_other = mine_ref[top : top + heads, :], other_ref[top : top + heads, :]
    end_mine, end_other = mine_ref[top + heads :, :], other_ref[top + heads :, :]
    same = jnp.where(end_mine[:1] == end_other[:1], 1.0, 0.0)
    scale_mine = jnp.where(mine_later, 1.0, jnp.exp(final_other) * same)
    scale_other = jnp.where(mine_later, jnp.exp(final_mine) * same, 1.0)
    for head in range(heads):
        rows = slice(head * size, (head + 1) * size)
        out_ref[rows, :] = (
            scale_mine[head : head + 1] * mine_ref[rows, :]
            + scale_other[head : head + 1] * other_ref[rows, :]
        )
    out_ref[top : top + heads, :] = final_mine + final_other
    out_ref[top + heads :, :] = jnp.where(mine_later, end_mine, end_other)


def joined(order, mine, other, heads, after=(), through=()):
    rows, size = mine.shape
    message = pltpu.VMEM((rows, size), F32)
    vmem, anywhere = pl.BlockSpec(memory_space=pltpu.VMEM), pl.BlockSpec(memory_space=pl.ANY)

    def kernel(order_ref, mine_ref, other_ref, *rest):
        rest = rest[: len(through)] + rest[len(through) + len(after) :]
        join_kernel(heads, order_ref, mine_ref, other_ref, *rest)

    return pl.pallas_call(
        kernel,
        in_specs=[pl.BlockSpec(memory_space=pltpu.SMEM), vmem, vmem]
        + [vmem] * len(through)
        + [anywhere] * len(after),
        out_specs=[vmem] * (len(through) + 1),
        out_shape=[message] * (len(through) + 1),
        compiler_params=pltpu.CompilerParams(vmem_limit_bytes=8 * MIB),
        cost_estimate=pl.CostEstimate(
            flops=3 * rows * size, bytes_accessed=12 * rows * size, transcendentals=0
        ),
        name="join_windows",
    )(order, mine, other, *through, *after)


def make_mask(seg_ref, mask_ref):
    tokens = seg_ref.shape[1]
    seg = seg_ref[...].astype(F32)
    column = as_column(seg, 128)
    for start in range(0, tokens, 128):
        across = lax.broadcasted_iota(jnp.int32, (tokens, 128), 1) + start
        down = lax.broadcasted_iota(jnp.int32, (tokens, 128), 0)
        seen = (column == seg[:, start : start + 128]) & (across <= down)
        mask_ref[:, start : start + 128] = jnp.where(seen, 0.0, -1e30)


def intra_kernel(first, heads, mask_ref, a_ref, gain_ref, q_ref, k_ref, v_ref, g_ref, *refs):
    tokens = mask_ref.shape[0]
    size = q_ref.shape[1] // heads
    block = min(tokens, 256)
    copies = []
    if len(refs) > 2:
        sources, (o_ref, gate_ref, *targets), sems = refs[:4], refs[4:-1], refs[-1]
        wide = pl.ds((first + heads) * size, heads * size)
        for i, (source, target) in enumerate(zip(sources, targets)):
            copies.append(pltpu.make_async_copy(source.at[:, wide], target, sems.at[i]))
            copies[-1].start()
    else:
        o_ref, gate_ref = refs
    for j in range(heads):
        columns = slice(j * size, (j + 1) * size)
        a_row = a_ref[first + j : first + j + 1, :] * 1.4426950408889634
        a_column = as_column(a_row, 128)
        for start in range(0, tokens, block):
            here, upto = slice(start, start + block), slice(0, start + block)
            scores = lax.dot_general(
                q_ref[here, columns], k_ref[upto, columns], NT, preferred_element_type=F32
            )
            spread = jnp.concatenate([a_column[here]] * ((start + block) // 128), axis=1)
            weight = jnp.exp2(spread - a_row[:, upto] + mask_ref[here, upto])
            probs = (scores * weight).astype(BF16)
            o_ref[here, columns] = lax.dot_general(
                probs, v_ref[upto, columns], NN, preferred_element_type=F32
            )
        half = 0.5 * gain_ref[:, (first + j) * size : (first + j + 1) * size]
        gate_ref[:, columns] = half + half * jnp.tanh(0.5 * g_ref[:, columns].astype(F32))
    for copy in copies:
        copy.wait()


def intra(mask, a, gain, near, far, first, heads):
    tokens, size = mask.shape[0], gain.shape[1] // a.shape[0]
    if first + heads == a.shape[0]:
        far = ()
    vmem = pl.BlockSpec(memory_space=pltpu.VMEM)
    o, gate, *following = pl.pallas_call(
        functools.partial(intra_kernel, first, heads),
        in_specs=[vmem] * 7 + [pl.BlockSpec(memory_space=pltpu.HBM)] * len(far),
        out_specs=[vmem] * (2 + len(far)),
        out_shape=[pltpu.VMEM((tokens, heads * size), F32)] * 2
        + [pltpu.VMEM((tokens, heads * size), BF16)] * len(far),
        scratch_shapes=[pltpu.SemaphoreType.DMA((4,))] if far else [],
        compiler_params=pltpu.CompilerParams(vmem_limit_bytes=8 * MIB),
        cost_estimate=pl.CostEstimate(
            flops=3 * tokens * tokens * heads * size,
            bytes_accessed=3 * MIB,
            transcendentals=tokens * tokens * heads,
        ),
        name="intra_span",
    )(mask, a, gain, *near, *far)
    return (o, gate, near[0]), following


def final_kernel(
    first,
    heads,
    order_ref,
    seg_ref,
    own_ref,
    pair_ref,
    before_ref,
    o_ref,
    gate_ref,
    q_ref,
    a_ref,
    *rest,
):
    gated_hbm, snap_hbm, token_ref, gated_ref, snap_ref, sems = rest[-6:]
    token_ref[...] = jnp.zeros_like(token_ref)
    tokens, size = q_ref.shape[0], own_ref.shape[1]
    block = min(tokens, 256)
    top = heads * size
    second = (order_ref[0] & 1) == 1
    ends = slice(top + heads, top + heads + 1)
    finals = slice(top, top + heads)
    own_end, pair_end, before_end = own_ref[ends, :], pair_ref[ends, :], before_ref[ends, :]
    previous = jnp.where(second, pair_end, before_end)
    kept = jnp.where(own_end == previous, 1.0, 0.0)
    bridged = jnp.where(pair_end == before_end, 1.0, 0.0)
    own_decay = jnp.exp(own_ref[finals, :]) * kept
    from_before = jnp.where(second, jnp.exp(pair_ref[finals, :]) * bridged, 1.0)
    from_before = jnp.where(order_ref[0] >= 2, from_before, 0.0)
    from_pair = jnp.where(second, 1.0, 0.0)
    valid = seg_ref[...].astype(F32) == previous[:, :1]
    copies = []
    for j in range(heads):
        rows = columns = slice(j * size, (j + 1) * size)
        state = from_before[j : j + 1] * before_ref[rows, :] + from_pair * pair_ref[rows, :]
        snap_ref[j] = own_decay[j : j + 1] * state + own_ref[rows, :]
        high = state.astype(BF16)
        low = (state - high.astype(F32)).astype(BF16)
        q = q_ref[:, columns]
        both = jnp.concatenate([high, low], axis=0)
        decay = jnp.where(valid, jnp.exp(a_ref[first + j : first + j + 1, :]), 0.0)
        decay = as_column(decay, size)
        for start in range(0, tokens, block):
            here = slice(start, start + block)
            inter = lax.dot_general(
                jnp.concatenate([q[here], q[here]], axis=1), both, NN, preferred_element_type=F32
            )
            mixed = o_ref[here, columns] + inter * decay[here]
            mean_square = jnp.mean(mixed * mixed, axis=1, keepdims=True)
            gated = mixed * lax.rsqrt(mean_square + 1e-06) * gate_ref[here, columns]
            gated_ref[here, columns] = gated.astype(BF16)
        if j % 2 == 1 or j == heads - 1:
            begin = j - j % 2
            width = (j + 1 - begin) * size
            heads_here = pl.ds(first + begin, j + 1 - begin)
            place = pl.ds((first + begin) * size, width)
            for source, target in (
                (gated_ref.at[:, pl.ds(begin * size, width)], gated_hbm.at[:, place]),
                (snap_ref.at[pl.ds(begin, j + 1 - begin)], snap_hbm.at[0, heads_here]),
            ):
                copies.append(pltpu.make_async_copy(source, target, sems.at[len(copies)]))
                copies[-1].start()
    for copy in copies:
        copy.wait()


def finish(order, seg, own, pair, before, o, gate, q, a, so_far, first, heads):
    tokens, size = q.shape[0], q.shape[1] // heads
    total = a.shape[0]
    vmem, anywhere = pl.BlockSpec(memory_space=pltpu.VMEM), pl.BlockSpec(memory_space=pl.ANY)
    return pl.pallas_call(
        functools.partial(final_kernel, first, heads),
        in_specs=[pl.BlockSpec(memory_space=pltpu.SMEM)] + [vmem] * 8 + [anywhere] * len(so_far),
        out_specs=[anywhere, anywhere, vmem],
        out_shape=[
            jax.ShapeDtypeStruct((tokens, total * size), BF16),
            jax.ShapeDtypeStruct((1, total, size, size), F32),
            pltpu.VMEM((8, 128), F32),
        ],
        scratch_shapes=[
            pltpu.VMEM((tokens, heads * size), BF16),
            pltpu.VMEM((heads, size, size), F32),
            pltpu.SemaphoreType.DMA((2 * heads,)),
        ],
        input_output_aliases={9 + i: i for i in range(len(so_far))},
        compiler_params=pltpu.CompilerParams(vmem_limit_bytes=8 * MIB),
        cost_estimate=pl.CostEstimate(
            flops=4 * tokens * heads * size * size,
            bytes_accessed=4 * MIB,
            transcendentals=2 * tokens * heads * size,
        ),
        name="finish",
    )(order, seg, own, pair, before, o, gate, q, a, *so_far)


def shards(q, k, v, g, segment, decay_exponent, retention, norm_gain):
    heads = decay_exponent.shape[0]
    tokens = q.shape[0]
    count = lax.axis_size("seq")
    place = lax.axis_index("seq")
    reach = max(1, count // 4)
    chunk = 4
    firsts = list(range(0, heads, chunk))
    last = len(firsts) - 1
    far = lambda x: pltpu.with_memory_space_constraint(x, pltpu.HBM)
    q, k, v, g = far(q), far(k), far(v), far(g)
    gain = norm_gain.reshape(1, -1)
    order = jnp.where(place >= 2, 2 + (place & 1), place & 1).astype(jnp.int32).reshape(1)
    swap = [(c, c ^ 1) for c in range(count)]
    turn = [(c, (c + 2) % count) for c in range(count)]

    pair, before, inside, done = {}, {}, {}, {}
    result = ()

    own0, a, w, seg, k0, v0 = first_message(
        far(segment.reshape(1, tokens)),
        far(decay_exponent.reshape(1, heads)),
        far(retention),
        k,
        v,
        heads,
        chunk,
    )
    own = [own0]
    pair[0] = lax.ppermute(own[0], "seq", swap)
    messages, mask, q0, g0 = rest_messages(seg, a, w, q, k, v, g, chunk)
    own += messages
    near = (q0, k0, v0, g0)
    pair[1] = lax.ppermute(own[1], "seq", swap)

    inside[0], near = intra(mask, a, gain, near, (q, k, v, g), 0, chunk)
    for i in range(last + 1):
        if i < last:
            inside[i + 1], near = intra(mask, a, gain, near, (q, k, v, g), firsts[i + 1], chunk)
        after = (inside[0][0], inside[min(i + 1, last)][0]) + ((done[0],) if i == last else ())
        through = (own[i + 2],) if i + 2 <= last else ()
        *through, both = joined(order, own[i], pair[i], chunk, after, through)
        if through:
            own[i + 2] = through[0]
            pair[i + 2] = lax.ppermute(own[i + 2], "seq", swap)
        before[i] = lax.ppermute(both, "seq", turn)
        window = 2
        if window < reach:
            before[i] = jnp.where(place >= 2, before[i], 0.0)
        while window < reach:
            past = lax.ppermute(before[i], "seq", [(c, c + window) for c in range(count - window)])
            (before[i],) = joined(jnp.ones((1,), jnp.int32), before[i], past, chunk)
            window *= 2
        for j in {last - 1: (0,), last: range(1, last + 1)}.get(i, ()):
            *result, done[j] = finish(
                order, seg, own[j], pair[j], before[j], *inside[j], a, result, firsts[j], chunk
            )
    return tuple(result)


def solution(mesh):
    placed = (
        P(("groups", "seq"), "wt"),
        P(("groups", "seq"), "wt"),
        P(("groups", "seq"), "wt"),
        P(("groups", "seq"), "wt"),
        P(("groups", "seq")),
        P("wt"),
        P("wt", ("groups", "seq")),
        P("wt"),
    )
    return jax.shard_map(
        shards,
        mesh=mesh,
        in_specs=placed,
        out_specs=(P(("groups", "seq"), "wt"), P(("groups", "seq"), "wt", None, None)),
        check_vma=False,
    )
```

```python
import functools

import jax
import jax.numpy as jnp
from jax import lax
from jax.experimental import pallas as pl
from jax.experimental.pallas import tpu as pltpu
from jax.sharding import PartitionSpec as P

F32 = jnp.float32
BF16 = jnp.bfloat16
NN = (((1,), (0,)), ((), ()))
NT = (((1,), (1,)), ((), ()))
MIB = 1 << 20


def vmem_spec(shape, index_map):
    return pl.BlockSpec(shape, index_map)


def as_column(row, lanes):
    return jnp.broadcast_to(row, (lanes, row.shape[1])).T


def meta_rows(heads):
    return -(-(heads + 1) // 8) * 8


def put_message(msg_ref, first, heads, size, w_ref, finals, end, k_ref, v_ref):
    top = heads * size
    for j in range(heads):
        columns = slice(j * size, (j + 1) * size)
        weight = w_ref[first + j : first + j + 1, :]
        keyed = (k_ref[:, columns].astype(F32).T * weight).astype(BF16)
        msg_ref[columns, :] = lax.dot_general(
            keyed, v_ref[:, columns], NN, preferred_element_type=F32
        )
    msg_ref[top : top + heads, :] = jnp.broadcast_to(finals, (heads, size))
    below = meta_rows(heads) - heads
    msg_ref[top + heads :, :] = jnp.broadcast_to(end.astype(F32), (below, size))


def first_kernel(
    heads,
    chunk,
    order_ref,
    seg_hbm,
    exponent_hbm,
    keep_hbm,
    k_hbm,
    v_hbm,
    msg_ref,
    a_ref,
    w_ref,
    seg_ref,
    k_ref,
    v_ref,
    exponent_ref,
    keep_ref,
    sems,
):
    tokens = seg_ref.shape[1]
    size = msg_ref.shape[1]
    wide = pl.ds(0, chunk * size)
    copies = [
        pltpu.make_async_copy(source, target, sems.at[i])
        for i, (source, target) in enumerate(
            [
                (keep_hbm, keep_ref),
                (exponent_hbm, exponent_ref),
                (seg_hbm, seg_ref),
                (k_hbm.at[:, wide], k_ref),
                (v_hbm.at[:, wide], v_ref),
            ]
        )
    ]
    for copy in copies:
        copy.start()
    earlier = lax.broadcasted_iota(jnp.int32, (tokens, tokens), 0)
    later = lax.broadcasted_iota(jnp.int32, (tokens, tokens), 1)
    upper = jnp.where(earlier <= later, 1.0, 0.0).astype(BF16)
    across = lax.broadcasted_iota(jnp.int32, (heads, heads), 1)
    down = lax.broadcasted_iota(jnp.int32, (heads, heads), 0)
    for copy in copies[:3]:
        copy.wait()
    spread = jnp.broadcast_to(exponent_ref[...], (heads, heads))
    exponent = jnp.sum(jnp.where(across == down, spread, 0).astype(F32), axis=1, keepdims=True)
    a = -jnp.exp2(-exponent) + jnp.log(keep_ref[...])
    high = a.astype(BF16)
    rest = a - high.astype(F32)
    middle = rest.astype(BF16)
    low = (rest - middle.astype(F32)).astype(BF16)
    parts = jnp.concatenate([high, middle, low], axis=0)
    sums = lax.dot_general(parts, upper, NN, preferred_element_type=F32)
    cumulative = sums[:heads] + (sums[heads : 2 * heads] + sums[2 * heads :])
    a_ref[...] = cumulative
    final = cumulative[:, tokens - 1 :]
    seg = seg_ref[...]
    last = seg[:, tokens - 1 :]
    w_ref[...] = jnp.where(seg == last, jnp.exp(final - cumulative), 0.0)
    for copy in copies[3:]:
        copy.wait()
    put_message(msg_ref, 0, chunk, size, w_ref, final[:chunk], last, k_ref, v_ref)


def first_message(order, seg, exponent, keep, k, v, heads, chunk):
    tokens, size = k.shape[0], k.shape[1] // heads
    rows = chunk * size + meta_rows(chunk)
    return pl.pallas_call(
        functools.partial(first_kernel, heads, chunk),
        in_specs=[pl.BlockSpec(memory_space=pltpu.SMEM)]
        + [pl.BlockSpec(memory_space=pltpu.HBM)] * 5,
        out_specs=[pl.BlockSpec(memory_space=pltpu.VMEM)] * 6,
        out_shape=[
            pltpu.VMEM((rows, size), F32),
            pltpu.VMEM((heads, tokens), F32),
            pltpu.VMEM((heads, tokens), F32),
            pltpu.VMEM((1, tokens), jnp.int32),
            pltpu.VMEM((tokens, chunk * size), BF16),
            pltpu.VMEM((tokens, chunk * size), BF16),
        ],
        scratch_shapes=[
            pltpu.VMEM((1, heads), jnp.int32),
            pltpu.VMEM((heads, tokens), F32),
            pltpu.SemaphoreType.DMA((5,)),
        ],
        compiler_params=pltpu.CompilerParams(vmem_limit_bytes=8 * MIB),
        cost_estimate=pl.CostEstimate(
            flops=2 * tokens * chunk * size * size, bytes_accessed=2 * MIB, transcendentals=0
        ),
        name="first_message",
    )(order, seg, exponent, keep, k, v)


def rest_kernel(chunk, seg_ref, a_ref, w_ref, q_hbm, k_hbm, v_hbm, g_hbm, *refs):
    tokens = seg_ref.shape[1]
    count = a_ref.shape[0] // chunk
    messages, refs = refs[: count - 1], refs[count - 1 :]
    mask_ref, refs, sems = refs[0], refs[1:-1], refs[-1]
    k_refs, refs = refs[: count - 1], refs[count - 1 :]
    v_refs, refs = refs[: count - 1], refs[count - 1 :]
    q_refs, g_refs = refs[:count], refs[count:]
    size = messages[0].shape[1]
    pairs = []
    for i in range(1, count):
        wide = pl.ds(i * chunk * size, chunk * size)
        pairs += [(k_hbm.at[:, wide], k_refs[i - 1]), (v_hbm.at[:, wide], v_refs[i - 1])]
    for i in range(count):
        wide = pl.ds(i * chunk * size, chunk * size)
        pairs += [(q_hbm.at[:, wide], q_refs[i]), (g_hbm.at[:, wide], g_refs[i])]
    copies = [pltpu.make_async_copy(*pair, sems.at[i]) for i, pair in enumerate(pairs)]
    for copy in copies:
        copy.start()
    make_mask(seg_ref, mask_ref)
    last = seg_ref[:, tokens - 1 :]
    for i, msg_ref in enumerate(messages):
        copies[2 * i].wait()
        copies[2 * i + 1].wait()
        first = (i + 1) * chunk
        final = a_ref[first : first + chunk, tokens - 1 :]
        put_message(msg_ref, first, chunk, size, w_ref, final, last, k_refs[i], v_refs[i])
    for copy in copies[2 * len(messages) :]:
        copy.wait()


def rest_messages(seg, a, w, q, k, v, g, chunk):
    heads = a.shape[0]
    tokens, size = k.shape[0], k.shape[1] // heads
    count = heads // chunk
    rows = chunk * size + meta_rows(chunk)
    arrays = 4 * count - 2
    out = pl.pallas_call(
        functools.partial(rest_kernel, chunk),
        in_specs=[pl.BlockSpec(memory_space=pltpu.VMEM)] * 3
        + [pl.BlockSpec(memory_space=pltpu.HBM)] * 4,
        out_specs=[pl.BlockSpec(memory_space=pltpu.VMEM)] * (count + arrays),
        out_shape=[pltpu.VMEM((rows, size), F32)] * (count - 1)
        + [pltpu.VMEM((tokens, tokens), F32)]
        + [pltpu.VMEM((tokens, chunk * size), BF16)] * arrays,
        scratch_shapes=[pltpu.SemaphoreType.DMA((arrays,))],
        compiler_params=pltpu.CompilerParams(vmem_limit_bytes=8 * MIB),
        cost_estimate=pl.CostEstimate(
            flops=2 * tokens * heads * size * size, bytes_accessed=8 * MIB, transcendentals=0
        ),
        name="rest_messages",
    )(seg, a, w, q, k, v, g)
    messages, mask, out = out[: count - 1], out[count - 1], out[count:]
    k_near, out = out[: count - 1], out[count - 1 :]
    v_near, out = out[: count - 1], out[count - 1 :]
    return messages, mask, k_near, v_near, out[:count], out[count:]


def join_kernel(heads, order_ref, mine_ref, other_ref, *rest):
    *copied, out_ref = rest
    if copied:
        copied[-1][...] = copied[0][...]
    size = mine_ref.shape[1]
    top = heads * size
    mine_later = (order_ref[0] & 1) == 1
    final_mine, final_other = mine_ref[top : top + heads, :], other_ref[top : top + heads, :]
    end_mine, end_other = mine_ref[top + heads :, :], other_ref[top + heads :, :]
    same = jnp.where(end_mine[:1] == end_other[:1], 1.0, 0.0)
    scale_mine = jnp.where(mine_later, 1.0, jnp.exp(final_other) * same)
    scale_other = jnp.where(mine_later, jnp.exp(final_mine) * same, 1.0)
    for head in range(heads):
        rows = slice(head * size, (head + 1) * size)
        out_ref[rows, :] = (
            scale_mine[head : head + 1] * mine_ref[rows, :]
            + scale_other[head : head + 1] * other_ref[rows, :]
        )
    out_ref[top : top + heads, :] = final_mine + final_other
    out_ref[top + heads :, :] = jnp.where(mine_later, end_mine, end_other)


def joined(order, mine, other, heads, after=(), through=()):
    rows, size = mine.shape
    message = pltpu.VMEM((rows, size), F32)
    vmem, anywhere = pl.BlockSpec(memory_space=pltpu.VMEM), pl.BlockSpec(memory_space=pl.ANY)

    def kernel(order_ref, mine_ref, other_ref, *rest):
        rest = rest[: len(through)] + rest[len(through) + len(after) :]
        join_kernel(heads, order_ref, mine_ref, other_ref, *rest)

    return pl.pallas_call(
        kernel,
        in_specs=[pl.BlockSpec(memory_space=pltpu.SMEM), vmem, vmem]
        + [vmem] * len(through)
        + [anywhere] * len(after),
        out_specs=[vmem] * (len(through) + 1),
        out_shape=[message] * (len(through) + 1),
        compiler_params=pltpu.CompilerParams(vmem_limit_bytes=8 * MIB),
        cost_estimate=pl.CostEstimate(
            flops=3 * rows * size, bytes_accessed=12 * rows * size, transcendentals=0
        ),
        name="join_windows",
    )(order, mine, other, *through, *after)


def make_mask(seg_ref, mask_ref):
    tokens = seg_ref.shape[1]
    seg = seg_ref[...].astype(F32)
    column = as_column(seg, 128)
    for start in range(0, tokens, 128):
        across = lax.broadcasted_iota(jnp.int32, (tokens, 128), 1) + start
        down = lax.broadcasted_iota(jnp.int32, (tokens, 128), 0)
        seen = (column == seg[:, start : start + 128]) & (across <= down)
        mask_ref[:, start : start + 128] = jnp.where(seen, 0.0, -1e30)


def intra_kernel(
    first, heads, mask_ref, a_ref, gain_ref, q_ref, k_ref, v_ref, g_ref, o_ref, gate_ref
):
    tokens = mask_ref.shape[0]
    size = q_ref.shape[1] // heads
    block = min(tokens, 256)
    for j in range(heads):
        columns = slice(j * size, (j + 1) * size)
        a_row = a_ref[first + j : first + j + 1, :] * 1.4426950408889634
        a_column = as_column(a_row, 128)
        for start in range(0, tokens, block):
            here, upto = slice(start, start + block), slice(0, start + block)
            scores = lax.dot_general(
                q_ref[here, columns], k_ref[upto, columns], NT, preferred_element_type=F32
            )
            spread = jnp.concatenate([a_column[here]] * ((start + block) // 128), axis=1)
            weight = jnp.exp2(spread - a_row[:, upto] + mask_ref[here, upto])
            probs = (scores * weight).astype(BF16)
            o_ref[here, columns] = lax.dot_general(
                probs, v_ref[upto, columns], NN, preferred_element_type=F32
            )
        half = 0.5 * gain_ref[:, (first + j) * size : (first + j + 1) * size]
        gate_ref[:, columns] = half + half * jnp.tanh(0.5 * g_ref[:, columns].astype(F32))


def intra(mask, a, gain, q, k, v, g, first, heads):
    tokens, size = mask.shape[0], gain.shape[1] // a.shape[0]
    vmem = pl.BlockSpec(memory_space=pltpu.VMEM)
    o, gate = pl.pallas_call(
        functools.partial(intra_kernel, first, heads),
        in_specs=[vmem] * 7,
        out_specs=[vmem] * 2,
        out_shape=[pltpu.VMEM((tokens, heads * size), F32)] * 2,
        compiler_params=pltpu.CompilerParams(vmem_limit_bytes=8 * MIB),
        cost_estimate=pl.CostEstimate(
            flops=3 * tokens * tokens * heads * size,
            bytes_accessed=3 * MIB,
            transcendentals=tokens * tokens * heads,
        ),
        name="intra_span",
    )(mask, a, gain, q, k, v, g)
    return o, gate, q


def final_kernel(
    first,
    heads,
    order_ref,
    seg_ref,
    own_ref,
    pair_ref,
    before_ref,
    o_ref,
    gate_ref,
    q_ref,
    a_ref,
    *rest,
):
    rest = rest[2 * (first > 0) :]
    gated_hbm, snap_hbm, gated_ref, snap_ref, sems = rest[:2] + rest[-3:]
    if first == 0:
        rest[2][...] = jnp.zeros_like(rest[2])
    tokens, size = q_ref.shape[0], own_ref.shape[1]
    block = min(tokens, 256)
    top = heads * size
    second = (order_ref[0] & 1) == 1
    ends = slice(top + heads, top + heads + 1)
    finals = slice(top, top + heads)
    own_end, pair_end, before_end = own_ref[ends, :], pair_ref[ends, :], before_ref[ends, :]
    previous = jnp.where(second, pair_end, before_end)
    kept = jnp.where(own_end == previous, 1.0, 0.0)
    bridged = jnp.where(pair_end == before_end, 1.0, 0.0)
    own_decay = jnp.exp(own_ref[finals, :]) * kept
    from_before = jnp.where(second, jnp.exp(pair_ref[finals, :]) * bridged, 1.0)
    from_before = jnp.where(order_ref[0] >= 2, from_before, 0.0)
    from_pair = jnp.where(second, 1.0, 0.0)
    valid = seg_ref[...].astype(F32) == previous[:, :1]
    copies = []
    for j in range(heads):
        rows = columns = slice(j * size, (j + 1) * size)
        state = from_before[j : j + 1] * before_ref[rows, :] + from_pair * pair_ref[rows, :]
        snap_ref[j] = own_decay[j : j + 1] * state + own_ref[rows, :]
        high = state.astype(BF16)
        low = (state - high.astype(F32)).astype(BF16)
        q = q_ref[:, columns]
        both = jnp.concatenate([high, low], axis=0)
        decay = jnp.where(valid, jnp.exp(a_ref[first + j : first + j + 1, :]), 0.0)
        decay = as_column(decay, size)
        for start in range(0, tokens, block):
            here = slice(start, start + block)
            inter = lax.dot_general(
                jnp.concatenate([q[here], q[here]], axis=1), both, NN, preferred_element_type=F32
            )
            mixed = o_ref[here, columns] + inter * decay[here]
            mean_square = jnp.mean(mixed * mixed, axis=1, keepdims=True)
            gated = mixed * lax.rsqrt(mean_square + 1e-06) * gate_ref[here, columns]
            gated_ref[here, columns] = gated.astype(BF16)
        if j % 2 == 1 or j == heads - 1:
            begin = j - j % 2
            width = (j + 1 - begin) * size
            heads_here = pl.ds(first + begin, j + 1 - begin)
            place = pl.ds((first + begin) * size, width)
            for source, target in (
                (gated_ref.at[:, pl.ds(begin * size, width)], gated_hbm.at[:, place]),
                (snap_ref.at[pl.ds(begin, j + 1 - begin)], snap_hbm.at[0, heads_here]),
            ):
                copies.append(pltpu.make_async_copy(source, target, sems.at[len(copies)]))
                copies[-1].start()
    for copy in copies:
        copy.wait()


def finish(order, seg, own, pair, before, o, gate, q, a, so_far, first, heads):
    tokens, size = q.shape[0], q.shape[1] // heads
    total = a.shape[0]
    vmem, anywhere = pl.BlockSpec(memory_space=pltpu.VMEM), pl.BlockSpec(memory_space=pl.ANY)
    return pl.pallas_call(
        functools.partial(final_kernel, first, heads),
        in_specs=[pl.BlockSpec(memory_space=pltpu.SMEM)] + [vmem] * 8 + [anywhere] * len(so_far),
        out_specs=[anywhere, anywhere] + [vmem] * (first == 0),
        out_shape=[
            jax.ShapeDtypeStruct((tokens, total * size), BF16),
            jax.ShapeDtypeStruct((1, total, size, size), F32),
        ]
        + [pltpu.VMEM((8, 128), F32)] * (first == 0),
        scratch_shapes=[
            pltpu.VMEM((tokens, heads * size), BF16),
            pltpu.VMEM((heads, size, size), F32),
            pltpu.SemaphoreType.DMA((2 * heads,)),
        ],
        input_output_aliases={9 + i: i for i in range(len(so_far))},
        compiler_params=pltpu.CompilerParams(vmem_limit_bytes=8 * MIB),
        cost_estimate=pl.CostEstimate(
            flops=4 * tokens * heads * size * size,
            bytes_accessed=4 * MIB,
            transcendentals=2 * tokens * heads * size,
        ),
        name="finish",
    )(order, seg, own, pair, before, o, gate, q, a, *so_far)


def shards(q, k, v, g, segment, decay_exponent, retention, norm_gain):
    heads = decay_exponent.shape[0]
    tokens = q.shape[0]
    count = lax.axis_size("seq")
    place = lax.axis_index("seq")
    reach = max(1, count // 4)
    chunk = 4
    firsts = list(range(0, heads, chunk))
    last = len(firsts) - 1
    far = lambda x: pltpu.with_memory_space_constraint(x, pltpu.HBM)
    q, k, v, g = far(q), far(k), far(v), far(g)
    gain = norm_gain.reshape(1, -1)
    order = jnp.where(place >= 2, 2 + (place & 1), place & 1).astype(jnp.int32).reshape(1)
    swap = [(c, c ^ 1) for c in range(count)]
    turn = [(c, (c + 2) % count) for c in range(count)]

    pair, before, inside = {}, {}, {}
    result = ()

    own0, a, w, seg, k0, v0 = first_message(
        order,
        far(segment.reshape(1, tokens)),
        far(decay_exponent.reshape(1, heads)),
        far(retention),
        k,
        v,
        heads,
        chunk,
    )
    own = [own0]
    pair[0] = lax.ppermute(own[0], "seq", swap)
    messages, mask, k_near, v_near, q_near, g_near = rest_messages(seg, a, w, q, k, v, g, chunk)
    own += messages
    k_near, v_near = [k0, *k_near], [v0, *v_near]
    pair[1] = lax.ppermute(own[1], "seq", swap)

    for i, first in enumerate(firsts):
        inside[i] = intra(
            mask, a, gain, q_near[i], k_near[i], v_near[i], g_near[i], first, chunk
        )
        after = (inside[i][0],) + ((done,) if i == last else ())
        through = (own[i + 2],) if i + 2 <= last else ()
        *through, both = joined(order, own[i], pair[i], chunk, after, through)
        if through:
            own[i + 2] = through[0]
            pair[i + 2] = lax.ppermute(own[i + 2], "seq", swap)
        before[i] = lax.ppermute(both, "seq", turn)
        window = 2
        if window < reach:
            before[i] = jnp.where(place >= 2, before[i], 0.0)
        while window < reach:
            past = lax.ppermute(before[i], "seq", [(c, c + window) for c in range(count - window)])
            (before[i],) = joined(jnp.ones((1,), jnp.int32), before[i], past, chunk)
            window *= 2
        for j in {last - 1: (0,), last: range(1, last + 1)}.get(i, ()):
            result = finish(
                order, seg, own[j], pair[j], before[j], *inside[j], a, result, firsts[j], chunk
            )
            if j == 0:
                *result, done = result
    return tuple(result)


def solution(mesh):
    placed = (
        P(("groups", "seq"), "wt"),
        P(("groups", "seq"), "wt"),
        P(("groups", "seq"), "wt"),
        P(("groups", "seq"), "wt"),
        P(("groups", "seq")),
        P("wt"),
        P("wt", ("groups", "seq")),
        P("wt"),
    )
    return jax.shard_map(
        shards,
        mesh=mesh,
        in_specs=placed,
        out_specs=(P(("groups", "seq"), "wt"), P(("groups", "seq"), "wt", None, None)),
        check_vma=False,
    )
```

```python
import functools

import jax
import jax.numpy as jnp
from jax import lax
from jax.experimental import pallas as pl
from jax.experimental.pallas import tpu as pltpu
from jax.sharding import PartitionSpec as P

F32 = jnp.float32
BF16 = jnp.bfloat16
NN = (((1,), (0,)), ((), ()))
NT = (((1,), (1,)), ((), ()))
MIB = 1 << 20
SHORT = pl.CostEstimate(flops=1, bytes_accessed=1, transcendentals=0)


def vmem_spec(shape, index_map):
    return pl.BlockSpec(shape, index_map)


def as_column(row, lanes):
    return jnp.broadcast_to(row, (lanes, row.shape[1])).T


def meta_rows(heads):
    return -(-(heads + 1) // 8) * 8


def put_message(msg_ref, first, heads, size, w_ref, finals, end, k_ref, v_ref):
    top = heads * size
    for j in range(heads):
        columns = slice(j * size, (j + 1) * size)
        weight = w_ref[first + j : first + j + 1, :]
        keyed = (k_ref[:, columns].astype(F32).T * weight).astype(BF16)
        msg_ref[columns, :] = lax.dot_general(
            keyed, v_ref[:, columns], NN, preferred_element_type=F32
        )
    msg_ref[top : top + heads, :] = jnp.broadcast_to(finals, (heads, size))
    below = meta_rows(heads) - heads
    msg_ref[top + heads :, :] = jnp.broadcast_to(end.astype(F32), (below, size))


def first_kernel(heads, chunks, order_ref, seg_hbm, exponent_hbm, keep_hbm, k_hbm, v_hbm, *refs):
    number = len(chunks)
    messages, refs = refs[:number], refs[number:]
    (a_ref, w_ref, seg_ref), refs = refs[:3], refs[3:]
    k_refs, v_refs, refs = refs[:number], refs[number : 2 * number], refs[2 * number :]
    exponent_ref, keep_ref, sems = refs
    tokens = seg_ref.shape[1]
    size = messages[0].shape[1]
    pairs = [(keep_hbm, keep_ref), (exponent_hbm, exponent_ref), (seg_hbm, seg_ref)]
    for i, (first, many) in enumerate(chunks):
        wide = pl.ds(first * size, many * size)
        pairs += [(k_hbm.at[:, wide], k_refs[i]), (v_hbm.at[:, wide], v_refs[i])]
    copies = [pltpu.make_async_copy(*pair, sems.at[i]) for i, pair in enumerate(pairs)]
    for copy in copies:
        copy.start()
    earlier = lax.broadcasted_iota(jnp.int32, (tokens, tokens), 0)
    later = lax.broadcasted_iota(jnp.int32, (tokens, tokens), 1)
    upper = jnp.where(earlier <= later, 1.0, 0.0).astype(BF16)
    across = lax.broadcasted_iota(jnp.int32, (heads, heads), 1)
    down = lax.broadcasted_iota(jnp.int32, (heads, heads), 0)
    for copy in copies[:3]:
        copy.wait()
    spread = jnp.broadcast_to(exponent_ref[...], (heads, heads))
    exponent = jnp.sum(jnp.where(across == down, spread, 0).astype(F32), axis=1, keepdims=True)
    a = -jnp.exp2(-exponent) + jnp.log(keep_ref[...])
    high = a.astype(BF16)
    rest = a - high.astype(F32)
    middle = rest.astype(BF16)
    low = (rest - middle.astype(F32)).astype(BF16)
    parts = jnp.concatenate([high, middle, low], axis=0)
    sums = lax.dot_general(parts, upper, NN, preferred_element_type=F32)
    cumulative = sums[:heads] + (sums[heads : 2 * heads] + sums[2 * heads :])
    a_ref[...] = cumulative
    final = cumulative[:, tokens - 1 :]
    seg = seg_ref[...]
    last = seg[:, tokens - 1 :]
    w_ref[...] = jnp.where(seg == last, jnp.exp(final - cumulative), 0.0)
    for i, (first, many) in enumerate(chunks):
        copies[3 + 2 * i].wait()
        copies[4 + 2 * i].wait()
        finals = final[first : first + many]
        put_message(messages[i], first, many, size, w_ref, finals, last, k_refs[i], v_refs[i])


def message_of(size, many):
    return pltpu.VMEM((many * size + meta_rows(many), size), F32)


def first_messages(order, seg, exponent, keep, k, v, heads, chunks):
    tokens, size = k.shape[0], k.shape[1] // heads
    near = [pltpu.VMEM((tokens, many * size), BF16) for _, many in chunks]
    shapes = [message_of(size, many) for _, many in chunks]
    shapes += [pltpu.VMEM((heads, tokens), F32)] * 2 + [pltpu.VMEM((1, tokens), jnp.int32)]
    shapes += near + near
    number = len(chunks)
    out = pl.pallas_call(
        functools.partial(first_kernel, heads, chunks),
        in_specs=[pl.BlockSpec(memory_space=pltpu.SMEM)]
        + [pl.BlockSpec(memory_space=pltpu.HBM)] * 5,
        out_specs=[pl.BlockSpec(memory_space=pltpu.VMEM)] * len(shapes),
        out_shape=shapes,
        scratch_shapes=[
            pltpu.VMEM((1, heads), jnp.int32),
            pltpu.VMEM((heads, tokens), F32),
            pltpu.SemaphoreType.DMA((3 + 2 * number,)),
        ],
        compiler_params=pltpu.CompilerParams(vmem_limit_bytes=8 * MIB),
        cost_estimate=SHORT,
        name="first_messages",
    )(order, seg, exponent, keep, k, v)
    messages, (a, w, seg), out = out[:number], out[number : number + 3], out[number + 3 :]
    return messages, a, w, seg, out[:number], out[number:]


def rest_kernel(chunks, done, seg_ref, a_ref, w_ref, q_hbm, k_hbm, v_hbm, g_hbm, *refs):
    tokens = seg_ref.shape[1]
    left, number = chunks[done:], len(chunks)
    messages, mask_ref, refs, sems = refs[: len(left)], refs[len(left)], refs[len(left) + 1 : -1], refs[-1]
    k_refs, refs = refs[: len(left)], refs[len(left) :]
    v_refs, refs = refs[: len(left)], refs[len(left) :]
    q_refs, g_refs = refs[:number], refs[number:]
    size = messages[0].shape[1]
    pairs = []
    for i, (first, many) in enumerate(left):
        wide = pl.ds(first * size, many * size)
        pairs += [(k_hbm.at[:, wide], k_refs[i]), (v_hbm.at[:, wide], v_refs[i])]
    for i, (first, many) in enumerate(chunks):
        wide = pl.ds(first * size, many * size)
        pairs += [(q_hbm.at[:, wide], q_refs[i]), (g_hbm.at[:, wide], g_refs[i])]
    copies = [pltpu.make_async_copy(*pair, sems.at[i]) for i, pair in enumerate(pairs)]
    for copy in copies:
        copy.start()
    make_mask(seg_ref, mask_ref)
    last = seg_ref[:, tokens - 1 :]
    for i, (first, many) in enumerate(left):
        copies[2 * i].wait()
        copies[2 * i + 1].wait()
        final = a_ref[first : first + many, tokens - 1 :]
        put_message(messages[i], first, many, size, w_ref, final, last, k_refs[i], v_refs[i])
    for copy in copies[2 * len(left) :]:
        copy.wait()


def rest_messages(seg, a, w, q, k, v, g, chunks, done):
    heads = a.shape[0]
    tokens, size = k.shape[0], k.shape[1] // heads
    near = [pltpu.VMEM((tokens, many * size), BF16) for _, many in chunks]
    shapes = [message_of(size, many) for _, many in chunks[done:]]
    shapes += [pltpu.VMEM((tokens, tokens), F32)] + near[done:] * 2 + near * 2
    left, number = len(chunks) - done, len(chunks)
    out = pl.pallas_call(
        functools.partial(rest_kernel, chunks, done),
        in_specs=[pl.BlockSpec(memory_space=pltpu.VMEM)] * 3
        + [pl.BlockSpec(memory_space=pltpu.HBM)] * 4,
        out_specs=[pl.BlockSpec(memory_space=pltpu.VMEM)] * len(shapes),
        out_shape=shapes,
        scratch_shapes=[pltpu.SemaphoreType.DMA((2 * (left + number),))],
        compiler_params=pltpu.CompilerParams(vmem_limit_bytes=8 * MIB),
        cost_estimate=SHORT,
        name="rest_messages",
    )(seg, a, w, q, k, v, g)
    messages, mask, out = out[:left], out[left], out[left + 1 :]
    k_near, v_near, out = out[:left], out[left : 2 * left], out[2 * left :]
    return messages, mask, k_near, v_near, out[:number], out[number:]


def join_kernel(heads, order_ref, mine_ref, other_ref, out_ref):
    size = mine_ref.shape[1]
    top = heads * size
    mine_later = (order_ref[0] & 1) == 1
    final_mine, final_other = mine_ref[top : top + heads, :], other_ref[top : top + heads, :]
    end_mine, end_other = mine_ref[top + heads :, :], other_ref[top + heads :, :]
    same = jnp.where(end_mine[:1] == end_other[:1], 1.0, 0.0)
    scale_mine = jnp.where(mine_later, 1.0, jnp.exp(final_other) * same)
    scale_other = jnp.where(mine_later, jnp.exp(final_mine) * same, 1.0)
    for head in range(heads):
        rows = slice(head * size, (head + 1) * size)
        out_ref[rows, :] = (
            scale_mine[head : head + 1] * mine_ref[rows, :]
            + scale_other[head : head + 1] * other_ref[rows, :]
        )
    out_ref[top : top + heads, :] = final_mine + final_other
    out_ref[top + heads :, :] = jnp.where(mine_later, end_mine, end_other)


def small_call(kernel, name, order, first, second, after):
    vmem = pl.BlockSpec(memory_space=pltpu.VMEM)
    return pl.pallas_call(
        lambda order_ref, first_ref, second_ref, *rest: kernel(
            order_ref, first_ref, second_ref, rest[-1]
        ),
        in_specs=[pl.BlockSpec(memory_space=pltpu.SMEM), vmem, vmem]
        + [pl.BlockSpec(memory_space=pl.ANY)] * len(after),
        out_specs=vmem,
        out_shape=pltpu.VMEM(first.shape, F32),
        compiler_params=pltpu.CompilerParams(vmem_limit_bytes=8 * MIB),
        cost_estimate=SHORT,
        name=name,
    )(order, first, second, *after)


def joined(order, mine, other, heads, after=()):
    return small_call(
        functools.partial(join_kernel, heads), "join_windows", order, mine, other, after
    )


def pick_kernel(order_ref, even_ref, odd_ref, out_ref):
    odd = (order_ref[0] & 1) == 1

    @pl.when(odd)
    def _():
        out_ref[...] = odd_ref[...]

    @pl.when(jnp.logical_not(odd))
    def _():
        out_ref[...] = even_ref[...]


def picked(order, even, odd, after=()):
    return small_call(pick_kernel, "pick_message", order, even, odd, after)


def make_mask(seg_ref, mask_ref):
    tokens = seg_ref.shape[1]
    seg = seg_ref[...].astype(F32)
    column = as_column(seg, 128)
    for start in range(0, tokens, 128):
        across = lax.broadcasted_iota(jnp.int32, (tokens, 128), 1) + start
        down = lax.broadcasted_iota(jnp.int32, (tokens, 128), 0)
        seen = (column == seg[:, start : start + 128]) & (across <= down)
        mask_ref[:, start : start + 128] = jnp.where(seen, 0.0, -1e30)


def intra_kernel(
    first, heads, through, after, mask_ref, a_ref, gain_ref, q_ref, k_ref, v_ref, g_ref, *refs
):
    o_ref, gate_ref, *copied = refs[through + after :]
    for source, target in zip(refs[:through], copied):
        target[...] = source[...]
    tokens = mask_ref.shape[0]
    size = q_ref.shape[1] // heads
    block = min(tokens, 256)
    for j in range(heads):
        columns = slice(j * size, (j + 1) * size)
        a_row = a_ref[first + j : first + j + 1, :] * 1.4426950408889634
        a_column = as_column(a_row, 128)
        for start in range(0, tokens, block):
            here, upto = slice(start, start + block), slice(0, start + block)
            scores = lax.dot_general(
                q_ref[here, columns], k_ref[upto, columns], NT, preferred_element_type=F32
            )
            spread = jnp.concatenate([a_column[here]] * ((start + block) // 128), axis=1)
            weight = jnp.exp2(spread - a_row[:, upto] + mask_ref[here, upto])
            probs = (scores * weight).astype(BF16)
            o_ref[here, columns] = lax.dot_general(
                probs, v_ref[upto, columns], NN, preferred_element_type=F32
            )
        half = 0.5 * gain_ref[:, (first + j) * size : (first + j + 1) * size]
        gate_ref[:, columns] = half + half * jnp.tanh(0.5 * g_ref[:, columns].astype(F32))


def intra(mask, a, gain, q, k, v, g, first, heads, through=(), after=()):
    tokens, size = mask.shape[0], gain.shape[1] // a.shape[0]
    vmem = pl.BlockSpec(memory_space=pltpu.VMEM)
    o, gate, *copied = pl.pallas_call(
        functools.partial(intra_kernel, first, heads, len(through), len(after)),
        in_specs=[vmem] * (7 + len(through)) + [pl.BlockSpec(memory_space=pl.ANY)] * len(after),
        out_specs=[vmem] * (2 + len(through)),
        out_shape=[pltpu.VMEM((tokens, heads * size), F32)] * 2
        + [pltpu.VMEM(x.shape, x.dtype) for x in through],
        compiler_params=pltpu.CompilerParams(vmem_limit_bytes=8 * MIB),
        cost_estimate=SHORT,
        name="intra_span",
    )(mask, a, gain, q, k, v, g, *through, *after)
    return (o, gate, q), copied


def final_kernel(
    first,
    heads,
    kind,
    unread,
    order_ref,
    seg_ref,
    own_ref,
    near_ref,
    past_ref,
    o_ref,
    gate_ref,
    q_ref,
    a_ref,
    *rest,
):
    gated_hbm, snap_hbm, gated_ref, snap_ref, sems = rest[unread:]
    tokens, size = q_ref.shape[0], own_ref.shape[1]
    block = min(tokens, 256)
    top = heads * size
    place = order_ref[0]
    ends = slice(top + heads, top + heads + 1)
    finals = slice(top, top + heads)
    own_end, near_end, past_end = own_ref[ends, :], near_ref[ends, :], past_ref[ends, :]
    bridged = jnp.exp(near_ref[finals, :]) * jnp.where(near_end == past_end, 1.0, 0.0)
    if kind == "pair":
        odd = (place & 1) == 1
        previous = jnp.where(odd, near_end, past_end)
        scale_near = jnp.where(odd, 1.0, 0.0)
        scale_past = jnp.where(odd, bridged, 1.0)
    else:
        previous = near_end
        scale_near = jnp.where(place > 0, 1.0, 0.0)
        scale_past = bridged
    scale_past = jnp.where(place >= 2, scale_past, 0.0)
    own_decay = jnp.exp(own_ref[finals, :]) * jnp.where(own_end == previous, 1.0, 0.0)
    valid = seg_ref[...].astype(F32) == previous[:, :1]
    copies = []
    for j in range(heads):
        rows = columns = slice(j * size, (j + 1) * size)
        state = scale_past[j : j + 1] * past_ref[rows, :] + scale_near * near_ref[rows, :]
        snap_ref[j] = own_decay[j : j + 1] * state + own_ref[rows, :]
        high = state.astype(BF16)
        low = (state - high.astype(F32)).astype(BF16)
        q = q_ref[:, columns]
        both = jnp.concatenate([high, low], axis=0)
        decay = jnp.where(valid, jnp.exp(a_ref[first + j : first + j + 1, :]), 0.0)
        decay = as_column(decay, size)
        for start in range(0, tokens, block):
            here = slice(start, start + block)
            inter = lax.dot_general(
                jnp.concatenate([q[here], q[here]], axis=1), both, NN, preferred_element_type=F32
            )
            mixed = o_ref[here, columns] + inter * decay[here]
            mean_square = jnp.mean(mixed * mixed, axis=1, keepdims=True)
            gated = mixed * lax.rsqrt(mean_square + 1e-06) * gate_ref[here, columns]
            gated_ref[here, columns] = gated.astype(BF16)
        if j % 2 == 1 or j == heads - 1:
            begin = j - j % 2
            width = (j + 1 - begin) * size
            heads_here = pl.ds(first + begin, j + 1 - begin)
            place = pl.ds((first + begin) * size, width)
            for source, target in (
                (gated_ref.at[:, pl.ds(begin * size, width)], gated_hbm.at[:, place]),
                (snap_ref.at[pl.ds(begin, j + 1 - begin)], snap_hbm.at[0, heads_here]),
            ):
                copies.append(pltpu.make_async_copy(source, target, sems.at[len(copies)]))
                copies[-1].start()
    for copy in copies:
        copy.wait()


def finish(order, seg, own, near, past, o, gate, q, a, so_far, after, first, heads, kind):
    tokens, size = q.shape[0], q.shape[1] // heads
    total = a.shape[0]
    vmem, anywhere = pl.BlockSpec(memory_space=pltpu.VMEM), pl.BlockSpec(memory_space=pl.ANY)
    unread = len(so_far) + len(after)
    return pl.pallas_call(
        functools.partial(final_kernel, first, heads, kind, unread),
        in_specs=[pl.BlockSpec(memory_space=pltpu.SMEM)] + [vmem] * 8 + [anywhere] * unread,
        out_specs=[anywhere, anywhere],
        out_shape=[
            jax.ShapeDtypeStruct((tokens, total * size), BF16),
            jax.ShapeDtypeStruct((1, total, size, size), F32),
        ],
        scratch_shapes=[
            pltpu.VMEM((tokens, heads * size), BF16),
            pltpu.VMEM((heads, size, size), F32),
            pltpu.SemaphoreType.DMA((2 * heads,)),
        ],
        input_output_aliases={9 + i: i for i in range(len(so_far))},
        compiler_params=pltpu.CompilerParams(vmem_limit_bytes=8 * MIB),
        cost_estimate=SHORT,
        name="finish",
    )(order, seg, own, near, past, o, gate, q, a, *so_far, *after)


def shards(q, k, v, g, segment, decay_exponent, retention, norm_gain):
    heads = decay_exponent.shape[0]
    tokens = q.shape[0]
    count = lax.axis_size("seq")
    place = lax.axis_index("seq")
    reach = max(1, count // 4)
    far = lambda x: pltpu.with_memory_space_constraint(x, pltpu.HBM)
    q, k, v, g = far(q), far(k), far(v), far(g)
    gain = norm_gain.reshape(1, -1)
    order = jnp.where(place >= 2, 2 + (place & 1), place & 1).astype(jnp.int32).reshape(1)
    later = jnp.ones((1,), jnp.int32)
    swap = lambda x: lax.ppermute(x, "seq", [(c, c ^ 1) for c in range(count)])
    turn = lambda x: lax.ppermute(x, "seq", [(c, (c + 2) % count) for c in range(count)])

    half = heads // 2
    small = half * 3 // 8
    big = half - small
    chunks = [(0, big), (half, big), (big, small), (half + big, small)]

    def widened(x, many, shift, window):
        while window < reach:
            past = lax.ppermute(x, "seq", [(c, c + shift) for c in range(count - shift)])
            x = joined(later, x, past, many)
            shift, window = 2 * shift, 2 * window
        return x

    own, a, w, seg, k_near, v_near = first_messages(
        order,
        far(segment.reshape(1, tokens)),
        far(decay_exponent.reshape(1, heads)),
        far(retention),
        k,
        v,
        heads,
        chunks[:2],
    )
    near, past, inside = {}, {}, {}
    near[1] = swap(own[1])
    past[0] = turn(own[0])
    messages, mask, k_rest, v_rest, q_near, g_near = rest_messages(
        seg, a, w, q, k, v, g, chunks, 2
    )
    own, k_near, v_near = [*own, *messages], [*k_near, *k_rest], [*v_near, *v_rest]

    def look_inside(i, through=(), after=()):
        inside[i], copied = intra(
            mask, a, gain, q_near[i], k_near[i], v_near[i], g_near[i], *chunks[i], through, after
        )
        return copied

    own[2], own[3] = look_inside(0, (own[2], own[3]))
    past[2] = turn(own[2])
    near[3] = swap(own[3])
    look_inside(1, (), (own[2], own[3]))

    def second_hops(i, after):
        picks = picked(order, own[i], past[i], after)
        near[i] = swap(picks)
        both = joined(order, own[i + 1], near[i + 1], chunks[i + 1][1], (picks,))
        past[i + 1] = turn(both)
        return both

    both = second_hops(0, (inside[1][0],))
    look_inside(2, (), (both,))
    look_inside(3, (), (both,))
    both = second_hops(2, (inside[2][0], inside[3][0]))

    if reach > 2:
        for i, (_, many) in enumerate(chunks):
            if i % 2 == 0:
                near[i] = jnp.where(place >= 1, near[i], 0.0)
                past[i] = jnp.where(place >= 2, past[i], 0.0)
                near[i] = widened(joined(later, near[i], past[i], many), many, 2, 2)
                past[i] = jnp.zeros_like(near[i])
            else:
                past[i] = widened(jnp.where(place >= 2, past[i], 0.0), many, 2, 2)

    result = ()
    for i, (first, many) in enumerate(chunks):
        result = finish(
            order, seg, own[i], near[i], past[i], *inside[i], a, result, (both,), first, many,
            ("span", "pair")[i % 2],
        )
    return tuple(result)


def solution(mesh):
    placed = (
        P(("groups", "seq"), "wt"),
        P(("groups", "seq"), "wt"),
        P(("groups", "seq"), "wt"),
        P(("groups", "seq"), "wt"),
        P(("groups", "seq")),
        P("wt"),
        P("wt", ("groups", "seq")),
        P("wt"),
    )
    return jax.shard_map(
        shards,
        mesh=mesh,
        in_specs=placed,
        out_specs=(P(("groups", "seq"), "wt"), P(("groups", "seq"), "wt", None, None)),
        check_vma=False,
    )
```

```python
import functools

import jax
import jax.numpy as jnp
from jax import lax
from jax.experimental import pallas as pl
from jax.experimental.pallas import tpu as pltpu
from jax.sharding import PartitionSpec as P

F32 = jnp.float32
BF16 = jnp.bfloat16
NN = (((1,), (0,)), ((), ()))
NT = (((1,), (1,)), ((), ()))
MIB = 1 << 20
SHORT = pl.CostEstimate(flops=1, bytes_accessed=1, transcendentals=0)


def vmem_spec(shape, index_map):
    return pl.BlockSpec(shape, index_map)


def as_column(row, lanes):
    return jnp.broadcast_to(row, (lanes, row.shape[1])).T


def meta_rows(heads):
    return -(-(heads + 1) // 8) * 8


def put_message(msg_ref, first, heads, size, w_ref, finals, end, k_ref, v_ref):
    top = heads * size
    for j in range(heads):
        columns = slice(j * size, (j + 1) * size)
        weight = w_ref[first + j : first + j + 1, :]
        keyed = (k_ref[:, columns].astype(F32).T * weight).astype(BF16)
        msg_ref[columns, :] = lax.dot_general(
            keyed, v_ref[:, columns], NN, preferred_element_type=F32
        )
    msg_ref[top : top + heads, :] = jnp.broadcast_to(finals, (heads, size))
    below = meta_rows(heads) - heads
    msg_ref[top + heads :, :] = jnp.broadcast_to(end.astype(F32), (below, size))


def first_kernel(heads, chunks, order_ref, seg_hbm, exponent_hbm, keep_hbm, k_hbm, v_hbm, *refs):
    number = len(chunks)
    messages, refs = refs[:number], refs[number:]
    (a_ref, w_ref, seg_ref), refs = refs[:3], refs[3:]
    k_refs, v_refs, refs = refs[:number], refs[number : 2 * number], refs[2 * number :]
    exponent_ref, keep_ref, sems = refs
    tokens = seg_ref.shape[1]
    size = messages[0].shape[1]
    pairs = [(keep_hbm, keep_ref), (exponent_hbm, exponent_ref), (seg_hbm, seg_ref)]
    for i, (first, many) in enumerate(chunks):
        wide = pl.ds(first * size, many * size)
        pairs += [(k_hbm.at[:, wide], k_refs[i]), (v_hbm.at[:, wide], v_refs[i])]
    copies = [pltpu.make_async_copy(*pair, sems.at[i]) for i, pair in enumerate(pairs)]
    for copy in copies:
        copy.start()
    earlier = lax.broadcasted_iota(jnp.int32, (tokens, tokens), 0)
    later = lax.broadcasted_iota(jnp.int32, (tokens, tokens), 1)
    upper = jnp.where(earlier <= later, 1.0, 0.0).astype(BF16)
    across = lax.broadcasted_iota(jnp.int32, (heads, heads), 1)
    down = lax.broadcasted_iota(jnp.int32, (heads, heads), 0)
    for copy in copies[:3]:
        copy.wait()
    spread = jnp.broadcast_to(exponent_ref[...], (heads, heads))
    exponent = jnp.sum(jnp.where(across == down, spread, 0).astype(F32), axis=1, keepdims=True)
    a = -jnp.exp2(-exponent) + jnp.log(keep_ref[...])
    high = a.astype(BF16)
    rest = a - high.astype(F32)
    middle = rest.astype(BF16)
    low = (rest - middle.astype(F32)).astype(BF16)
    parts = jnp.concatenate([high, middle, low], axis=0)
    sums = lax.dot_general(parts, upper, NN, preferred_element_type=F32)
    cumulative = sums[:heads] + (sums[heads : 2 * heads] + sums[2 * heads :])
    a_ref[...] = cumulative
    final = cumulative[:, tokens - 1 :]
    seg = seg_ref[...]
    last = seg[:, tokens - 1 :]
    w_ref[...] = jnp.where(seg == last, jnp.exp(final - cumulative), 0.0)
    for i, (first, many) in enumerate(chunks):
        copies[3 + 2 * i].wait()
        copies[4 + 2 * i].wait()
        finals = final[first : first + many]
        put_message(messages[i], first, many, size, w_ref, finals, last, k_refs[i], v_refs[i])


def message_of(size, many):
    return pltpu.VMEM((many * size + meta_rows(many), size), F32)


def first_messages(order, seg, exponent, keep, k, v, heads, chunks):
    tokens, size = k.shape[0], k.shape[1] // heads
    near = [pltpu.VMEM((tokens, many * size), BF16) for _, many in chunks]
    shapes = [message_of(size, many) for _, many in chunks]
    shapes += [pltpu.VMEM((heads, tokens), F32)] * 2 + [pltpu.VMEM((1, tokens), jnp.int32)]
    shapes += near + near
    number = len(chunks)
    out = pl.pallas_call(
        functools.partial(first_kernel, heads, chunks),
        in_specs=[pl.BlockSpec(memory_space=pltpu.SMEM)]
        + [pl.BlockSpec(memory_space=pltpu.HBM)] * 5,
        out_specs=[pl.BlockSpec(memory_space=pltpu.VMEM)] * len(shapes),
        out_shape=shapes,
        scratch_shapes=[
            pltpu.VMEM((1, heads), jnp.int32),
            pltpu.VMEM((heads, tokens), F32),
            pltpu.SemaphoreType.DMA((3 + 2 * number,)),
        ],
        compiler_params=pltpu.CompilerParams(vmem_limit_bytes=8 * MIB),
        cost_estimate=SHORT,
        name="first_messages",
    )(order, seg, exponent, keep, k, v)
    messages, (a, w, seg), out = out[:number], out[number : number + 3], out[number + 3 :]
    return messages, a, w, seg, out[:number], out[number:]


def rest_kernel(chunks, done, seg_ref, a_ref, w_ref, q_hbm, k_hbm, v_hbm, g_hbm, *refs):
    tokens = seg_ref.shape[1]
    left, number = chunks[done:], len(chunks)
    messages, mask_ref, refs, sems = refs[: len(left)], refs[len(left)], refs[len(left) + 1 : -1], refs[-1]
    k_refs, refs = refs[: len(left)], refs[len(left) :]
    v_refs, refs = refs[: len(left)], refs[len(left) :]
    q_refs, g_refs = refs[:number], refs[number:]
    size = messages[0].shape[1]
    pairs = []
    for i, (first, many) in enumerate(left):
        wide = pl.ds(first * size, many * size)
        pairs += [(k_hbm.at[:, wide], k_refs[i]), (v_hbm.at[:, wide], v_refs[i])]
    for i, (first, many) in enumerate(chunks):
        wide = pl.ds(first * size, many * size)
        pairs += [(q_hbm.at[:, wide], q_refs[i]), (g_hbm.at[:, wide], g_refs[i])]
    copies = [pltpu.make_async_copy(*pair, sems.at[i]) for i, pair in enumerate(pairs)]
    for copy in copies:
        copy.start()
    make_mask(seg_ref, mask_ref)
    last = seg_ref[:, tokens - 1 :]
    for i, (first, many) in enumerate(left):
        copies[2 * i].wait()
        copies[2 * i + 1].wait()
        final = a_ref[first : first + many, tokens - 1 :]
        put_message(messages[i], first, many, size, w_ref, final, last, k_refs[i], v_refs[i])
    for copy in copies[2 * len(left) :]:
        copy.wait()


def rest_messages(seg, a, w, q, k, v, g, chunks, done):
    heads = a.shape[0]
    tokens, size = k.shape[0], k.shape[1] // heads
    near = [pltpu.VMEM((tokens, many * size), BF16) for _, many in chunks]
    shapes = [message_of(size, many) for _, many in chunks[done:]]
    shapes += [pltpu.VMEM((tokens, tokens), F32)] + near[done:] * 2 + near * 2
    left, number = len(chunks) - done, len(chunks)
    out = pl.pallas_call(
        functools.partial(rest_kernel, chunks, done),
        in_specs=[pl.BlockSpec(memory_space=pltpu.VMEM)] * 3
        + [pl.BlockSpec(memory_space=pltpu.HBM)] * 4,
        out_specs=[pl.BlockSpec(memory_space=pltpu.VMEM)] * len(shapes),
        out_shape=shapes,
        scratch_shapes=[pltpu.SemaphoreType.DMA((2 * (left + number),))],
        compiler_params=pltpu.CompilerParams(vmem_limit_bytes=8 * MIB),
        cost_estimate=SHORT,
        name="rest_messages",
    )(seg, a, w, q, k, v, g)
    messages, mask, out = out[:left], out[left], out[left + 1 :]
    k_near, v_near, out = out[:left], out[left : 2 * left], out[2 * left :]
    return messages, mask, k_near, v_near, out[:number], out[number:]


def join_kernel(heads, order_ref, mine_ref, other_ref, out_ref):
    size = mine_ref.shape[1]
    top = heads * size
    mine_later = (order_ref[0] & 1) == 1
    final_mine, final_other = mine_ref[top : top + heads, :], other_ref[top : top + heads, :]
    end_mine, end_other = mine_ref[top + heads :, :], other_ref[top + heads :, :]
    same = jnp.where(end_mine[:1] == end_other[:1], 1.0, 0.0)
    scale_mine = jnp.where(mine_later, 1.0, jnp.exp(final_other) * same)
    scale_other = jnp.where(mine_later, jnp.exp(final_mine) * same, 1.0)
    for head in range(heads):
        rows = slice(head * size, (head + 1) * size)
        out_ref[rows, :] = (
            scale_mine[head : head + 1] * mine_ref[rows, :]
            + scale_other[head : head + 1] * other_ref[rows, :]
        )
    out_ref[top : top + heads, :] = final_mine + final_other
    out_ref[top + heads :, :] = jnp.where(mine_later, end_mine, end_other)


def small_call(kernel, name, order, first, second, after):
    vmem = pl.BlockSpec(memory_space=pltpu.VMEM)
    return pl.pallas_call(
        lambda order_ref, first_ref, second_ref, *rest: kernel(
            order_ref, first_ref, second_ref, rest[-1]
        ),
        in_specs=[pl.BlockSpec(memory_space=pltpu.SMEM), vmem, vmem]
        + [pl.BlockSpec(memory_space=pl.ANY)] * len(after),
        out_specs=vmem,
        out_shape=pltpu.VMEM(first.shape, F32),
        compiler_params=pltpu.CompilerParams(vmem_limit_bytes=8 * MIB),
        cost_estimate=SHORT,
        name=name,
    )(order, first, second, *after)


def joined(order, mine, other, heads, after=()):
    return small_call(
        functools.partial(join_kernel, heads), "join_windows", order, mine, other, after
    )


def pick_kernel(order_ref, even_ref, odd_ref, out_ref):
    odd = (order_ref[0] & 1) == 1

    @pl.when(odd)
    def _():
        out_ref[...] = odd_ref[...]

    @pl.when(jnp.logical_not(odd))
    def _():
        out_ref[...] = even_ref[...]


def picked(order, even, odd, after=()):
    return small_call(pick_kernel, "pick_message", order, even, odd, after)


def make_mask(seg_ref, mask_ref):
    tokens = seg_ref.shape[1]
    seg = seg_ref[...].astype(F32)
    column = as_column(seg, 128)
    for start in range(0, tokens, 128):
        across = lax.broadcasted_iota(jnp.int32, (tokens, 128), 1) + start
        down = lax.broadcasted_iota(jnp.int32, (tokens, 128), 0)
        seen = (column == seg[:, start : start + 128]) & (across <= down)
        mask_ref[:, start : start + 128] = jnp.where(seen, 0.0, -1e30)


def intra_kernel(
    first, heads, through, after, mask_ref, a_ref, gain_ref, q_ref, k_ref, v_ref, g_ref, *refs
):
    o_ref, gate_ref, *copied = refs[through + after :]
    for source, target in zip(refs[:through], copied):
        target[...] = source[...]
    tokens = mask_ref.shape[0]
    size = q_ref.shape[1] // heads
    block = min(tokens, 256)
    for j in range(heads):
        columns = slice(j * size, (j + 1) * size)
        a_row = a_ref[first + j : first + j + 1, :] * 1.4426950408889634
        a_column = as_column(a_row, 128)
        for start in range(0, tokens, block):
            here, upto = slice(start, start + block), slice(0, start + block)
            scores = lax.dot_general(
                q_ref[here, columns], k_ref[upto, columns], NT, preferred_element_type=F32
            )
            spread = jnp.concatenate([a_column[here]] * ((start + block) // 128), axis=1)
            weight = jnp.exp2(spread - a_row[:, upto] + mask_ref[here, upto])
            probs = (scores * weight).astype(BF16)
            o_ref[here, columns] = lax.dot_general(
                probs, v_ref[upto, columns], NN, preferred_element_type=F32
            )
        half = 0.5 * gain_ref[:, (first + j) * size : (first + j + 1) * size]
        gate_ref[:, columns] = half + half * jnp.tanh(0.5 * g_ref[:, columns].astype(F32))


def intra(mask, a, gain, q, k, v, g, first, heads, through=(), after=()):
    tokens, size = mask.shape[0], gain.shape[1] // a.shape[0]
    vmem = pl.BlockSpec(memory_space=pltpu.VMEM)
    o, gate, *copied = pl.pallas_call(
        functools.partial(intra_kernel, first, heads, len(through), len(after)),
        in_specs=[vmem] * (7 + len(through)) + [pl.BlockSpec(memory_space=pl.ANY)] * len(after),
        out_specs=[vmem] * (2 + len(through)),
        out_shape=[pltpu.VMEM((tokens, heads * size), F32)] * 2
        + [pltpu.VMEM(x.shape, x.dtype) for x in through],
        compiler_params=pltpu.CompilerParams(vmem_limit_bytes=8 * MIB),
        cost_estimate=SHORT,
        name="intra_span",
    )(mask, a, gain, q, k, v, g, *through, *after)
    return (o, gate, q), copied


def final_kernel(groups, unread, order_ref, seg_ref, a_ref, *rest):
    number = len(groups)
    inputs, rest = rest[: 6 * number], rest[6 * number + unread :]
    gated_hbm, snap_hbm, *scratch, sems = rest
    place = order_ref[0]
    seg = seg_ref[...].astype(F32)
    copies = []
    for i, (first, heads, kind) in enumerate(groups):
        own_ref, near_ref, past_ref, o_ref, gate_ref, q_ref = inputs[6 * i : 6 * i + 6]
        gated_ref, snap_ref = scratch[2 * i : 2 * i + 2]
        tokens, size = q_ref.shape[0], own_ref.shape[1]
        block = min(tokens, 256)
        top = heads * size
        ends = slice(top + heads, top + heads + 1)
        finals = slice(top, top + heads)
        own_end, near_end, past_end = own_ref[ends, :], near_ref[ends, :], past_ref[ends, :]
        bridged = jnp.exp(near_ref[finals, :]) * jnp.where(near_end == past_end, 1.0, 0.0)
        if kind == "pair":
            odd = (place & 1) == 1
            previous = jnp.where(odd, near_end, past_end)
            scale_near = jnp.where(odd, 1.0, 0.0)
            scale_past = jnp.where(odd, bridged, 1.0)
        else:
            previous = near_end
            scale_near = jnp.where(place > 0, 1.0, 0.0)
            scale_past = bridged
        scale_past = jnp.where(place >= 2, scale_past, 0.0)
        own_decay = jnp.exp(own_ref[finals, :]) * jnp.where(own_end == previous, 1.0, 0.0)
        valid = seg == previous[:, :1]
        for j in range(heads):
            rows = columns = slice(j * size, (j + 1) * size)
            state = scale_past[j : j + 1] * past_ref[rows, :] + scale_near * near_ref[rows, :]
            snap_ref[j] = own_decay[j : j + 1] * state + own_ref[rows, :]
            high = state.astype(BF16)
            low = (state - high.astype(F32)).astype(BF16)
            q = q_ref[:, columns]
            both = jnp.concatenate([high, low], axis=0)
            decay = jnp.where(valid, jnp.exp(a_ref[first + j : first + j + 1, :]), 0.0)
            decay = as_column(decay, size)
            for start in range(0, tokens, block):
                here = slice(start, start + block)
                inter = lax.dot_general(
                    jnp.concatenate([q[here], q[here]], axis=1),
                    both,
                    NN,
                    preferred_element_type=F32,
                )
                mixed = o_ref[here, columns] + inter * decay[here]
                mean_square = jnp.mean(mixed * mixed, axis=1, keepdims=True)
                gated = mixed * lax.rsqrt(mean_square + 1e-06) * gate_ref[here, columns]
                gated_ref[here, columns] = gated.astype(BF16)
            if j % 2 == 1 or j == heads - 1:
                begin = j - j % 2
                width = (j + 1 - begin) * size
                heads_here = pl.ds(first + begin, j + 1 - begin)
                there = pl.ds((first + begin) * size, width)
                for source, target in (
                    (gated_ref.at[:, pl.ds(begin * size, width)], gated_hbm.at[:, there]),
                    (snap_ref.at[pl.ds(begin, j + 1 - begin)], snap_hbm.at[0, heads_here]),
                ):
                    copies.append(pltpu.make_async_copy(source, target, sems.at[len(copies)]))
                    copies[-1].start()
    for copy in copies:
        copy.wait()


def finish(order, seg, a, groups, arrays, so_far, after):
    total, tokens = a.shape
    size = arrays[0].shape[1]
    vmem, anywhere = pl.BlockSpec(memory_space=pltpu.VMEM), pl.BlockSpec(memory_space=pl.ANY)
    unread = len(so_far) + len(after)
    scratch = []
    for _, many, _ in groups:
        scratch.append(pltpu.VMEM((tokens, many * size), BF16))
        scratch.append(pltpu.VMEM((many, size, size), F32))
    return pl.pallas_call(
        functools.partial(final_kernel, groups, unread),
        in_specs=[pl.BlockSpec(memory_space=pltpu.SMEM)]
        + [vmem] * (2 + len(arrays))
        + [anywhere] * unread,
        out_specs=[anywhere, anywhere],
        out_shape=[
            jax.ShapeDtypeStruct((tokens, total * size), BF16),
            jax.ShapeDtypeStruct((1, total, size, size), F32),
        ],
        scratch_shapes=scratch + [pltpu.SemaphoreType.DMA((2 * total,))],
        input_output_aliases={3 + len(arrays) + i: i for i in range(len(so_far))},
        compiler_params=pltpu.CompilerParams(vmem_limit_bytes=12 * MIB),
        cost_estimate=SHORT,
        name="finish",
    )(order, seg, a, *arrays, *so_far, *after)


def shards(q, k, v, g, segment, decay_exponent, retention, norm_gain):
    heads = decay_exponent.shape[0]
    tokens = q.shape[0]
    count = lax.axis_size("seq")
    place = lax.axis_index("seq")
    reach = max(1, count // 4)
    far = lambda x: pltpu.with_memory_space_constraint(x, pltpu.HBM)
    q, k, v, g = far(q), far(k), far(v), far(g)
    gain = norm_gain.reshape(1, -1)
    order = jnp.where(place >= 2, 2 + (place & 1), place & 1).astype(jnp.int32).reshape(1)
    later = jnp.ones((1,), jnp.int32)
    swap = lambda x: lax.ppermute(x, "seq", [(c, c ^ 1) for c in range(count)])
    turn = lambda x: lax.ppermute(x, "seq", [(c, (c + 2) % count) for c in range(count)])

    half = heads // 2
    small = half * 3 // 8
    big = half - small
    chunks = [(0, big), (half, big), (big, small), (half + big, small)]

    def widened(x, many, shift, window):
        while window < reach:
            past = lax.ppermute(x, "seq", [(c, c + shift) for c in range(count - shift)])
            x = joined(later, x, past, many)
            shift, window = 2 * shift, 2 * window
        return x

    own, a, w, seg, k_near, v_near = first_messages(
        order,
        far(segment.reshape(1, tokens)),
        far(decay_exponent.reshape(1, heads)),
        far(retention),
        k,
        v,
        heads,
        chunks[:2],
    )
    near, past, inside = {}, {}, {}
    near[1] = swap(own[1])
    past[0] = turn(own[0])
    messages, mask, k_rest, v_rest, q_near, g_near = rest_messages(
        seg, a, w, q, k, v, g, chunks, 2
    )
    own, k_near, v_near = [*own, *messages], [*k_near, *k_rest], [*v_near, *v_rest]

    def look_inside(i, through=(), after=()):
        inside[i], copied = intra(
            mask, a, gain, q_near[i], k_near[i], v_near[i], g_near[i], *chunks[i], through, after
        )
        return copied

    def pair_first(i, after):
        both = joined(order, own[i], near[i], chunks[i][1], after)
        past[i] = turn(both)
        return both

    def pair_last(i, after):
        message = picked(order, own[i], past[i], after)
        near[i] = swap(message)
        return message

    own[2], own[3] = look_inside(0, (own[2], own[3]))
    near[3] = swap(own[3])
    first_done = pair_first(1, (own[2],))
    past[2] = turn(own[2])
    second_done = pair_last(0, (first_done,))
    look_inside(1, (), (second_done,))
    look_inside(2, (), (inside[1][0],))
    look_inside(3, (), (inside[2][0],))
    second_done = pair_last(2, (inside[3][0],))
    first_done = pair_first(3, (second_done,))

    if reach > 2:
        for i, (_, many) in enumerate(chunks):
            if i % 2 == 0:
                near[i] = jnp.where(place >= 1, near[i], 0.0)
                past[i] = jnp.where(place >= 2, past[i], 0.0)
                near[i] = widened(joined(later, near[i], past[i], many), many, 2, 2)
                past[i] = jnp.zeros_like(near[i])
            else:
                past[i] = widened(jnp.where(place >= 2, past[i], 0.0), many, 2, 2)

    result = ()
    for group in ((0, 1), (2, 3)):
        groups = [(*chunks[i], ("span", "pair")[i % 2]) for i in group]
        arrays = [x for i in group for x in (own[i], near[i], past[i], *inside[i])]
        result = finish(order, seg, a, groups, arrays, result, (first_done,))
    return tuple(result)


def solution(mesh):
    placed = (
        P(("groups", "seq"), "wt"),
        P(("groups", "seq"), "wt"),
        P(("groups", "seq"), "wt"),
        P(("groups", "seq"), "wt"),
        P(("groups", "seq")),
        P("wt"),
        P("wt", ("groups", "seq")),
        P("wt"),
    )
    return jax.shard_map(
        shards,
        mesh=mesh,
        in_specs=placed,
        out_specs=(P(("groups", "seq"), "wt"), P(("groups", "seq"), "wt", None, None)),
        check_vma=False,
    )
```

```python
import functools

import jax
import jax.numpy as jnp
from jax import lax
from jax.experimental import pallas as pl
from jax.experimental.pallas import tpu as pltpu
from jax.sharding import PartitionSpec as P

F32 = jnp.float32
BF16 = jnp.bfloat16
NN = (((1,), (0,)), ((), ()))
NT = (((1,), (1,)), ((), ()))
MIB = 1 << 20
SHORT = pl.CostEstimate(flops=1, bytes_accessed=1, transcendentals=0)


def vmem_spec(shape, index_map):
    return pl.BlockSpec(shape, index_map)


def as_column(row, lanes):
    return jnp.broadcast_to(row, (lanes, row.shape[1])).T


def meta_rows(heads):
    return -(-(heads + 1) // 8) * 8


def put_message(msg_ref, first, heads, size, w_ref, finals, end, k_ref, v_ref):
    top = heads * size
    for j in range(heads):
        columns = slice(j * size, (j + 1) * size)
        weight = w_ref[first + j : first + j + 1, :]
        keyed = (k_ref[:, columns].astype(F32).T * weight).astype(BF16)
        msg_ref[columns, :] = lax.dot_general(
            keyed, v_ref[:, columns], NN, preferred_element_type=F32
        )
    msg_ref[top : top + heads, :] = jnp.broadcast_to(finals, (heads, size))
    below = meta_rows(heads) - heads
    msg_ref[top + heads :, :] = jnp.broadcast_to(end.astype(F32), (below, size))


def first_kernel(heads, chunks, order_ref, seg_hbm, exponent_hbm, keep_hbm, k_hbm, v_hbm, *refs):
    number = len(chunks)
    messages, refs = refs[:number], refs[number:]
    (a_ref, w_ref, seg_ref), refs = refs[:3], refs[3:]
    k_refs, v_refs, refs = refs[:number], refs[number : 2 * number], refs[2 * number :]
    exponent_ref, keep_ref, sems = refs
    tokens = seg_ref.shape[1]
    size = messages[0].shape[1]
    pairs = [(keep_hbm, keep_ref), (exponent_hbm, exponent_ref), (seg_hbm, seg_ref)]
    for i, (first, many) in enumerate(chunks):
        wide = pl.ds(first * size, many * size)
        pairs += [(k_hbm.at[:, wide], k_refs[i]), (v_hbm.at[:, wide], v_refs[i])]
    copies = [pltpu.make_async_copy(*pair, sems.at[i]) for i, pair in enumerate(pairs)]
    for copy in copies:
        copy.start()
    earlier = lax.broadcasted_iota(jnp.int32, (tokens, tokens), 0)
    later = lax.broadcasted_iota(jnp.int32, (tokens, tokens), 1)
    upper = jnp.where(earlier <= later, 1.0, 0.0).astype(BF16)
    across = lax.broadcasted_iota(jnp.int32, (heads, heads), 1)
    down = lax.broadcasted_iota(jnp.int32, (heads, heads), 0)
    for copy in copies[:3]:
        copy.wait()
    spread = jnp.broadcast_to(exponent_ref[...], (heads, heads))
    exponent = jnp.sum(jnp.where(across == down, spread, 0).astype(F32), axis=1, keepdims=True)
    a = -jnp.exp2(-exponent) + jnp.log(keep_ref[...])
    high = a.astype(BF16)
    rest = a - high.astype(F32)
    middle = rest.astype(BF16)
    low = (rest - middle.astype(F32)).astype(BF16)
    parts = jnp.concatenate([high, middle, low], axis=0)
    sums = lax.dot_general(parts, upper, NN, preferred_element_type=F32)
    cumulative = sums[:heads] + (sums[heads : 2 * heads] + sums[2 * heads :])
    a_ref[...] = cumulative
    final = cumulative[:, tokens - 1 :]
    seg = seg_ref[...]
    last = seg[:, tokens - 1 :]
    w_ref[...] = jnp.where(seg == last, jnp.exp(final - cumulative), 0.0)
    for i, (first, many) in enumerate(chunks):
        copies[3 + 2 * i].wait()
        copies[4 + 2 * i].wait()
        finals = final[first : first + many]
        put_message(messages[i], first, many, size, w_ref, finals, last, k_refs[i], v_refs[i])


def message_of(size, many):
    return pltpu.VMEM((many * size + meta_rows(many), size), F32)


def first_messages(order, seg, exponent, keep, k, v, heads, chunks):
    tokens, size = k.shape[0], k.shape[1] // heads
    near = [pltpu.VMEM((tokens, many * size), BF16) for _, many in chunks]
    shapes = [message_of(size, many) for _, many in chunks]
    shapes += [pltpu.VMEM((heads, tokens), F32)] * 2 + [pltpu.VMEM((1, tokens), jnp.int32)]
    shapes += near + near
    number = len(chunks)
    out = pl.pallas_call(
        functools.partial(first_kernel, heads, chunks),
        in_specs=[pl.BlockSpec(memory_space=pltpu.SMEM)]
        + [pl.BlockSpec(memory_space=pltpu.HBM)] * 5,
        out_specs=[pl.BlockSpec(memory_space=pltpu.VMEM)] * len(shapes),
        out_shape=shapes,
        scratch_shapes=[
            pltpu.VMEM((1, heads), jnp.int32),
            pltpu.VMEM((heads, tokens), F32),
            pltpu.SemaphoreType.DMA((3 + 2 * number,)),
        ],
        compiler_params=pltpu.CompilerParams(vmem_limit_bytes=8 * MIB),
        cost_estimate=SHORT,
        name="first_messages",
    )(order, seg, exponent, keep, k, v)
    messages, (a, w, seg), out = out[:number], out[number : number + 3], out[number + 3 :]
    return messages, a, w, seg, out[:number], out[number:]


def rest_kernel(chunks, done, seg_ref, a_ref, w_ref, q_hbm, k_hbm, v_hbm, g_hbm, *refs):
    tokens = seg_ref.shape[1]
    left, number = chunks[done:], len(chunks)
    messages, mask_ref, refs, sems = refs[: len(left)], refs[len(left)], refs[len(left) + 1 : -1], refs[-1]
    k_refs, refs = refs[: len(left)], refs[len(left) :]
    v_refs, refs = refs[: len(left)], refs[len(left) :]
    q_refs, g_refs = refs[:number], refs[number:]
    size = messages[0].shape[1]
    pairs = []
    for i, (first, many) in enumerate(left):
        wide = pl.ds(first * size, many * size)
        pairs += [(k_hbm.at[:, wide], k_refs[i]), (v_hbm.at[:, wide], v_refs[i])]
    for i, (first, many) in enumerate(chunks):
        wide = pl.ds(first * size, many * size)
        pairs += [(q_hbm.at[:, wide], q_refs[i]), (g_hbm.at[:, wide], g_refs[i])]
    copies = [pltpu.make_async_copy(*pair, sems.at[i]) for i, pair in enumerate(pairs)]
    for copy in copies:
        copy.start()
    make_mask(seg_ref, mask_ref)
    last = seg_ref[:, tokens - 1 :]
    for i, (first, many) in enumerate(left):
        copies[2 * i].wait()
        copies[2 * i + 1].wait()
        final = a_ref[first : first + many, tokens - 1 :]
        put_message(messages[i], first, many, size, w_ref, final, last, k_refs[i], v_refs[i])
    for copy in copies[2 * len(left) :]:
        copy.wait()


def rest_messages(seg, a, w, q, k, v, g, chunks, done):
    heads = a.shape[0]
    tokens, size = k.shape[0], k.shape[1] // heads
    near = [pltpu.VMEM((tokens, many * size), BF16) for _, many in chunks]
    shapes = [message_of(size, many) for _, many in chunks[done:]]
    shapes += [pltpu.VMEM((tokens, tokens), F32)] + near[done:] * 2 + near * 2
    left, number = len(chunks) - done, len(chunks)
    out = pl.pallas_call(
        functools.partial(rest_kernel, chunks, done),
        in_specs=[pl.BlockSpec(memory_space=pltpu.VMEM)] * 3
        + [pl.BlockSpec(memory_space=pltpu.HBM)] * 4,
        out_specs=[pl.BlockSpec(memory_space=pltpu.VMEM)] * len(shapes),
        out_shape=shapes,
        scratch_shapes=[pltpu.SemaphoreType.DMA((2 * (left + number),))],
        compiler_params=pltpu.CompilerParams(vmem_limit_bytes=8 * MIB),
        cost_estimate=SHORT,
        name="rest_messages",
    )(seg, a, w, q, k, v, g)
    messages, mask, out = out[:left], out[left], out[left + 1 :]
    k_near, v_near, out = out[:left], out[left : 2 * left], out[2 * left :]
    return messages, mask, k_near, v_near, out[:number], out[number:]


def join_kernel(heads, order_ref, mine_ref, other_ref, out_ref):
    size = mine_ref.shape[1]
    top = heads * size
    mine_later = (order_ref[0] & 1) == 1
    final_mine, final_other = mine_ref[top : top + heads, :], other_ref[top : top + heads, :]
    end_mine, end_other = mine_ref[top + heads :, :], other_ref[top + heads :, :]
    same = jnp.where(end_mine[:1] == end_other[:1], 1.0, 0.0)
    scale_mine = jnp.where(mine_later, 1.0, jnp.exp(final_other) * same)
    scale_other = jnp.where(mine_later, jnp.exp(final_mine) * same, 1.0)
    for head in range(heads):
        rows = slice(head * size, (head + 1) * size)
        out_ref[rows, :] = (
            scale_mine[head : head + 1] * mine_ref[rows, :]
            + scale_other[head : head + 1] * other_ref[rows, :]
        )
    out_ref[top : top + heads, :] = final_mine + final_other
    out_ref[top + heads :, :] = jnp.where(mine_later, end_mine, end_other)


def small_call(kernel, name, order, arrays, after):
    vmem = pl.BlockSpec(memory_space=pltpu.VMEM)
    return pl.pallas_call(
        lambda *refs: kernel(*refs[: 1 + len(arrays)], refs[-1]),
        in_specs=[pl.BlockSpec(memory_space=pltpu.SMEM)]
        + [vmem] * len(arrays)
        + [pl.BlockSpec(memory_space=pl.ANY)] * len(after),
        out_specs=vmem,
        out_shape=pltpu.VMEM(arrays[0].shape, F32),
        compiler_params=pltpu.CompilerParams(vmem_limit_bytes=8 * MIB),
        cost_estimate=SHORT,
        name=name,
    )(order, *arrays, *after)


def joined(order, mine, other, heads, after=()):
    return small_call(
        functools.partial(join_kernel, heads), "join_windows", order, (mine, other), after
    )


def pick_kernel(order_ref, even_ref, odd_ref, out_ref):
    odd = (order_ref[0] & 1) == 1

    @pl.when(odd)
    def _():
        out_ref[...] = odd_ref[...]

    @pl.when(jnp.logical_not(odd))
    def _():
        out_ref[...] = even_ref[...]


def picked(order, even, odd, after=()):
    return small_call(pick_kernel, "pick_message", order, (even, odd), after)


def make_mask(seg_ref, mask_ref):
    tokens = seg_ref.shape[1]
    seg = seg_ref[...].astype(F32)
    column = as_column(seg, 128)
    for start in range(0, tokens, 128):
        across = lax.broadcasted_iota(jnp.int32, (tokens, 128), 1) + start
        down = lax.broadcasted_iota(jnp.int32, (tokens, 128), 0)
        seen = (column == seg[:, start : start + 128]) & (across <= down)
        mask_ref[:, start : start + 128] = jnp.where(seen, 0.0, -1e30)


def intra_kernel(
    first, heads, through, after, mask_ref, a_ref, gain_ref, q_ref, k_ref, v_ref, g_ref, *refs
):
    o_ref, gate_ref, decay_ref, *copied = refs[through + after :]
    for source, target in zip(refs[:through], copied):
        target[...] = source[...]
    tokens = mask_ref.shape[0]
    size = q_ref.shape[1] // heads
    block = min(tokens, 256)
    for j in range(heads):
        columns = slice(j * size, (j + 1) * size)
        a_row = a_ref[first + j : first + j + 1, :] * 1.4426950408889634
        a_column = as_column(a_row, 128)
        decay_ref[:, columns] = jnp.exp2(a_column)
        for start in range(0, tokens, block):
            here, upto = slice(start, start + block), slice(0, start + block)
            scores = lax.dot_general(
                q_ref[here, columns], k_ref[upto, columns], NT, preferred_element_type=F32
            )
            spread = jnp.concatenate([a_column[here]] * ((start + block) // 128), axis=1)
            weight = jnp.exp2(spread - a_row[:, upto] + mask_ref[here, upto])
            probs = (scores * weight).astype(BF16)
            o_ref[here, columns] = lax.dot_general(
                probs, v_ref[upto, columns], NN, preferred_element_type=F32
            )
        half = 0.5 * gain_ref[:, (first + j) * size : (first + j + 1) * size]
        gate_ref[:, columns] = half + half * jnp.tanh(0.5 * g_ref[:, columns].astype(F32))


def intra(mask, a, gain, q, k, v, g, first, heads, through=(), after=()):
    tokens, size = mask.shape[0], gain.shape[1] // a.shape[0]
    vmem = pl.BlockSpec(memory_space=pltpu.VMEM)
    o, gate, decay, *copied = pl.pallas_call(
        functools.partial(intra_kernel, first, heads, len(through), len(after)),
        in_specs=[vmem] * (7 + len(through)) + [pl.BlockSpec(memory_space=pl.ANY)] * len(after),
        out_specs=[vmem] * (3 + len(through)),
        out_shape=[pltpu.VMEM((tokens, heads * size), F32)] * 3
        + [pltpu.VMEM(x.shape, x.dtype) for x in through],
        compiler_params=pltpu.CompilerParams(vmem_limit_bytes=8 * MIB),
        cost_estimate=SHORT,
        name="intra_span",
    )(mask, a, gain, q, k, v, g, *through, *after)
    return (o, gate, decay, q), copied


def final_kernel(groups, unread, order_ref, seg_ref, *rest):
    number = len(groups)
    inputs, rest = rest[: 7 * number], rest[7 * number + unread :]
    gated_hbm, snap_hbm, *scratch, sems = rest
    place = order_ref[0]
    seg = seg_ref[...].astype(F32)
    copies, work = [], []

    def send(source, target):
        copies.append(pltpu.make_async_copy(source, target, sems.at[len(copies)]))
        copies[-1].start()

    for i, (first, heads, kind) in enumerate(groups):
        own_ref, near_ref, past_ref, o_ref, gate_ref, decay_ref, q_ref = inputs[7 * i : 7 * i + 7]
        gated_ref, snap_ref = scratch[2 * i : 2 * i + 2]
        size = own_ref.shape[1]
        top = heads * size
        ends = slice(top + heads, top + heads + 1)
        finals = slice(top, top + heads)
        own_end, near_end, past_end = own_ref[ends, :], near_ref[ends, :], past_ref[ends, :]
        bridged = jnp.exp(near_ref[finals, :]) * jnp.where(near_end == past_end, 1.0, 0.0)
        if kind == "pair":
            odd = (place & 1) == 1
            previous = jnp.where(odd, near_end, past_end)
            scale_near = jnp.where(odd, 1.0, 0.0)
            scale_past = jnp.where(odd, bridged, 1.0)
        else:
            previous = near_end
            scale_near = jnp.where(place > 0, 1.0, 0.0)
            scale_past = bridged
        scale_past = jnp.where(place >= 2, scale_past, 0.0)
        own_decay = jnp.exp(own_ref[finals, :]) * jnp.where(own_end == previous, 1.0, 0.0)
        valid = as_column(jnp.where(seg == previous[:, :1], 1.0, 0.0), size)
        for j in range(heads):
            rows = slice(j * size, (j + 1) * size)
            state = scale_past[j : j + 1] * past_ref[rows, :] + scale_near * near_ref[rows, :]
            snap_ref[j] = own_decay[j : j + 1] * state + own_ref[rows, :]
            high = state.astype(BF16)
            low = (state - high.astype(F32)).astype(BF16)
            both = jnp.concatenate([high, low], axis=0)
            work.append((i, j, first, heads, both, valid, (o_ref, gate_ref, decay_ref, q_ref)))
        send(snap_ref, snap_hbm.at[0, pl.ds(first, heads)])

    for i, j, first, heads, both, valid, (o_ref, gate_ref, decay_ref, q_ref) in work:
        gated_ref = scratch[2 * i]
        tokens, size = valid.shape
        block = min(tokens, 256)
        columns = slice(j * size, (j + 1) * size)
        for start in range(0, tokens, block):
            here = slice(start, start + block)
            q = q_ref[here, columns]
            inter = lax.dot_general(
                jnp.concatenate([q, q], axis=1), both, NN, preferred_element_type=F32
            )
            mixed = o_ref[here, columns] + inter * (decay_ref[here, columns] * valid[here])
            mean_square = jnp.mean(mixed * mixed, axis=1, keepdims=True)
            gated = mixed * lax.rsqrt(mean_square + 1e-06) * gate_ref[here, columns]
            gated_ref[here, columns] = gated.astype(BF16)
        if j % 2 == 1 or j == heads - 1:
            begin = j - j % 2
            width = (j + 1 - begin) * size
            there = pl.ds((first + begin) * size, width)
            send(gated_ref.at[:, pl.ds(begin * size, width)], gated_hbm.at[:, there])
    for copy in copies:
        copy.wait()


def finish(order, seg, total, groups, arrays, so_far, after):
    tokens, size = seg.shape[1], arrays[0].shape[1]
    vmem, anywhere = pl.BlockSpec(memory_space=pltpu.VMEM), pl.BlockSpec(memory_space=pl.ANY)
    unread = len(so_far) + len(after)
    scratch = []
    for _, many, _ in groups:
        scratch.append(pltpu.VMEM((tokens, many * size), BF16))
        scratch.append(pltpu.VMEM((many, size, size), F32))
    return pl.pallas_call(
        functools.partial(final_kernel, groups, unread),
        in_specs=[pl.BlockSpec(memory_space=pltpu.SMEM)]
        + [vmem] * (1 + len(arrays))
        + [anywhere] * unread,
        out_specs=[anywhere, anywhere],
        out_shape=[
            jax.ShapeDtypeStruct((tokens, total * size), BF16),
            jax.ShapeDtypeStruct((1, total, size, size), F32),
        ],
        scratch_shapes=scratch + [pltpu.SemaphoreType.DMA((2 * total,))],
        input_output_aliases={2 + len(arrays) + i: i for i in range(len(so_far))},
        compiler_params=pltpu.CompilerParams(vmem_limit_bytes=12 * MIB),
        cost_estimate=SHORT,
        name="finish",
    )(order, seg, *arrays, *so_far, *after)


def shards(q, k, v, g, segment, decay_exponent, retention, norm_gain):
    heads = decay_exponent.shape[0]
    tokens = q.shape[0]
    count = lax.axis_size("seq")
    place = lax.axis_index("seq")
    reach = max(1, count // 4)
    far = lambda x: pltpu.with_memory_space_constraint(x, pltpu.HBM)
    q, k, v, g = far(q), far(k), far(v), far(g)
    gain = norm_gain.reshape(1, -1)
    order = jnp.where(place >= 2, 2 + (place & 1), place & 1).astype(jnp.int32).reshape(1)
    later = jnp.ones((1,), jnp.int32)
    swap = lambda x: lax.ppermute(x, "seq", [(c, c ^ 1) for c in range(count)])
    turn = lambda x: lax.ppermute(x, "seq", [(c, (c + 2) % count) for c in range(count)])

    half = heads // 2
    small = half * 3 // 8
    big = half - small
    chunks = [(0, big), (half, big), (big, small), (half + big, small)]

    def widened(x, many, shift, window):
        while window < reach:
            past = lax.ppermute(x, "seq", [(c, c + shift) for c in range(count - shift)])
            x = joined(later, x, past, many)
            shift, window = 2 * shift, 2 * window
        return x

    own, a, w, seg, k_near, v_near = first_messages(
        order,
        far(segment.reshape(1, tokens)),
        far(decay_exponent.reshape(1, heads)),
        far(retention),
        k,
        v,
        heads,
        chunks[:2],
    )
    near, past, inside = {}, {}, {}
    near[1] = swap(own[1])
    past[0] = turn(own[0])
    messages, mask, k_rest, v_rest, q_near, g_near = rest_messages(
        seg, a, w, q, k, v, g, chunks, 2
    )
    own, k_near, v_near = [*own, *messages], [*k_near, *k_rest], [*v_near, *v_rest]

    def look_inside(i, through=(), after=()):
        inside[i], copied = intra(
            mask, a, gain, q_near[i], k_near[i], v_near[i], g_near[i], *chunks[i], through, after
        )
        return copied

    def pair_first(i, after):
        both = joined(order, own[i], near[i], chunks[i][1], after)
        past[i] = turn(both)
        return both

    def pair_last(i, after):
        message = picked(order, own[i], past[i], after)
        near[i] = swap(message)
        return message

    own[2], own[3] = look_inside(0, (own[2], own[3]))
    near[3] = swap(own[3])
    past[2] = turn(own[2])
    first_done = pair_first(1, (own[2],))
    look_inside(1, (), (first_done,))
    second_done = pair_last(0, (inside[1][0],))
    look_inside(2, (), (second_done,))
    look_inside(3, (), (inside[2][0],))
    second_done = pair_last(2, (inside[3][0],))
    first_done = pair_first(3, (second_done,))

    if reach > 2:
        for i, (_, many) in enumerate(chunks):
            past[i] = jnp.where(place >= 2, past[i], 0.0)
            if i % 2 == 0:
                near[i] = jnp.where(place >= 1, near[i], 0.0)
                near[i] = widened(joined(later, near[i], past[i], many), many, 2, 2)
                past[i] = jnp.zeros_like(near[i])
            else:
                past[i] = widened(past[i], many, 2, 2)

    result = ()
    for group in ((0, 1), (2, 3)):
        groups = [(*chunks[i], ("span", "pair")[i % 2]) for i in group]
        arrays = [x for i in group for x in (own[i], near[i], past[i], *inside[i])]
        result = finish(order, seg, heads, groups, arrays, result, (first_done,))
    return tuple(result)


def solution(mesh):
    placed = (
        P(("groups", "seq"), "wt"),
        P(("groups", "seq"), "wt"),
        P(("groups", "seq"), "wt"),
        P(("groups", "seq"), "wt"),
        P(("groups", "seq")),
        P("wt"),
        P("wt", ("groups", "seq")),
        P("wt"),
    )
    return jax.shard_map(
        shards,
        mesh=mesh,
        in_specs=placed,
        out_specs=(P(("groups", "seq"), "wt"), P(("groups", "seq"), "wt", None, None)),
        check_vma=False,
    )
```

```python
import functools

import jax
import jax.numpy as jnp
from jax import lax
from jax.experimental import pallas as pl
from jax.experimental.pallas import tpu as pltpu
from jax.sharding import PartitionSpec as P

F32 = jnp.float32
BF16 = jnp.bfloat16
NN = (((1,), (0,)), ((), ()))
NT = (((1,), (1,)), ((), ()))
MIB = 1 << 20
SHORT = pl.CostEstimate(flops=1, bytes_accessed=1, transcendentals=0)


def vmem_spec(shape, index_map):
    return pl.BlockSpec(shape, index_map)


def as_column(row, lanes):
    return jnp.broadcast_to(row, (lanes, row.shape[1])).T


def meta_rows(heads):
    return -(-(heads + 1) // 8) * 8


def put_message(msg_ref, first, heads, size, w_ref, finals, end, k_ref, v_ref):
    top = heads * size
    for j in range(heads):
        columns = slice(j * size, (j + 1) * size)
        weight = w_ref[first + j : first + j + 1, :]
        keyed = (k_ref[:, columns].astype(F32).T * weight).astype(BF16)
        msg_ref[columns, :] = lax.dot_general(
            keyed, v_ref[:, columns], NN, preferred_element_type=F32
        )
    msg_ref[top : top + heads, :] = jnp.broadcast_to(finals, (heads, size))
    below = meta_rows(heads) - heads
    msg_ref[top + heads :, :] = jnp.broadcast_to(end.astype(F32), (below, size))


def first_kernel(heads, chunks, order_ref, seg_hbm, exponent_hbm, keep_hbm, k_hbm, v_hbm, *refs):
    number = len(chunks)
    messages, refs = refs[:number], refs[number:]
    (a_ref, w_ref, seg_ref), refs = refs[:3], refs[3:]
    k_refs, v_refs, refs = refs[:number], refs[number : 2 * number], refs[2 * number :]
    exponent_ref, keep_ref, sems = refs
    tokens = seg_ref.shape[1]
    size = messages[0].shape[1]
    pairs = [(keep_hbm, keep_ref), (exponent_hbm, exponent_ref), (seg_hbm, seg_ref)]
    for i, (first, many) in enumerate(chunks):
        wide = pl.ds(first * size, many * size)
        pairs += [(k_hbm.at[:, wide], k_refs[i]), (v_hbm.at[:, wide], v_refs[i])]
    copies = [pltpu.make_async_copy(*pair, sems.at[i]) for i, pair in enumerate(pairs)]
    for copy in copies:
        copy.start()
    earlier = lax.broadcasted_iota(jnp.int32, (tokens, tokens), 0)
    later = lax.broadcasted_iota(jnp.int32, (tokens, tokens), 1)
    upper = jnp.where(earlier <= later, 1.0, 0.0).astype(BF16)
    across = lax.broadcasted_iota(jnp.int32, (heads, heads), 1)
    down = lax.broadcasted_iota(jnp.int32, (heads, heads), 0)
    for copy in copies[:3]:
        copy.wait()
    spread = jnp.broadcast_to(exponent_ref[...], (heads, heads))
    exponent = jnp.sum(jnp.where(across == down, spread, 0).astype(F32), axis=1, keepdims=True)
    a = -jnp.exp2(-exponent) + jnp.log(keep_ref[...])
    high = a.astype(BF16)
    rest = a - high.astype(F32)
    middle = rest.astype(BF16)
    low = (rest - middle.astype(F32)).astype(BF16)
    parts = jnp.concatenate([high, middle, low], axis=0)
    sums = lax.dot_general(parts, upper, NN, preferred_element_type=F32)
    cumulative = sums[:heads] + (sums[heads : 2 * heads] + sums[2 * heads :])
    a_ref[...] = cumulative
    final = cumulative[:, tokens - 1 :]
    seg = seg_ref[...]
    last = seg[:, tokens - 1 :]
    w_ref[...] = jnp.where(seg == last, jnp.exp(final - cumulative), 0.0)
    for i, (first, many) in enumerate(chunks):
        copies[3 + 2 * i].wait()
        copies[4 + 2 * i].wait()
        finals = final[first : first + many]
        put_message(messages[i], first, many, size, w_ref, finals, last, k_refs[i], v_refs[i])


def message_of(size, many):
    return pltpu.VMEM((many * size + meta_rows(many), size), F32)


def first_messages(order, seg, exponent, keep, k, v, heads, chunks):
    tokens, size = k.shape[0], k.shape[1] // heads
    near = [pltpu.VMEM((tokens, many * size), BF16) for _, many in chunks]
    shapes = [message_of(size, many) for _, many in chunks]
    shapes += [pltpu.VMEM((heads, tokens), F32)] * 2 + [pltpu.VMEM((1, tokens), jnp.int32)]
    shapes += near + near
    number = len(chunks)
    out = pl.pallas_call(
        functools.partial(first_kernel, heads, chunks),
        in_specs=[pl.BlockSpec(memory_space=pltpu.SMEM)]
        + [pl.BlockSpec(memory_space=pltpu.HBM)] * 5,
        out_specs=[pl.BlockSpec(memory_space=pltpu.VMEM)] * len(shapes),
        out_shape=shapes,
        scratch_shapes=[
            pltpu.VMEM((1, heads), jnp.int32),
            pltpu.VMEM((heads, tokens), F32),
            pltpu.SemaphoreType.DMA((3 + 2 * number,)),
        ],
        compiler_params=pltpu.CompilerParams(vmem_limit_bytes=8 * MIB),
        cost_estimate=SHORT,
        name="first_messages",
    )(order, seg, exponent, keep, k, v)
    messages, (a, w, seg), out = out[:number], out[number : number + 3], out[number + 3 :]
    return messages, a, w, seg, out[:number], out[number:]


def rest_kernel(chunks, done, seg_ref, a_ref, w_ref, q_hbm, k_hbm, v_hbm, g_hbm, *refs):
    tokens = seg_ref.shape[1]
    left, number = chunks[done:], len(chunks)
    messages, mask_ref, refs, sems = refs[: len(left)], refs[len(left)], refs[len(left) + 1 : -1], refs[-1]
    k_refs, refs = refs[: len(left)], refs[len(left) :]
    v_refs, refs = refs[: len(left)], refs[len(left) :]
    q_refs, g_refs = refs[:number], refs[number:]
    size = messages[0].shape[1]
    pairs = []
    for i, (first, many) in enumerate(left):
        wide = pl.ds(first * size, many * size)
        pairs += [(k_hbm.at[:, wide], k_refs[i]), (v_hbm.at[:, wide], v_refs[i])]
    for i, (first, many) in enumerate(chunks):
        wide = pl.ds(first * size, many * size)
        pairs += [(q_hbm.at[:, wide], q_refs[i]), (g_hbm.at[:, wide], g_refs[i])]
    copies = [pltpu.make_async_copy(*pair, sems.at[i]) for i, pair in enumerate(pairs)]
    for copy in copies:
        copy.start()
    make_mask(seg_ref, mask_ref)
    last = seg_ref[:, tokens - 1 :]
    for i, (first, many) in enumerate(left):
        copies[2 * i].wait()
        copies[2 * i + 1].wait()
        final = a_ref[first : first + many, tokens - 1 :]
        put_message(messages[i], first, many, size, w_ref, final, last, k_refs[i], v_refs[i])
    for copy in copies[2 * len(left) :]:
        copy.wait()


def rest_messages(seg, a, w, q, k, v, g, chunks, done):
    heads = a.shape[0]
    tokens, size = k.shape[0], k.shape[1] // heads
    near = [pltpu.VMEM((tokens, many * size), BF16) for _, many in chunks]
    shapes = [message_of(size, many) for _, many in chunks[done:]]
    shapes += [pltpu.VMEM((tokens, tokens), F32)] + near[done:] * 2 + near * 2
    left, number = len(chunks) - done, len(chunks)
    out = pl.pallas_call(
        functools.partial(rest_kernel, chunks, done),
        in_specs=[pl.BlockSpec(memory_space=pltpu.VMEM)] * 3
        + [pl.BlockSpec(memory_space=pltpu.HBM)] * 4,
        out_specs=[pl.BlockSpec(memory_space=pltpu.VMEM)] * len(shapes),
        out_shape=shapes,
        scratch_shapes=[pltpu.SemaphoreType.DMA((2 * (left + number),))],
        compiler_params=pltpu.CompilerParams(vmem_limit_bytes=8 * MIB),
        cost_estimate=SHORT,
        name="rest_messages",
    )(seg, a, w, q, k, v, g)
    messages, mask, out = out[:left], out[left], out[left + 1 :]
    k_near, v_near, out = out[:left], out[left : 2 * left], out[2 * left :]
    return messages, mask, k_near, v_near, out[:number], out[number:]


def join_kernel(heads, order_ref, mine_ref, other_ref, out_ref):
    size = mine_ref.shape[1]
    top = heads * size
    mine_later = (order_ref[0] & 1) == 1
    final_mine, final_other = mine_ref[top : top + heads, :], other_ref[top : top + heads, :]
    end_mine, end_other = mine_ref[top + heads :, :], other_ref[top + heads :, :]
    same = jnp.where(end_mine[:1] == end_other[:1], 1.0, 0.0)
    scale_mine = jnp.where(mine_later, 1.0, jnp.exp(final_other) * same)
    scale_other = jnp.where(mine_later, jnp.exp(final_mine) * same, 1.0)
    for head in range(heads):
        rows = slice(head * size, (head + 1) * size)
        out_ref[rows, :] = (
            scale_mine[head : head + 1] * mine_ref[rows, :]
            + scale_other[head : head + 1] * other_ref[rows, :]
        )
    out_ref[top : top + heads, :] = final_mine + final_other
    out_ref[top + heads :, :] = jnp.where(mine_later, end_mine, end_other)


def small_call(kernel, name, order, arrays, after):
    vmem = pl.BlockSpec(memory_space=pltpu.VMEM)
    return pl.pallas_call(
        lambda *refs: kernel(*refs[: 1 + len(arrays)], refs[-1]),
        in_specs=[pl.BlockSpec(memory_space=pltpu.SMEM)]
        + [vmem] * len(arrays)
        + [pl.BlockSpec(memory_space=pl.ANY)] * len(after),
        out_specs=vmem,
        out_shape=pltpu.VMEM(arrays[0].shape, F32),
        compiler_params=pltpu.CompilerParams(vmem_limit_bytes=8 * MIB),
        cost_estimate=SHORT,
        name=name,
    )(order, *arrays, *after)


def joined(order, mine, other, heads, after=()):
    return small_call(
        functools.partial(join_kernel, heads), "join_windows", order, (mine, other), after
    )


def pick_kernel(order_ref, even_ref, odd_ref, out_ref):
    odd = (order_ref[0] & 1) == 1

    @pl.when(odd)
    def _():
        out_ref[...] = odd_ref[...]

    @pl.when(jnp.logical_not(odd))
    def _():
        out_ref[...] = even_ref[...]


def picked(order, even, odd, after=()):
    return small_call(pick_kernel, "pick_message", order, (even, odd), after)


def make_mask(seg_ref, mask_ref):
    tokens = seg_ref.shape[1]
    seg = seg_ref[...].astype(F32)
    column = as_column(seg, 128)
    for start in range(0, tokens, 128):
        across = lax.broadcasted_iota(jnp.int32, (tokens, 128), 1) + start
        down = lax.broadcasted_iota(jnp.int32, (tokens, 128), 0)
        seen = (column == seg[:, start : start + 128]) & (across <= down)
        mask_ref[:, start : start + 128] = jnp.where(seen, 0.0, -1e30)


def intra_kernel(
    first, heads, through, after, mask_ref, a_ref, gain_ref, q_ref, k_ref, v_ref, g_ref, *refs
):
    o_ref, gate_ref, decay_ref, *copied = refs[through + after :]
    for source, target in zip(refs[:through], copied):
        target[...] = source[...]
    tokens = mask_ref.shape[0]
    size = q_ref.shape[1] // heads
    block = min(tokens, 256)
    for j in range(heads):
        columns = slice(j * size, (j + 1) * size)
        a_row = a_ref[first + j : first + j + 1, :] * 1.4426950408889634
        a_column = as_column(a_row, 128)
        decay_ref[:, columns] = jnp.exp2(a_column)
        for start in range(0, tokens, block):
            here, upto = slice(start, start + block), slice(0, start + block)
            scores = lax.dot_general(
                q_ref[here, columns], k_ref[upto, columns], NT, preferred_element_type=F32
            )
            spread = jnp.concatenate([a_column[here]] * ((start + block) // 128), axis=1)
            weight = jnp.exp2(spread - a_row[:, upto] + mask_ref[here, upto])
            probs = (scores * weight).astype(BF16)
            o_ref[here, columns] = lax.dot_general(
                probs, v_ref[upto, columns], NN, preferred_element_type=F32
            )
        half = 0.5 * gain_ref[:, (first + j) * size : (first + j + 1) * size]
        gate_ref[:, columns] = half + half * jnp.tanh(0.5 * g_ref[:, columns].astype(F32))


def intra(mask, a, gain, q, k, v, g, first, heads, through=(), after=()):
    tokens, size = mask.shape[0], gain.shape[1] // a.shape[0]
    vmem = pl.BlockSpec(memory_space=pltpu.VMEM)
    o, gate, decay, *copied = pl.pallas_call(
        functools.partial(intra_kernel, first, heads, len(through), len(after)),
        in_specs=[vmem] * (7 + len(through)) + [pl.BlockSpec(memory_space=pl.ANY)] * len(after),
        out_specs=[vmem] * (3 + len(through)),
        out_shape=[pltpu.VMEM((tokens, heads * size), F32)] * 3
        + [pltpu.VMEM(x.shape, x.dtype) for x in through],
        compiler_params=pltpu.CompilerParams(vmem_limit_bytes=8 * MIB),
        cost_estimate=SHORT,
        name="intra_span",
    )(mask, a, gain, q, k, v, g, *through, *after)
    return (o, gate, decay, q), copied


def final_kernel(groups, unread, order_ref, seg_ref, *rest):
    number = len(groups)
    inputs, rest = rest[: 7 * number], rest[7 * number + unread :]
    gated_hbm, snap_hbm, *scratch, sems = rest
    place = order_ref[0]
    seg = seg_ref[...].astype(F32)
    copies, work = [], []

    def send(source, target):
        copies.append(pltpu.make_async_copy(source, target, sems.at[len(copies)]))
        copies[-1].start()

    for i, (first, heads, kind) in enumerate(groups):
        own_ref, near_ref, past_ref, o_ref, gate_ref, decay_ref, q_ref = inputs[7 * i : 7 * i + 7]
        gated_ref, snap_ref = scratch[2 * i : 2 * i + 2]
        size = own_ref.shape[1]
        top = heads * size
        ends = slice(top + heads, top + heads + 1)
        finals = slice(top, top + heads)
        own_end, near_end, past_end = own_ref[ends, :], near_ref[ends, :], past_ref[ends, :]
        bridged = jnp.exp(near_ref[finals, :]) * jnp.where(near_end == past_end, 1.0, 0.0)
        if kind == "pair":
            odd = (place & 1) == 1
            previous = jnp.where(odd, near_end, past_end)
            scale_near = jnp.where(odd, 1.0, 0.0)
            scale_past = jnp.where(odd, bridged, 1.0)
        else:
            previous = near_end
            scale_near = jnp.where(place > 0, 1.0, 0.0)
            scale_past = bridged
        scale_past = jnp.where(place >= 2, scale_past, 0.0)
        own_decay = jnp.exp(own_ref[finals, :]) * jnp.where(own_end == previous, 1.0, 0.0)
        valid = as_column(jnp.where(seg == previous[:, :1], 1.0, 0.0), size)
        for j in range(heads):
            rows = slice(j * size, (j + 1) * size)
            state = scale_past[j : j + 1] * past_ref[rows, :] + scale_near * near_ref[rows, :]
            snap_ref[j] = own_decay[j : j + 1] * state + own_ref[rows, :]
            high = state.astype(BF16)
            low = (state - high.astype(F32)).astype(BF16)
            both = jnp.concatenate([high, low], axis=0)
            work.append((i, j, first, heads, both, valid, (o_ref, gate_ref, decay_ref, q_ref)))
        send(snap_ref, snap_hbm.at[0, pl.ds(first, heads)])

    for i, j, first, heads, both, valid, (o_ref, gate_ref, decay_ref, q_ref) in work:
        gated_ref = scratch[2 * i]
        tokens, size = valid.shape
        block = min(tokens, 256)
        columns = slice(j * size, (j + 1) * size)
        for start in range(0, tokens, block):
            here = slice(start, start + block)
            q = q_ref[here, columns]
            inter = lax.dot_general(
                jnp.concatenate([q, q], axis=1), both, NN, preferred_element_type=F32
            )
            mixed = o_ref[here, columns] + inter * (decay_ref[here, columns] * valid[here])
            mean_square = jnp.mean(mixed * mixed, axis=1, keepdims=True)
            gated = mixed * lax.rsqrt(mean_square + 1e-06) * gate_ref[here, columns]
            gated_ref[here, columns] = gated.astype(BF16)
        if j % 2 == 1 or j == heads - 1:
            begin = j - j % 2
            width = (j + 1 - begin) * size
            there = pl.ds((first + begin) * size, width)
            send(gated_ref.at[:, pl.ds(begin * size, width)], gated_hbm.at[:, there])
    for copy in copies:
        copy.wait()


def finish(order, seg, total, groups, arrays, so_far, after):
    tokens, size = seg.shape[1], arrays[0].shape[1]
    vmem, anywhere = pl.BlockSpec(memory_space=pltpu.VMEM), pl.BlockSpec(memory_space=pl.ANY)
    unread = len(so_far) + len(after)
    scratch = []
    for _, many, _ in groups:
        scratch.append(pltpu.VMEM((tokens, many * size), BF16))
        scratch.append(pltpu.VMEM((many, size, size), F32))
    return pl.pallas_call(
        functools.partial(final_kernel, groups, unread),
        in_specs=[pl.BlockSpec(memory_space=pltpu.SMEM)]
        + [vmem] * (1 + len(arrays))
        + [anywhere] * unread,
        out_specs=[anywhere, anywhere],
        out_shape=[
            jax.ShapeDtypeStruct((tokens, total * size), BF16),
            jax.ShapeDtypeStruct((1, total, size, size), F32),
        ],
        scratch_shapes=scratch + [pltpu.SemaphoreType.DMA((2 * total,))],
        input_output_aliases={2 + len(arrays) + i: i for i in range(len(so_far))},
        compiler_params=pltpu.CompilerParams(vmem_limit_bytes=12 * MIB),
        cost_estimate=SHORT,
        name="finish",
    )(order, seg, *arrays, *so_far, *after)


def shards(q, k, v, g, segment, decay_exponent, retention, norm_gain):
    heads = decay_exponent.shape[0]
    tokens = q.shape[0]
    count = lax.axis_size("seq")
    place = lax.axis_index("seq")
    reach = max(1, count // 4)
    far = lambda x: pltpu.with_memory_space_constraint(x, pltpu.HBM)
    q, k, v, g = far(q), far(k), far(v), far(g)
    gain = norm_gain.reshape(1, -1)
    order = jnp.where(place >= 2, 2 + (place & 1), place & 1).astype(jnp.int32).reshape(1)
    later = jnp.ones((1,), jnp.int32)
    swap = lambda x: lax.ppermute(x, "seq", [(c, c ^ 1) for c in range(count)])
    turn = lambda x: lax.ppermute(x, "seq", [(c, (c + 2) % count) for c in range(count)])

    half = heads // 2
    small = half // 2
    big = half - small
    chunks = [(0, big), (half, big), (big, small), (half + big, small)]

    def widened(x, many, shift, window):
        while window < reach:
            past = lax.ppermute(x, "seq", [(c, c + shift) for c in range(count - shift)])
            x = joined(later, x, past, many)
            shift, window = 2 * shift, 2 * window
        return x

    own, a, w, seg, k_near, v_near = first_messages(
        order,
        far(segment.reshape(1, tokens)),
        far(decay_exponent.reshape(1, heads)),
        far(retention),
        k,
        v,
        heads,
        chunks[:2],
    )
    near, past, inside = {}, {}, {}
    near[1] = swap(own[1])
    past[0] = turn(own[0])
    messages, mask, k_rest, v_rest, q_near, g_near = rest_messages(
        seg, a, w, q, k, v, g, chunks, 2
    )
    own, k_near, v_near = [*own, *messages], [*k_near, *k_rest], [*v_near, *v_rest]

    def look_inside(i, through=(), after=()):
        inside[i], copied = intra(
            mask, a, gain, q_near[i], k_near[i], v_near[i], g_near[i], *chunks[i], through, after
        )
        return copied

    def pair_first(i, after):
        both = joined(order, own[i], near[i], chunks[i][1], after)
        past[i] = turn(both)
        return both

    def pair_last(i, after):
        message = picked(order, own[i], past[i], after)
        near[i] = swap(message)
        return message

    near[3] = swap(own[3])
    past[2] = turn(own[2])
    first_done = pair_first(1, ())
    look_inside(0, (), (first_done,))
    look_inside(1, (), (inside[0][0],))
    second_done = pair_last(0, (inside[1][0],))
    look_inside(2, (), (second_done,))
    look_inside(3, (), (inside[2][0],))
    first_done = pair_first(3, (inside[3][0],))
    second_done = pair_last(2, (first_done,))

    if reach > 2:
        for i, (_, many) in enumerate(chunks):
            past[i] = jnp.where(place >= 2, past[i], 0.0)
            if i % 2 == 0:
                near[i] = jnp.where(place >= 1, near[i], 0.0)
                near[i] = widened(joined(later, near[i], past[i], many), many, 2, 2)
                past[i] = jnp.zeros_like(near[i])
            else:
                past[i] = widened(past[i], many, 2, 2)

    result = ()
    for group in ((0, 1), (2, 3)):
        groups = [(*chunks[i], ("span", "pair")[i % 2]) for i in group]
        arrays = [x for i in group for x in (own[i], near[i], past[i], *inside[i])]
        result = finish(order, seg, heads, groups, arrays, result, (second_done,))
    return tuple(result)


def solution(mesh):
    placed = (
        P(("groups", "seq"), "wt"),
        P(("groups", "seq"), "wt"),
        P(("groups", "seq"), "wt"),
        P(("groups", "seq"), "wt"),
        P(("groups", "seq")),
        P("wt"),
        P("wt", ("groups", "seq")),
        P("wt"),
    )
    return jax.shard_map(
        shards,
        mesh=mesh,
        in_specs=placed,
        out_specs=(P(("groups", "seq"), "wt"), P(("groups", "seq"), "wt", None, None)),
        check_vma=False,
    )
```

```python
import functools

import jax
import jax.numpy as jnp
from jax import lax
from jax.experimental import pallas as pl
from jax.experimental.pallas import tpu as pltpu
from jax.sharding import PartitionSpec as P

F32 = jnp.float32
BF16 = jnp.bfloat16
NN = (((1,), (0,)), ((), ()))
NT = (((1,), (1,)), ((), ()))
MIB = 1 << 20
SHORT = pl.CostEstimate(flops=1, bytes_accessed=1, transcendentals=0)


def vmem_spec(shape, index_map):
    return pl.BlockSpec(shape, index_map)


def as_column(row, lanes):
    return jnp.broadcast_to(row, (lanes, row.shape[1])).T


def meta_rows(heads):
    return -(-(heads + 1) // 8) * 8


def put_message(msg_ref, first, heads, size, w_ref, finals, end, k_ref, v_ref):
    top = heads * size
    for j in range(heads):
        columns = slice(j * size, (j + 1) * size)
        weight = w_ref[first + j : first + j + 1, :]
        keyed = (k_ref[:, columns].astype(F32).T * weight).astype(BF16)
        msg_ref[columns, :] = lax.dot_general(
            keyed, v_ref[:, columns], NN, preferred_element_type=F32
        )
    msg_ref[top : top + heads, :] = jnp.broadcast_to(finals, (heads, size))
    below = meta_rows(heads) - heads
    msg_ref[top + heads :, :] = jnp.broadcast_to(end.astype(F32), (below, size))


def first_kernel(heads, chunks, order_ref, seg_hbm, exponent_hbm, keep_hbm, k_hbm, v_hbm, *refs):
    number = len(chunks)
    messages, refs = refs[:number], refs[number:]
    (a_ref, w_ref, seg_ref), refs = refs[:3], refs[3:]
    k_refs, v_refs, refs = refs[:number], refs[number : 2 * number], refs[2 * number :]
    exponent_ref, keep_ref, sems = refs
    tokens = seg_ref.shape[1]
    size = messages[0].shape[1]
    pairs = [(keep_hbm, keep_ref), (exponent_hbm, exponent_ref), (seg_hbm, seg_ref)]
    for i, (first, many) in enumerate(chunks):
        wide = pl.ds(first * size, many * size)
        pairs += [(k_hbm.at[:, wide], k_refs[i]), (v_hbm.at[:, wide], v_refs[i])]
    copies = [pltpu.make_async_copy(*pair, sems.at[i]) for i, pair in enumerate(pairs)]
    for copy in copies:
        copy.start()
    earlier = lax.broadcasted_iota(jnp.int32, (tokens, tokens), 0)
    later = lax.broadcasted_iota(jnp.int32, (tokens, tokens), 1)
    upper = jnp.where(earlier <= later, 1.0, 0.0).astype(BF16)
    across = lax.broadcasted_iota(jnp.int32, (heads, heads), 1)
    down = lax.broadcasted_iota(jnp.int32, (heads, heads), 0)
    for copy in copies[:3]:
        copy.wait()
    spread = jnp.broadcast_to(exponent_ref[...], (heads, heads))
    exponent = jnp.sum(jnp.where(across == down, spread, 0).astype(F32), axis=1, keepdims=True)
    a = -jnp.exp2(-exponent) + jnp.log(keep_ref[...])
    high = a.astype(BF16)
    rest = a - high.astype(F32)
    middle = rest.astype(BF16)
    low = (rest - middle.astype(F32)).astype(BF16)
    parts = jnp.concatenate([high, middle, low], axis=0)
    sums = lax.dot_general(parts, upper, NN, preferred_element_type=F32)
    cumulative = sums[:heads] + (sums[heads : 2 * heads] + sums[2 * heads :])
    a_ref[...] = cumulative
    final = cumulative[:, tokens - 1 :]
    seg = seg_ref[...]
    last = seg[:, tokens - 1 :]
    w_ref[...] = jnp.where(seg == last, jnp.exp(final - cumulative), 0.0)
    for i, (first, many) in enumerate(chunks):
        copies[3 + 2 * i].wait()
        copies[4 + 2 * i].wait()
        finals = final[first : first + many]
        put_message(messages[i], first, many, size, w_ref, finals, last, k_refs[i], v_refs[i])


def message_of(size, many):
    return pltpu.VMEM((many * size + meta_rows(many), size), F32)


def first_messages(order, seg, exponent, keep, k, v, heads, chunks):
    tokens, size = k.shape[0], k.shape[1] // heads
    near = [pltpu.VMEM((tokens, many * size), BF16) for _, many in chunks]
    shapes = [message_of(size, many) for _, many in chunks]
    shapes += [pltpu.VMEM((heads, tokens), F32)] * 2 + [pltpu.VMEM((1, tokens), jnp.int32)]
    shapes += near + near
    number = len(chunks)
    out = pl.pallas_call(
        functools.partial(first_kernel, heads, chunks),
        in_specs=[pl.BlockSpec(memory_space=pltpu.SMEM)]
        + [pl.BlockSpec(memory_space=pltpu.HBM)] * 5,
        out_specs=[pl.BlockSpec(memory_space=pltpu.VMEM)] * len(shapes),
        out_shape=shapes,
        scratch_shapes=[
            pltpu.VMEM((1, heads), jnp.int32),
            pltpu.VMEM((heads, tokens), F32),
            pltpu.SemaphoreType.DMA((3 + 2 * number,)),
        ],
        compiler_params=pltpu.CompilerParams(vmem_limit_bytes=8 * MIB),
        cost_estimate=SHORT,
        name="first_messages",
    )(order, seg, exponent, keep, k, v)
    messages, (a, w, seg), out = out[:number], out[number : number + 3], out[number + 3 :]
    return messages, a, w, seg, out[:number], out[number:]


def rest_kernel(chunks, done, seg_ref, a_ref, w_ref, q_hbm, k_hbm, v_hbm, g_hbm, *refs):
    tokens = seg_ref.shape[1]
    left, number = chunks[done:], len(chunks)
    messages, mask_ref, refs, sems = refs[: len(left)], refs[len(left)], refs[len(left) + 1 : -1], refs[-1]
    k_refs, refs = refs[: len(left)], refs[len(left) :]
    v_refs, refs = refs[: len(left)], refs[len(left) :]
    q_refs, g_refs = refs[:number], refs[number:]
    size = messages[0].shape[1]
    pairs = []
    for i, (first, many) in enumerate(left):
        wide = pl.ds(first * size, many * size)
        pairs += [(k_hbm.at[:, wide], k_refs[i]), (v_hbm.at[:, wide], v_refs[i])]
    for i, (first, many) in enumerate(chunks):
        wide = pl.ds(first * size, many * size)
        pairs += [(q_hbm.at[:, wide], q_refs[i]), (g_hbm.at[:, wide], g_refs[i])]
    copies = [pltpu.make_async_copy(*pair, sems.at[i]) for i, pair in enumerate(pairs)]
    for copy in copies:
        copy.start()
    make_mask(seg_ref, mask_ref)
    last = seg_ref[:, tokens - 1 :]
    for i, (first, many) in enumerate(left):
        copies[2 * i].wait()
        copies[2 * i + 1].wait()
        final = a_ref[first : first + many, tokens - 1 :]
        put_message(messages[i], first, many, size, w_ref, final, last, k_refs[i], v_refs[i])
    for copy in copies[2 * len(left) :]:
        copy.wait()


def rest_messages(seg, a, w, q, k, v, g, chunks, done):
    heads = a.shape[0]
    tokens, size = k.shape[0], k.shape[1] // heads
    near = [pltpu.VMEM((tokens, many * size), BF16) for _, many in chunks]
    shapes = [message_of(size, many) for _, many in chunks[done:]]
    shapes += [pltpu.VMEM((tokens, tokens), F32)] + near[done:] * 2 + near * 2
    left, number = len(chunks) - done, len(chunks)
    out = pl.pallas_call(
        functools.partial(rest_kernel, chunks, done),
        in_specs=[pl.BlockSpec(memory_space=pltpu.VMEM)] * 3
        + [pl.BlockSpec(memory_space=pltpu.HBM)] * 4,
        out_specs=[pl.BlockSpec(memory_space=pltpu.VMEM)] * len(shapes),
        out_shape=shapes,
        scratch_shapes=[pltpu.SemaphoreType.DMA((2 * (left + number),))],
        compiler_params=pltpu.CompilerParams(vmem_limit_bytes=8 * MIB),
        cost_estimate=SHORT,
        name="rest_messages",
    )(seg, a, w, q, k, v, g)
    messages, mask, out = out[:left], out[left], out[left + 1 :]
    k_near, v_near, out = out[:left], out[left : 2 * left], out[2 * left :]
    return messages, mask, k_near, v_near, out[:number], out[number:]


def join_kernel(heads, order_ref, mine_ref, other_ref, out_ref):
    size = mine_ref.shape[1]
    top = heads * size
    mine_later = (order_ref[0] & 1) == 1
    final_mine, final_other = mine_ref[top : top + heads, :], other_ref[top : top + heads, :]
    end_mine, end_other = mine_ref[top + heads :, :], other_ref[top + heads :, :]
    same = jnp.where(end_mine[:1] == end_other[:1], 1.0, 0.0)
    scale_mine = jnp.where(mine_later, 1.0, jnp.exp(final_other) * same)
    scale_other = jnp.where(mine_later, jnp.exp(final_mine) * same, 1.0)
    for head in range(heads):
        rows = slice(head * size, (head + 1) * size)
        out_ref[rows, :] = (
            scale_mine[head : head + 1] * mine_ref[rows, :]
            + scale_other[head : head + 1] * other_ref[rows, :]
        )
    out_ref[top : top + heads, :] = final_mine + final_other
    out_ref[top + heads :, :] = jnp.where(mine_later, end_mine, end_other)


def small_call(kernel, name, order, arrays, after):
    vmem = pl.BlockSpec(memory_space=pltpu.VMEM)
    return pl.pallas_call(
        lambda *refs: kernel(*refs[: 1 + len(arrays)], refs[-1]),
        in_specs=[pl.BlockSpec(memory_space=pltpu.SMEM)]
        + [vmem] * len(arrays)
        + [pl.BlockSpec(memory_space=pl.ANY)] * len(after),
        out_specs=vmem,
        out_shape=pltpu.VMEM(arrays[0].shape, F32),
        compiler_params=pltpu.CompilerParams(vmem_limit_bytes=8 * MIB),
        cost_estimate=SHORT,
        name=name,
    )(order, *arrays, *after)


def joined(order, mine, other, heads, after=()):
    return small_call(
        functools.partial(join_kernel, heads), "join_windows", order, (mine, other), after
    )


def pick_kernel(order_ref, even_ref, odd_ref, out_ref):
    odd = (order_ref[0] & 1) == 1

    @pl.when(odd)
    def _():
        out_ref[...] = odd_ref[...]

    @pl.when(jnp.logical_not(odd))
    def _():
        out_ref[...] = even_ref[...]


def picked(order, even, odd, after=()):
    return small_call(pick_kernel, "pick_message", order, (even, odd), after)


def make_mask(seg_ref, mask_ref):
    tokens = seg_ref.shape[1]
    seg = seg_ref[...].astype(F32)
    column = as_column(seg, 128)
    for start in range(0, tokens, 128):
        across = lax.broadcasted_iota(jnp.int32, (tokens, 128), 1) + start
        down = lax.broadcasted_iota(jnp.int32, (tokens, 128), 0)
        seen = (column == seg[:, start : start + 128]) & (across <= down)
        mask_ref[:, start : start + 128] = jnp.where(seen, 0.0, -1e30)


def intra_kernel(
    first, heads, through, after, mask_ref, a_ref, gain_ref, q_ref, k_ref, v_ref, g_ref, *refs
):
    o_ref, gate_ref, decay_ref, *copied = refs[through + after :]
    for source, target in zip(refs[:through], copied):
        target[...] = source[...]
    tokens = mask_ref.shape[0]
    size = q_ref.shape[1] // heads
    block = min(tokens, 256)
    for j in range(heads):
        columns = slice(j * size, (j + 1) * size)
        a_row = a_ref[first + j : first + j + 1, :] * 1.4426950408889634
        a_column = as_column(a_row, 128)
        decay_ref[:, columns] = jnp.exp2(a_column)
        for start in range(0, tokens, block):
            here, upto = slice(start, start + block), slice(0, start + block)
            scores = lax.dot_general(
                q_ref[here, columns], k_ref[upto, columns], NT, preferred_element_type=F32
            )
            spread = jnp.concatenate([a_column[here]] * ((start + block) // 128), axis=1)
            weight = jnp.exp2(spread - a_row[:, upto] + mask_ref[here, upto])
            probs = (scores * weight).astype(BF16)
            o_ref[here, columns] = lax.dot_general(
                probs, v_ref[upto, columns], NN, preferred_element_type=F32
            )
        half = 0.5 * gain_ref[:, (first + j) * size : (first + j + 1) * size]
        gate_ref[:, columns] = half + half * jnp.tanh(0.5 * g_ref[:, columns].astype(F32))


def intra(mask, a, gain, q, k, v, g, first, heads, through=(), after=()):
    tokens, size = mask.shape[0], gain.shape[1] // a.shape[0]
    vmem = pl.BlockSpec(memory_space=pltpu.VMEM)
    o, gate, decay, *copied = pl.pallas_call(
        functools.partial(intra_kernel, first, heads, len(through), len(after)),
        in_specs=[vmem] * (7 + len(through)) + [pl.BlockSpec(memory_space=pl.ANY)] * len(after),
        out_specs=[vmem] * (3 + len(through)),
        out_shape=[pltpu.VMEM((tokens, heads * size), F32)] * 3
        + [pltpu.VMEM(x.shape, x.dtype) for x in through],
        compiler_params=pltpu.CompilerParams(vmem_limit_bytes=8 * MIB),
        cost_estimate=SHORT,
        name="intra_span",
    )(mask, a, gain, q, k, v, g, *through, *after)
    return (o, gate, decay, q), copied


def final_kernel(groups, unread, order_ref, seg_ref, *rest):
    number = len(groups)
    inputs, rest = rest[: 7 * number], rest[7 * number + unread :]
    gated_hbm, snap_hbm, *scratch, sems = rest
    place = order_ref[0]
    seg = seg_ref[...].astype(F32)
    copies, work = [], []

    def send(source, target):
        copies.append(pltpu.make_async_copy(source, target, sems.at[len(copies)]))
        copies[-1].start()

    for i, (first, heads, kind) in enumerate(groups):
        own_ref, near_ref, past_ref, o_ref, gate_ref, decay_ref, q_ref = inputs[7 * i : 7 * i + 7]
        gated_ref, snap_ref = scratch[2 * i : 2 * i + 2]
        size = own_ref.shape[1]
        top = heads * size
        ends = slice(top + heads, top + heads + 1)
        finals = slice(top, top + heads)
        own_end, near_end, past_end = own_ref[ends, :], near_ref[ends, :], past_ref[ends, :]
        bridged = jnp.exp(near_ref[finals, :]) * jnp.where(near_end == past_end, 1.0, 0.0)
        if kind == "pair":
            odd = (place & 1) == 1
            previous = jnp.where(odd, near_end, past_end)
            scale_near = jnp.where(odd, 1.0, 0.0)
            scale_past = jnp.where(odd, bridged, 1.0)
        else:
            previous = near_end
            scale_near = jnp.where(place > 0, 1.0, 0.0)
            scale_past = bridged
        scale_past = jnp.where(place >= 2, scale_past, 0.0)
        own_decay = jnp.exp(own_ref[finals, :]) * jnp.where(own_end == previous, 1.0, 0.0)
        valid = as_column(jnp.where(seg == previous[:, :1], 1.0, 0.0), size)
        for j in range(heads):
            rows = slice(j * size, (j + 1) * size)
            state = scale_past[j : j + 1] * past_ref[rows, :] + scale_near * near_ref[rows, :]
            snap_ref[j] = own_decay[j : j + 1] * state + own_ref[rows, :]
            high = state.astype(BF16)
            low = (state - high.astype(F32)).astype(BF16)
            both = jnp.concatenate([high, low], axis=0)
            work.append((i, j, first, heads, both, valid, (o_ref, gate_ref, decay_ref, q_ref)))
        send(snap_ref, snap_hbm.at[0, pl.ds(first, heads)])

    for i, j, first, heads, both, valid, (o_ref, gate_ref, decay_ref, q_ref) in work:
        gated_ref = scratch[2 * i]
        tokens, size = valid.shape
        block = min(tokens, 256)
        columns = slice(j * size, (j + 1) * size)
        for start in range(0, tokens, block):
            here = slice(start, start + block)
            q = q_ref[here, columns]
            inter = lax.dot_general(
                jnp.concatenate([q, q], axis=1), both, NN, preferred_element_type=F32
            )
            mixed = o_ref[here, columns] + inter * (decay_ref[here, columns] * valid[here])
            mean_square = jnp.mean(mixed * mixed, axis=1, keepdims=True)
            gated = mixed * lax.rsqrt(mean_square + 1e-06) * gate_ref[here, columns]
            gated_ref[here, columns] = gated.astype(BF16)
        if j % 2 == 1 or j == heads - 1:
            begin = j - j % 2
            width = (j + 1 - begin) * size
            there = pl.ds((first + begin) * size, width)
            send(gated_ref.at[:, pl.ds(begin * size, width)], gated_hbm.at[:, there])
    for copy in copies:
        copy.wait()


def finish(order, seg, total, groups, arrays, so_far, after):
    tokens, size = seg.shape[1], arrays[0].shape[1]
    vmem, anywhere = pl.BlockSpec(memory_space=pltpu.VMEM), pl.BlockSpec(memory_space=pl.ANY)
    unread = len(so_far) + len(after)
    scratch = []
    for _, many, _ in groups:
        scratch.append(pltpu.VMEM((tokens, many * size), BF16))
        scratch.append(pltpu.VMEM((many, size, size), F32))
    return pl.pallas_call(
        functools.partial(final_kernel, groups, unread),
        in_specs=[pl.BlockSpec(memory_space=pltpu.SMEM)]
        + [vmem] * (1 + len(arrays))
        + [anywhere] * unread,
        out_specs=[anywhere, anywhere],
        out_shape=[
            jax.ShapeDtypeStruct((tokens, total * size), BF16),
            jax.ShapeDtypeStruct((1, total, size, size), F32),
        ],
        scratch_shapes=scratch + [pltpu.SemaphoreType.DMA((2 * total,))],
        input_output_aliases={2 + len(arrays) + i: i for i in range(len(so_far))},
        compiler_params=pltpu.CompilerParams(vmem_limit_bytes=12 * MIB),
        cost_estimate=SHORT,
        name="finish",
    )(order, seg, *arrays, *so_far, *after)


def shards(q, k, v, g, segment, decay_exponent, retention, norm_gain):
    heads = decay_exponent.shape[0]
    tokens = q.shape[0]
    count = lax.axis_size("seq")
    place = lax.axis_index("seq")
    reach = max(1, count // 4)
    far = lambda x: pltpu.with_memory_space_constraint(x, pltpu.HBM)
    q, k, v, g = far(q), far(k), far(v), far(g)
    gain = norm_gain.reshape(1, -1)
    order = jnp.where(place >= 2, 2 + (place & 1), place & 1).astype(jnp.int32).reshape(1)
    later = jnp.ones((1,), jnp.int32)
    swap = lambda x: lax.ppermute(x, "seq", [(c, c ^ 1) for c in range(count)])
    turn = lambda x: lax.ppermute(x, "seq", [(c, (c + 2) % count) for c in range(count)])
    ahead = lambda x: lax.ppermute(x, "seq", [(c, c + 2) for c in range(count - 2)])

    half = heads // 2
    small = half // 2
    big = half - small
    chunks = [(0, big), (half, big), (big, small), (half + big, small)]

    def widened(x, many, shift, window):
        while window < reach:
            past = lax.ppermute(x, "seq", [(c, c + shift) for c in range(count - shift)])
            x = joined(later, x, past, many)
            shift, window = 2 * shift, 2 * window
        return x

    own, a, w, seg, k_near, v_near = first_messages(
        order,
        far(segment.reshape(1, tokens)),
        far(decay_exponent.reshape(1, heads)),
        far(retention),
        k,
        v,
        heads,
        chunks[:2],
    )
    near, past, inside = {}, {}, {}
    near[1] = swap(own[1])
    past[0] = turn(own[0])
    messages, mask, k_rest, v_rest, q_near, g_near = rest_messages(
        seg, a, w, q, k, v, g, chunks, 2
    )
    own, k_near, v_near = [*own, *messages], [*k_near, *k_rest], [*v_near, *v_rest]

    def look_inside(i, through=(), after=()):
        inside[i], copied = intra(
            mask, a, gain, q_near[i], k_near[i], v_near[i], g_near[i], *chunks[i], through, after
        )
        return copied

    def pair_first(i, after, move):
        both = joined(order, own[i], near[i], chunks[i][1], after)
        past[i] = move(both)
        return both

    def pair_last(i, after):
        message = picked(order, own[i], past[i], after)
        near[i] = swap(message)
        return message

    near[3] = swap(own[3])
    past[2] = turn(own[2])
    first_done = pair_first(1, (), turn)
    look_inside(0, (), (first_done,))
    look_inside(1, (), (inside[0][0],))
    second_done = pair_last(0, (inside[1][0],))
    look_inside(2, (), (second_done,))
    look_inside(3, (), (inside[2][0],))
    second_done = pair_last(2, (inside[3][0],))
    first_done = pair_first(3, (second_done,), ahead)

    if reach > 2:
        for i, (_, many) in enumerate(chunks):
            past[i] = jnp.where(place >= 2, past[i], 0.0)
            if i % 2 == 0:
                near[i] = jnp.where(place >= 1, near[i], 0.0)
                near[i] = widened(joined(later, near[i], past[i], many), many, 2, 2)
                past[i] = jnp.zeros_like(near[i])
            else:
                past[i] = widened(past[i], many, 2, 2)

    result = ()
    for group in ((0,), (1,), (3,), (2,)):
        groups = [(*chunks[i], ("span", "pair")[i % 2]) for i in group]
        arrays = [x for i in group for x in (own[i], near[i], past[i], *inside[i])]
        result = finish(order, seg, heads, groups, arrays, result, (first_done,))
    return tuple(result)


def solution(mesh):
    placed = (
        P(("groups", "seq"), "wt"),
        P(("groups", "seq"), "wt"),
        P(("groups", "seq"), "wt"),
        P(("groups", "seq"), "wt"),
        P(("groups", "seq")),
        P("wt"),
        P("wt", ("groups", "seq")),
        P("wt"),
    )
    return jax.shard_map(
        shards,
        mesh=mesh,
        in_specs=placed,
        out_specs=(P(("groups", "seq"), "wt"), P(("groups", "seq"), "wt", None, None)),
        check_vma=False,
    )
```

```python
import functools

import jax
import jax.numpy as jnp
from jax import lax
from jax.experimental import pallas as pl
from jax.experimental.pallas import tpu as pltpu
from jax.sharding import PartitionSpec as P

F32 = jnp.float32
BF16 = jnp.bfloat16
NN = (((1,), (0,)), ((), ()))
NT = (((1,), (1,)), ((), ()))
MIB = 1 << 20
SHORT = pl.CostEstimate(flops=1, bytes_accessed=1, transcendentals=0)


def vmem_spec(shape, index_map):
    return pl.BlockSpec(shape, index_map)


def as_column(row, lanes):
    return jnp.broadcast_to(row, (lanes, row.shape[1])).T


def meta_rows(heads):
    return -(-(heads + 1) // 8) * 8


def put_message(msg_ref, first, heads, size, w_ref, finals, end, k_ref, v_ref):
    top = heads * size
    for j in range(heads):
        columns = slice(j * size, (j + 1) * size)
        weight = w_ref[first + j : first + j + 1, :]
        keyed = (k_ref[:, columns].astype(F32).T * weight).astype(BF16)
        msg_ref[columns, :] = lax.dot_general(
            keyed, v_ref[:, columns], NN, preferred_element_type=F32
        )
    msg_ref[top : top + heads, :] = jnp.broadcast_to(finals, (heads, size))
    below = meta_rows(heads) - heads
    msg_ref[top + heads :, :] = jnp.broadcast_to(end.astype(F32), (below, size))


def first_kernel(heads, chunks, order_ref, seg_hbm, exponent_hbm, keep_hbm, k_hbm, v_hbm, *refs):
    number = len(chunks)
    messages, refs = refs[:number], refs[number:]
    (a_ref, w_ref, seg_ref), refs = refs[:3], refs[3:]
    k_refs, v_refs, refs = refs[:number], refs[number : 2 * number], refs[2 * number :]
    exponent_ref, keep_ref, sems = refs
    tokens = seg_ref.shape[1]
    size = messages[0].shape[1]
    pairs = [(keep_hbm, keep_ref), (exponent_hbm, exponent_ref), (seg_hbm, seg_ref)]
    for i, (first, many) in enumerate(chunks):
        wide = pl.ds(first * size, many * size)
        pairs += [(k_hbm.at[:, wide], k_refs[i]), (v_hbm.at[:, wide], v_refs[i])]
    copies = [pltpu.make_async_copy(*pair, sems.at[i]) for i, pair in enumerate(pairs)]
    for copy in copies:
        copy.start()
    earlier = lax.broadcasted_iota(jnp.int32, (tokens, tokens), 0)
    later = lax.broadcasted_iota(jnp.int32, (tokens, tokens), 1)
    upper = jnp.where(earlier <= later, 1.0, 0.0).astype(BF16)
    across = lax.broadcasted_iota(jnp.int32, (heads, heads), 1)
    down = lax.broadcasted_iota(jnp.int32, (heads, heads), 0)
    for copy in copies[:3]:
        copy.wait()
    spread = jnp.broadcast_to(exponent_ref[...], (heads, heads))
    exponent = jnp.sum(jnp.where(across == down, spread, 0).astype(F32), axis=1, keepdims=True)
    a = -jnp.exp2(-exponent) + jnp.log(keep_ref[...])
    high = a.astype(BF16)
    rest = a - high.astype(F32)
    middle = rest.astype(BF16)
    low = (rest - middle.astype(F32)).astype(BF16)
    parts = jnp.concatenate([high, middle, low], axis=0)
    sums = lax.dot_general(parts, upper, NN, preferred_element_type=F32)
    cumulative = sums[:heads] + (sums[heads : 2 * heads] + sums[2 * heads :])
    a_ref[...] = cumulative
    final = cumulative[:, tokens - 1 :]
    seg = seg_ref[...]
    last = seg[:, tokens - 1 :]
    w_ref[...] = jnp.where(seg == last, jnp.exp(final - cumulative), 0.0)
    for i, (first, many) in enumerate(chunks):
        copies[3 + 2 * i].wait()
        copies[4 + 2 * i].wait()
        finals = final[first : first + many]
        put_message(messages[i], first, many, size, w_ref, finals, last, k_refs[i], v_refs[i])


def message_of(size, many):
    return pltpu.VMEM((many * size + meta_rows(many), size), F32)


def first_messages(order, seg, exponent, keep, k, v, heads, chunks):
    tokens, size = k.shape[0], k.shape[1] // heads
    near = [pltpu.VMEM((tokens, many * size), BF16) for _, many in chunks]
    shapes = [message_of(size, many) for _, many in chunks]
    shapes += [pltpu.VMEM((heads, tokens), F32)] * 2 + [pltpu.VMEM((1, tokens), jnp.int32)]
    shapes += near + near
    number = len(chunks)
    out = pl.pallas_call(
        functools.partial(first_kernel, heads, chunks),
        in_specs=[pl.BlockSpec(memory_space=pltpu.SMEM)]
        + [pl.BlockSpec(memory_space=pltpu.HBM)] * 5,
        out_specs=[pl.BlockSpec(memory_space=pltpu.VMEM)] * len(shapes),
        out_shape=shapes,
        scratch_shapes=[
            pltpu.VMEM((1, heads), jnp.int32),
            pltpu.VMEM((heads, tokens), F32),
            pltpu.SemaphoreType.DMA((3 + 2 * number,)),
        ],
        compiler_params=pltpu.CompilerParams(vmem_limit_bytes=8 * MIB),
        cost_estimate=SHORT,
        name="first_messages",
    )(order, seg, exponent, keep, k, v)
    messages, (a, w, seg), out = out[:number], out[number : number + 3], out[number + 3 :]
    return messages, a, w, seg, out[:number], out[number:]


def rest_kernel(chunks, done, seg_ref, a_ref, w_ref, q_hbm, k_hbm, v_hbm, g_hbm, *refs):
    tokens = seg_ref.shape[1]
    left, number = chunks[done:], len(chunks)
    messages, mask_ref, refs, sems = refs[: len(left)], refs[len(left)], refs[len(left) + 1 : -1], refs[-1]
    k_refs, refs = refs[: len(left)], refs[len(left) :]
    v_refs, refs = refs[: len(left)], refs[len(left) :]
    q_refs, g_refs = refs[:number], refs[number:]
    size = messages[0].shape[1]
    pairs = []
    for i, (first, many) in enumerate(left):
        wide = pl.ds(first * size, many * size)
        pairs += [(k_hbm.at[:, wide], k_refs[i]), (v_hbm.at[:, wide], v_refs[i])]
    for i, (first, many) in enumerate(chunks):
        wide = pl.ds(first * size, many * size)
        pairs += [(q_hbm.at[:, wide], q_refs[i]), (g_hbm.at[:, wide], g_refs[i])]
    copies = [pltpu.make_async_copy(*pair, sems.at[i]) for i, pair in enumerate(pairs)]
    for copy in copies:
        copy.start()
    make_mask(seg_ref, mask_ref)
    last = seg_ref[:, tokens - 1 :]
    for i, (first, many) in enumerate(left):
        copies[2 * i].wait()
        copies[2 * i + 1].wait()
        final = a_ref[first : first + many, tokens - 1 :]
        put_message(messages[i], first, many, size, w_ref, final, last, k_refs[i], v_refs[i])
    for copy in copies[2 * len(left) :]:
        copy.wait()


def rest_messages(seg, a, w, q, k, v, g, chunks, done):
    heads = a.shape[0]
    tokens, size = k.shape[0], k.shape[1] // heads
    near = [pltpu.VMEM((tokens, many * size), BF16) for _, many in chunks]
    shapes = [message_of(size, many) for _, many in chunks[done:]]
    shapes += [pltpu.VMEM((tokens, tokens), F32)] + near[done:] * 2 + near * 2
    left, number = len(chunks) - done, len(chunks)
    out = pl.pallas_call(
        functools.partial(rest_kernel, chunks, done),
        in_specs=[pl.BlockSpec(memory_space=pltpu.VMEM)] * 3
        + [pl.BlockSpec(memory_space=pltpu.HBM)] * 4,
        out_specs=[pl.BlockSpec(memory_space=pltpu.VMEM)] * len(shapes),
        out_shape=shapes,
        scratch_shapes=[pltpu.SemaphoreType.DMA((2 * (left + number),))],
        compiler_params=pltpu.CompilerParams(vmem_limit_bytes=8 * MIB),
        cost_estimate=SHORT,
        name="rest_messages",
    )(seg, a, w, q, k, v, g)
    messages, mask, out = out[:left], out[left], out[left + 1 :]
    k_near, v_near, out = out[:left], out[left : 2 * left], out[2 * left :]
    return messages, mask, k_near, v_near, out[:number], out[number:]


def join_kernel(heads, order_ref, mine_ref, other_ref, out_ref):
    size = mine_ref.shape[1]
    top = heads * size
    mine_later = (order_ref[0] & 1) == 1
    final_mine, final_other = mine_ref[top : top + heads, :], other_ref[top : top + heads, :]
    end_mine, end_other = mine_ref[top + heads :, :], other_ref[top + heads :, :]
    same = jnp.where(end_mine[:1] == end_other[:1], 1.0, 0.0)
    scale_mine = jnp.where(mine_later, 1.0, jnp.exp(final_other) * same)
    scale_other = jnp.where(mine_later, jnp.exp(final_mine) * same, 1.0)
    for head in range(heads):
        rows = slice(head * size, (head + 1) * size)
        out_ref[rows, :] = (
            scale_mine[head : head + 1] * mine_ref[rows, :]
            + scale_other[head : head + 1] * other_ref[rows, :]
        )
    out_ref[top : top + heads, :] = final_mine + final_other
    out_ref[top + heads :, :] = jnp.where(mine_later, end_mine, end_other)


def small_call(kernel, name, order, arrays, after):
    vmem = pl.BlockSpec(memory_space=pltpu.VMEM)
    return pl.pallas_call(
        lambda *refs: kernel(*refs[: 1 + len(arrays)], refs[-1]),
        in_specs=[pl.BlockSpec(memory_space=pltpu.SMEM)]
        + [vmem] * len(arrays)
        + [pl.BlockSpec(memory_space=pl.ANY)] * len(after),
        out_specs=vmem,
        out_shape=pltpu.VMEM(arrays[0].shape, F32),
        compiler_params=pltpu.CompilerParams(vmem_limit_bytes=8 * MIB),
        cost_estimate=SHORT,
        name=name,
    )(order, *arrays, *after)


def joined(order, mine, other, heads, after=()):
    return small_call(
        functools.partial(join_kernel, heads), "join_windows", order, (mine, other), after
    )


def pick_kernel(order_ref, own_ref, *refs):
    *past, out_ref = refs
    for code, source in enumerate((own_ref, past[-1], own_ref, past[0])):

        @pl.when((order_ref[0] & 3) == code)
        def _(source=source):
            out_ref[...] = source[...]


def picked(order, own, past, after=()):
    return small_call(pick_kernel, "pick_message", order, (own, *past), after)


def make_mask(seg_ref, mask_ref):
    tokens = seg_ref.shape[1]
    seg = seg_ref[...].astype(F32)
    column = as_column(seg, 128)
    for start in range(0, tokens, 128):
        across = lax.broadcasted_iota(jnp.int32, (tokens, 128), 1) + start
        down = lax.broadcasted_iota(jnp.int32, (tokens, 128), 0)
        seen = (column == seg[:, start : start + 128]) & (across <= down)
        mask_ref[:, start : start + 128] = jnp.where(seen, 0.0, -1e30)


def intra_kernel(
    first, heads, through, after, mask_ref, a_ref, gain_ref, q_ref, k_ref, v_ref, g_ref, *refs
):
    o_ref, gate_ref, decay_ref, *copied = refs[through + after :]
    for source, target in zip(refs[:through], copied):
        target[...] = source[...]
    tokens = mask_ref.shape[0]
    size = q_ref.shape[1] // heads
    block = min(tokens, 256)
    for j in range(heads):
        columns = slice(j * size, (j + 1) * size)
        a_row = a_ref[first + j : first + j + 1, :] * 1.4426950408889634
        a_column = as_column(a_row, 128)
        decay_ref[:, columns] = jnp.exp2(a_column)
        for start in range(0, tokens, block):
            here, upto = slice(start, start + block), slice(0, start + block)
            scores = lax.dot_general(
                q_ref[here, columns], k_ref[upto, columns], NT, preferred_element_type=F32
            )
            spread = jnp.concatenate([a_column[here]] * ((start + block) // 128), axis=1)
            weight = jnp.exp2(spread - a_row[:, upto] + mask_ref[here, upto])
            probs = (scores * weight).astype(BF16)
            o_ref[here, columns] = lax.dot_general(
                probs, v_ref[upto, columns], NN, preferred_element_type=F32
            )
        half = 0.5 * gain_ref[:, (first + j) * size : (first + j + 1) * size]
        gate_ref[:, columns] = half + half * jnp.tanh(0.5 * g_ref[:, columns].astype(F32))


def intra(mask, a, gain, q, k, v, g, first, heads, through=(), after=()):
    tokens, size = mask.shape[0], gain.shape[1] // a.shape[0]
    vmem = pl.BlockSpec(memory_space=pltpu.VMEM)
    o, gate, decay, *copied = pl.pallas_call(
        functools.partial(intra_kernel, first, heads, len(through), len(after)),
        in_specs=[vmem] * (7 + len(through)) + [pl.BlockSpec(memory_space=pl.ANY)] * len(after),
        out_specs=[vmem] * (3 + len(through)),
        out_shape=[pltpu.VMEM((tokens, heads * size), F32)] * 3
        + [pltpu.VMEM(x.shape, x.dtype) for x in through],
        compiler_params=pltpu.CompilerParams(vmem_limit_bytes=8 * MIB),
        cost_estimate=SHORT,
        name="intra_span",
    )(mask, a, gain, q, k, v, g, *through, *after)
    return (o, gate, decay, q), copied


def final_kernel(groups, unread, order_ref, seg_ref, *rest):
    number = len(groups)
    inputs, rest = rest[: 8 * number], rest[8 * number + unread :]
    gated_hbm, snap_hbm, *scratch, sems = rest
    place = order_ref[0]
    seg = seg_ref[...].astype(F32)
    copies, work = [], []

    def send(source, target):
        copies.append(pltpu.make_async_copy(source, target, sems.at[len(copies)]))
        copies[-1].start()

    for i, (first, heads, kind) in enumerate(groups):
        own_ref, near_ref, *past, o_ref, gate_ref, decay_ref, q_ref = inputs[8 * i : 8 * i + 8]
        past_of = lambda rows: jnp.where((place & 2) == 2, past[0][rows, :], past[1][rows, :])
        gated_ref, snap_ref = scratch[2 * i : 2 * i + 2]
        size = own_ref.shape[1]
        top = heads * size
        ends = slice(top + heads, top + heads + 1)
        finals = slice(top, top + heads)
        own_end, near_end, past_end = own_ref[ends, :], near_ref[ends, :], past_of(ends)
        bridged = jnp.exp(near_ref[finals, :]) * jnp.where(near_end == past_end, 1.0, 0.0)
        if kind == "pair":
            odd = (place & 1) == 1
            previous = jnp.where(odd, near_end, past_end)
            scale_near = jnp.where(odd, 1.0, 0.0)
            scale_past = jnp.where(odd, bridged, 1.0)
        else:
            previous = near_end
            scale_near = jnp.where(place == 4, 0.0, 1.0)
            scale_past = bridged
        scale_past = jnp.where(place >= 4, 0.0, scale_past)
        own_decay = jnp.exp(own_ref[finals, :]) * jnp.where(own_end == previous, 1.0, 0.0)
        valid = as_column(jnp.where(seg == previous[:, :1], 1.0, 0.0), size)
        for j in range(heads):
            rows = slice(j * size, (j + 1) * size)
            state = scale_past[j : j + 1] * past_of(rows) + scale_near * near_ref[rows, :]
            snap_ref[j] = own_decay[j : j + 1] * state + own_ref[rows, :]
            high = state.astype(BF16)
            low = (state - high.astype(F32)).astype(BF16)
            both = jnp.concatenate([high, low], axis=0)
            work.append((i, j, first, heads, both, valid, (o_ref, gate_ref, decay_ref, q_ref)))
        send(snap_ref, snap_hbm.at[0, pl.ds(first, heads)])

    for i, j, first, heads, both, valid, (o_ref, gate_ref, decay_ref, q_ref) in work:
        gated_ref = scratch[2 * i]
        tokens, size = valid.shape
        block = min(tokens, 256)
        columns = slice(j * size, (j + 1) * size)
        for start in range(0, tokens, block):
            here = slice(start, start + block)
            q = q_ref[here, columns]
            inter = lax.dot_general(
                jnp.concatenate([q, q], axis=1), both, NN, preferred_element_type=F32
            )
            mixed = o_ref[here, columns] + inter * (decay_ref[here, columns] * valid[here])
            mean_square = jnp.mean(mixed * mixed, axis=1, keepdims=True)
            gated = mixed * lax.rsqrt(mean_square + 1e-06) * gate_ref[here, columns]
            gated_ref[here, columns] = gated.astype(BF16)
        if j % 2 == 1 or j == heads - 1:
            begin = j - j % 2
            width = (j + 1 - begin) * size
            there = pl.ds((first + begin) * size, width)
            send(gated_ref.at[:, pl.ds(begin * size, width)], gated_hbm.at[:, there])
    for copy in copies:
        copy.wait()


def finish(order, seg, total, groups, arrays, so_far, after):
    tokens, size = seg.shape[1], arrays[0].shape[1]
    vmem, anywhere = pl.BlockSpec(memory_space=pltpu.VMEM), pl.BlockSpec(memory_space=pl.ANY)
    unread = len(so_far) + len(after)
    scratch = []
    for _, many, _ in groups:
        scratch.append(pltpu.VMEM((tokens, many * size), BF16))
        scratch.append(pltpu.VMEM((many, size, size), F32))
    return pl.pallas_call(
        functools.partial(final_kernel, groups, unread),
        in_specs=[pl.BlockSpec(memory_space=pltpu.SMEM)]
        + [vmem] * (1 + len(arrays))
        + [anywhere] * unread,
        out_specs=[anywhere, anywhere],
        out_shape=[
            jax.ShapeDtypeStruct((tokens, total * size), BF16),
            jax.ShapeDtypeStruct((1, total, size, size), F32),
        ],
        scratch_shapes=scratch + [pltpu.SemaphoreType.DMA((2 * total,))],
        input_output_aliases={2 + len(arrays) + i: i for i in range(len(so_far))},
        compiler_params=pltpu.CompilerParams(vmem_limit_bytes=12 * MIB),
        cost_estimate=SHORT,
        name="finish",
    )(order, seg, *arrays, *so_far, *after)


def shards(q, k, v, g, segment, decay_exponent, retention, norm_gain):
    heads = decay_exponent.shape[0]
    tokens = q.shape[0]
    count = lax.axis_size("seq")
    place = lax.axis_index("seq")
    reach = max(1, count // 4)
    far = lambda x: pltpu.with_memory_space_constraint(x, pltpu.HBM)
    q, k, v, g = far(q), far(k), far(v), far(g)
    gain = norm_gain.reshape(1, -1)
    order = ((place & 3) + jnp.where(place < 2, 4, 0)).astype(jnp.int32).reshape(1)
    later = jnp.ones((1,), jnp.int32)
    swap = lambda x: lax.ppermute(x, "seq", [(c, c ^ 1) for c in range(count)])
    turn = lambda x: (lax.ppermute(x, "seq", [(c, (c + 2) % count) for c in range(count)]),)
    other = [[c + 2 if c // 2 % 2 == way else c - 2 for c in range(count)] for way in (0, 1)]
    other = [[d if 0 <= d < count else c for c, d in enumerate(row)] for row in other]
    swaps = lambda x: tuple(lax.ppermute(x, "seq", list(enumerate(row))) for row in other)

    half = heads // 2
    small = half // 2
    big = half - small
    chunks = [(0, big), (half, big), (big, small), (half + big, small)]

    def widened(x, many, shift, window):
        while window < reach:
            past = lax.ppermute(x, "seq", [(c, c + shift) for c in range(count - shift)])
            x = joined(later, x, past, many)
            shift, window = 2 * shift, 2 * window
        return x

    own, a, w, seg, k_near, v_near = first_messages(
        order,
        far(segment.reshape(1, tokens)),
        far(decay_exponent.reshape(1, heads)),
        far(retention),
        k,
        v,
        heads,
        chunks[:2],
    )
    near, past, inside = {}, {}, {}
    near[1] = swap(own[1])
    past[0] = swaps(own[0])
    messages, mask, k_rest, v_rest, q_near, g_near = rest_messages(
        seg, a, w, q, k, v, g, chunks, 2
    )
    own, k_near, v_near = [*own, *messages], [*k_near, *k_rest], [*v_near, *v_rest]

    def look_inside(i, through=(), after=()):
        inside[i], copied = intra(
            mask, a, gain, q_near[i], k_near[i], v_near[i], g_near[i], *chunks[i], through, after
        )
        return copied

    def pair_last(i, after):
        message = picked(order, own[i], past[i], after)
        near[i] = swap(message)
        return message

    near[3] = swap(own[3])
    past[2] = turn(own[2])
    look_inside(0)
    first_done = joined(order, own[1], near[1], chunks[1][1], (inside[0][0],))
    second_done = pair_last(0, (first_done,))
    (first_done,) = look_inside(1, (first_done,), (second_done,))
    past[1] = turn(first_done)
    look_inside(2, (), (first_done,))
    second_done = pair_last(2, (inside[2][0],))
    look_inside(3, (), (second_done,))
    first_done = joined(order, own[3], near[3], chunks[3][1], (inside[3][0],))
    past[3] = swaps(first_done)

    if reach > 2:
        for i, (_, many) in enumerate(chunks):
            before = jnp.where((place & 2) == 2, past[i][0], past[i][-1])
            before = jnp.where(place >= 2, before, 0.0)
            if i % 2 == 0:
                near[i] = jnp.where(place >= 1, near[i], 0.0)
                near[i] = widened(joined(later, near[i], before, many), many, 2, 2)
                before = jnp.zeros_like(before)
            else:
                before = widened(before, many, 2, 2)
            past[i] = (before,)

    result = ()
    for group in ((0, 1), (2, 3)):
        groups = [(*chunks[i], ("span", "pair")[i % 2]) for i in group]
        arrays = [x for i in group for x in (own[i], near[i], past[i][0], past[i][-1], *inside[i])]
        result = finish(order, seg, heads, groups, arrays, result, (first_done,))
    return tuple(result)


def solution(mesh):
    placed = (
        P(("groups", "seq"), "wt"),
        P(("groups", "seq"), "wt"),
        P(("groups", "seq"), "wt"),
        P(("groups", "seq"), "wt"),
        P(("groups", "seq")),
        P("wt"),
        P("wt", ("groups", "seq")),
        P("wt"),
    )
    return jax.shard_map(
        shards,
        mesh=mesh,
        in_specs=placed,
        out_specs=(P(("groups", "seq"), "wt"), P(("groups", "seq"), "wt", None, None)),
        check_vma=False,
    )
```

```python
import functools

import jax
import jax.numpy as jnp
from jax import lax
from jax.experimental import pallas as pl
from jax.experimental.pallas import tpu as pltpu
from jax.sharding import PartitionSpec as P

F32 = jnp.float32
BF16 = jnp.bfloat16
NN = (((1,), (0,)), ((), ()))
NT = (((1,), (1,)), ((), ()))
MIB = 1 << 20
SHORT = pl.CostEstimate(flops=1, bytes_accessed=1, transcendentals=0)


def vmem_spec(shape, index_map):
    return pl.BlockSpec(shape, index_map)


def as_column(row, lanes):
    return jnp.broadcast_to(row, (lanes, row.shape[1])).T


def meta_rows(heads):
    return -(-(heads + 1) // 8) * 8


def put_message(msg_ref, first, heads, size, w_ref, finals, end, k_ref, v_ref):
    top = heads * size
    for j in range(heads):
        columns = slice(j * size, (j + 1) * size)
        weight = w_ref[first + j : first + j + 1, :]
        keyed = (k_ref[:, columns].astype(F32).T * weight).astype(BF16)
        msg_ref[columns, :] = lax.dot_general(
            keyed, v_ref[:, columns], NN, preferred_element_type=F32
        )
    msg_ref[top : top + heads, :] = jnp.broadcast_to(finals, (heads, size))
    below = meta_rows(heads) - heads
    msg_ref[top + heads :, :] = jnp.broadcast_to(end.astype(F32), (below, size))


def first_kernel(heads, chunks, order_ref, seg_hbm, exponent_hbm, keep_hbm, k_hbm, v_hbm, *refs):
    number = len(chunks)
    messages, refs = refs[:number], refs[number:]
    (a_ref, w_ref, seg_ref), refs = refs[:3], refs[3:]
    k_refs, v_refs, refs = refs[:number], refs[number : 2 * number], refs[2 * number :]
    exponent_ref, keep_ref, sems = refs
    tokens = seg_ref.shape[1]
    size = messages[0].shape[1]
    pairs = [(keep_hbm, keep_ref), (exponent_hbm, exponent_ref), (seg_hbm, seg_ref)]
    for i, (first, many) in enumerate(chunks):
        wide = pl.ds(first * size, many * size)
        pairs += [(k_hbm.at[:, wide], k_refs[i]), (v_hbm.at[:, wide], v_refs[i])]
    copies = [pltpu.make_async_copy(*pair, sems.at[i]) for i, pair in enumerate(pairs)]
    for copy in copies:
        copy.start()
    earlier = lax.broadcasted_iota(jnp.int32, (tokens, tokens), 0)
    later = lax.broadcasted_iota(jnp.int32, (tokens, tokens), 1)
    upper = jnp.where(earlier <= later, 1.0, 0.0).astype(BF16)
    across = lax.broadcasted_iota(jnp.int32, (heads, heads), 1)
    down = lax.broadcasted_iota(jnp.int32, (heads, heads), 0)
    for copy in copies[:3]:
        copy.wait()
    spread = jnp.broadcast_to(exponent_ref[...], (heads, heads))
    exponent = jnp.sum(jnp.where(across == down, spread, 0).astype(F32), axis=1, keepdims=True)
    a = -jnp.exp2(-exponent) + jnp.log(keep_ref[...])
    high = a.astype(BF16)
    rest = a - high.astype(F32)
    middle = rest.astype(BF16)
    low = (rest - middle.astype(F32)).astype(BF16)
    parts = jnp.concatenate([high, middle, low], axis=0)
    sums = lax.dot_general(parts, upper, NN, preferred_element_type=F32)
    cumulative = sums[:heads] + (sums[heads : 2 * heads] + sums[2 * heads :])
    a_ref[...] = cumulative
    final = cumulative[:, tokens - 1 :]
    seg = seg_ref[...]
    last = seg[:, tokens - 1 :]
    w_ref[...] = jnp.where(seg == last, jnp.exp(final - cumulative), 0.0)
    for i, (first, many) in enumerate(chunks):
        copies[3 + 2 * i].wait()
        copies[4 + 2 * i].wait()
        finals = final[first : first + many]
        put_message(messages[i], first, many, size, w_ref, finals, last, k_refs[i], v_refs[i])


def message_of(size, many):
    return pltpu.VMEM((many * size + meta_rows(many), size), F32)


def first_messages(order, seg, exponent, keep, k, v, heads, chunks):
    tokens, size = k.shape[0], k.shape[1] // heads
    near = [pltpu.VMEM((tokens, many * size), BF16) for _, many in chunks]
    shapes = [message_of(size, many) for _, many in chunks]
    shapes += [pltpu.VMEM((heads, tokens), F32)] * 2 + [pltpu.VMEM((1, tokens), jnp.int32)]
    shapes += near + near
    number = len(chunks)
    out = pl.pallas_call(
        functools.partial(first_kernel, heads, chunks),
        in_specs=[pl.BlockSpec(memory_space=pltpu.SMEM)]
        + [pl.BlockSpec(memory_space=pltpu.HBM)] * 5,
        out_specs=[pl.BlockSpec(memory_space=pltpu.VMEM)] * len(shapes),
        out_shape=shapes,
        scratch_shapes=[
            pltpu.VMEM((1, heads), jnp.int32),
            pltpu.VMEM((heads, tokens), F32),
            pltpu.SemaphoreType.DMA((3 + 2 * number,)),
        ],
        compiler_params=pltpu.CompilerParams(vmem_limit_bytes=8 * MIB),
        cost_estimate=SHORT,
        name="first_messages",
    )(order, seg, exponent, keep, k, v)
    messages, (a, w, seg), out = out[:number], out[number : number + 3], out[number + 3 :]
    return messages, a, w, seg, out[:number], out[number:]


def rest_kernel(chunks, done, seg_ref, a_ref, w_ref, q_hbm, k_hbm, v_hbm, g_hbm, *refs):
    tokens = seg_ref.shape[1]
    left, number = chunks[done:], len(chunks)
    messages, mask_ref, refs, sems = refs[: len(left)], refs[len(left)], refs[len(left) + 1 : -1], refs[-1]
    k_refs, refs = refs[: len(left)], refs[len(left) :]
    v_refs, refs = refs[: len(left)], refs[len(left) :]
    q_refs, g_refs = refs[:number], refs[number:]
    size = messages[0].shape[1]
    pairs = []
    for i, (first, many) in enumerate(left):
        wide = pl.ds(first * size, many * size)
        pairs += [(k_hbm.at[:, wide], k_refs[i]), (v_hbm.at[:, wide], v_refs[i])]
    for i, (first, many) in enumerate(chunks):
        wide = pl.ds(first * size, many * size)
        pairs += [(q_hbm.at[:, wide], q_refs[i]), (g_hbm.at[:, wide], g_refs[i])]
    copies = [pltpu.make_async_copy(*pair, sems.at[i]) for i, pair in enumerate(pairs)]
    for copy in copies:
        copy.start()
    make_mask(seg_ref, mask_ref)
    last = seg_ref[:, tokens - 1 :]
    for i, (first, many) in enumerate(left):
        copies[2 * i].wait()
        copies[2 * i + 1].wait()
        final = a_ref[first : first + many, tokens - 1 :]
        put_message(messages[i], first, many, size, w_ref, final, last, k_refs[i], v_refs[i])
    for copy in copies[2 * len(left) :]:
        copy.wait()


def rest_messages(seg, a, w, q, k, v, g, chunks, done):
    heads = a.shape[0]
    tokens, size = k.shape[0], k.shape[1] // heads
    near = [pltpu.VMEM((tokens, many * size), BF16) for _, many in chunks]
    shapes = [message_of(size, many) for _, many in chunks[done:]]
    shapes += [pltpu.VMEM((tokens, tokens), F32)] + near[done:] * 2 + near * 2
    left, number = len(chunks) - done, len(chunks)
    out = pl.pallas_call(
        functools.partial(rest_kernel, chunks, done),
        in_specs=[pl.BlockSpec(memory_space=pltpu.VMEM)] * 3
        + [pl.BlockSpec(memory_space=pltpu.HBM)] * 4,
        out_specs=[pl.BlockSpec(memory_space=pltpu.VMEM)] * len(shapes),
        out_shape=shapes,
        scratch_shapes=[pltpu.SemaphoreType.DMA((2 * (left + number),))],
        compiler_params=pltpu.CompilerParams(vmem_limit_bytes=8 * MIB),
        cost_estimate=SHORT,
        name="rest_messages",
    )(seg, a, w, q, k, v, g)
    messages, mask, out = out[:left], out[left], out[left + 1 :]
    k_near, v_near, out = out[:left], out[left : 2 * left], out[2 * left :]
    return messages, mask, k_near, v_near, out[:number], out[number:]


def join_kernel(heads, order_ref, mine_ref, other_ref, out_ref):
    size = mine_ref.shape[1]
    top = heads * size
    mine_later = (order_ref[0] & 1) == 1
    final_mine, final_other = mine_ref[top : top + heads, :], other_ref[top : top + heads, :]
    end_mine, end_other = mine_ref[top + heads :, :], other_ref[top + heads :, :]
    same = jnp.where(end_mine[:1] == end_other[:1], 1.0, 0.0)
    scale_mine = jnp.where(mine_later, 1.0, jnp.exp(final_other) * same)
    scale_other = jnp.where(mine_later, jnp.exp(final_mine) * same, 1.0)
    for head in range(heads):
        rows = slice(head * size, (head + 1) * size)
        out_ref[rows, :] = (
            scale_mine[head : head + 1] * mine_ref[rows, :]
            + scale_other[head : head + 1] * other_ref[rows, :]
        )
    out_ref[top : top + heads, :] = final_mine + final_other
    out_ref[top + heads :, :] = jnp.where(mine_later, end_mine, end_other)


def small_call(kernel, name, order, arrays, after):
    vmem = pl.BlockSpec(memory_space=pltpu.VMEM)
    return pl.pallas_call(
        lambda *refs: kernel(*refs[: 1 + len(arrays)], refs[-1]),
        in_specs=[pl.BlockSpec(memory_space=pltpu.SMEM)]
        + [vmem] * len(arrays)
        + [pl.BlockSpec(memory_space=pl.ANY)] * len(after),
        out_specs=vmem,
        out_shape=pltpu.VMEM(arrays[0].shape, F32),
        compiler_params=pltpu.CompilerParams(vmem_limit_bytes=8 * MIB),
        cost_estimate=SHORT,
        name=name,
    )(order, *arrays, *after)


def joined(order, mine, other, heads, after=()):
    return small_call(
        functools.partial(join_kernel, heads), "join_windows", order, (mine, other), after
    )


def pick_kernel(order_ref, even_ref, odd_ref, out_ref):
    odd = (order_ref[0] & 1) == 1

    @pl.when(odd)
    def _():
        out_ref[...] = odd_ref[...]

    @pl.when(jnp.logical_not(odd))
    def _():
        out_ref[...] = even_ref[...]


def picked(order, even, odd, after=()):
    return small_call(pick_kernel, "pick_message", order, (even, odd), after)


def make_mask(seg_ref, mask_ref):
    tokens = seg_ref.shape[1]
    seg = seg_ref[...].astype(F32)
    column = as_column(seg, 128)
    for start in range(0, tokens, 128):
        across = lax.broadcasted_iota(jnp.int32, (tokens, 128), 1) + start
        down = lax.broadcasted_iota(jnp.int32, (tokens, 128), 0)
        seen = (column == seg[:, start : start + 128]) & (across <= down)
        mask_ref[:, start : start + 128] = jnp.where(seen, 0.0, -1e30)


def intra_kernel(
    first, heads, through, after, mask_ref, a_ref, gain_ref, q_ref, k_ref, v_ref, g_ref, *refs
):
    o_ref, gate_ref, decay_ref, *copied = refs[through + after :]
    for source, target in zip(refs[:through], copied):
        target[...] = source[...]
    tokens = mask_ref.shape[0]
    size = q_ref.shape[1] // heads
    block = min(tokens, 256)
    for j in range(heads):
        columns = slice(j * size, (j + 1) * size)
        a_row = a_ref[first + j : first + j + 1, :] * 1.4426950408889634
        a_column = as_column(a_row, 128)
        decay_ref[:, columns] = jnp.exp2(a_column)
        for start in range(0, tokens, block):
            here, upto = slice(start, start + block), slice(0, start + block)
            scores = lax.dot_general(
                q_ref[here, columns], k_ref[upto, columns], NT, preferred_element_type=F32
            )
            spread = jnp.concatenate([a_column[here]] * ((start + block) // 128), axis=1)
            weight = jnp.exp2(spread - a_row[:, upto] + mask_ref[here, upto])
            probs = (scores * weight).astype(BF16)
            o_ref[here, columns] = lax.dot_general(
                probs, v_ref[upto, columns], NN, preferred_element_type=F32
            )
        half = 0.5 * gain_ref[:, (first + j) * size : (first + j + 1) * size]
        gate_ref[:, columns] = half + half * jnp.tanh(0.5 * g_ref[:, columns].astype(F32))


def intra(mask, a, gain, q, k, v, g, first, heads, through=(), after=()):
    tokens, size = mask.shape[0], gain.shape[1] // a.shape[0]
    vmem = pl.BlockSpec(memory_space=pltpu.VMEM)
    o, gate, decay, *copied = pl.pallas_call(
        functools.partial(intra_kernel, first, heads, len(through), len(after)),
        in_specs=[vmem] * (7 + len(through)) + [pl.BlockSpec(memory_space=pl.ANY)] * len(after),
        out_specs=[vmem] * (3 + len(through)),
        out_shape=[pltpu.VMEM((tokens, heads * size), F32)] * 3
        + [pltpu.VMEM(x.shape, x.dtype) for x in through],
        compiler_params=pltpu.CompilerParams(vmem_limit_bytes=8 * MIB),
        cost_estimate=SHORT,
        name="intra_span",
    )(mask, a, gain, q, k, v, g, *through, *after)
    return (o, gate, decay, q), copied


def final_kernel(groups, unread, order_ref, seg_ref, *rest):
    number = len(groups)
    inputs, rest = rest[: 7 * number], rest[7 * number + unread :]
    gated_hbm, snap_hbm, *scratch, sems = rest
    place = order_ref[0]
    seg = seg_ref[...].astype(F32)
    copies, work = [], []

    def send(source, target):
        copies.append(pltpu.make_async_copy(source, target, sems.at[len(copies)]))
        copies[-1].start()

    for i, (first, heads, kind) in enumerate(groups):
        own_ref, near_ref, past_ref, o_ref, gate_ref, decay_ref, q_ref = inputs[7 * i : 7 * i + 7]
        gated_ref, snap_ref = scratch[2 * i : 2 * i + 2]
        size = own_ref.shape[1]
        top = heads * size
        ends = slice(top + heads, top + heads + 1)
        finals = slice(top, top + heads)
        own_end, near_end, past_end = own_ref[ends, :], near_ref[ends, :], past_ref[ends, :]
        bridged = jnp.exp(near_ref[finals, :]) * jnp.where(near_end == past_end, 1.0, 0.0)
        if kind == "pair":
            odd = (place & 1) == 1
            previous = jnp.where(odd, near_end, past_end)
            scale_near = jnp.where(odd, 1.0, 0.0)
            scale_past = jnp.where(odd, bridged, 1.0)
        else:
            previous = near_end
            scale_near = jnp.where(place > 0, 1.0, 0.0)
            scale_past = bridged
        scale_past = jnp.where(place >= 2, scale_past, 0.0)
        own_decay = jnp.exp(own_ref[finals, :]) * jnp.where(own_end == previous, 1.0, 0.0)
        valid = as_column(jnp.where(seg == previous[:, :1], 1.0, 0.0), size)
        for j in range(heads):
            rows = slice(j * size, (j + 1) * size)
            state = scale_past[j : j + 1] * past_ref[rows, :] + scale_near * near_ref[rows, :]
            snap_ref[j] = own_decay[j : j + 1] * state + own_ref[rows, :]
            high = state.astype(BF16)
            low = (state - high.astype(F32)).astype(BF16)
            both = jnp.concatenate([high, low], axis=0)
            work.append((i, j, first, heads, both, valid, (o_ref, gate_ref, decay_ref, q_ref)))
        send(snap_ref, snap_hbm.at[0, pl.ds(first, heads)])

    for i, j, first, heads, both, valid, (o_ref, gate_ref, decay_ref, q_ref) in work:
        gated_ref = scratch[2 * i]
        tokens, size = valid.shape
        block = min(tokens, 256)
        columns = slice(j * size, (j + 1) * size)
        for start in range(0, tokens, block):
            here = slice(start, start + block)
            q = q_ref[here, columns]
            inter = lax.dot_general(
                jnp.concatenate([q, q], axis=1), both, NN, preferred_element_type=F32
            )
            mixed = o_ref[here, columns] + inter * (decay_ref[here, columns] * valid[here])
            mean_square = jnp.mean(mixed * mixed, axis=1, keepdims=True)
            gated = mixed * lax.rsqrt(mean_square + 1e-06) * gate_ref[here, columns]
            gated_ref[here, columns] = gated.astype(BF16)
        if j % 2 == 1 or j == heads - 1:
            begin = j - j % 2
            width = (j + 1 - begin) * size
            there = pl.ds((first + begin) * size, width)
            send(gated_ref.at[:, pl.ds(begin * size, width)], gated_hbm.at[:, there])
    for copy in copies:
        copy.wait()


def finish(order, seg, total, groups, arrays, so_far, after):
    tokens, size = seg.shape[1], arrays[0].shape[1]
    vmem, anywhere = pl.BlockSpec(memory_space=pltpu.VMEM), pl.BlockSpec(memory_space=pl.ANY)
    unread = len(so_far) + len(after)
    scratch = []
    for _, many, _ in groups:
        scratch.append(pltpu.VMEM((tokens, many * size), BF16))
        scratch.append(pltpu.VMEM((many, size, size), F32))
    return pl.pallas_call(
        functools.partial(final_kernel, groups, unread),
        in_specs=[pl.BlockSpec(memory_space=pltpu.SMEM)]
        + [vmem] * (1 + len(arrays))
        + [anywhere] * unread,
        out_specs=[anywhere, anywhere],
        out_shape=[
            jax.ShapeDtypeStruct((tokens, total * size), BF16),
            jax.ShapeDtypeStruct((1, total, size, size), F32),
        ],
        scratch_shapes=scratch + [pltpu.SemaphoreType.DMA((2 * total,))],
        input_output_aliases={2 + len(arrays) + i: i for i in range(len(so_far))},
        compiler_params=pltpu.CompilerParams(vmem_limit_bytes=12 * MIB),
        cost_estimate=SHORT,
        name="finish",
    )(order, seg, *arrays, *so_far, *after)


def shards(q, k, v, g, segment, decay_exponent, retention, norm_gain):
    heads = decay_exponent.shape[0]
    tokens = q.shape[0]
    count = lax.axis_size("seq")
    place = lax.axis_index("seq")
    reach = max(1, count // 4)
    far = lambda x: pltpu.with_memory_space_constraint(x, pltpu.HBM)
    q, k, v, g = far(q), far(k), far(v), far(g)
    gain = norm_gain.reshape(1, -1)
    order = jnp.where(place >= 2, 2 + (place & 1), place & 1).astype(jnp.int32).reshape(1)
    later = jnp.ones((1,), jnp.int32)
    swap = lambda x: lax.ppermute(x, "seq", [(c, c ^ 1) for c in range(count)])
    turn = lambda x: lax.ppermute(x, "seq", [(c, (c + 2) % count) for c in range(count)])
    ahead = lambda x: lax.ppermute(x, "seq", [(c, c + 2) for c in range(count - 2)])

    half = heads // 2
    small = half // 2
    big = half - small
    chunks = [(0, big), (half, big), (big, small), (half + big, small)]

    def widened(x, many, shift, window):
        while window < reach:
            past = lax.ppermute(x, "seq", [(c, c + shift) for c in range(count - shift)])
            x = joined(later, x, past, many)
            shift, window = 2 * shift, 2 * window
        return x

    own, a, w, seg, k_near, v_near = first_messages(
        order,
        far(segment.reshape(1, tokens)),
        far(decay_exponent.reshape(1, heads)),
        far(retention),
        k,
        v,
        heads,
        chunks[:2],
    )
    near, past, inside = {}, {}, {}
    near[1] = swap(own[1])
    past[0] = turn(own[0])
    messages, mask, k_rest, v_rest, q_near, g_near = rest_messages(
        seg, a, w, q, k, v, g, chunks, 2
    )
    own, k_near, v_near = [*own, *messages], [*k_near, *k_rest], [*v_near, *v_rest]

    def look_inside(i, through=(), after=()):
        inside[i], copied = intra(
            mask, a, gain, q_near[i], k_near[i], v_near[i], g_near[i], *chunks[i], through, after
        )
        return copied

    def pair_last(i, after):
        message = picked(order, own[i], past[i], after)
        near[i] = swap(message)
        return message

    near[3] = swap(own[3])
    past[2] = turn(own[2])
    look_inside(0)
    first_done = joined(order, own[1], near[1], chunks[1][1], (inside[0][0],))
    second_done = pair_last(0, (first_done,))
    (first_done,) = look_inside(1, (first_done,), (second_done,))
    past[1] = turn(first_done)
    look_inside(2, (), (first_done,))
    second_done = pair_last(2, (inside[2][0],))
    look_inside(3, (), (second_done,))
    first_done = joined(order, own[3], near[3], chunks[3][1], (inside[3][0],))
    past[3] = ahead(first_done)

    if reach > 2:
        for i, (_, many) in enumerate(chunks):
            past[i] = jnp.where(place >= 2, past[i], 0.0)
            if i % 2 == 0:
                near[i] = jnp.where(place >= 1, near[i], 0.0)
                near[i] = widened(joined(later, near[i], past[i], many), many, 2, 2)
                past[i] = jnp.zeros_like(near[i])
            else:
                past[i] = widened(past[i], many, 2, 2)

    result = ()
    for group in ((0, 1), (2, 3)):
        groups = [(*chunks[i], ("span", "pair")[i % 2]) for i in group]
        arrays = [x for i in group for x in (own[i], near[i], past[i], *inside[i])]
        result = finish(order, seg, heads, groups, arrays, result, (first_done,))
    return tuple(result)


def solution(mesh):
    placed = (
        P(("groups", "seq"), "wt"),
        P(("groups", "seq"), "wt"),
        P(("groups", "seq"), "wt"),
        P(("groups", "seq"), "wt"),
        P(("groups", "seq")),
        P("wt"),
        P("wt", ("groups", "seq")),
        P("wt"),
    )
    return jax.shard_map(
        shards,
        mesh=mesh,
        in_specs=placed,
        out_specs=(P(("groups", "seq"), "wt"), P(("groups", "seq"), "wt", None, None)),
        check_vma=False,
    )
```

```python
import functools

import jax
import jax.numpy as jnp
from jax import lax
from jax.experimental import pallas as pl
from jax.experimental.pallas import tpu as pltpu
from jax.sharding import PartitionSpec as P

F32 = jnp.float32
BF16 = jnp.bfloat16
NN = (((1,), (0,)), ((), ()))
NT = (((1,), (1,)), ((), ()))
MIB = 1 << 20
SHORT = pl.CostEstimate(flops=1, bytes_accessed=1, transcendentals=0)


def vmem_spec(shape, index_map):
    return pl.BlockSpec(shape, index_map)


def as_column(row, lanes):
    return jnp.broadcast_to(row, (lanes, row.shape[1])).T


def meta_rows(heads):
    return -(-(heads + 1) // 8) * 8


def put_message(msg_ref, first, heads, size, w_ref, finals, end, k_ref, v_ref):
    top = heads * size
    for j in range(heads):
        columns = slice(j * size, (j + 1) * size)
        weight = w_ref[first + j : first + j + 1, :]
        keyed = (k_ref[:, columns].astype(F32).T * weight).astype(BF16)
        msg_ref[columns, :] = lax.dot_general(
            keyed, v_ref[:, columns], NN, preferred_element_type=F32
        )
    msg_ref[top : top + heads, :] = jnp.broadcast_to(finals, (heads, size))
    below = meta_rows(heads) - heads
    msg_ref[top + heads :, :] = jnp.broadcast_to(end.astype(F32), (below, size))


def first_kernel(heads, chunks, order_ref, seg_hbm, exponent_hbm, keep_hbm, k_hbm, v_hbm, *refs):
    number = len(chunks)
    messages, refs = refs[:number], refs[number:]
    (a_ref, w_ref, seg_ref), refs = refs[:3], refs[3:]
    k_refs, v_refs, refs = refs[:number], refs[number : 2 * number], refs[2 * number :]
    exponent_ref, keep_ref, sems = refs
    tokens = seg_ref.shape[1]
    size = messages[0].shape[1]
    pairs = [(keep_hbm, keep_ref), (exponent_hbm, exponent_ref), (seg_hbm, seg_ref)]
    for i, (first, many) in enumerate(chunks):
        wide = pl.ds(first * size, many * size)
        pairs += [(k_hbm.at[:, wide], k_refs[i]), (v_hbm.at[:, wide], v_refs[i])]
    copies = [pltpu.make_async_copy(*pair, sems.at[i]) for i, pair in enumerate(pairs)]
    for copy in copies:
        copy.start()
    earlier = lax.broadcasted_iota(jnp.int32, (128, 128), 0)
    later = lax.broadcasted_iota(jnp.int32, (128, 128), 1)
    upper = jnp.where(earlier <= later, 1.0, 0.0).astype(BF16)
    across = lax.broadcasted_iota(jnp.int32, (heads, heads), 1)
    down = lax.broadcasted_iota(jnp.int32, (heads, heads), 0)
    for copy in copies[:3]:
        copy.wait()
    spread = jnp.broadcast_to(exponent_ref[...], (heads, heads))
    exponent = jnp.sum(jnp.where(across == down, spread, 0).astype(F32), axis=1, keepdims=True)
    a = -jnp.exp2(-exponent) + jnp.log(keep_ref[...])
    a = jnp.concatenate([a[:, i : i + 128] for i in range(0, tokens, 128)], axis=0)
    high = a.astype(BF16)
    rest = a - high.astype(F32)
    middle = rest.astype(BF16)
    low = (rest - middle.astype(F32)).astype(BF16)
    sums = [
        lax.dot_general(part, upper, NN, preferred_element_type=F32) for part in (high, middle, low)
    ]
    sums = sums[0] + (sums[1] + sums[2])
    blocks = [sums[i : i + heads] for i in range(0, sums.shape[0], heads)]
    for i in range(1, len(blocks)):
        blocks[i] = blocks[i] + blocks[i - 1][:, 127:]
    cumulative = jnp.concatenate(blocks, axis=1)
    a_ref[...] = cumulative
    final = cumulative[:, tokens - 1 :]
    seg = seg_ref[...]
    last = seg[:, tokens - 1 :]
    w_ref[...] = jnp.where(seg == last, jnp.exp(final - cumulative), 0.0)
    for i, (first, many) in enumerate(chunks):
        copies[3 + 2 * i].wait()
        copies[4 + 2 * i].wait()
        finals = final[first : first + many]
        put_message(messages[i], first, many, size, w_ref, finals, last, k_refs[i], v_refs[i])


def message_of(size, many):
    return pltpu.VMEM((many * size + meta_rows(many), size), F32)


def first_messages(order, seg, exponent, keep, k, v, heads, chunks):
    tokens, size = k.shape[0], k.shape[1] // heads
    near = [pltpu.VMEM((tokens, many * size), BF16) for _, many in chunks]
    shapes = [message_of(size, many) for _, many in chunks]
    shapes += [pltpu.VMEM((heads, tokens), F32)] * 2 + [pltpu.VMEM((1, tokens), jnp.int32)]
    shapes += near + near
    number = len(chunks)
    out = pl.pallas_call(
        functools.partial(first_kernel, heads, chunks),
        in_specs=[pl.BlockSpec(memory_space=pltpu.SMEM)]
        + [pl.BlockSpec(memory_space=pltpu.HBM)] * 5,
        out_specs=[pl.BlockSpec(memory_space=pltpu.VMEM)] * len(shapes),
        out_shape=shapes,
        scratch_shapes=[
            pltpu.VMEM((1, heads), jnp.int32),
            pltpu.VMEM((heads, tokens), F32),
            pltpu.SemaphoreType.DMA((3 + 2 * number,)),
        ],
        compiler_params=pltpu.CompilerParams(vmem_limit_bytes=8 * MIB),
        cost_estimate=SHORT,
        name="first_messages",
    )(order, seg, exponent, keep, k, v)
    messages, (a, w, seg), out = out[:number], out[number : number + 3], out[number + 3 :]
    return messages, a, w, seg, out[:number], out[number:]


def rest_kernel(chunks, done, seg_ref, a_ref, w_ref, q_hbm, k_hbm, v_hbm, g_hbm, *refs):
    tokens = seg_ref.shape[1]
    left, number = chunks[done:], len(chunks)
    messages, mask_ref, refs, sems = refs[: len(left)], refs[len(left)], refs[len(left) + 1 : -1], refs[-1]
    k_refs, refs = refs[: len(left)], refs[len(left) :]
    v_refs, refs = refs[: len(left)], refs[len(left) :]
    q_refs, g_refs = refs[:number], refs[number:]
    size = messages[0].shape[1]
    pairs = []
    for i, (first, many) in enumerate(left):
        wide = pl.ds(first * size, many * size)
        pairs += [(k_hbm.at[:, wide], k_refs[i]), (v_hbm.at[:, wide], v_refs[i])]
    for i, (first, many) in enumerate(chunks):
        wide = pl.ds(first * size, many * size)
        pairs += [(q_hbm.at[:, wide], q_refs[i]), (g_hbm.at[:, wide], g_refs[i])]
    copies = [pltpu.make_async_copy(*pair, sems.at[i]) for i, pair in enumerate(pairs)]
    for copy in copies:
        copy.start()
    make_mask(seg_ref, mask_ref)
    last = seg_ref[:, tokens - 1 :]
    for i, (first, many) in enumerate(left):
        copies[2 * i].wait()
        copies[2 * i + 1].wait()
        final = a_ref[first : first + many, tokens - 1 :]
        put_message(messages[i], first, many, size, w_ref, final, last, k_refs[i], v_refs[i])
    for copy in copies[2 * len(left) :]:
        copy.wait()


def rest_messages(seg, a, w, q, k, v, g, chunks, done):
    heads = a.shape[0]
    tokens, size = k.shape[0], k.shape[1] // heads
    near = [pltpu.VMEM((tokens, many * size), BF16) for _, many in chunks]
    shapes = [message_of(size, many) for _, many in chunks[done:]]
    shapes += [pltpu.VMEM((tokens, tokens), F32)] + near[done:] * 2 + near * 2
    left, number = len(chunks) - done, len(chunks)
    out = pl.pallas_call(
        functools.partial(rest_kernel, chunks, done),
        in_specs=[pl.BlockSpec(memory_space=pltpu.VMEM)] * 3
        + [pl.BlockSpec(memory_space=pltpu.HBM)] * 4,
        out_specs=[pl.BlockSpec(memory_space=pltpu.VMEM)] * len(shapes),
        out_shape=shapes,
        scratch_shapes=[pltpu.SemaphoreType.DMA((2 * (left + number),))],
        compiler_params=pltpu.CompilerParams(vmem_limit_bytes=8 * MIB),
        cost_estimate=SHORT,
        name="rest_messages",
    )(seg, a, w, q, k, v, g)
    messages, mask, out = out[:left], out[left], out[left + 1 :]
    k_near, v_near, out = out[:left], out[left : 2 * left], out[2 * left :]
    return messages, mask, k_near, v_near, out[:number], out[number:]


def join_kernel(heads, order_ref, mine_ref, other_ref, out_ref):
    size = mine_ref.shape[1]
    top = heads * size
    mine_later = (order_ref[0] & 1) == 1
    final_mine, final_other = mine_ref[top : top + heads, :], other_ref[top : top + heads, :]
    end_mine, end_other = mine_ref[top + heads :, :], other_ref[top + heads :, :]
    same = jnp.where(end_mine[:1] == end_other[:1], 1.0, 0.0)
    scale_mine = jnp.where(mine_later, 1.0, jnp.exp(final_other) * same)
    scale_other = jnp.where(mine_later, jnp.exp(final_mine) * same, 1.0)
    for head in range(heads):
        rows = slice(head * size, (head + 1) * size)
        out_ref[rows, :] = (
            scale_mine[head : head + 1] * mine_ref[rows, :]
            + scale_other[head : head + 1] * other_ref[rows, :]
        )
    out_ref[top : top + heads, :] = final_mine + final_other
    out_ref[top + heads :, :] = jnp.where(mine_later, end_mine, end_other)


def small_call(kernel, name, order, arrays, after):
    vmem = pl.BlockSpec(memory_space=pltpu.VMEM)
    return pl.pallas_call(
        lambda *refs: kernel(*refs[: 1 + len(arrays)], refs[-1]),
        in_specs=[pl.BlockSpec(memory_space=pltpu.SMEM)]
        + [vmem] * len(arrays)
        + [pl.BlockSpec(memory_space=pl.ANY)] * len(after),
        out_specs=vmem,
        out_shape=pltpu.VMEM(arrays[0].shape, F32),
        compiler_params=pltpu.CompilerParams(vmem_limit_bytes=8 * MIB),
        cost_estimate=SHORT,
        name=name,
    )(order, *arrays, *after)


def joined(order, mine, other, heads, after=()):
    return small_call(
        functools.partial(join_kernel, heads), "join_windows", order, (mine, other), after
    )


def picked(order, even, odd, after=(), through=()):
    vmem = pl.BlockSpec(memory_space=pltpu.VMEM)

    def kernel(order_ref, even_ref, odd_ref, *refs):
        outs = refs[len(through) + len(after) :]
        for source, target in zip(refs, outs[1:]):
            target[...] = source[...]
        odd = (order_ref[0] & 1) == 1

        @pl.when(odd)
        def _():
            outs[0][...] = odd_ref[...]

        @pl.when(jnp.logical_not(odd))
        def _():
            outs[0][...] = even_ref[...]

    return pl.pallas_call(
        kernel,
        in_specs=[pl.BlockSpec(memory_space=pltpu.SMEM)]
        + [vmem] * (2 + len(through))
        + [pl.BlockSpec(memory_space=pl.ANY)] * len(after),
        out_specs=[vmem] * (1 + len(through)),
        out_shape=[pltpu.VMEM(x.shape, F32) for x in (even, *through)],
        compiler_params=pltpu.CompilerParams(vmem_limit_bytes=8 * MIB),
        cost_estimate=SHORT,
        name="pick_message",
    )(order, even, odd, *through, *after)


def make_mask(seg_ref, mask_ref):
    tokens = seg_ref.shape[1]
    seg = seg_ref[...].astype(F32)
    column = as_column(seg, 128)
    for start in range(0, tokens, 128):
        across = lax.broadcasted_iota(jnp.int32, (tokens, 128), 1) + start
        down = lax.broadcasted_iota(jnp.int32, (tokens, 128), 0)
        seen = (column == seg[:, start : start + 128]) & (across <= down)
        mask_ref[:, start : start + 128] = jnp.where(seen, 0.0, -1e30)


def intra_kernel(
    first, heads, through, after, mask_ref, a_ref, gain_ref, q_ref, k_ref, v_ref, g_ref, *refs
):
    o_ref, gate_ref, decay_ref, *copied = refs[through + after :]
    for source, target in zip(refs[:through], copied):
        target[...] = source[...]
    tokens = mask_ref.shape[0]
    size = q_ref.shape[1] // heads
    block = min(tokens, 256)
    for j in range(heads):
        columns = slice(j * size, (j + 1) * size)
        a_row = a_ref[first + j : first + j + 1, :] * 1.4426950408889634
        a_column = as_column(a_row, 128)
        decay_ref[:, columns] = jnp.exp2(a_column)
        for start in range(0, tokens, block):
            here, upto = slice(start, start + block), slice(0, start + block)
            scores = lax.dot_general(
                q_ref[here, columns], k_ref[upto, columns], NT, preferred_element_type=F32
            )
            spread = jnp.concatenate([a_column[here]] * ((start + block) // 128), axis=1)
            weight = jnp.exp2(spread - a_row[:, upto] + mask_ref[here, upto])
            probs = (scores * weight).astype(BF16)
            o_ref[here, columns] = lax.dot_general(
                probs, v_ref[upto, columns], NN, preferred_element_type=F32
            )
        half = 0.5 * gain_ref[:, (first + j) * size : (first + j + 1) * size]
        gate_ref[:, columns] = half + half * jnp.tanh(0.5 * g_ref[:, columns].astype(F32))


def intra(mask, a, gain, q, k, v, g, first, heads, through=(), after=()):
    tokens, size = mask.shape[0], gain.shape[1] // a.shape[0]
    vmem = pl.BlockSpec(memory_space=pltpu.VMEM)
    o, gate, decay, *copied = pl.pallas_call(
        functools.partial(intra_kernel, first, heads, len(through), len(after)),
        in_specs=[vmem] * (7 + len(through)) + [pl.BlockSpec(memory_space=pl.ANY)] * len(after),
        out_specs=[vmem] * (3 + len(through)),
        out_shape=[pltpu.VMEM((tokens, heads * size), F32)] * 3
        + [pltpu.VMEM(x.shape, x.dtype) for x in through],
        compiler_params=pltpu.CompilerParams(vmem_limit_bytes=8 * MIB),
        cost_estimate=SHORT,
        name="intra_span",
    )(mask, a, gain, q, k, v, g, *through, *after)
    return (o, gate, decay, q), copied


def final_kernel(groups, unread, order_ref, seg_ref, *rest):
    number = len(groups)
    inputs, rest = rest[: 7 * number], rest[7 * number + unread :]
    gated_hbm, snap_hbm, *scratch, sems = rest
    place = order_ref[0]
    seg = seg_ref[...].astype(F32)
    copies, work = [], []

    def send(source, target):
        copies.append(pltpu.make_async_copy(source, target, sems.at[len(copies)]))
        copies[-1].start()

    for i, (first, heads, kind) in enumerate(groups):
        own_ref, near_ref, past_ref, o_ref, gate_ref, decay_ref, q_ref = inputs[7 * i : 7 * i + 7]
        gated_ref, snap_ref = scratch[2 * i : 2 * i + 2]
        size = own_ref.shape[1]
        top = heads * size
        ends = slice(top + heads, top + heads + 1)
        finals = slice(top, top + heads)
        own_end, near_end, past_end = own_ref[ends, :], near_ref[ends, :], past_ref[ends, :]
        bridged = jnp.exp(near_ref[finals, :]) * jnp.where(near_end == past_end, 1.0, 0.0)
        if kind == "pair":
            odd = (place & 1) == 1
            previous = jnp.where(odd, near_end, past_end)
            scale_near = jnp.where(odd, 1.0, 0.0)
            scale_past = jnp.where(odd, bridged, 1.0)
        else:
            previous = near_end
            scale_near = jnp.where(place > 0, 1.0, 0.0)
            scale_past = bridged
        scale_past = jnp.where(place >= 2, scale_past, 0.0)
        own_decay = jnp.exp(own_ref[finals, :]) * jnp.where(own_end == previous, 1.0, 0.0)
        valid = as_column(jnp.where(seg == previous[:, :1], 1.0, 0.0), size)
        for j in range(heads):
            rows = slice(j * size, (j + 1) * size)
            state = scale_past[j : j + 1] * past_ref[rows, :] + scale_near * near_ref[rows, :]
            snap_ref[j] = own_decay[j : j + 1] * state + own_ref[rows, :]
            high = state.astype(BF16)
            low = (state - high.astype(F32)).astype(BF16)
            both = jnp.concatenate([high, low], axis=0)
            work.append((i, j, first, heads, both, valid, (o_ref, gate_ref, decay_ref, q_ref)))
        send(snap_ref, snap_hbm.at[0, pl.ds(first, heads)])

    for i, j, first, heads, both, valid, (o_ref, gate_ref, decay_ref, q_ref) in work:
        gated_ref = scratch[2 * i]
        tokens, size = valid.shape
        block = min(tokens, 256)
        columns = slice(j * size, (j + 1) * size)
        for start in range(0, tokens, block):
            here = slice(start, start + block)
            q = q_ref[here, columns]
            inter = lax.dot_general(
                jnp.concatenate([q, q], axis=1), both, NN, preferred_element_type=F32
            )
            mixed = o_ref[here, columns] + inter * (decay_ref[here, columns] * valid[here])
            mean_square = jnp.mean(mixed * mixed, axis=1, keepdims=True)
            gated = mixed * lax.rsqrt(mean_square + 1e-06) * gate_ref[here, columns]
            gated_ref[here, columns] = gated.astype(BF16)
        if j % 2 == 1 or j == heads - 1:
            begin = j - j % 2
            width = (j + 1 - begin) * size
            there = pl.ds((first + begin) * size, width)
            send(gated_ref.at[:, pl.ds(begin * size, width)], gated_hbm.at[:, there])
    for copy in copies:
        copy.wait()


def finish(order, seg, total, groups, arrays, so_far, after):
    tokens, size = seg.shape[1], arrays[0].shape[1]
    vmem, anywhere = pl.BlockSpec(memory_space=pltpu.VMEM), pl.BlockSpec(memory_space=pl.ANY)
    unread = len(so_far) + len(after)
    scratch = []
    for _, many, _ in groups:
        scratch.append(pltpu.VMEM((tokens, many * size), BF16))
        scratch.append(pltpu.VMEM((many, size, size), F32))
    return pl.pallas_call(
        functools.partial(final_kernel, groups, unread),
        in_specs=[pl.BlockSpec(memory_space=pltpu.SMEM)]
        + [vmem] * (1 + len(arrays))
        + [anywhere] * unread,
        out_specs=[anywhere, anywhere],
        out_shape=[
            jax.ShapeDtypeStruct((tokens, total * size), BF16),
            jax.ShapeDtypeStruct((1, total, size, size), F32),
        ],
        scratch_shapes=scratch + [pltpu.SemaphoreType.DMA((2 * total,))],
        input_output_aliases={2 + len(arrays) + i: i for i in range(len(so_far))},
        compiler_params=pltpu.CompilerParams(vmem_limit_bytes=12 * MIB),
        cost_estimate=SHORT,
        name="finish",
    )(order, seg, *arrays, *so_far, *after)


def shards(q, k, v, g, segment, decay_exponent, retention, norm_gain):
    heads = decay_exponent.shape[0]
    tokens = q.shape[0]
    count = lax.axis_size("seq")
    place = lax.axis_index("seq")
    reach = max(1, count // 4)
    far = lambda x: pltpu.with_memory_space_constraint(x, pltpu.HBM)
    q, k, v, g = far(q), far(k), far(v), far(g)
    gain = norm_gain.reshape(1, -1)
    order = jnp.where(place >= 2, 2 + (place & 1), place & 1).astype(jnp.int32).reshape(1)
    later = jnp.ones((1,), jnp.int32)
    swap = lambda x: lax.ppermute(x, "seq", [(c, c ^ 1) for c in range(count)])
    turn = lambda x: lax.ppermute(x, "seq", [(c, (c + 2) % count) for c in range(count)])
    ahead = lambda x: lax.ppermute(x, "seq", [(c, c + 2) for c in range(count - 2)])

    half = heads // 2
    small = half // 2
    big = half - small
    chunks = [(0, big), (half, big), (big, small), (half + big, small)]

    def widened(x, many, shift, window):
        while window < reach:
            past = lax.ppermute(x, "seq", [(c, c + shift) for c in range(count - shift)])
            x = joined(later, x, past, many)
            shift, window = 2 * shift, 2 * window
        return x

    own, a, w, seg, k_near, v_near = first_messages(
        order,
        far(segment.reshape(1, tokens)),
        far(decay_exponent.reshape(1, heads)),
        far(retention),
        k,
        v,
        heads,
        chunks[:2],
    )
    near, past, inside = {}, {}, {}
    near[1] = swap(own[1])
    past[0] = turn(own[0])
    messages, mask, k_rest, v_rest, q_near, g_near = rest_messages(
        seg, a, w, q, k, v, g, chunks, 2
    )
    own, k_near, v_near = [*own, *messages], [*k_near, *k_rest], [*v_near, *v_rest]

    def look_inside(i, through=(), after=()):
        inside[i], copied = intra(
            mask, a, gain, q_near[i], k_near[i], v_near[i], g_near[i], *chunks[i], through, after
        )
        return copied

    def pair_last(i, after, through=()):
        message, *copied = picked(order, own[i], past[i], after, through)
        near[i] = swap(message)
        return message, *copied

    near[3] = swap(own[3])
    past[2] = turn(own[2])
    look_inside(0)
    both = joined(order, own[1], near[1], chunks[1][1], (inside[0][0],))
    message, both = pair_last(0, (), (both,))
    past[1] = turn(both)
    look_inside(1, (), (message,))
    look_inside(2, (), (inside[1][0],))
    both = joined(order, own[3], near[3], chunks[3][1], (inside[2][0],))
    message, both = pair_last(2, (), (both,))
    past[3] = ahead(both)
    look_inside(3, (), (message,))

    if reach > 2:
        for i, (_, many) in enumerate(chunks):
            past[i] = jnp.where(place >= 2, past[i], 0.0)
            if i % 2 == 0:
                near[i] = jnp.where(place >= 1, near[i], 0.0)
                near[i] = widened(joined(later, near[i], past[i], many), many, 2, 2)
                past[i] = jnp.zeros_like(near[i])
            else:
                past[i] = widened(past[i], many, 2, 2)

    result = ()
    for group in ((0, 1), (2, 3)):
        groups = [(*chunks[i], ("span", "pair")[i % 2]) for i in group]
        arrays = [x for i in group for x in (own[i], near[i], past[i], *inside[i])]
        result = finish(order, seg, heads, groups, arrays, result, (inside[3][0],))
    return tuple(result)


def solution(mesh):
    placed = (
        P(("groups", "seq"), "wt"),
        P(("groups", "seq"), "wt"),
        P(("groups", "seq"), "wt"),
        P(("groups", "seq"), "wt"),
        P(("groups", "seq")),
        P("wt"),
        P("wt", ("groups", "seq")),
        P("wt"),
    )
    return jax.shard_map(
        shards,
        mesh=mesh,
        in_specs=placed,
        out_specs=(P(("groups", "seq"), "wt"), P(("groups", "seq"), "wt", None, None)),
        check_vma=False,
    )
```

```python
import functools

import jax
import jax.numpy as jnp
from jax import lax
from jax.experimental import pallas as pl
from jax.experimental.pallas import tpu as pltpu
from jax.sharding import PartitionSpec as P

F32 = jnp.float32
BF16 = jnp.bfloat16
NN = (((1,), (0,)), ((), ()))
NT = (((1,), (1,)), ((), ()))
MIB = 1 << 20
SHORT = pl.CostEstimate(flops=1, bytes_accessed=1, transcendentals=0)


def vmem_spec(shape, index_map):
    return pl.BlockSpec(shape, index_map)


def as_column(row, lanes):
    return jnp.broadcast_to(row, (lanes, row.shape[1])).T


def meta_rows(heads):
    return -(-(heads + 1) // 8) * 8


def put_message(msg_ref, first, heads, size, w_ref, finals, end, k_ref, v_ref):
    top = heads * size
    for j in range(heads):
        columns = slice(j * size, (j + 1) * size)
        weight = w_ref[first + j : first + j + 1, :]
        keyed = (k_ref[:, columns].astype(F32).T * weight).astype(BF16)
        msg_ref[columns, :] = lax.dot_general(
            keyed, v_ref[:, columns], NN, preferred_element_type=F32
        )
    msg_ref[top : top + heads, :] = jnp.broadcast_to(finals, (heads, size))
    below = meta_rows(heads) - heads
    msg_ref[top + heads :, :] = jnp.broadcast_to(end.astype(F32), (below, size))


def first_kernel(heads, chunks, order_ref, seg_hbm, exponent_hbm, keep_hbm, k_hbm, v_hbm, *refs):
    number = len(chunks)
    (msg_ref, a_ref, w_ref, seg_ref), refs = refs[:4], refs[4:]
    k_refs, v_refs, refs = refs[:number], refs[number : 2 * number], refs[2 * number :]
    exponent_ref, keep_ref, sems = refs
    tokens = seg_ref.shape[1]
    size = msg_ref.shape[1]
    pairs = [(keep_hbm, keep_ref), (exponent_hbm, exponent_ref), (seg_hbm, seg_ref)]
    for i, (first, many) in enumerate(chunks):
        wide = pl.ds(first * size, many * size)
        pairs += [(k_hbm.at[:, wide], k_refs[i]), (v_hbm.at[:, wide], v_refs[i])]
    copies = [pltpu.make_async_copy(*pair, sems.at[i]) for i, pair in enumerate(pairs)]
    for copy in copies:
        copy.start()
    earlier = lax.broadcasted_iota(jnp.int32, (tokens, tokens), 0)
    later = lax.broadcasted_iota(jnp.int32, (tokens, tokens), 1)
    upper = jnp.where(earlier <= later, 1.0, 0.0).astype(BF16)
    across = lax.broadcasted_iota(jnp.int32, (heads, heads), 1)
    down = lax.broadcasted_iota(jnp.int32, (heads, heads), 0)
    for copy in copies[:3]:
        copy.wait()
    spread = jnp.broadcast_to(exponent_ref[...], (heads, heads))
    exponent = jnp.sum(jnp.where(across == down, spread, 0).astype(F32), axis=1, keepdims=True)
    a = -jnp.exp2(-exponent) + jnp.log(keep_ref[...])
    high = a.astype(BF16)
    rest = a - high.astype(F32)
    middle = rest.astype(BF16)
    low = (rest - middle.astype(F32)).astype(BF16)
    parts = jnp.concatenate([high, middle, low], axis=0)
    sums = lax.dot_general(parts, upper, NN, preferred_element_type=F32)
    cumulative = sums[:heads] + (sums[heads : 2 * heads] + sums[2 * heads :])
    a_ref[...] = cumulative
    final = cumulative[:, tokens - 1 :]
    seg = seg_ref[...]
    last = seg[:, tokens - 1 :]
    w_ref[...] = jnp.where(seg == last, jnp.exp(final - cumulative), 0.0)
    for copy in copies[3:5]:
        copy.wait()
    first, many = chunks[0]
    finals = final[first : first + many]
    put_message(msg_ref, first, many, size, w_ref, finals, last, k_refs[0], v_refs[0])
    for copy in copies[5:]:
        copy.wait()


def message_of(size, many):
    return pltpu.VMEM((many * size + meta_rows(many), size), F32)


def first_message(order, seg, exponent, keep, k, v, heads, chunks):
    tokens, size = k.shape[0], k.shape[1] // heads
    near = [pltpu.VMEM((tokens, many * size), BF16) for _, many in chunks]
    shapes = [message_of(size, chunks[0][1])]
    shapes += [pltpu.VMEM((heads, tokens), F32)] * 2 + [pltpu.VMEM((1, tokens), jnp.int32)]
    shapes += near + near
    number = len(chunks)
    out = pl.pallas_call(
        functools.partial(first_kernel, heads, chunks),
        in_specs=[pl.BlockSpec(memory_space=pltpu.SMEM)]
        + [pl.BlockSpec(memory_space=pltpu.HBM)] * 5,
        out_specs=[pl.BlockSpec(memory_space=pltpu.VMEM)] * len(shapes),
        out_shape=shapes,
        scratch_shapes=[
            pltpu.VMEM((1, heads), jnp.int32),
            pltpu.VMEM((heads, tokens), F32),
            pltpu.SemaphoreType.DMA((3 + 2 * number,)),
        ],
        compiler_params=pltpu.CompilerParams(vmem_limit_bytes=8 * MIB),
        cost_estimate=SHORT,
        name="first_message",
    )(order, seg, exponent, keep, k, v)
    (message, a, w, seg), out = out[:4], out[4:]
    return message, a, w, seg, out[:number], out[number:]


def second_message(seg, a, w, k, v, first, heads):
    tokens, size = k.shape[0], k.shape[1] // heads

    def kernel(seg_ref, a_ref, w_ref, k_ref, v_ref, msg_ref):
        final = a_ref[first : first + heads, tokens - 1 :]
        last = seg_ref[:, tokens - 1 :]
        put_message(msg_ref, first, heads, size, w_ref, final, last, k_ref, v_ref)

    return pl.pallas_call(
        kernel,
        in_specs=[pl.BlockSpec(memory_space=pltpu.VMEM)] * 5,
        out_specs=pl.BlockSpec(memory_space=pltpu.VMEM),
        out_shape=message_of(size, heads),
        compiler_params=pltpu.CompilerParams(vmem_limit_bytes=8 * MIB),
        cost_estimate=SHORT,
        name="second_message",
    )(seg, a, w, k, v)


def rest_kernel(chunks, done, seg_ref, a_ref, w_ref, q_hbm, k_hbm, v_hbm, g_hbm, *refs):
    tokens = seg_ref.shape[1]
    left, number = chunks[done:], len(chunks)
    messages, mask_ref, refs, sems = refs[: len(left)], refs[len(left)], refs[len(left) + 1 : -1], refs[-1]
    k_refs, refs = refs[: len(left)], refs[len(left) :]
    v_refs, refs = refs[: len(left)], refs[len(left) :]
    q_refs, g_refs = refs[:number], refs[number:]
    size = messages[0].shape[1]
    pairs = []
    for i, (first, many) in enumerate(left):
        wide = pl.ds(first * size, many * size)
        pairs += [(k_hbm.at[:, wide], k_refs[i]), (v_hbm.at[:, wide], v_refs[i])]
    for i, (first, many) in enumerate(chunks):
        wide = pl.ds(first * size, many * size)
        pairs += [(q_hbm.at[:, wide], q_refs[i]), (g_hbm.at[:, wide], g_refs[i])]
    copies = [pltpu.make_async_copy(*pair, sems.at[i]) for i, pair in enumerate(pairs)]
    for copy in copies:
        copy.start()
    make_mask(seg_ref, mask_ref)
    last = seg_ref[:, tokens - 1 :]
    for i, (first, many) in enumerate(left):
        copies[2 * i].wait()
        copies[2 * i + 1].wait()
        final = a_ref[first : first + many, tokens - 1 :]
        put_message(messages[i], first, many, size, w_ref, final, last, k_refs[i], v_refs[i])
    for copy in copies[2 * len(left) :]:
        copy.wait()


def rest_messages(seg, a, w, q, k, v, g, chunks, done):
    heads = a.shape[0]
    tokens, size = k.shape[0], k.shape[1] // heads
    near = [pltpu.VMEM((tokens, many * size), BF16) for _, many in chunks]
    shapes = [message_of(size, many) for _, many in chunks[done:]]
    shapes += [pltpu.VMEM((tokens, tokens), F32)] + near[done:] * 2 + near * 2
    left, number = len(chunks) - done, len(chunks)
    out = pl.pallas_call(
        functools.partial(rest_kernel, chunks, done),
        in_specs=[pl.BlockSpec(memory_space=pltpu.VMEM)] * 3
        + [pl.BlockSpec(memory_space=pltpu.HBM)] * 4,
        out_specs=[pl.BlockSpec(memory_space=pltpu.VMEM)] * len(shapes),
        out_shape=shapes,
        scratch_shapes=[pltpu.SemaphoreType.DMA((2 * (left + number),))],
        compiler_params=pltpu.CompilerParams(vmem_limit_bytes=8 * MIB),
        cost_estimate=SHORT,
        name="rest_messages",
    )(seg, a, w, q, k, v, g)
    messages, mask, out = out[:left], out[left], out[left + 1 :]
    k_near, v_near, out = out[:left], out[left : 2 * left], out[2 * left :]
    return messages, mask, k_near, v_near, out[:number], out[number:]


def join_kernel(heads, order_ref, mine_ref, other_ref, out_ref):
    size = mine_ref.shape[1]
    top = heads * size
    mine_later = (order_ref[0] & 1) == 1
    final_mine, final_other = mine_ref[top : top + heads, :], other_ref[top : top + heads, :]
    end_mine, end_other = mine_ref[top + heads :, :], other_ref[top + heads :, :]
    same = jnp.where(end_mine[:1] == end_other[:1], 1.0, 0.0)
    scale_mine = jnp.where(mine_later, 1.0, jnp.exp(final_other) * same)
    scale_other = jnp.where(mine_later, jnp.exp(final_mine) * same, 1.0)
    for head in range(heads):
        rows = slice(head * size, (head + 1) * size)
        out_ref[rows, :] = (
            scale_mine[head : head + 1] * mine_ref[rows, :]
            + scale_other[head : head + 1] * other_ref[rows, :]
        )
    out_ref[top : top + heads, :] = final_mine + final_other
    out_ref[top + heads :, :] = jnp.where(mine_later, end_mine, end_other)


def small_call(kernel, name, order, arrays, after):
    vmem = pl.BlockSpec(memory_space=pltpu.VMEM)
    return pl.pallas_call(
        lambda *refs: kernel(*refs[: 1 + len(arrays)], refs[-1]),
        in_specs=[pl.BlockSpec(memory_space=pltpu.SMEM)]
        + [vmem] * len(arrays)
        + [pl.BlockSpec(memory_space=pl.ANY)] * len(after),
        out_specs=vmem,
        out_shape=pltpu.VMEM(arrays[0].shape, F32),
        compiler_params=pltpu.CompilerParams(vmem_limit_bytes=8 * MIB),
        cost_estimate=SHORT,
        name=name,
    )(order, *arrays, *after)


def joined(order, mine, other, heads, after=()):
    return small_call(
        functools.partial(join_kernel, heads), "join_windows", order, (mine, other), after
    )


def picked(order, even, odd, after=(), through=()):
    vmem = pl.BlockSpec(memory_space=pltpu.VMEM)

    def kernel(order_ref, even_ref, odd_ref, *refs):
        outs = refs[len(through) + len(after) :]
        for source, target in zip(refs, outs[1:]):
            target[...] = source[...]
        odd = (order_ref[0] & 1) == 1

        @pl.when(odd)
        def _():
            outs[0][...] = odd_ref[...]

        @pl.when(jnp.logical_not(odd))
        def _():
            outs[0][...] = even_ref[...]

    return pl.pallas_call(
        kernel,
        in_specs=[pl.BlockSpec(memory_space=pltpu.SMEM)]
        + [vmem] * (2 + len(through))
        + [pl.BlockSpec(memory_space=pl.ANY)] * len(after),
        out_specs=[vmem] * (1 + len(through)),
        out_shape=[pltpu.VMEM(x.shape, F32) for x in (even, *through)],
        compiler_params=pltpu.CompilerParams(vmem_limit_bytes=8 * MIB),
        cost_estimate=SHORT,
        name="pick_message",
    )(order, even, odd, *through, *after)


def make_mask(seg_ref, mask_ref):
    tokens = seg_ref.shape[1]
    seg = seg_ref[...].astype(F32)
    column = as_column(seg, 128)
    for start in range(0, tokens, 128):
        across = lax.broadcasted_iota(jnp.int32, (tokens, 128), 1) + start
        down = lax.broadcasted_iota(jnp.int32, (tokens, 128), 0)
        seen = (column == seg[:, start : start + 128]) & (across <= down)
        mask_ref[:, start : start + 128] = jnp.where(seen, 0.0, -1e30)


def intra_kernel(
    first, heads, through, after, mask_ref, a_ref, gain_ref, q_ref, k_ref, v_ref, g_ref, *refs
):
    o_ref, gate_ref, decay_ref, *copied = refs[through + after :]
    for source, target in zip(refs[:through], copied):
        target[...] = source[...]
    tokens = mask_ref.shape[0]
    size = q_ref.shape[1] // heads
    block = min(tokens, 256)
    for j in range(heads):
        columns = slice(j * size, (j + 1) * size)
        a_row = a_ref[first + j : first + j + 1, :] * 1.4426950408889634
        a_column = as_column(a_row, 128)
        decay_ref[:, columns] = jnp.exp2(a_column)
        for start in range(0, tokens, block):
            here, upto = slice(start, start + block), slice(0, start + block)
            scores = lax.dot_general(
                q_ref[here, columns], k_ref[upto, columns], NT, preferred_element_type=F32
            )
            spread = jnp.concatenate([a_column[here]] * ((start + block) // 128), axis=1)
            weight = jnp.exp2(spread - a_row[:, upto] + mask_ref[here, upto])
            probs = (scores * weight).astype(BF16)
            o_ref[here, columns] = lax.dot_general(
                probs, v_ref[upto, columns], NN, preferred_element_type=F32
            )
        half = 0.5 * size**0.5 * gain_ref[:, (first + j) * size : (first + j + 1) * size]
        gate_ref[:, columns] = half + half * jnp.tanh(0.5 * g_ref[:, columns].astype(F32))


def intra(mask, a, gain, q, k, v, g, first, heads, through=(), after=()):
    tokens, size = mask.shape[0], gain.shape[1] // a.shape[0]
    vmem = pl.BlockSpec(memory_space=pltpu.VMEM)
    o, gate, decay, *copied = pl.pallas_call(
        functools.partial(intra_kernel, first, heads, len(through), len(after)),
        in_specs=[vmem] * (7 + len(through)) + [pl.BlockSpec(memory_space=pl.ANY)] * len(after),
        out_specs=[vmem] * (3 + len(through)),
        out_shape=[pltpu.VMEM((tokens, heads * size), F32)] * 3
        + [pltpu.VMEM(x.shape, x.dtype) for x in through],
        compiler_params=pltpu.CompilerParams(vmem_limit_bytes=8 * MIB),
        cost_estimate=SHORT,
        name="intra_span",
    )(mask, a, gain, q, k, v, g, *through, *after)
    return (o, gate, decay, q), copied


def final_kernel(groups, unread, order_ref, seg_ref, *rest):
    number = len(groups)
    inputs, rest = rest[: 7 * number], rest[7 * number + unread :]
    gated_hbm, snap_hbm, *scratch, inter_ref, sems = rest
    place = order_ref[0]
    seg = seg_ref[...].astype(F32)
    copies, work = [], []

    def send(source, target):
        copies.append(pltpu.make_async_copy(source, target, sems.at[len(copies)]))
        copies[-1].start()

    for i, (first, heads, kind) in enumerate(groups):
        own_ref, near_ref, past_ref, o_ref, gate_ref, decay_ref, q_ref = inputs[7 * i : 7 * i + 7]
        gated_ref, snap_ref = scratch[2 * i : 2 * i + 2]
        size = own_ref.shape[1]
        top = heads * size
        ends = slice(top + heads, top + heads + 1)
        finals = slice(top, top + heads)
        own_end, near_end, past_end = own_ref[ends, :], near_ref[ends, :], past_ref[ends, :]
        bridged = jnp.exp(near_ref[finals, :]) * jnp.where(near_end == past_end, 1.0, 0.0)
        if kind == "pair":
            odd = (place & 1) == 1
            previous = jnp.where(odd, near_end, past_end)
            scale_near = jnp.where(odd, 1.0, 0.0)
            scale_past = jnp.where(odd, bridged, 1.0)
        else:
            previous = near_end
            scale_near = jnp.where(place > 0, 1.0, 0.0)
            scale_past = bridged
        scale_past = jnp.where(place >= 2, scale_past, 0.0)
        own_decay = jnp.exp(own_ref[finals, :]) * jnp.where(own_end == previous, 1.0, 0.0)
        valid = as_column(jnp.where(seg == previous[:, :1], 1.0, 0.0), size)
        for j in range(heads):
            rows = slice(j * size, (j + 1) * size)
            state = scale_past[j : j + 1] * past_ref[rows, :] + scale_near * near_ref[rows, :]
            snap_ref[j] = own_decay[j : j + 1] * state + own_ref[rows, :]
            high = state.astype(BF16)
            low = (state - high.astype(F32)).astype(BF16)
            both = jnp.concatenate([high, low], axis=0)
            work.append((i, j, first, heads, both, valid, (o_ref, gate_ref, decay_ref, q_ref)))
        send(snap_ref, snap_hbm.at[0, pl.ds(first, heads)])

    for number, (i, j, first, heads, both, valid, arrays) in enumerate(work):
        o_ref, gate_ref, decay_ref, q_ref = arrays
        gated_ref = scratch[2 * i]
        tokens, size = valid.shape
        columns = slice(j * size, (j + 1) * size)
        q = q_ref[:, columns]
        inter_ref[number % 4] = lax.dot_general(
            jnp.concatenate([q, q], axis=1), both, NN, preferred_element_type=F32
        )
        for start in range(0, tokens, 64):
            here = slice(start, start + 64)
            inter = inter_ref[number % 4, here, :]
            mixed = o_ref[here, columns] + inter * (decay_ref[here, columns] * valid[here])
            square = jnp.sum(mixed * mixed, axis=1, keepdims=True)
            gated = mixed * lax.rsqrt(square + size * 1e-06) * gate_ref[here, columns]
            gated_ref[here, columns] = gated.astype(BF16)
        if j % 2 == 1 or j == heads - 1:
            begin = j - j % 2
            width = (j + 1 - begin) * size
            there = pl.ds((first + begin) * size, width)
            send(gated_ref.at[:, pl.ds(begin * size, width)], gated_hbm.at[:, there])
    for copy in copies:
        copy.wait()


def finish(order, seg, total, groups, arrays, so_far, after):
    tokens, size = seg.shape[1], arrays[0].shape[1]
    vmem, anywhere = pl.BlockSpec(memory_space=pltpu.VMEM), pl.BlockSpec(memory_space=pl.ANY)
    unread = len(so_far) + len(after)
    scratch = []
    for _, many, _ in groups:
        scratch.append(pltpu.VMEM((tokens, many * size), BF16))
        scratch.append(pltpu.VMEM((many, size, size), F32))
    return pl.pallas_call(
        functools.partial(final_kernel, groups, unread),
        in_specs=[pl.BlockSpec(memory_space=pltpu.SMEM)]
        + [vmem] * (1 + len(arrays))
        + [anywhere] * unread,
        out_specs=[anywhere, anywhere],
        out_shape=[
            jax.ShapeDtypeStruct((tokens, total * size), BF16),
            jax.ShapeDtypeStruct((1, total, size, size), F32),
        ],
        scratch_shapes=scratch
        + [pltpu.VMEM((4, tokens, size), F32), pltpu.SemaphoreType.DMA((2 * total,))],
        input_output_aliases={2 + len(arrays) + i: i for i in range(len(so_far))},
        compiler_params=pltpu.CompilerParams(vmem_limit_bytes=12 * MIB),
        cost_estimate=SHORT,
        name="finish",
    )(order, seg, *arrays, *so_far, *after)


def shards(q, k, v, g, segment, decay_exponent, retention, norm_gain):
    heads = decay_exponent.shape[0]
    tokens = q.shape[0]
    count = lax.axis_size("seq")
    place = lax.axis_index("seq")
    reach = max(1, count // 4)
    far = lambda x: pltpu.with_memory_space_constraint(x, pltpu.HBM)
    q, k, v, g = far(q), far(k), far(v), far(g)
    gain = norm_gain.reshape(1, -1)
    order = jnp.where(place >= 2, 2 + (place & 1), place & 1).astype(jnp.int32).reshape(1)
    later = jnp.ones((1,), jnp.int32)
    swap = lambda x: lax.ppermute(x, "seq", [(c, c ^ 1) for c in range(count)])
    turn = lambda x: lax.ppermute(x, "seq", [(c, (c + 2) % count) for c in range(count)])
    ahead = lambda x: lax.ppermute(x, "seq", [(c, c + 2) for c in range(count - 2)])

    half = heads // 2
    even, odd = half // 2, half // 2
    chunks = [(0, half - even), (half, half - odd), (half - even, even), (heads - odd, odd)]

    def widened(x, many, shift, window):
        while window < reach:
            past = lax.ppermute(x, "seq", [(c, c + shift) for c in range(count - shift)])
            x = joined(later, x, past, many)
            shift, window = 2 * shift, 2 * window
        return x

    message, a, w, seg, k_near, v_near = first_message(
        order,
        far(segment.reshape(1, tokens)),
        far(decay_exponent.reshape(1, heads)),
        far(retention),
        k,
        v,
        heads,
        (chunks[1], chunks[0]),
    )
    k_near, v_near = k_near[::-1], v_near[::-1]
    near, past, inside = {}, {}, {}
    near[1] = swap(message)
    own = [second_message(seg, a, w, k_near[0], v_near[0], *chunks[0]), message]
    past[0] = turn(own[0])
    messages, mask, k_rest, v_rest, q_near, g_near = rest_messages(
        seg, a, w, q, k, v, g, chunks, 2
    )
    own, k_near, v_near = [*own, *messages], [*k_near, *k_rest], [*v_near, *v_rest]

    def look_inside(i, through=(), after=()):
        inside[i], copied = intra(
            mask, a, gain, q_near[i], k_near[i], v_near[i], g_near[i], *chunks[i], through, after
        )
        return copied

    def pair_last(i, after, through=()):
        message, *copied = picked(order, own[i], past[i], after, through)
        near[i] = swap(message)
        return message, *copied

    near[3] = swap(own[3])
    past[2] = turn(own[2])
    look_inside(0)
    both = joined(order, own[1], near[1], chunks[1][1], (inside[0][0],))
    message, both = pair_last(0, (), (both,))
    past[1] = turn(both)
    look_inside(1, (), (message,))
    look_inside(2, (), (inside[1][0],))
    both = joined(order, own[3], near[3], chunks[3][1], (inside[2][0],))
    message, both = pair_last(2, (), (both,))
    past[3] = ahead(both)
    look_inside(3, (), (message,))

    if reach > 2:
        for i, (_, many) in enumerate(chunks):
            past[i] = jnp.where(place >= 2, past[i], 0.0)
            if i % 2 == 0:
                near[i] = jnp.where(place >= 1, near[i], 0.0)
                near[i] = widened(joined(later, near[i], past[i], many), many, 2, 2)
                past[i] = jnp.zeros_like(near[i])
            else:
                past[i] = widened(past[i], many, 2, 2)

    result = ()
    for group in ((0, 1), (2, 3)):
        groups = [(*chunks[i], ("span", "pair")[i % 2]) for i in group]
        arrays = [x for i in group for x in (own[i], near[i], past[i], *inside[i])]
        result = finish(order, seg, heads, groups, arrays, result, (inside[3][0],))
    return tuple(result)


def solution(mesh):
    placed = (
        P(("groups", "seq"), "wt"),
        P(("groups", "seq"), "wt"),
        P(("groups", "seq"), "wt"),
        P(("groups", "seq"), "wt"),
        P(("groups", "seq")),
        P("wt"),
        P("wt", ("groups", "seq")),
        P("wt"),
    )
    return jax.shard_map(
        shards,
        mesh=mesh,
        in_specs=placed,
        out_specs=(P(("groups", "seq"), "wt"), P(("groups", "seq"), "wt", None, None)),
        check_vma=False,
    )
```

```python
import functools

import jax
import jax.numpy as jnp
from jax import lax
from jax.experimental import pallas as pl
from jax.experimental.pallas import tpu as pltpu
from jax.sharding import PartitionSpec as P

F32 = jnp.float32
BF16 = jnp.bfloat16
NN = (((1,), (0,)), ((), ()))
NT = (((1,), (1,)), ((), ()))
MIB = 1 << 20
SHORT = pl.CostEstimate(flops=1, bytes_accessed=1, transcendentals=0)


def vmem_spec(shape, index_map):
    return pl.BlockSpec(shape, index_map)


def as_column(row, lanes):
    return jnp.broadcast_to(row, (lanes, row.shape[1])).T


def meta_rows(heads):
    return -(-(heads + 1) // 8) * 8


def put_message(msg_ref, first, heads, size, w_ref, finals, end, k_ref, v_ref):
    top = heads * size
    for j in range(heads):
        columns = slice(j * size, (j + 1) * size)
        weight = w_ref[first + j : first + j + 1, :]
        keyed = (k_ref[:, columns].astype(F32).T * weight).astype(BF16)
        msg_ref[columns, :] = lax.dot_general(
            keyed, v_ref[:, columns], NN, preferred_element_type=F32
        )
    msg_ref[top : top + heads, :] = jnp.broadcast_to(finals, (heads, size))
    below = meta_rows(heads) - heads
    msg_ref[top + heads :, :] = jnp.broadcast_to(end.astype(F32), (below, size))


def first_kernel(heads, chunks, order_ref, seg_hbm, exponent_hbm, keep_hbm, k_hbm, v_hbm, *refs):
    number = len(chunks)
    (msg_ref, a_ref, w_ref, seg_ref), refs = refs[:4], refs[4:]
    k_refs, v_refs, refs = refs[:number], refs[number : 2 * number], refs[2 * number :]
    exponent_ref, keep_ref, sems = refs
    tokens = seg_ref.shape[1]
    size = msg_ref.shape[1]
    pairs = [(keep_hbm, keep_ref), (exponent_hbm, exponent_ref), (seg_hbm, seg_ref)]
    for i, (first, many) in enumerate(chunks):
        wide = pl.ds(first * size, many * size)
        pairs += [(k_hbm.at[:, wide], k_refs[i]), (v_hbm.at[:, wide], v_refs[i])]
    copies = [pltpu.make_async_copy(*pair, sems.at[i]) for i, pair in enumerate(pairs)]
    for copy in copies:
        copy.start()
    earlier = lax.broadcasted_iota(jnp.int32, (tokens, tokens), 0)
    later = lax.broadcasted_iota(jnp.int32, (tokens, tokens), 1)
    upper = jnp.where(earlier <= later, 1.0, 0.0).astype(BF16)
    across = lax.broadcasted_iota(jnp.int32, (heads, heads), 1)
    down = lax.broadcasted_iota(jnp.int32, (heads, heads), 0)
    for copy in copies[:3]:
        copy.wait()
    spread = jnp.broadcast_to(exponent_ref[...], (heads, heads))
    exponent = jnp.sum(jnp.where(across == down, spread, 0).astype(F32), axis=1, keepdims=True)
    a = -jnp.exp2(-exponent) + jnp.log(keep_ref[...])
    high = a.astype(BF16)
    rest = a - high.astype(F32)
    middle = rest.astype(BF16)
    low = (rest - middle.astype(F32)).astype(BF16)
    parts = jnp.concatenate([high, middle, low], axis=0)
    sums = lax.dot_general(parts, upper, NN, preferred_element_type=F32)
    cumulative = sums[:heads] + (sums[heads : 2 * heads] + sums[2 * heads :])
    a_ref[...] = cumulative
    final = cumulative[:, tokens - 1 :]
    seg = seg_ref[...]
    last = seg[:, tokens - 1 :]
    w_ref[...] = jnp.where(seg == last, jnp.exp(final - cumulative), 0.0)
    for copy in copies[3:5]:
        copy.wait()
    first, many = chunks[0]
    finals = final[first : first + many]
    put_message(msg_ref, first, many, size, w_ref, finals, last, k_refs[0], v_refs[0])
    for copy in copies[5:]:
        copy.wait()


def message_of(size, many):
    return pltpu.VMEM((many * size + meta_rows(many), size), F32)


def first_message(order, seg, exponent, keep, k, v, heads, chunks):
    tokens, size = k.shape[0], k.shape[1] // heads
    near = [pltpu.VMEM((tokens, many * size), BF16) for _, many in chunks]
    shapes = [message_of(size, chunks[0][1])]
    shapes += [pltpu.VMEM((heads, tokens), F32)] * 2 + [pltpu.VMEM((1, tokens), jnp.int32)]
    shapes += near + near
    number = len(chunks)
    out = pl.pallas_call(
        functools.partial(first_kernel, heads, chunks),
        in_specs=[pl.BlockSpec(memory_space=pltpu.SMEM)]
        + [pl.BlockSpec(memory_space=pltpu.HBM)] * 5,
        out_specs=[pl.BlockSpec(memory_space=pltpu.VMEM)] * len(shapes),
        out_shape=shapes,
        scratch_shapes=[
            pltpu.VMEM((1, heads), jnp.int32),
            pltpu.VMEM((heads, tokens), F32),
            pltpu.SemaphoreType.DMA((3 + 2 * number,)),
        ],
        compiler_params=pltpu.CompilerParams(vmem_limit_bytes=8 * MIB),
        cost_estimate=SHORT,
        name="first_message",
    )(order, seg, exponent, keep, k, v)
    (message, a, w, seg), out = out[:4], out[4:]
    return message, a, w, seg, out[:number], out[number:]


def second_message(seg, a, w, k, v, first, heads):
    tokens, size = k.shape[0], k.shape[1] // heads

    def kernel(seg_ref, a_ref, w_ref, k_ref, v_ref, msg_ref):
        final = a_ref[first : first + heads, tokens - 1 :]
        last = seg_ref[:, tokens - 1 :]
        put_message(msg_ref, first, heads, size, w_ref, final, last, k_ref, v_ref)

    return pl.pallas_call(
        kernel,
        in_specs=[pl.BlockSpec(memory_space=pltpu.VMEM)] * 5,
        out_specs=pl.BlockSpec(memory_space=pltpu.VMEM),
        out_shape=message_of(size, heads),
        compiler_params=pltpu.CompilerParams(vmem_limit_bytes=8 * MIB),
        cost_estimate=SHORT,
        name="second_message",
    )(seg, a, w, k, v)


def rest_kernel(chunks, done, seg_ref, a_ref, w_ref, q_hbm, k_hbm, v_hbm, g_hbm, *refs):
    tokens = seg_ref.shape[1]
    left, number = chunks[done:], len(chunks)
    messages, mask_ref, refs, sems = refs[: len(left)], refs[len(left)], refs[len(left) + 1 : -1], refs[-1]
    k_refs, refs = refs[: len(left)], refs[len(left) :]
    v_refs, refs = refs[: len(left)], refs[len(left) :]
    q_refs, g_refs = refs[:number], refs[number:]
    size = messages[0].shape[1]
    pairs = []
    for i, (first, many) in enumerate(left):
        wide = pl.ds(first * size, many * size)
        pairs += [(k_hbm.at[:, wide], k_refs[i]), (v_hbm.at[:, wide], v_refs[i])]
    for i, (first, many) in enumerate(chunks):
        wide = pl.ds(first * size, many * size)
        pairs += [(q_hbm.at[:, wide], q_refs[i]), (g_hbm.at[:, wide], g_refs[i])]
    copies = [pltpu.make_async_copy(*pair, sems.at[i]) for i, pair in enumerate(pairs)]
    for copy in copies:
        copy.start()
    make_mask(seg_ref, mask_ref)
    last = seg_ref[:, tokens - 1 :]
    for i, (first, many) in enumerate(left):
        copies[2 * i].wait()
        copies[2 * i + 1].wait()
        final = a_ref[first : first + many, tokens - 1 :]
        put_message(messages[i], first, many, size, w_ref, final, last, k_refs[i], v_refs[i])
    for copy in copies[2 * len(left) :]:
        copy.wait()


def rest_messages(seg, a, w, q, k, v, g, chunks, done):
    heads = a.shape[0]
    tokens, size = k.shape[0], k.shape[1] // heads
    near = [pltpu.VMEM((tokens, many * size), BF16) for _, many in chunks]
    shapes = [message_of(size, many) for _, many in chunks[done:]]
    shapes += [pltpu.VMEM((tokens, tokens), F32)] + near[done:] * 2 + near * 2
    left, number = len(chunks) - done, len(chunks)
    out = pl.pallas_call(
        functools.partial(rest_kernel, chunks, done),
        in_specs=[pl.BlockSpec(memory_space=pltpu.VMEM)] * 3
        + [pl.BlockSpec(memory_space=pltpu.HBM)] * 4,
        out_specs=[pl.BlockSpec(memory_space=pltpu.VMEM)] * len(shapes),
        out_shape=shapes,
        scratch_shapes=[pltpu.SemaphoreType.DMA((2 * (left + number),))],
        compiler_params=pltpu.CompilerParams(vmem_limit_bytes=8 * MIB),
        cost_estimate=SHORT,
        name="rest_messages",
    )(seg, a, w, q, k, v, g)
    messages, mask, out = out[:left], out[left], out[left + 1 :]
    k_near, v_near, out = out[:left], out[left : 2 * left], out[2 * left :]
    return messages, mask, k_near, v_near, out[:number], out[number:]


def join_kernel(heads, order_ref, mine_ref, other_ref, out_ref):
    size = mine_ref.shape[1]
    top = heads * size
    mine_later = (order_ref[0] & 1) == 1
    final_mine, final_other = mine_ref[top : top + heads, :], other_ref[top : top + heads, :]
    end_mine, end_other = mine_ref[top + heads :, :], other_ref[top + heads :, :]
    same = jnp.where(end_mine[:1] == end_other[:1], 1.0, 0.0)
    scale_mine = jnp.where(mine_later, 1.0, jnp.exp(final_other) * same)
    scale_other = jnp.where(mine_later, jnp.exp(final_mine) * same, 1.0)
    for head in range(heads):
        rows = slice(head * size, (head + 1) * size)
        out_ref[rows, :] = (
            scale_mine[head : head + 1] * mine_ref[rows, :]
            + scale_other[head : head + 1] * other_ref[rows, :]
        )
    out_ref[top : top + heads, :] = final_mine + final_other
    out_ref[top + heads :, :] = jnp.where(mine_later, end_mine, end_other)


def small_call(kernel, name, order, arrays, after):
    vmem = pl.BlockSpec(memory_space=pltpu.VMEM)
    return pl.pallas_call(
        lambda *refs: kernel(*refs[: 1 + len(arrays)], refs[-1]),
        in_specs=[pl.BlockSpec(memory_space=pltpu.SMEM)]
        + [vmem] * len(arrays)
        + [pl.BlockSpec(memory_space=pl.ANY)] * len(after),
        out_specs=vmem,
        out_shape=pltpu.VMEM(arrays[0].shape, F32),
        compiler_params=pltpu.CompilerParams(vmem_limit_bytes=8 * MIB),
        cost_estimate=SHORT,
        name=name,
    )(order, *arrays, *after)


def joined(order, mine, other, heads, after=()):
    return small_call(
        functools.partial(join_kernel, heads), "join_windows", order, (mine, other), after
    )


def picked(order, even, odd, after=(), through=()):
    vmem = pl.BlockSpec(memory_space=pltpu.VMEM)

    def kernel(order_ref, even_ref, odd_ref, *refs):
        outs = refs[len(through) + len(after) :]
        for source, target in zip(refs, outs[1:]):
            target[...] = source[...]
        odd = (order_ref[0] & 1) == 1

        @pl.when(odd)
        def _():
            outs[0][...] = odd_ref[...]

        @pl.when(jnp.logical_not(odd))
        def _():
            outs[0][...] = even_ref[...]

    return pl.pallas_call(
        kernel,
        in_specs=[pl.BlockSpec(memory_space=pltpu.SMEM)]
        + [vmem] * (2 + len(through))
        + [pl.BlockSpec(memory_space=pl.ANY)] * len(after),
        out_specs=[vmem] * (1 + len(through)),
        out_shape=[pltpu.VMEM(x.shape, F32) for x in (even, *through)],
        compiler_params=pltpu.CompilerParams(vmem_limit_bytes=8 * MIB),
        cost_estimate=SHORT,
        name="pick_message",
    )(order, even, odd, *through, *after)


def make_mask(seg_ref, mask_ref):
    tokens = seg_ref.shape[1]
    seg = seg_ref[...].astype(F32)
    column = as_column(seg, 128)
    for start in range(0, tokens, 128):
        across = lax.broadcasted_iota(jnp.int32, (tokens, 128), 1) + start
        down = lax.broadcasted_iota(jnp.int32, (tokens, 128), 0)
        seen = (column == seg[:, start : start + 128]) & (across <= down)
        mask_ref[:, start : start + 128] = jnp.where(seen, 0.0, -1e30)


def intra_kernel(
    first, heads, through, after, mask_ref, a_ref, gain_ref, q_ref, k_ref, v_ref, g_ref, *refs
):
    o_ref, gate_ref, decay_ref, *copied = refs[through + after :]
    for source, target in zip(refs[:through], copied):
        target[...] = source[...]
    tokens = mask_ref.shape[0]
    size = q_ref.shape[1] // heads
    block = min(tokens, 256)
    for j in range(heads):
        columns = slice(j * size, (j + 1) * size)
        a_row = a_ref[first + j : first + j + 1, :] * 1.4426950408889634
        a_column = as_column(a_row, 128)
        decay_ref[:, columns] = jnp.exp2(a_column)
        for start in range(0, tokens, block):
            here, upto = slice(start, start + block), slice(0, start + block)
            scores = lax.dot_general(
                q_ref[here, columns], k_ref[upto, columns], NT, preferred_element_type=F32
            )
            spread = jnp.concatenate([a_column[here]] * ((start + block) // 128), axis=1)
            weight = jnp.exp2(spread - a_row[:, upto] + mask_ref[here, upto])
            probs = (scores * weight).astype(BF16)
            o_ref[here, columns] = lax.dot_general(
                probs, v_ref[upto, columns], NN, preferred_element_type=F32
            )
        half = 0.5 * size**0.5 * gain_ref[:, (first + j) * size : (first + j + 1) * size]
        gate_ref[:, columns] = half + half * jnp.tanh(0.5 * g_ref[:, columns].astype(F32))


def intra(mask, a, gain, q, k, v, g, first, heads, through=(), after=()):
    tokens, size = mask.shape[0], gain.shape[1] // a.shape[0]
    vmem = pl.BlockSpec(memory_space=pltpu.VMEM)
    o, gate, decay, *copied = pl.pallas_call(
        functools.partial(intra_kernel, first, heads, len(through), len(after)),
        in_specs=[vmem] * (7 + len(through)) + [pl.BlockSpec(memory_space=pl.ANY)] * len(after),
        out_specs=[vmem] * (3 + len(through)),
        out_shape=[pltpu.VMEM((tokens, heads * size), F32)] * 3
        + [pltpu.VMEM(x.shape, x.dtype) for x in through],
        compiler_params=pltpu.CompilerParams(vmem_limit_bytes=8 * MIB),
        cost_estimate=SHORT,
        name="intra_span",
    )(mask, a, gain, q, k, v, g, *through, *after)
    return (o, gate, decay, q), copied


def final_kernel(groups, unread, order_ref, seg_ref, *rest):
    number = len(groups)
    inputs, rest = rest[: 7 * number], rest[7 * number + unread :]
    gated_hbm, snap_hbm, *scratch, inter_ref, sems = rest
    place = order_ref[0]
    seg = seg_ref[...].astype(F32)
    copies, work = [], []

    def send(source, target):
        copies.append(pltpu.make_async_copy(source, target, sems.at[len(copies)]))
        copies[-1].start()

    for i, (first, heads, kind) in enumerate(groups):
        own_ref, near_ref, past_ref = inputs[7 * i : 7 * i + 3]
        gated_ref, snap_ref = scratch[2 * i : 2 * i + 2]
        size = own_ref.shape[1]
        top = heads * size
        ends = slice(top + heads, top + heads + 1)
        finals = slice(top, top + heads)
        own_end, near_end, past_end = own_ref[ends, :], near_ref[ends, :], past_ref[ends, :]
        bridged = jnp.exp(near_ref[finals, :]) * jnp.where(near_end == past_end, 1.0, 0.0)
        if kind == "pair":
            odd = (place & 1) == 1
            previous = jnp.where(odd, near_end, past_end)
            scale_near = jnp.where(odd, 1.0, 0.0)
            scale_past = jnp.where(odd, bridged, 1.0)
        else:
            previous = near_end
            scale_near = jnp.where(place > 0, 1.0, 0.0)
            scale_past = bridged
        scale_past = jnp.where(place >= 2, scale_past, 0.0)
        own_decay = jnp.exp(own_ref[finals, :]) * jnp.where(own_end == previous, 1.0, 0.0)
        number_valid = jnp.sum(
            jnp.where(seg == previous[:, :1], 1.0, 0.0), axis=1, keepdims=True
        )
        for j in range(heads):
            rows = slice(j * size, (j + 1) * size)
            state = scale_past[j : j + 1] * past_ref[rows, :] + scale_near * near_ref[rows, :]
            snap_ref[j] = own_decay[j : j + 1] * state + own_ref[rows, :]
            high = state.astype(BF16)
            low = (state - high.astype(F32)).astype(BF16)
            both = jnp.concatenate([high, low], axis=0)
            work.append((i, j, first, heads, both, number_valid, inputs[7 * i + 3 : 7 * i + 7]))
        send(snap_ref, snap_hbm.at[0, pl.ds(first, heads)])

    rows = lax.broadcasted_iota(jnp.int32, (64, 128), 0).astype(F32)
    for number, (i, j, first, heads, both, number_valid, arrays) in enumerate(work):
        o_ref, gate_ref, decay_ref, q_ref = arrays
        gated_ref = scratch[2 * i]
        tokens, size = seg.shape[1], q_ref.shape[1] // heads
        columns = slice(j * size, (j + 1) * size)
        q = q_ref[:, columns]
        inter_ref[number % 4] = lax.dot_general(
            jnp.concatenate([q, q], axis=1), both, NN, preferred_element_type=F32
        )
        for start in range(0, tokens, 64):
            here = slice(start, start + 64)
            inter = inter_ref[number % 4, here, :]
            inter = jnp.where(rows < number_valid - start, inter * decay_ref[here, columns], 0.0)
            mixed = o_ref[here, columns] + inter
            square = jnp.sum(mixed * mixed, axis=1, keepdims=True)
            gated = mixed * lax.rsqrt(square + size * 1e-06) * gate_ref[here, columns]
            gated_ref[here, columns] = gated.astype(BF16)
        if j % 2 == 1 or j == heads - 1:
            begin = j - j % 2
            width = (j + 1 - begin) * size
            there = pl.ds((first + begin) * size, width)
            send(gated_ref.at[:, pl.ds(begin * size, width)], gated_hbm.at[:, there])
    for copy in copies:
        copy.wait()


def finish(order, seg, total, groups, arrays, so_far, after):
    tokens, size = seg.shape[1], arrays[0].shape[1]
    vmem, anywhere = pl.BlockSpec(memory_space=pltpu.VMEM), pl.BlockSpec(memory_space=pl.ANY)
    unread = len(so_far) + len(after)
    scratch = []
    for _, many, _ in groups:
        scratch.append(pltpu.VMEM((tokens, many * size), BF16))
        scratch.append(pltpu.VMEM((many, size, size), F32))
    return pl.pallas_call(
        functools.partial(final_kernel, groups, unread),
        in_specs=[pl.BlockSpec(memory_space=pltpu.SMEM)]
        + [vmem] * (1 + len(arrays))
        + [anywhere] * unread,
        out_specs=[anywhere, anywhere],
        out_shape=[
            jax.ShapeDtypeStruct((tokens, total * size), BF16),
            jax.ShapeDtypeStruct((1, total, size, size), F32),
        ],
        scratch_shapes=scratch
        + [pltpu.VMEM((4, tokens, size), F32), pltpu.SemaphoreType.DMA((2 * total,))],
        input_output_aliases={2 + len(arrays) + i: i for i in range(len(so_far))},
        compiler_params=pltpu.CompilerParams(vmem_limit_bytes=12 * MIB),
        cost_estimate=SHORT,
        name="finish",
    )(order, seg, *arrays, *so_far, *after)


def shards(q, k, v, g, segment, decay_exponent, retention, norm_gain):
    heads = decay_exponent.shape[0]
    tokens = q.shape[0]
    count = lax.axis_size("seq")
    place = lax.axis_index("seq")
    reach = max(1, count // 4)
    far = lambda x: pltpu.with_memory_space_constraint(x, pltpu.HBM)
    q, k, v, g = far(q), far(k), far(v), far(g)
    gain = norm_gain.reshape(1, -1)
    order = jnp.where(place >= 2, 2 + (place & 1), place & 1).astype(jnp.int32).reshape(1)
    later = jnp.ones((1,), jnp.int32)
    swap = lambda x: lax.ppermute(x, "seq", [(c, c ^ 1) for c in range(count)])
    turn = lambda x: lax.ppermute(x, "seq", [(c, (c + 2) % count) for c in range(count)])
    ahead = lambda x: lax.ppermute(x, "seq", [(c, c + 2) for c in range(count - 2)])

    half = heads // 2
    even, odd = half // 2, half // 2
    chunks = [(0, half - even), (half, half - odd), (half - even, even), (heads - odd, odd)]

    def widened(x, many, shift, window):
        while window < reach:
            past = lax.ppermute(x, "seq", [(c, c + shift) for c in range(count - shift)])
            x = joined(later, x, past, many)
            shift, window = 2 * shift, 2 * window
        return x

    message, a, w, seg, k_near, v_near = first_message(
        order,
        far(segment.reshape(1, tokens)),
        far(decay_exponent.reshape(1, heads)),
        far(retention),
        k,
        v,
        heads,
        (chunks[1], chunks[0]),
    )
    k_near, v_near = k_near[::-1], v_near[::-1]
    near, past, inside = {}, {}, {}
    near[1] = swap(message)
    own = [second_message(seg, a, w, k_near[0], v_near[0], *chunks[0]), message]
    past[0] = turn(own[0])
    messages, mask, k_rest, v_rest, q_near, g_near = rest_messages(
        seg, a, w, q, k, v, g, chunks, 2
    )
    own, k_near, v_near = [*own, *messages], [*k_near, *k_rest], [*v_near, *v_rest]

    def look_inside(i, through=(), after=()):
        inside[i], copied = intra(
            mask, a, gain, q_near[i], k_near[i], v_near[i], g_near[i], *chunks[i], through, after
        )
        return copied

    def pair_last(i, after, through=()):
        message, *copied = picked(order, own[i], past[i], after, through)
        near[i] = swap(message)
        return message, *copied

    near[3] = swap(own[3])
    past[2] = turn(own[2])
    look_inside(0)
    both = joined(order, own[1], near[1], chunks[1][1], (inside[0][0],))
    message, both = pair_last(0, (), (both,))
    past[1] = turn(both)
    look_inside(1, (), (message,))
    both = joined(order, own[3], near[3], chunks[3][1], (inside[1][0],))
    past[3] = ahead(both)
    (message,) = pair_last(2, (both,))
    look_inside(2, (), (message,))
    look_inside(3, (), (inside[2][0],))

    if reach > 2:
        for i, (_, many) in enumerate(chunks):
            past[i] = jnp.where(place >= 2, past[i], 0.0)
            if i % 2 == 0:
                near[i] = jnp.where(place >= 1, near[i], 0.0)
                near[i] = widened(joined(later, near[i], past[i], many), many, 2, 2)
                past[i] = jnp.zeros_like(near[i])
            else:
                past[i] = widened(past[i], many, 2, 2)

    result = ()
    for group in ((0, 1), (3, 2)):
        groups = [(*chunks[i], ("span", "pair")[i % 2]) for i in group]
        arrays = [x for i in group for x in (own[i], near[i], past[i], *inside[i])]
        result = finish(order, seg, heads, groups, arrays, result, (inside[3][0],))
    return tuple(result)


def solution(mesh):
    placed = (
        P(("groups", "seq"), "wt"),
        P(("groups", "seq"), "wt"),
        P(("groups", "seq"), "wt"),
        P(("groups", "seq"), "wt"),
        P(("groups", "seq")),
        P("wt"),
        P("wt", ("groups", "seq")),
        P("wt"),
    )
    return jax.shard_map(
        shards,
        mesh=mesh,
        in_specs=placed,
        out_specs=(P(("groups", "seq"), "wt"), P(("groups", "seq"), "wt", None, None)),
        check_vma=False,
    )
```

```python
import functools

import jax
import jax.numpy as jnp
from jax import lax
from jax.experimental import pallas as pl
from jax.experimental.pallas import tpu as pltpu
from jax.sharding import PartitionSpec as P

F32 = jnp.float32
BF16 = jnp.bfloat16
NN = (((1,), (0,)), ((), ()))
NT = (((1,), (1,)), ((), ()))
MIB = 1 << 20
SHORT = pl.CostEstimate(flops=1, bytes_accessed=1, transcendentals=0)


def vmem_spec(shape, index_map):
    return pl.BlockSpec(shape, index_map)


def as_column(row, lanes):
    return jnp.broadcast_to(row, (lanes, row.shape[1])).T


def meta_rows(heads):
    return -(-(heads + 1) // 8) * 8


def put_message(msg_ref, first, heads, size, w_ref, finals, end, k_ref, v_ref):
    top = heads * size
    for j in range(heads):
        columns = slice(j * size, (j + 1) * size)
        weight = w_ref[first + j : first + j + 1, :]
        keyed = (k_ref[:, columns].astype(F32).T * weight).astype(BF16)
        msg_ref[columns, :] = lax.dot_general(
            keyed, v_ref[:, columns], NN, preferred_element_type=F32
        )
    msg_ref[top : top + heads, :] = jnp.broadcast_to(finals, (heads, size))
    below = meta_rows(heads) - heads
    msg_ref[top + heads :, :] = jnp.broadcast_to(end.astype(F32), (below, size))


def first_kernel(heads, chunks, order_ref, seg_hbm, exponent_hbm, keep_hbm, k_hbm, v_hbm, *refs):
    number = len(chunks)
    (msg_ref, a_ref, w_ref, seg_ref), refs = refs[:4], refs[4:]
    k_refs, v_refs, refs = refs[:number], refs[number : 2 * number], refs[2 * number :]
    exponent_ref, keep_ref, sems = refs
    tokens = seg_ref.shape[1]
    size = msg_ref.shape[1]
    pairs = [(keep_hbm, keep_ref), (exponent_hbm, exponent_ref), (seg_hbm, seg_ref)]
    for i, (first, many) in enumerate(chunks):
        wide = pl.ds(first * size, many * size)
        pairs += [(k_hbm.at[:, wide], k_refs[i]), (v_hbm.at[:, wide], v_refs[i])]
    copies = [pltpu.make_async_copy(*pair, sems.at[i]) for i, pair in enumerate(pairs)]
    for copy in copies:
        copy.start()
    part = min(tokens, 256)
    earlier = lax.broadcasted_iota(jnp.int32, (part, part), 0)
    later = lax.broadcasted_iota(jnp.int32, (part, part), 1)
    upper = jnp.where(earlier <= later, 1.0, 0.0).astype(BF16)
    across = lax.broadcasted_iota(jnp.int32, (heads, heads), 1)
    down = lax.broadcasted_iota(jnp.int32, (heads, heads), 0)
    for copy in copies[:5]:
        copy.wait()
    spread = jnp.broadcast_to(exponent_ref[...], (heads, heads))
    exponent = jnp.sum(jnp.where(across == down, spread, 0).astype(F32), axis=1, keepdims=True)
    a = -jnp.exp2(-exponent) + jnp.log(keep_ref[...])
    a = jnp.concatenate([a[:, i : i + part] for i in range(0, tokens, part)], axis=0)
    high = a.astype(BF16)
    rest = a - high.astype(F32)
    middle = rest.astype(BF16)
    low = (rest - middle.astype(F32)).astype(BF16)
    pieces = jnp.concatenate([high, middle, low], axis=0)
    sums = lax.dot_general(pieces, upper, NN, preferred_element_type=F32)
    rows = a.shape[0]
    sums = sums[:rows] + (sums[rows : 2 * rows] + sums[2 * rows :])
    parts = [sums[i : i + heads] for i in range(0, rows, heads)]
    for i in range(1, len(parts)):
        parts[i] = parts[i] + parts[i - 1][:, part - 1 :]
    cumulative = jnp.concatenate(parts, axis=1)
    a_ref[...] = cumulative
    final = cumulative[:, tokens - 1 :]
    seg = seg_ref[...]
    last = seg[:, tokens - 1 :]
    w_ref[...] = jnp.where(seg == last, jnp.exp(final - cumulative), 0.0)
    first, many = chunks[0]
    finals = final[first : first + many]
    put_message(msg_ref, first, many, size, w_ref, finals, last, k_refs[0], v_refs[0])
    for copy in copies[5:]:
        copy.wait()


def message_of(size, many):
    return pltpu.VMEM((many * size + meta_rows(many), size), F32)


def first_message(order, seg, exponent, keep, k, v, heads, chunks):
    tokens, size = k.shape[0], k.shape[1] // heads
    near = [pltpu.VMEM((tokens, many * size), BF16) for _, many in chunks]
    shapes = [message_of(size, chunks[0][1])]
    shapes += [pltpu.VMEM((heads, tokens), F32)] * 2 + [pltpu.VMEM((1, tokens), jnp.int32)]
    shapes += near + near
    number = len(chunks)
    out = pl.pallas_call(
        functools.partial(first_kernel, heads, chunks),
        in_specs=[pl.BlockSpec(memory_space=pltpu.SMEM)]
        + [pl.BlockSpec(memory_space=pltpu.HBM)] * 5,
        out_specs=[pl.BlockSpec(memory_space=pltpu.VMEM)] * len(shapes),
        out_shape=shapes,
        scratch_shapes=[
            pltpu.VMEM((1, heads), jnp.int32),
            pltpu.VMEM((heads, tokens), F32),
            pltpu.SemaphoreType.DMA((3 + 2 * number,)),
        ],
        compiler_params=pltpu.CompilerParams(vmem_limit_bytes=8 * MIB),
        cost_estimate=SHORT,
        name="first_message",
    )(order, seg, exponent, keep, k, v)
    (message, a, w, seg), out = out[:4], out[4:]
    return message, a, w, seg, out[:number], out[number:]


def second_message(seg, a, w, k, v, first, heads):
    tokens, size = k.shape[0], k.shape[1] // heads

    def kernel(seg_ref, a_ref, w_ref, k_ref, v_ref, msg_ref):
        final = a_ref[first : first + heads, tokens - 1 :]
        last = seg_ref[:, tokens - 1 :]
        put_message(msg_ref, first, heads, size, w_ref, final, last, k_ref, v_ref)

    return pl.pallas_call(
        kernel,
        in_specs=[pl.BlockSpec(memory_space=pltpu.VMEM)] * 5,
        out_specs=pl.BlockSpec(memory_space=pltpu.VMEM),
        out_shape=message_of(size, heads),
        compiler_params=pltpu.CompilerParams(vmem_limit_bytes=8 * MIB),
        cost_estimate=SHORT,
        name="second_message",
    )(seg, a, w, k, v)


def rest_kernel(chunks, done, seg_ref, a_ref, w_ref, q_hbm, k_hbm, v_hbm, g_hbm, *refs):
    tokens = seg_ref.shape[1]
    left, number = chunks[done:], len(chunks)
    messages, mask_ref, refs, sems = refs[: len(left)], refs[len(left)], refs[len(left) + 1 : -1], refs[-1]
    k_refs, refs = refs[: len(left)], refs[len(left) :]
    v_refs, refs = refs[: len(left)], refs[len(left) :]
    q_refs, g_refs = refs[:number], refs[number:]
    size = messages[0].shape[1]
    pairs = []
    for i, (first, many) in enumerate(left):
        wide = pl.ds(first * size, many * size)
        pairs += [(k_hbm.at[:, wide], k_refs[i]), (v_hbm.at[:, wide], v_refs[i])]
    for i, (first, many) in enumerate(chunks):
        wide = pl.ds(first * size, many * size)
        pairs += [(q_hbm.at[:, wide], q_refs[i]), (g_hbm.at[:, wide], g_refs[i])]
    copies = [pltpu.make_async_copy(*pair, sems.at[i]) for i, pair in enumerate(pairs)]
    for copy in copies:
        copy.start()
    make_mask(seg_ref, mask_ref)
    last = seg_ref[:, tokens - 1 :]
    for i, (first, many) in enumerate(left):
        copies[2 * i].wait()
        copies[2 * i + 1].wait()
        final = a_ref[first : first + many, tokens - 1 :]
        put_message(messages[i], first, many, size, w_ref, final, last, k_refs[i], v_refs[i])
    for copy in copies[2 * len(left) :]:
        copy.wait()


def rest_messages(seg, a, w, q, k, v, g, chunks, done):
    heads = a.shape[0]
    tokens, size = k.shape[0], k.shape[1] // heads
    near = [pltpu.VMEM((tokens, many * size), BF16) for _, many in chunks]
    shapes = [message_of(size, many) for _, many in chunks[done:]]
    shapes += [pltpu.VMEM((tokens, tokens), F32)] + near[done:] * 2 + near * 2
    left, number = len(chunks) - done, len(chunks)
    out = pl.pallas_call(
        functools.partial(rest_kernel, chunks, done),
        in_specs=[pl.BlockSpec(memory_space=pltpu.VMEM)] * 3
        + [pl.BlockSpec(memory_space=pltpu.HBM)] * 4,
        out_specs=[pl.BlockSpec(memory_space=pltpu.VMEM)] * len(shapes),
        out_shape=shapes,
        scratch_shapes=[pltpu.SemaphoreType.DMA((2 * (left + number),))],
        compiler_params=pltpu.CompilerParams(vmem_limit_bytes=8 * MIB),
        cost_estimate=SHORT,
        name="rest_messages",
    )(seg, a, w, q, k, v, g)
    messages, mask, out = out[:left], out[left], out[left + 1 :]
    k_near, v_near, out = out[:left], out[left : 2 * left], out[2 * left :]
    return messages, mask, k_near, v_near, out[:number], out[number:]


def join_kernel(heads, order_ref, mine_ref, other_ref, out_ref):
    size = mine_ref.shape[1]
    top = heads * size
    mine_later = (order_ref[0] & 1) == 1
    final_mine, final_other = mine_ref[top : top + heads, :], other_ref[top : top + heads, :]
    end_mine, end_other = mine_ref[top + heads :, :], other_ref[top + heads :, :]
    same = jnp.where(end_mine[:1] == end_other[:1], 1.0, 0.0)
    scale_mine = jnp.where(mine_later, 1.0, jnp.exp(final_other) * same)
    scale_other = jnp.where(mine_later, jnp.exp(final_mine) * same, 1.0)
    for head in range(heads):
        rows = slice(head * size, (head + 1) * size)
        out_ref[rows, :] = (
            scale_mine[head : head + 1] * mine_ref[rows, :]
            + scale_other[head : head + 1] * other_ref[rows, :]
        )
    out_ref[top : top + heads, :] = final_mine + final_other
    out_ref[top + heads :, :] = jnp.where(mine_later, end_mine, end_other)


def small_call(kernel, name, order, arrays, after):
    vmem = pl.BlockSpec(memory_space=pltpu.VMEM)
    return pl.pallas_call(
        lambda *refs: kernel(*refs[: 1 + len(arrays)], refs[-1]),
        in_specs=[pl.BlockSpec(memory_space=pltpu.SMEM)]
        + [vmem] * len(arrays)
        + [pl.BlockSpec(memory_space=pl.ANY)] * len(after),
        out_specs=vmem,
        out_shape=pltpu.VMEM(arrays[0].shape, F32),
        compiler_params=pltpu.CompilerParams(vmem_limit_bytes=8 * MIB),
        cost_estimate=SHORT,
        name=name,
    )(order, *arrays, *after)


def joined(order, mine, other, heads, after=()):
    return small_call(
        functools.partial(join_kernel, heads), "join_windows", order, (mine, other), after
    )


def picked(order, even, odd, after=(), through=()):
    vmem = pl.BlockSpec(memory_space=pltpu.VMEM)

    def kernel(order_ref, even_ref, odd_ref, *refs):
        outs = refs[len(through) + len(after) :]
        for source, target in zip(refs, outs[1:]):
            target[...] = source[...]
        odd = (order_ref[0] & 1) == 1

        @pl.when(odd)
        def _():
            outs[0][...] = odd_ref[...]

        @pl.when(jnp.logical_not(odd))
        def _():
            outs[0][...] = even_ref[...]

    return pl.pallas_call(
        kernel,
        in_specs=[pl.BlockSpec(memory_space=pltpu.SMEM)]
        + [vmem] * (2 + len(through))
        + [pl.BlockSpec(memory_space=pl.ANY)] * len(after),
        out_specs=[vmem] * (1 + len(through)),
        out_shape=[pltpu.VMEM(x.shape, F32) for x in (even, *through)],
        compiler_params=pltpu.CompilerParams(vmem_limit_bytes=8 * MIB),
        cost_estimate=SHORT,
        name="pick_message",
    )(order, even, odd, *through, *after)


def make_mask(seg_ref, mask_ref):
    tokens = seg_ref.shape[1]
    seg = seg_ref[...].astype(F32)
    column = as_column(seg, 128)
    for start in range(0, tokens, 128):
        across = lax.broadcasted_iota(jnp.int32, (tokens, 128), 1) + start
        down = lax.broadcasted_iota(jnp.int32, (tokens, 128), 0)
        seen = (column == seg[:, start : start + 128]) & (across <= down)
        mask_ref[:, start : start + 128] = jnp.where(seen, 0.0, -1e30)


def intra_kernel(
    first, heads, through, after, mask_ref, a_ref, gain_ref, q_ref, k_ref, v_ref, g_ref, *refs
):
    o_ref, gate_ref, decay_ref, *copied = refs[through + after :]
    for source, target in zip(refs[:through], copied):
        target[...] = source[...]
    tokens = mask_ref.shape[0]
    size = q_ref.shape[1] // heads
    block = min(tokens, 256)
    for j in range(heads):
        columns = slice(j * size, (j + 1) * size)
        a_row = a_ref[first + j : first + j + 1, :] * 1.4426950408889634
        a_column = as_column(a_row, 128)
        decay_ref[:, columns] = jnp.exp2(a_column)
        for start in range(0, tokens, block):
            here, upto = slice(start, start + block), slice(0, start + block)
            scores = lax.dot_general(
                q_ref[here, columns], k_ref[upto, columns], NT, preferred_element_type=F32
            )
            spread = jnp.concatenate([a_column[here]] * ((start + block) // 128), axis=1)
            weight = jnp.exp2(spread - a_row[:, upto] + mask_ref[here, upto])
            probs = (scores * weight).astype(BF16)
            o_ref[here, columns] = lax.dot_general(
                probs, v_ref[upto, columns], NN, preferred_element_type=F32
            )
        half = 0.5 * size**0.5 * gain_ref[:, (first + j) * size : (first + j + 1) * size]
        gate_ref[:, columns] = half + half * jnp.tanh(0.5 * g_ref[:, columns].astype(F32))


def intra(mask, a, gain, q, k, v, g, first, heads, through=(), after=()):
    tokens, size = mask.shape[0], gain.shape[1] // a.shape[0]
    vmem = pl.BlockSpec(memory_space=pltpu.VMEM)
    o, gate, decay, *copied = pl.pallas_call(
        functools.partial(intra_kernel, first, heads, len(through), len(after)),
        in_specs=[vmem] * (7 + len(through)) + [pl.BlockSpec(memory_space=pl.ANY)] * len(after),
        out_specs=[vmem] * (3 + len(through)),
        out_shape=[pltpu.VMEM((tokens, heads * size), F32)] * 3
        + [pltpu.VMEM(x.shape, x.dtype) for x in through],
        compiler_params=pltpu.CompilerParams(vmem_limit_bytes=8 * MIB),
        cost_estimate=SHORT,
        name="intra_span",
    )(mask, a, gain, q, k, v, g, *through, *after)
    return (o, gate, decay, q), copied


def final_kernel(groups, unread, order_ref, seg_ref, *rest):
    number = len(groups)
    inputs, rest = rest[: 7 * number], rest[7 * number + unread :]
    gated_hbm, snap_hbm, *scratch, inter_ref, sems = rest
    place = order_ref[0]
    seg = seg_ref[...].astype(F32)
    copies, work = [], []

    def send(source, target):
        copies.append(pltpu.make_async_copy(source, target, sems.at[len(copies)]))
        copies[-1].start()

    for i, (first, heads, kind) in enumerate(groups):
        own_ref, near_ref, past_ref = inputs[7 * i : 7 * i + 3]
        gated_ref, snap_ref = scratch[2 * i : 2 * i + 2]
        size = own_ref.shape[1]
        top = heads * size
        ends = slice(top + heads, top + heads + 1)
        finals = slice(top, top + heads)
        own_end, near_end, past_end = own_ref[ends, :], near_ref[ends, :], past_ref[ends, :]
        bridged = jnp.exp(near_ref[finals, :]) * jnp.where(near_end == past_end, 1.0, 0.0)
        if kind == "pair":
            odd = (place & 1) == 1
            previous = jnp.where(odd, near_end, past_end)
            scale_near = jnp.where(odd, 1.0, 0.0)
            scale_past = jnp.where(odd, bridged, 1.0)
        else:
            previous = near_end
            scale_near = jnp.where(place > 0, 1.0, 0.0)
            scale_past = bridged
        scale_past = jnp.where(place >= 2, scale_past, 0.0)
        own_decay = jnp.exp(own_ref[finals, :]) * jnp.where(own_end == previous, 1.0, 0.0)
        number_valid = jnp.sum(
            jnp.where(seg == previous[:, :1], 1.0, 0.0), axis=1, keepdims=True
        )
        for j in range(heads):
            rows = slice(j * size, (j + 1) * size)
            state = scale_past[j : j + 1] * past_ref[rows, :] + scale_near * near_ref[rows, :]
            snap_ref[j] = own_decay[j : j + 1] * state + own_ref[rows, :]
            high = state.astype(BF16)
            low = (state - high.astype(F32)).astype(BF16)
            both = jnp.concatenate([high, low], axis=0)
            work.append((i, j, first, heads, both, number_valid, inputs[7 * i + 3 : 7 * i + 7]))
        send(snap_ref, snap_hbm.at[0, pl.ds(first, heads)])

    rows = lax.broadcasted_iota(jnp.int32, (64, 128), 0).astype(F32)
    for number, (i, j, first, heads, both, number_valid, arrays) in enumerate(work):
        o_ref, gate_ref, decay_ref, q_ref = arrays
        gated_ref = scratch[2 * i]
        tokens, size = seg.shape[1], q_ref.shape[1] // heads
        columns = slice(j * size, (j + 1) * size)
        q = q_ref[:, columns]
        inter_ref[number % 4] = lax.dot_general(
            jnp.concatenate([q, q], axis=1), both, NN, preferred_element_type=F32
        )
        for start in range(0, tokens, 64):
            here = slice(start, start + 64)
            inter = inter_ref[number % 4, here, :]
            inter = jnp.where(rows < number_valid - start, inter * decay_ref[here, columns], 0.0)
            mixed = o_ref[here, columns] + inter
            square = jnp.sum(mixed * mixed, axis=1, keepdims=True)
            gated = mixed * lax.rsqrt(square + size * 1e-06) * gate_ref[here, columns]
            gated_ref[here, columns] = gated.astype(BF16)
        alone = number + 2 >= len(work)
        if alone or j % 2 == 1 or j == heads - 1:
            begin = j if alone else j - j % 2
            width = (j + 1 - begin) * size
            there = pl.ds((first + begin) * size, width)
            send(gated_ref.at[:, pl.ds(begin * size, width)], gated_hbm.at[:, there])
    for copy in copies:
        copy.wait()


def finish(order, seg, total, groups, arrays, so_far, after):
    tokens, size = seg.shape[1], arrays[0].shape[1]
    vmem, anywhere = pl.BlockSpec(memory_space=pltpu.VMEM), pl.BlockSpec(memory_space=pl.ANY)
    unread = len(so_far) + len(after)
    scratch = []
    for _, many, _ in groups:
        scratch.append(pltpu.VMEM((tokens, many * size), BF16))
        scratch.append(pltpu.VMEM((many, size, size), F32))
    return pl.pallas_call(
        functools.partial(final_kernel, groups, unread),
        in_specs=[pl.BlockSpec(memory_space=pltpu.SMEM)]
        + [vmem] * (1 + len(arrays))
        + [anywhere] * unread,
        out_specs=[anywhere, anywhere],
        out_shape=[
            jax.ShapeDtypeStruct((tokens, total * size), BF16),
            jax.ShapeDtypeStruct((1, total, size, size), F32),
        ],
        scratch_shapes=scratch
        + [pltpu.VMEM((4, tokens, size), F32), pltpu.SemaphoreType.DMA((2 * total,))],
        input_output_aliases={2 + len(arrays) + i: i for i in range(len(so_far))},
        compiler_params=pltpu.CompilerParams(vmem_limit_bytes=12 * MIB),
        cost_estimate=SHORT,
        name="finish",
    )(order, seg, *arrays, *so_far, *after)


def shards(q, k, v, g, segment, decay_exponent, retention, norm_gain):
    heads = decay_exponent.shape[0]
    tokens = q.shape[0]
    count = lax.axis_size("seq")
    place = lax.axis_index("seq")
    reach = max(1, count // 4)
    far = lambda x: pltpu.with_memory_space_constraint(x, pltpu.HBM)
    q, k, v, g = far(q), far(k), far(v), far(g)
    gain = norm_gain.reshape(1, -1)
    order = jnp.where(place >= 2, 2 + (place & 1), place & 1).astype(jnp.int32).reshape(1)
    later = jnp.ones((1,), jnp.int32)
    swap = lambda x: lax.ppermute(x, "seq", [(c, c ^ 1) for c in range(count)])
    turn = lambda x: lax.ppermute(x, "seq", [(c, (c + 2) % count) for c in range(count)])
    ahead = lambda x: lax.ppermute(x, "seq", [(c, c + 2) for c in range(count - 2)])

    half = heads // 2
    even, odd = half // 2, half // 2
    chunks = [(0, half - even), (half, half - odd), (half - even, even), (heads - odd, odd)]

    def widened(x, many, shift, window):
        while window < reach:
            past = lax.ppermute(x, "seq", [(c, c + shift) for c in range(count - shift)])
            x = joined(later, x, past, many)
            shift, window = 2 * shift, 2 * window
        return x

    message, a, w, seg, k_near, v_near = first_message(
        order,
        far(segment.reshape(1, tokens)),
        far(decay_exponent.reshape(1, heads)),
        far(retention),
        k,
        v,
        heads,
        (chunks[1], chunks[0]),
    )
    k_near, v_near = k_near[::-1], v_near[::-1]
    near, past, inside = {}, {}, {}
    near[1] = swap(message)
    own = [second_message(seg, a, w, k_near[0], v_near[0], *chunks[0]), message]
    past[0] = turn(own[0])
    messages, mask, k_rest, v_rest, q_near, g_near = rest_messages(
        seg, a, w, q, k, v, g, chunks, 2
    )
    own, k_near, v_near = [*own, *messages], [*k_near, *k_rest], [*v_near, *v_rest]

    def look_inside(i, through=(), after=()):
        inside[i], copied = intra(
            mask, a, gain, q_near[i], k_near[i], v_near[i], g_near[i], *chunks[i], through, after
        )
        return copied

    def pair_last(i, after, through=()):
        message, *copied = picked(order, own[i], past[i], after, through)
        near[i] = swap(message)
        return message, *copied

    near[3] = swap(own[3])
    past[2] = turn(own[2])
    look_inside(0)
    both = joined(order, own[1], near[1], chunks[1][1], (inside[0][0],))
    message, both = pair_last(0, (), (both,))
    past[1] = turn(both)
    look_inside(1, (), (message,))
    look_inside(2, (), (inside[1][0],))
    both = joined(order, own[3], near[3], chunks[3][1], (inside[2][0],))
    message, both = pair_last(2, (), (both,))
    past[3] = ahead(both)
    look_inside(3, (), (message,))

    if reach > 2:
        for i, (_, many) in enumerate(chunks):
            past[i] = jnp.where(place >= 2, past[i], 0.0)
            if i % 2 == 0:
                near[i] = jnp.where(place >= 1, near[i], 0.0)
                near[i] = widened(joined(later, near[i], past[i], many), many, 2, 2)
                past[i] = jnp.zeros_like(near[i])
            else:
                past[i] = widened(past[i], many, 2, 2)

    result = ()
    for group in ((0, 1), (2, 3)):
        groups = [(*chunks[i], ("span", "pair")[i % 2]) for i in group]
        arrays = [x for i in group for x in (own[i], near[i], past[i], *inside[i])]
        result = finish(order, seg, heads, groups, arrays, result, (inside[3][0],))
    return tuple(result)


def solution(mesh):
    placed = (
        P(("groups", "seq"), "wt"),
        P(("groups", "seq"), "wt"),
        P(("groups", "seq"), "wt"),
        P(("groups", "seq"), "wt"),
        P(("groups", "seq")),
        P("wt"),
        P("wt", ("groups", "seq")),
        P("wt"),
    )
    return jax.shard_map(
        shards,
        mesh=mesh,
        in_specs=placed,
        out_specs=(P(("groups", "seq"), "wt"), P(("groups", "seq"), "wt", None, None)),
        check_vma=False,
    )
```

```python
import functools

import jax
import jax.numpy as jnp
from jax import lax
from jax.experimental import pallas as pl
from jax.experimental.pallas import tpu as pltpu
from jax.sharding import PartitionSpec as P

F32 = jnp.float32
BF16 = jnp.bfloat16
NN = (((1,), (0,)), ((), ()))
NT = (((1,), (1,)), ((), ()))
MIB = 1 << 20
SHORT = pl.CostEstimate(flops=1, bytes_accessed=1, transcendentals=0)


def vmem_spec(shape, index_map):
    return pl.BlockSpec(shape, index_map)


def as_column(row, lanes):
    return jnp.broadcast_to(row, (lanes, row.shape[1])).T


def meta_rows(heads):
    return -(-(heads + 1) // 8) * 8


def put_message(msg_ref, first, heads, size, w_ref, finals, end, k_ref, v_ref):
    top = heads * size
    for j in range(heads):
        columns = slice(j * size, (j + 1) * size)
        weight = w_ref[first + j : first + j + 1, :]
        keyed = (k_ref[:, columns].astype(F32).T * weight).astype(BF16)
        msg_ref[columns, :] = lax.dot_general(
            keyed, v_ref[:, columns], NN, preferred_element_type=F32
        )
    msg_ref[top : top + heads, :] = jnp.broadcast_to(finals, (heads, size))
    below = meta_rows(heads) - heads
    msg_ref[top + heads :, :] = jnp.broadcast_to(end.astype(F32), (below, size))


def first_kernel(heads, chunks, order_ref, seg_hbm, exponent_hbm, keep_hbm, k_hbm, v_hbm, *refs):
    number = len(chunks)
    (msg_ref, a_ref, w_ref, seg_ref), refs = refs[:4], refs[4:]
    k_refs, v_refs, refs = refs[:number], refs[number : 2 * number], refs[2 * number :]
    exponent_ref, keep_ref, sems = refs
    tokens = seg_ref.shape[1]
    size = msg_ref.shape[1]
    pairs = [(keep_hbm, keep_ref), (exponent_hbm, exponent_ref), (seg_hbm, seg_ref)]
    for i, (first, many) in enumerate(chunks):
        wide = pl.ds(first * size, many * size)
        for start in (0, tokens // 2):
            rows = pl.ds(start, tokens // 2)
            for source, target in ((k_hbm, k_refs[i]), (v_hbm, v_refs[i])):
                pairs.append((source.at[rows, wide], target.at[rows, :]))
    copies = [pltpu.make_async_copy(*pair, sems.at[i]) for i, pair in enumerate(pairs)]
    for copy in copies:
        copy.start()
    earlier = lax.broadcasted_iota(jnp.int32, (tokens, tokens), 0)
    later = lax.broadcasted_iota(jnp.int32, (tokens, tokens), 1)
    upper = jnp.where(earlier <= later, 1.0, 0.0).astype(BF16)
    across = lax.broadcasted_iota(jnp.int32, (heads, heads), 1)
    down = lax.broadcasted_iota(jnp.int32, (heads, heads), 0)
    for copy in copies[:3]:
        copy.wait()
    spread = jnp.broadcast_to(exponent_ref[...], (heads, heads))
    exponent = jnp.sum(jnp.where(across == down, spread, 0).astype(F32), axis=1, keepdims=True)
    a = -jnp.exp2(-exponent) + jnp.log(keep_ref[...])
    high = a.astype(BF16)
    rest = a - high.astype(F32)
    middle = rest.astype(BF16)
    low = (rest - middle.astype(F32)).astype(BF16)
    parts = jnp.concatenate([high, middle, low], axis=0)
    sums = lax.dot_general(parts, upper, NN, preferred_element_type=F32)
    cumulative = sums[:heads] + (sums[heads : 2 * heads] + sums[2 * heads :])
    a_ref[...] = cumulative
    final = cumulative[:, tokens - 1 :]
    seg = seg_ref[...]
    last = seg[:, tokens - 1 :]
    w_ref[...] = jnp.where(seg == last, jnp.exp(final - cumulative), 0.0)
    for copy in copies[3:7]:
        copy.wait()
    first, many = chunks[0]
    finals = final[first : first + many]
    put_message(msg_ref, first, many, size, w_ref, finals, last, k_refs[0], v_refs[0])
    for copy in copies[7:]:
        copy.wait()


def message_of(size, many):
    return pltpu.VMEM((many * size + meta_rows(many), size), F32)


def first_message(order, seg, exponent, keep, k, v, heads, chunks):
    tokens, size = k.shape[0], k.shape[1] // heads
    near = [pltpu.VMEM((tokens, many * size), BF16) for _, many in chunks]
    shapes = [message_of(size, chunks[0][1])]
    shapes += [pltpu.VMEM((heads, tokens), F32)] * 2 + [pltpu.VMEM((1, tokens), jnp.int32)]
    shapes += near + near
    number = len(chunks)
    out = pl.pallas_call(
        functools.partial(first_kernel, heads, chunks),
        in_specs=[pl.BlockSpec(memory_space=pltpu.SMEM)]
        + [pl.BlockSpec(memory_space=pltpu.HBM)] * 5,
        out_specs=[pl.BlockSpec(memory_space=pltpu.VMEM)] * len(shapes),
        out_shape=shapes,
        scratch_shapes=[
            pltpu.VMEM((1, heads), jnp.int32),
            pltpu.VMEM((heads, tokens), F32),
            pltpu.SemaphoreType.DMA((3 + 4 * number,)),
        ],
        compiler_params=pltpu.CompilerParams(vmem_limit_bytes=8 * MIB),
        cost_estimate=SHORT,
        name="first_message",
    )(order, seg, exponent, keep, k, v)
    (message, a, w, seg), out = out[:4], out[4:]
    return message, a, w, seg, out[:number], out[number:]


def second_message(seg, a, w, k, v, first, heads):
    tokens, size = k.shape[0], k.shape[1] // heads

    def kernel(seg_ref, a_ref, w_ref, k_ref, v_ref, msg_ref):
        final = a_ref[first : first + heads, tokens - 1 :]
        last = seg_ref[:, tokens - 1 :]
        put_message(msg_ref, first, heads, size, w_ref, final, last, k_ref, v_ref)

    return pl.pallas_call(
        kernel,
        in_specs=[pl.BlockSpec(memory_space=pltpu.VMEM)] * 5,
        out_specs=pl.BlockSpec(memory_space=pltpu.VMEM),
        out_shape=message_of(size, heads),
        compiler_params=pltpu.CompilerParams(vmem_limit_bytes=8 * MIB),
        cost_estimate=SHORT,
        name="second_message",
    )(seg, a, w, k, v)


def rest_kernel(chunks, done, seg_ref, a_ref, w_ref, q_hbm, k_hbm, v_hbm, g_hbm, *refs):
    tokens = seg_ref.shape[1]
    left, number = chunks[done:], len(chunks)
    messages, mask_ref, refs, sems = refs[: len(left)], refs[len(left)], refs[len(left) + 1 : -1], refs[-1]
    k_refs, refs = refs[: len(left)], refs[len(left) :]
    v_refs, refs = refs[: len(left)], refs[len(left) :]
    q_refs, g_refs = refs[:number], refs[number:]
    size = messages[0].shape[1]
    pairs = []
    for i, (first, many) in enumerate(left):
        wide = pl.ds(first * size, many * size)
        pairs += [(k_hbm.at[:, wide], k_refs[i]), (v_hbm.at[:, wide], v_refs[i])]
    for i, (first, many) in enumerate(chunks):
        wide = pl.ds(first * size, many * size)
        pairs += [(q_hbm.at[:, wide], q_refs[i]), (g_hbm.at[:, wide], g_refs[i])]
    copies = [pltpu.make_async_copy(*pair, sems.at[i]) for i, pair in enumerate(pairs)]
    for copy in copies:
        copy.start()
    make_mask(seg_ref, mask_ref)
    last = seg_ref[:, tokens - 1 :]
    for i, (first, many) in enumerate(left):
        copies[2 * i].wait()
        copies[2 * i + 1].wait()
        final = a_ref[first : first + many, tokens - 1 :]
        put_message(messages[i], first, many, size, w_ref, final, last, k_refs[i], v_refs[i])
    for copy in copies[2 * len(left) :]:
        copy.wait()


def rest_messages(seg, a, w, q, k, v, g, chunks, done):
    heads = a.shape[0]
    tokens, size = k.shape[0], k.shape[1] // heads
    near = [pltpu.VMEM((tokens, many * size), BF16) for _, many in chunks]
    shapes = [message_of(size, many) for _, many in chunks[done:]]
    shapes += [pltpu.VMEM((tokens, tokens), F32)] + near[done:] * 2 + near * 2
    left, number = len(chunks) - done, len(chunks)
    out = pl.pallas_call(
        functools.partial(rest_kernel, chunks, done),
        in_specs=[pl.BlockSpec(memory_space=pltpu.VMEM)] * 3
        + [pl.BlockSpec(memory_space=pltpu.HBM)] * 4,
        out_specs=[pl.BlockSpec(memory_space=pltpu.VMEM)] * len(shapes),
        out_shape=shapes,
        scratch_shapes=[pltpu.SemaphoreType.DMA((2 * (left + number),))],
        compiler_params=pltpu.CompilerParams(vmem_limit_bytes=8 * MIB),
        cost_estimate=SHORT,
        name="rest_messages",
    )(seg, a, w, q, k, v, g)
    messages, mask, out = out[:left], out[left], out[left + 1 :]
    k_near, v_near, out = out[:left], out[left : 2 * left], out[2 * left :]
    return messages, mask, k_near, v_near, out[:number], out[number:]


def join_kernel(heads, order_ref, mine_ref, other_ref, out_ref):
    size = mine_ref.shape[1]
    top = heads * size
    mine_later = (order_ref[0] & 1) == 1
    final_mine, final_other = mine_ref[top : top + heads, :], other_ref[top : top + heads, :]
    end_mine, end_other = mine_ref[top + heads :, :], other_ref[top + heads :, :]
    same = jnp.where(end_mine[:1] == end_other[:1], 1.0, 0.0)
    scale_mine = jnp.where(mine_later, 1.0, jnp.exp(final_other) * same)
    scale_other = jnp.where(mine_later, jnp.exp(final_mine) * same, 1.0)
    for head in range(heads):
        rows = slice(head * size, (head + 1) * size)
        out_ref[rows, :] = (
            scale_mine[head : head + 1] * mine_ref[rows, :]
            + scale_other[head : head + 1] * other_ref[rows, :]
        )
    out_ref[top : top + heads, :] = final_mine + final_other
    out_ref[top + heads :, :] = jnp.where(mine_later, end_mine, end_other)


def small_call(kernel, name, order, arrays, after):
    vmem = pl.BlockSpec(memory_space=pltpu.VMEM)
    return pl.pallas_call(
        lambda *refs: kernel(*refs[: 1 + len(arrays)], refs[-1]),
        in_specs=[pl.BlockSpec(memory_space=pltpu.SMEM)]
        + [vmem] * len(arrays)
        + [pl.BlockSpec(memory_space=pl.ANY)] * len(after),
        out_specs=vmem,
        out_shape=pltpu.VMEM(arrays[0].shape, F32),
        compiler_params=pltpu.CompilerParams(vmem_limit_bytes=8 * MIB),
        cost_estimate=SHORT,
        name=name,
    )(order, *arrays, *after)


def joined(order, mine, other, heads, after=()):
    return small_call(
        functools.partial(join_kernel, heads), "join_windows", order, (mine, other), after
    )


def picked(order, even, odd, after=(), through=()):
    vmem = pl.BlockSpec(memory_space=pltpu.VMEM)

    def kernel(order_ref, even_ref, odd_ref, *refs):
        outs = refs[len(through) + len(after) :]
        for source, target in zip(refs, outs[1:]):
            target[...] = source[...]
        odd = (order_ref[0] & 1) == 1

        @pl.when(odd)
        def _():
            outs[0][...] = odd_ref[...]

        @pl.when(jnp.logical_not(odd))
        def _():
            outs[0][...] = even_ref[...]

    return pl.pallas_call(
        kernel,
        in_specs=[pl.BlockSpec(memory_space=pltpu.SMEM)]
        + [vmem] * (2 + len(through))
        + [pl.BlockSpec(memory_space=pl.ANY)] * len(after),
        out_specs=[vmem] * (1 + len(through)),
        out_shape=[pltpu.VMEM(x.shape, F32) for x in (even, *through)],
        compiler_params=pltpu.CompilerParams(vmem_limit_bytes=8 * MIB),
        cost_estimate=SHORT,
        name="pick_message",
    )(order, even, odd, *through, *after)


def make_mask(seg_ref, mask_ref):
    tokens = seg_ref.shape[1]
    seg = seg_ref[...].astype(F32)
    column = as_column(seg, 128)
    for start in range(0, tokens, 128):
        across = lax.broadcasted_iota(jnp.int32, (tokens, 128), 1) + start
        down = lax.broadcasted_iota(jnp.int32, (tokens, 128), 0)
        seen = (column == seg[:, start : start + 128]) & (across <= down)
        mask_ref[:, start : start + 128] = jnp.where(seen, 0.0, -1e30)


def intra_kernel(
    first, heads, through, after, mask_ref, a_ref, gain_ref, q_ref, k_ref, v_ref, g_ref, *refs
):
    o_ref, gate_ref, decay_ref, *copied = refs[through + after :]
    for source, target in zip(refs[:through], copied):
        target[...] = source[...]
    tokens = mask_ref.shape[0]
    size = q_ref.shape[1] // heads
    block = min(tokens, 256)
    for j in range(heads):
        columns = slice(j * size, (j + 1) * size)
        a_row = a_ref[first + j : first + j + 1, :] * 1.4426950408889634
        a_column = as_column(a_row, 128)
        decay_ref[:, columns] = jnp.exp2(a_column)
        for start in range(0, tokens, block):
            here, upto = slice(start, start + block), slice(0, start + block)
            scores = lax.dot_general(
                q_ref[here, columns], k_ref[upto, columns], NT, preferred_element_type=F32
            )
            spread = jnp.concatenate([a_column[here]] * ((start + block) // 128), axis=1)
            weight = jnp.exp2(spread - a_row[:, upto] + mask_ref[here, upto])
            probs = (scores * weight).astype(BF16)
            o_ref[here, columns] = lax.dot_general(
                probs, v_ref[upto, columns], NN, preferred_element_type=F32
            )
        half = 0.5 * size**0.5 * gain_ref[:, (first + j) * size : (first + j + 1) * size]
        gate_ref[:, columns] = half + half * jnp.tanh(0.5 * g_ref[:, columns].astype(F32))


def intra(mask, a, gain, q, k, v, g, first, heads, through=(), after=()):
    tokens, size = mask.shape[0], gain.shape[1] // a.shape[0]
    vmem = pl.BlockSpec(memory_space=pltpu.VMEM)
    o, gate, decay, *copied = pl.pallas_call(
        functools.partial(intra_kernel, first, heads, len(through), len(after)),
        in_specs=[vmem] * (7 + len(through)) + [pl.BlockSpec(memory_space=pl.ANY)] * len(after),
        out_specs=[vmem] * (3 + len(through)),
        out_shape=[pltpu.VMEM((tokens, heads * size), F32)] * 3
        + [pltpu.VMEM(x.shape, x.dtype) for x in through],
        compiler_params=pltpu.CompilerParams(vmem_limit_bytes=8 * MIB),
        cost_estimate=SHORT,
        name="intra_span",
    )(mask, a, gain, q, k, v, g, *through, *after)
    return (o, gate, decay, q), copied


def final_kernel(groups, unread, order_ref, seg_ref, *rest):
    number = len(groups)
    inputs, rest = rest[: 7 * number], rest[7 * number + unread :]
    gated_hbm, snap_hbm, *scratch, inter_ref, sems = rest
    place = order_ref[0]
    seg = seg_ref[...].astype(F32)
    copies, work = [], []

    def send(source, target):
        copies.append(pltpu.make_async_copy(source, target, sems.at[len(copies)]))
        copies[-1].start()

    for i, (first, heads, kind) in enumerate(groups):
        own_ref, near_ref, past_ref = inputs[7 * i : 7 * i + 3]
        gated_ref, snap_ref = scratch[2 * i : 2 * i + 2]
        size = own_ref.shape[1]
        top = heads * size
        ends = slice(top + heads, top + heads + 1)
        finals = slice(top, top + heads)
        own_end, near_end, past_end = own_ref[ends, :], near_ref[ends, :], past_ref[ends, :]
        bridged = jnp.exp(near_ref[finals, :]) * jnp.where(near_end == past_end, 1.0, 0.0)
        if kind == "pair":
            odd = (place & 1) == 1
            previous = jnp.where(odd, near_end, past_end)
            scale_near = jnp.where(odd, 1.0, 0.0)
            scale_past = jnp.where(odd, bridged, 1.0)
        else:
            previous = near_end
            scale_near = jnp.where(place > 0, 1.0, 0.0)
            scale_past = bridged
        scale_past = jnp.where(place >= 2, scale_past, 0.0)
        own_decay = jnp.exp(own_ref[finals, :]) * jnp.where(own_end == previous, 1.0, 0.0)
        number_valid = jnp.sum(
            jnp.where(seg == previous[:, :1], 1.0, 0.0), axis=1, keepdims=True
        )
        for j in range(heads):
            rows = slice(j * size, (j + 1) * size)
            state = scale_past[j : j + 1] * past_ref[rows, :] + scale_near * near_ref[rows, :]
            snap_ref[j] = own_decay[j : j + 1] * state + own_ref[rows, :]
            high = state.astype(BF16)
            low = (state - high.astype(F32)).astype(BF16)
            both = jnp.concatenate([high, low], axis=0)
            work.append((i, j, first, heads, both, number_valid, inputs[7 * i + 3 : 7 * i + 7]))
        send(snap_ref, snap_hbm.at[0, pl.ds(first, heads)])

    rows = lax.broadcasted_iota(jnp.int32, (64, 128), 0).astype(F32)
    for number, (i, j, first, heads, both, number_valid, arrays) in enumerate(work):
        o_ref, gate_ref, decay_ref, q_ref = arrays
        gated_ref = scratch[2 * i]
        tokens, size = seg.shape[1], q_ref.shape[1] // heads
        columns = slice(j * size, (j + 1) * size)
        q = q_ref[:, columns]
        inter_ref[number % 4] = lax.dot_general(
            jnp.concatenate([q, q], axis=1), both, NN, preferred_element_type=F32
        )
        for start in range(0, tokens, 64):
            here = slice(start, start + 64)
            inter = inter_ref[number % 4, here, :]
            inter = jnp.where(rows < number_valid - start, inter * decay_ref[here, columns], 0.0)
            mixed = o_ref[here, columns] + inter
            square = jnp.sum(mixed * mixed, axis=1, keepdims=True)
            gated = mixed * lax.rsqrt(square + size * 1e-06) * gate_ref[here, columns]
            gated_ref[here, columns] = gated.astype(BF16)
        alone = number + 2 >= len(work)
        if alone or j % 2 == 1 or j == heads - 1:
            begin = j if alone else j - j % 2
            width = (j + 1 - begin) * size
            there = pl.ds((first + begin) * size, width)
            send(gated_ref.at[:, pl.ds(begin * size, width)], gated_hbm.at[:, there])
    for copy in copies:
        copy.wait()


def finish(order, seg, total, groups, arrays, so_far, after):
    tokens, size = seg.shape[1], arrays[0].shape[1]
    vmem, anywhere = pl.BlockSpec(memory_space=pltpu.VMEM), pl.BlockSpec(memory_space=pl.ANY)
    unread = len(so_far) + len(after)
    scratch = []
    for _, many, _ in groups:
        scratch.append(pltpu.VMEM((tokens, many * size), BF16))
        scratch.append(pltpu.VMEM((many, size, size), F32))
    return pl.pallas_call(
        functools.partial(final_kernel, groups, unread),
        in_specs=[pl.BlockSpec(memory_space=pltpu.SMEM)]
        + [vmem] * (1 + len(arrays))
        + [anywhere] * unread,
        out_specs=[anywhere, anywhere],
        out_shape=[
            jax.ShapeDtypeStruct((tokens, total * size), BF16),
            jax.ShapeDtypeStruct((1, total, size, size), F32),
        ],
        scratch_shapes=scratch
        + [pltpu.VMEM((4, tokens, size), F32), pltpu.SemaphoreType.DMA((2 * total,))],
        input_output_aliases={2 + len(arrays) + i: i for i in range(len(so_far))},
        compiler_params=pltpu.CompilerParams(vmem_limit_bytes=12 * MIB),
        cost_estimate=SHORT,
        name="finish",
    )(order, seg, *arrays, *so_far, *after)


def shards(q, k, v, g, segment, decay_exponent, retention, norm_gain):
    heads = decay_exponent.shape[0]
    tokens = q.shape[0]
    count = lax.axis_size("seq")
    place = lax.axis_index("seq")
    reach = max(1, count // 4)
    far = lambda x: pltpu.with_memory_space_constraint(x, pltpu.HBM)
    q, k, v, g = far(q), far(k), far(v), far(g)
    gain = norm_gain.reshape(1, -1)
    order = jnp.where(place >= 2, 2 + (place & 1), place & 1).astype(jnp.int32).reshape(1)
    later = jnp.ones((1,), jnp.int32)
    swap = lambda x: lax.ppermute(x, "seq", [(c, c ^ 1) for c in range(count)])
    turn = lambda x: lax.ppermute(x, "seq", [(c, (c + 2) % count) for c in range(count)])
    ahead = lambda x: lax.ppermute(x, "seq", [(c, c + 2) for c in range(count - 2)])

    half = heads // 2
    even, odd = half // 2, half // 2
    chunks = [(0, half - even), (half, half - odd), (half - even, even), (heads - odd, odd)]

    def widened(x, many, shift, window):
        while window < reach:
            past = lax.ppermute(x, "seq", [(c, c + shift) for c in range(count - shift)])
            x = joined(later, x, past, many)
            shift, window = 2 * shift, 2 * window
        return x

    message, a, w, seg, k_near, v_near = first_message(
        order,
        far(segment.reshape(1, tokens)),
        far(decay_exponent.reshape(1, heads)),
        far(retention),
        k,
        v,
        heads,
        (chunks[1], chunks[0]),
    )
    k_near, v_near = k_near[::-1], v_near[::-1]
    near, past, inside = {}, {}, {}
    near[1] = swap(message)
    own = [second_message(seg, a, w, k_near[0], v_near[0], *chunks[0]), message]
    past[0] = turn(own[0])
    messages, mask, k_rest, v_rest, q_near, g_near = rest_messages(
        seg, a, w, q, k, v, g, chunks, 2
    )
    own, k_near, v_near = [*own, *messages], [*k_near, *k_rest], [*v_near, *v_rest]

    def look_inside(i, through=(), after=()):
        inside[i], copied = intra(
            mask, a, gain, q_near[i], k_near[i], v_near[i], g_near[i], *chunks[i], through, after
        )
        return copied

    def pair_last(i, after, through=()):
        message, *copied = picked(order, own[i], past[i], after, through)
        near[i] = swap(message)
        return message, *copied

    near[3] = swap(own[3])
    past[2] = turn(own[2])
    look_inside(0)
    both = joined(order, own[1], near[1], chunks[1][1], (inside[0][0],))
    message, both = pair_last(0, (), (both,))
    past[1] = turn(both)
    look_inside(1, (), (message,))
    look_inside(2, (), (inside[1][0],))
    both = joined(order, own[3], near[3], chunks[3][1], (inside[2][0],))
    message, both = pair_last(2, (), (both,))
    past[3] = ahead(both)
    look_inside(3, (), (message,))

    if reach > 2:
        for i, (_, many) in enumerate(chunks):
            past[i] = jnp.where(place >= 2, past[i], 0.0)
            if i % 2 == 0:
                near[i] = jnp.where(place >= 1, near[i], 0.0)
                near[i] = widened(joined(later, near[i], past[i], many), many, 2, 2)
                past[i] = jnp.zeros_like(near[i])
            else:
                past[i] = widened(past[i], many, 2, 2)

    result = ()
    for group in ((0, 1), (2, 3)):
        groups = [(*chunks[i], ("span", "pair")[i % 2]) for i in group]
        arrays = [x for i in group for x in (own[i], near[i], past[i], *inside[i])]
        result = finish(order, seg, heads, groups, arrays, result, (inside[3][0],))
    return tuple(result)


def solution(mesh):
    placed = (
        P(("groups", "seq"), "wt"),
        P(("groups", "seq"), "wt"),
        P(("groups", "seq"), "wt"),
        P(("groups", "seq"), "wt"),
        P(("groups", "seq")),
        P("wt"),
        P("wt", ("groups", "seq")),
        P("wt"),
    )
    return jax.shard_map(
        shards,
        mesh=mesh,
        in_specs=placed,
        out_specs=(P(("groups", "seq"), "wt"), P(("groups", "seq"), "wt", None, None)),
        check_vma=False,
    )
```

```python
import functools

import jax
import jax.numpy as jnp
from jax import lax
from jax.experimental import pallas as pl
from jax.experimental.pallas import tpu as pltpu
from jax.sharding import PartitionSpec as P

F32 = jnp.float32
BF16 = jnp.bfloat16
NN = (((1,), (0,)), ((), ()))
NT = (((1,), (1,)), ((), ()))
MIB = 1 << 20
SHORT = pl.CostEstimate(flops=1, bytes_accessed=1, transcendentals=0)


def vmem_spec(shape, index_map):
    return pl.BlockSpec(shape, index_map)


def as_column(row, lanes):
    return jnp.broadcast_to(row, (lanes, row.shape[1])).T


def meta_rows(heads):
    return -(-(heads + 1) // 8) * 8


def put_message(msg_ref, first, heads, size, w_ref, finals, end, k_ref, v_ref):
    top = heads * size
    for j in range(heads):
        columns = slice(j * size, (j + 1) * size)
        weight = w_ref[first + j : first + j + 1, :]
        keyed = (k_ref[:, columns].astype(F32).T * weight).astype(BF16)
        msg_ref[columns, :] = lax.dot_general(
            keyed, v_ref[:, columns], NN, preferred_element_type=F32
        )
    msg_ref[top : top + heads, :] = jnp.broadcast_to(finals, (heads, size))
    below = meta_rows(heads) - heads
    msg_ref[top + heads :, :] = jnp.broadcast_to(end.astype(F32), (below, size))


def first_kernel(heads, chunks, order_ref, seg_hbm, exponent_hbm, keep_hbm, k_hbm, v_hbm, *refs):
    number = len(chunks)
    (msg_ref, a_ref, w_ref, seg_ref), refs = refs[:4], refs[4:]
    k_refs, v_refs, refs = refs[:number], refs[number : 2 * number], refs[2 * number :]
    exponent_ref, keep_ref, sems = refs
    tokens = seg_ref.shape[1]
    size = msg_ref.shape[1]
    pairs = [(keep_hbm, keep_ref), (exponent_hbm, exponent_ref), (seg_hbm, seg_ref)]
    for i, (first, many) in enumerate(chunks):
        wide = pl.ds(first * size, many * size)
        for start in (0, tokens // 2):
            rows = pl.ds(start, tokens // 2)
            for source, target in ((k_hbm, k_refs[i]), (v_hbm, v_refs[i])):
                pairs.append((source.at[rows, wide], target.at[rows, :]))
    copies = [pltpu.make_async_copy(*pair, sems.at[i]) for i, pair in enumerate(pairs)]
    for copy in copies:
        copy.start()
    earlier = lax.broadcasted_iota(jnp.int32, (tokens, tokens), 0)
    later = lax.broadcasted_iota(jnp.int32, (tokens, tokens), 1)
    upper = jnp.where(earlier <= later, 1.0, 0.0).astype(BF16)
    across = lax.broadcasted_iota(jnp.int32, (heads, heads), 1)
    down = lax.broadcasted_iota(jnp.int32, (heads, heads), 0)
    for copy in copies[:3]:
        copy.wait()
    spread = jnp.broadcast_to(exponent_ref[...], (heads, heads))
    exponent = jnp.sum(jnp.where(across == down, spread, 0).astype(F32), axis=1, keepdims=True)
    a = -jnp.exp2(-exponent) + jnp.log(keep_ref[...])
    high = a.astype(BF16)
    rest = a - high.astype(F32)
    middle = rest.astype(BF16)
    low = (rest - middle.astype(F32)).astype(BF16)
    parts = jnp.concatenate([high, middle, low], axis=0)
    sums = lax.dot_general(parts, upper, NN, preferred_element_type=F32)
    cumulative = sums[:heads] + (sums[heads : 2 * heads] + sums[2 * heads :])
    a_ref[...] = cumulative
    final = cumulative[:, tokens - 1 :]
    seg = seg_ref[...]
    last = seg[:, tokens - 1 :]
    w_ref[...] = jnp.where(seg == last, jnp.exp(final - cumulative), 0.0)
    for copy in copies[3:7]:
        copy.wait()
    first, many = chunks[0]
    finals = final[first : first + many]
    put_message(msg_ref, first, many, size, w_ref, finals, last, k_refs[0], v_refs[0])
    for copy in copies[7:]:
        copy.wait()


def message_of(size, many):
    return pltpu.VMEM((many * size + meta_rows(many), size), F32)


def first_message(order, seg, exponent, keep, k, v, heads, chunks):
    tokens, size = k.shape[0], k.shape[1] // heads
    near = [pltpu.VMEM((tokens, many * size), BF16) for _, many in chunks]
    shapes = [message_of(size, chunks[0][1])]
    shapes += [pltpu.VMEM((heads, tokens), F32)] * 2 + [pltpu.VMEM((1, tokens), jnp.int32)]
    shapes += near + near
    number = len(chunks)
    out = pl.pallas_call(
        functools.partial(first_kernel, heads, chunks),
        in_specs=[pl.BlockSpec(memory_space=pltpu.SMEM)]
        + [pl.BlockSpec(memory_space=pltpu.HBM)] * 5,
        out_specs=[pl.BlockSpec(memory_space=pltpu.VMEM)] * len(shapes),
        out_shape=shapes,
        scratch_shapes=[
            pltpu.VMEM((1, heads), jnp.int32),
            pltpu.VMEM((heads, tokens), F32),
            pltpu.SemaphoreType.DMA((3 + 4 * number,)),
        ],
        compiler_params=pltpu.CompilerParams(vmem_limit_bytes=8 * MIB),
        cost_estimate=SHORT,
        name="first_message",
    )(order, seg, exponent, keep, k, v)
    (message, a, w, seg), out = out[:4], out[4:]
    return message, a, w, seg, out[:number], out[number:]


def second_message(seg, a, w, k, v, first, heads):
    tokens, size = k.shape[0], k.shape[1] // heads

    def kernel(seg_ref, a_ref, w_ref, k_ref, v_ref, msg_ref):
        final = a_ref[first : first + heads, tokens - 1 :]
        last = seg_ref[:, tokens - 1 :]
        put_message(msg_ref, first, heads, size, w_ref, final, last, k_ref, v_ref)

    return pl.pallas_call(
        kernel,
        in_specs=[pl.BlockSpec(memory_space=pltpu.VMEM)] * 5,
        out_specs=pl.BlockSpec(memory_space=pltpu.VMEM),
        out_shape=message_of(size, heads),
        compiler_params=pltpu.CompilerParams(vmem_limit_bytes=8 * MIB),
        cost_estimate=SHORT,
        name="second_message",
    )(seg, a, w, k, v)


def rest_kernel(chunks, done, seg_ref, a_ref, w_ref, q_hbm, k_hbm, v_hbm, g_hbm, *refs):
    tokens = seg_ref.shape[1]
    left, number = chunks[done:], len(chunks)
    messages, mask_ref, refs, sems = refs[: len(left)], refs[len(left)], refs[len(left) + 1 : -1], refs[-1]
    k_refs, refs = refs[: len(left)], refs[len(left) :]
    v_refs, refs = refs[: len(left)], refs[len(left) :]
    q_refs, g_refs = refs[:number], refs[number:]
    size = messages[0].shape[1]
    pairs = []
    for i, (first, many) in enumerate(left):
        wide = pl.ds(first * size, many * size)
        pairs += [(k_hbm.at[:, wide], k_refs[i]), (v_hbm.at[:, wide], v_refs[i])]
    for i, (first, many) in enumerate(chunks):
        wide = pl.ds(first * size, many * size)
        pairs += [(q_hbm.at[:, wide], q_refs[i]), (g_hbm.at[:, wide], g_refs[i])]
    copies = [pltpu.make_async_copy(*pair, sems.at[i]) for i, pair in enumerate(pairs)]
    for copy in copies:
        copy.start()
    make_mask(seg_ref, mask_ref)
    last = seg_ref[:, tokens - 1 :]
    for i, (first, many) in enumerate(left):
        copies[2 * i].wait()
        copies[2 * i + 1].wait()
        final = a_ref[first : first + many, tokens - 1 :]
        put_message(messages[i], first, many, size, w_ref, final, last, k_refs[i], v_refs[i])
    for copy in copies[2 * len(left) :]:
        copy.wait()


def rest_messages(seg, a, w, q, k, v, g, chunks, done):
    heads = a.shape[0]
    tokens, size = k.shape[0], k.shape[1] // heads
    near = [pltpu.VMEM((tokens, many * size), BF16) for _, many in chunks]
    shapes = [message_of(size, many) for _, many in chunks[done:]]
    shapes += [pltpu.VMEM((tokens, tokens), F32)] + near[done:] * 2 + near * 2
    left, number = len(chunks) - done, len(chunks)
    out = pl.pallas_call(
        functools.partial(rest_kernel, chunks, done),
        in_specs=[pl.BlockSpec(memory_space=pltpu.VMEM)] * 3
        + [pl.BlockSpec(memory_space=pltpu.HBM)] * 4,
        out_specs=[pl.BlockSpec(memory_space=pltpu.VMEM)] * len(shapes),
        out_shape=shapes,
        scratch_shapes=[pltpu.SemaphoreType.DMA((2 * (left + number),))],
        compiler_params=pltpu.CompilerParams(vmem_limit_bytes=8 * MIB),
        cost_estimate=SHORT,
        name="rest_messages",
    )(seg, a, w, q, k, v, g)
    messages, mask, out = out[:left], out[left], out[left + 1 :]
    k_near, v_near, out = out[:left], out[left : 2 * left], out[2 * left :]
    return messages, mask, k_near, v_near, out[:number], out[number:]


def join_kernel(heads, order_ref, mine_ref, other_ref, out_ref):
    size = mine_ref.shape[1]
    top = heads * size
    mine_later = (order_ref[0] & 1) == 1
    final_mine, final_other = mine_ref[top : top + heads, :], other_ref[top : top + heads, :]
    end_mine, end_other = mine_ref[top + heads :, :], other_ref[top + heads :, :]
    same = jnp.where(end_mine[:1] == end_other[:1], 1.0, 0.0)
    scale_mine = jnp.where(mine_later, 1.0, jnp.exp(final_other) * same)
    scale_other = jnp.where(mine_later, jnp.exp(final_mine) * same, 1.0)
    for head in range(heads):
        rows = slice(head * size, (head + 1) * size)
        out_ref[rows, :] = (
            scale_mine[head : head + 1] * mine_ref[rows, :]
            + scale_other[head : head + 1] * other_ref[rows, :]
        )
    out_ref[top : top + heads, :] = final_mine + final_other
    out_ref[top + heads :, :] = jnp.where(mine_later, end_mine, end_other)


def small_call(kernel, name, order, arrays, after):
    vmem = pl.BlockSpec(memory_space=pltpu.VMEM)
    return pl.pallas_call(
        lambda *refs: kernel(*refs[: 1 + len(arrays)], refs[-1]),
        in_specs=[pl.BlockSpec(memory_space=pltpu.SMEM)]
        + [vmem] * len(arrays)
        + [pl.BlockSpec(memory_space=pl.ANY)] * len(after),
        out_specs=vmem,
        out_shape=pltpu.VMEM(arrays[0].shape, F32),
        compiler_params=pltpu.CompilerParams(vmem_limit_bytes=8 * MIB),
        cost_estimate=SHORT,
        name=name,
    )(order, *arrays, *after)


def joined(order, mine, other, heads, after=()):
    return small_call(
        functools.partial(join_kernel, heads), "join_windows", order, (mine, other), after
    )


def picked(order, even, odd, after=(), through=()):
    vmem = pl.BlockSpec(memory_space=pltpu.VMEM)

    def kernel(order_ref, even_ref, odd_ref, *refs):
        outs = refs[len(through) + len(after) :]
        for source, target in zip(refs, outs[1:]):
            target[...] = source[...]
        odd = (order_ref[0] & 1) == 1

        @pl.when(odd)
        def _():
            outs[0][...] = odd_ref[...]

        @pl.when(jnp.logical_not(odd))
        def _():
            outs[0][...] = even_ref[...]

    return pl.pallas_call(
        kernel,
        in_specs=[pl.BlockSpec(memory_space=pltpu.SMEM)]
        + [vmem] * (2 + len(through))
        + [pl.BlockSpec(memory_space=pl.ANY)] * len(after),
        out_specs=[vmem] * (1 + len(through)),
        out_shape=[pltpu.VMEM(x.shape, F32) for x in (even, *through)],
        compiler_params=pltpu.CompilerParams(vmem_limit_bytes=8 * MIB),
        cost_estimate=SHORT,
        name="pick_message",
    )(order, even, odd, *through, *after)


def make_mask(seg_ref, mask_ref):
    tokens = seg_ref.shape[1]
    seg = seg_ref[...].astype(F32)
    column = as_column(seg, 128)
    for start in range(0, tokens, 128):
        across = lax.broadcasted_iota(jnp.int32, (tokens, 128), 1) + start
        down = lax.broadcasted_iota(jnp.int32, (tokens, 128), 0)
        seen = (column == seg[:, start : start + 128]) & (across <= down)
        mask_ref[:, start : start + 128] = jnp.where(seen, 0.0, -1e30)


def intra_kernel(
    first, heads, through, after, mask_ref, a_ref, gain_ref, q_ref, k_ref, v_ref, g_ref, *refs
):
    o_ref, gate_ref, decay_ref, *copied = refs[through + after :]
    for source, target in zip(refs[:through], copied):
        target[...] = source[...]
    tokens = mask_ref.shape[0]
    size = q_ref.shape[1] // heads
    block = min(tokens, 256)
    for j in range(heads):
        columns = slice(j * size, (j + 1) * size)
        a_row = a_ref[first + j : first + j + 1, :] * 1.4426950408889634
        a_column = as_column(a_row, 128)
        decay_ref[:, columns] = jnp.exp2(a_column)
        for start in range(0, tokens, block):
            here, upto = slice(start, start + block), slice(0, start + block)
            scores = lax.dot_general(
                q_ref[here, columns], k_ref[upto, columns], NT, preferred_element_type=F32
            )
            spread = jnp.concatenate([a_column[here]] * ((start + block) // 128), axis=1)
            weight = jnp.exp2(spread - a_row[:, upto] + mask_ref[here, upto])
            probs = (scores * weight).astype(BF16)
            o_ref[here, columns] = lax.dot_general(
                probs, v_ref[upto, columns], NN, preferred_element_type=F32
            )
        half = 0.5 * size**0.5 * gain_ref[:, (first + j) * size : (first + j + 1) * size]
        gate_ref[:, columns] = half + half * jnp.tanh(0.5 * g_ref[:, columns].astype(F32))


def intra(mask, a, gain, q, k, v, g, first, heads, through=(), after=()):
    tokens, size = mask.shape[0], gain.shape[1] // a.shape[0]
    vmem = pl.BlockSpec(memory_space=pltpu.VMEM)
    o, gate, decay, *copied = pl.pallas_call(
        functools.partial(intra_kernel, first, heads, len(through), len(after)),
        in_specs=[vmem] * (7 + len(through)) + [pl.BlockSpec(memory_space=pl.ANY)] * len(after),
        out_specs=[vmem] * (3 + len(through)),
        out_shape=[pltpu.VMEM((tokens, heads * size), F32)] * 3
        + [pltpu.VMEM(x.shape, x.dtype) for x in through],
        compiler_params=pltpu.CompilerParams(vmem_limit_bytes=8 * MIB),
        cost_estimate=SHORT,
        name="intra_span",
    )(mask, a, gain, q, k, v, g, *through, *after)
    return (o, gate, decay, q), copied


def final_kernel(groups, unread, order_ref, seg_ref, *rest):
    number = len(groups)
    inputs, rest = rest[: 7 * number], rest[7 * number + unread :]
    gated_hbm, snap_hbm, *scratch, inter_ref, sems = rest
    place = order_ref[0]
    seg = seg_ref[...].astype(F32)
    copies, work = [], []

    def send(source, target):
        copies.append(pltpu.make_async_copy(source, target, sems.at[len(copies)]))
        copies[-1].start()

    for i, (first, heads, kind) in enumerate(groups):
        own_ref, near_ref, past_ref = inputs[7 * i : 7 * i + 3]
        size = own_ref.shape[1]
        top = heads * size
        ends = slice(top + heads, top + heads + 1)
        finals = slice(top, top + heads)
        own_end, near_end, past_end = own_ref[ends, :], near_ref[ends, :], past_ref[ends, :]
        bridged = jnp.exp(near_ref[finals, :]) * jnp.where(near_end == past_end, 1.0, 0.0)
        if kind == "pair":
            odd = (place & 1) == 1
            previous = jnp.where(odd, near_end, past_end)
            scale_near = jnp.where(odd, 1.0, 0.0)
            scale_past = jnp.where(odd, bridged, 1.0)
        else:
            previous = near_end
            scale_near = jnp.where(place > 0, 1.0, 0.0)
            scale_past = bridged
        scale_past = jnp.where(place >= 2, scale_past, 0.0)
        own_decay = jnp.exp(own_ref[finals, :]) * jnp.where(own_end == previous, 1.0, 0.0)
        number_valid = jnp.sum(
            jnp.where(seg == previous[:, :1], 1.0, 0.0), axis=1, keepdims=True
        )
        scales = scale_near, scale_past, own_decay, number_valid
        work += [(i, j, first, heads, scales) for j in range(heads)]

    tokens, size = seg.shape[1], inter_ref.shape[2]
    count_rows = lax.broadcasted_iota(jnp.int32, (64, size), 0).astype(F32)
    halves = {}

    def state_of(n):
        i, j, first, heads, (scale_near, scale_past, own_decay, _) = work[n]
        own_ref, near_ref, past_ref = inputs[7 * i : 7 * i + 3]
        snap_ref = scratch[2 * i + 1]
        rows = slice(j * size, (j + 1) * size)
        state = scale_past[j : j + 1] * past_ref[rows, :] + scale_near * near_ref[rows, :]
        snap_ref[j] = own_decay[j : j + 1] * state + own_ref[rows, :]
        high = state.astype(BF16)
        low = (state - high.astype(F32)).astype(BF16)
        halves[n] = jnp.concatenate([high, low], axis=0)
        if j == heads - 1:
            send(snap_ref, snap_hbm.at[0, pl.ds(first, heads)])

    def product_of(n):
        i, j = work[n][:2]
        q = inputs[7 * i + 6][:, j * size : (j + 1) * size]
        inter_ref[n % 4] = lax.dot_general(
            jnp.concatenate([q, q], axis=1), halves.pop(n), NN, preferred_element_type=F32
        )

    def output_of(n):
        i, j, first, heads, (*_, number_valid) = work[n]
        o_ref, gate_ref, decay_ref = inputs[7 * i + 3 : 7 * i + 6]
        gated_ref = scratch[2 * i]
        columns = slice(j * size, (j + 1) * size)
        for start in range(0, tokens, 64):
            here = slice(start, start + 64)
            inter = inter_ref[n % 4, here, :] * decay_ref[here, columns]
            inter = jnp.where(count_rows < number_valid - start, inter, 0.0)
            mixed = o_ref[here, columns] + inter
            square = jnp.sum(mixed * mixed, axis=1, keepdims=True)
            gated = mixed * lax.rsqrt(square + size * 1e-06) * gate_ref[here, columns]
            gated_ref[here, columns] = gated.astype(BF16)
        alone = n + 2 >= len(work)
        if alone or j % 2 == 1 or j == heads - 1:
            begin = j if alone else j - j % 2
            width = (j + 1 - begin) * size
            there = pl.ds((first + begin) * size, width)
            send(gated_ref.at[:, pl.ds(begin * size, width)], gated_hbm.at[:, there])

    for n in range(len(work) + 2):
        if n < len(work):
            state_of(n)
        if 0 <= n - 1 < len(work):
            product_of(n - 1)
        if n >= 2:
            output_of(n - 2)
    for copy in copies:
        copy.wait()


def finish(order, seg, total, groups, arrays, so_far, after):
    tokens, size = seg.shape[1], arrays[0].shape[1]
    vmem, anywhere = pl.BlockSpec(memory_space=pltpu.VMEM), pl.BlockSpec(memory_space=pl.ANY)
    unread = len(so_far) + len(after)
    scratch = []
    for _, many, _ in groups:
        scratch.append(pltpu.VMEM((tokens, many * size), BF16))
        scratch.append(pltpu.VMEM((many, size, size), F32))
    return pl.pallas_call(
        functools.partial(final_kernel, groups, unread),
        in_specs=[pl.BlockSpec(memory_space=pltpu.SMEM)]
        + [vmem] * (1 + len(arrays))
        + [anywhere] * unread,
        out_specs=[anywhere, anywhere],
        out_shape=[
            jax.ShapeDtypeStruct((tokens, total * size), BF16),
            jax.ShapeDtypeStruct((1, total, size, size), F32),
        ],
        scratch_shapes=scratch
        + [pltpu.VMEM((4, tokens, size), F32), pltpu.SemaphoreType.DMA((2 * total,))],
        input_output_aliases={2 + len(arrays) + i: i for i in range(len(so_far))},
        compiler_params=pltpu.CompilerParams(vmem_limit_bytes=12 * MIB),
        cost_estimate=SHORT,
        name="finish",
    )(order, seg, *arrays, *so_far, *after)


def shards(q, k, v, g, segment, decay_exponent, retention, norm_gain):
    heads = decay_exponent.shape[0]
    tokens = q.shape[0]
    count = lax.axis_size("seq")
    place = lax.axis_index("seq")
    reach = max(1, count // 4)
    far = lambda x: pltpu.with_memory_space_constraint(x, pltpu.HBM)
    q, k, v, g = far(q), far(k), far(v), far(g)
    gain = norm_gain.reshape(1, -1)
    order = jnp.where(place >= 2, 2 + (place & 1), place & 1).astype(jnp.int32).reshape(1)
    later = jnp.ones((1,), jnp.int32)
    swap = lambda x: lax.ppermute(x, "seq", [(c, c ^ 1) for c in range(count)])
    turn = lambda x: lax.ppermute(x, "seq", [(c, (c + 2) % count) for c in range(count)])
    ahead = lambda x: lax.ppermute(x, "seq", [(c, c + 2) for c in range(count - 2)])

    half = heads // 2
    even, odd = half // 2, half // 2
    chunks = [(0, half - even), (half, half - odd), (half - even, even), (heads - odd, odd)]

    def widened(x, many, shift, window):
        while window < reach:
            past = lax.ppermute(x, "seq", [(c, c + shift) for c in range(count - shift)])
            x = joined(later, x, past, many)
            shift, window = 2 * shift, 2 * window
        return x

    message, a, w, seg, k_near, v_near = first_message(
        order,
        far(segment.reshape(1, tokens)),
        far(decay_exponent.reshape(1, heads)),
        far(retention),
        k,
        v,
        heads,
        (chunks[1], chunks[0]),
    )
    k_near, v_near = k_near[::-1], v_near[::-1]
    near, past, inside = {}, {}, {}
    near[1] = swap(message)
    own = [second_message(seg, a, w, k_near[0], v_near[0], *chunks[0]), message]
    past[0] = turn(own[0])
    messages, mask, k_rest, v_rest, q_near, g_near = rest_messages(
        seg, a, w, q, k, v, g, chunks, 2
    )
    own, k_near, v_near = [*own, *messages], [*k_near, *k_rest], [*v_near, *v_rest]

    def look_inside(i, through=(), after=()):
        inside[i], copied = intra(
            mask, a, gain, q_near[i], k_near[i], v_near[i], g_near[i], *chunks[i], through, after
        )
        return copied

    def pair_last(i, after, through=()):
        message, *copied = picked(order, own[i], past[i], after, through)
        near[i] = swap(message)
        return message, *copied

    near[3] = swap(own[3])
    past[2] = turn(own[2])
    look_inside(0)
    both = joined(order, own[1], near[1], chunks[1][1], (inside[0][0],))
    message, both = pair_last(0, (), (both,))
    past[1] = turn(both)
    look_inside(1, (), (message,))
    look_inside(2, (), (inside[1][0],))
    both = joined(order, own[3], near[3], chunks[3][1], (inside[2][0],))
    message, both = pair_last(2, (), (both,))
    past[3] = ahead(both)
    look_inside(3, (), (message,))

    if reach > 2:
        for i, (_, many) in enumerate(chunks):
            past[i] = jnp.where(place >= 2, past[i], 0.0)
            if i % 2 == 0:
                near[i] = jnp.where(place >= 1, near[i], 0.0)
                near[i] = widened(joined(later, near[i], past[i], many), many, 2, 2)
                past[i] = jnp.zeros_like(near[i])
            else:
                past[i] = widened(past[i], many, 2, 2)

    result = ()
    for group in ((0, 1), (2, 3)):
        groups = [(*chunks[i], ("span", "pair")[i % 2]) for i in group]
        arrays = [x for i in group for x in (own[i], near[i], past[i], *inside[i])]
        result = finish(order, seg, heads, groups, arrays, result, (inside[3][0],))
    return tuple(result)


def solution(mesh):
    placed = (
        P(("groups", "seq"), "wt"),
        P(("groups", "seq"), "wt"),
        P(("groups", "seq"), "wt"),
        P(("groups", "seq"), "wt"),
        P(("groups", "seq")),
        P("wt"),
        P("wt", ("groups", "seq")),
        P("wt"),
    )
    return jax.shard_map(
        shards,
        mesh=mesh,
        in_specs=placed,
        out_specs=(P(("groups", "seq"), "wt"), P(("groups", "seq"), "wt", None, None)),
        check_vma=False,
    )
```

```python
import functools

import jax
import jax.numpy as jnp
from jax import lax
from jax.experimental import pallas as pl
from jax.experimental.pallas import tpu as pltpu
from jax.sharding import PartitionSpec as P

F32 = jnp.float32
BF16 = jnp.bfloat16
NN = (((1,), (0,)), ((), ()))
NT = (((1,), (1,)), ((), ()))
MIB = 1 << 20
SHORT = pl.CostEstimate(flops=1, bytes_accessed=1, transcendentals=0)


def vmem_spec(shape, index_map):
    return pl.BlockSpec(shape, index_map)


def as_column(row, lanes):
    return jnp.broadcast_to(row, (lanes, row.shape[1])).T


def meta_rows(heads):
    return -(-(heads + 1) // 8) * 8


def put_message(msg_ref, first, heads, size, w_ref, finals, end, k_ref, v_ref):
    top = heads * size
    for j in range(heads):
        columns = slice(j * size, (j + 1) * size)
        weight = w_ref[first + j : first + j + 1, :]
        keyed = (k_ref[:, columns].astype(F32).T * weight).astype(BF16)
        msg_ref[columns, :] = lax.dot_general(
            keyed, v_ref[:, columns], NN, preferred_element_type=F32
        )
    msg_ref[top : top + heads, :] = jnp.broadcast_to(finals, (heads, size))
    below = meta_rows(heads) - heads
    msg_ref[top + heads :, :] = jnp.broadcast_to(end.astype(F32), (below, size))


def first_kernel(heads, chunks, order_ref, seg_hbm, exponent_hbm, keep_hbm, k_hbm, v_hbm, *refs):
    number = len(chunks)
    (msg_ref, a_ref, w_ref, seg_ref), refs = refs[:4], refs[4:]
    k_refs, v_refs, refs = refs[:number], refs[number : 2 * number], refs[2 * number :]
    exponent_ref, keep_ref, sems = refs
    tokens = seg_ref.shape[1]
    size = msg_ref.shape[1]
    pairs = [(keep_hbm, keep_ref), (exponent_hbm, exponent_ref), (seg_hbm, seg_ref)]
    for i, (first, many) in enumerate(chunks):
        wide = pl.ds(first * size, many * size)
        pairs += [(k_hbm.at[:, wide], k_refs[i]), (v_hbm.at[:, wide], v_refs[i])]
    copies = [pltpu.make_async_copy(*pair, sems.at[i]) for i, pair in enumerate(pairs)]
    for copy in copies:
        copy.start()
    earlier = lax.broadcasted_iota(jnp.int32, (tokens, tokens), 0)
    later = lax.broadcasted_iota(jnp.int32, (tokens, tokens), 1)
    upper = jnp.where(earlier <= later, 1.0, 0.0).astype(BF16)
    across = lax.broadcasted_iota(jnp.int32, (heads, heads), 1)
    down = lax.broadcasted_iota(jnp.int32, (heads, heads), 0)
    for copy in copies[:3]:
        copy.wait()
    spread = jnp.broadcast_to(exponent_ref[...], (heads, heads))
    exponent = jnp.sum(jnp.where(across == down, spread, 0).astype(F32), axis=1, keepdims=True)
    a = -jnp.exp2(-exponent) + jnp.log(keep_ref[...])
    high = a.astype(BF16)
    rest = a - high.astype(F32)
    middle = rest.astype(BF16)
    low = (rest - middle.astype(F32)).astype(BF16)
    parts = jnp.concatenate([high, middle, low], axis=0)
    sums = lax.dot_general(parts, upper, NN, preferred_element_type=F32)
    cumulative = sums[:heads] + (sums[heads : 2 * heads] + sums[2 * heads :])
    a_ref[...] = cumulative
    final = cumulative[:, tokens - 1 :]
    seg = seg_ref[...]
    last = seg[:, tokens - 1 :]
    w_ref[...] = jnp.where(seg == last, jnp.exp(final - cumulative), 0.0)
    for copy in copies[3:5]:
        copy.wait()
    first, many = chunks[0]
    finals = final[first : first + many]
    put_message(msg_ref, first, many, size, w_ref, finals, last, k_refs[0], v_refs[0])
    for copy in copies[5:]:
        copy.wait()


def message_of(size, many):
    return pltpu.VMEM((many * size + meta_rows(many), size), F32)


def first_message(order, seg, exponent, keep, k, v, heads, chunks):
    tokens, size = k.shape[0], k.shape[1] // heads
    near = [pltpu.VMEM((tokens, many * size), BF16) for _, many in chunks]
    shapes = [message_of(size, chunks[0][1])]
    shapes += [pltpu.VMEM((heads, tokens), F32)] * 2 + [pltpu.VMEM((1, tokens), jnp.int32)]
    shapes += near + near
    number = len(chunks)
    out = pl.pallas_call(
        functools.partial(first_kernel, heads, chunks),
        in_specs=[pl.BlockSpec(memory_space=pltpu.SMEM)]
        + [pl.BlockSpec(memory_space=pltpu.HBM)] * 5,
        out_specs=[pl.BlockSpec(memory_space=pltpu.VMEM)] * len(shapes),
        out_shape=shapes,
        scratch_shapes=[
            pltpu.VMEM((1, heads), jnp.int32),
            pltpu.VMEM((heads, tokens), F32),
            pltpu.SemaphoreType.DMA((3 + 2 * number,)),
        ],
        compiler_params=pltpu.CompilerParams(vmem_limit_bytes=8 * MIB),
        cost_estimate=SHORT,
        name="first_message",
    )(order, seg, exponent, keep, k, v)
    (message, a, w, seg), out = out[:4], out[4:]
    return message, a, w, seg, out[:number], out[number:]


def second_message(seg, a, w, k, v, first, heads):
    tokens, size = k.shape[0], k.shape[1] // heads

    def kernel(seg_ref, a_ref, w_ref, k_ref, v_ref, msg_ref):
        final = a_ref[first : first + heads, tokens - 1 :]
        last = seg_ref[:, tokens - 1 :]
        put_message(msg_ref, first, heads, size, w_ref, final, last, k_ref, v_ref)

    return pl.pallas_call(
        kernel,
        in_specs=[pl.BlockSpec(memory_space=pltpu.VMEM)] * 5,
        out_specs=pl.BlockSpec(memory_space=pltpu.VMEM),
        out_shape=message_of(size, heads),
        compiler_params=pltpu.CompilerParams(vmem_limit_bytes=8 * MIB),
        cost_estimate=SHORT,
        name="second_message",
    )(seg, a, w, k, v)


def rest_kernel(chunks, done, seg_ref, a_ref, w_ref, q_hbm, k_hbm, v_hbm, g_hbm, *refs):
    tokens = seg_ref.shape[1]
    left, number = chunks[done:], len(chunks)
    messages, mask_ref, refs, sems = refs[: len(left)], refs[len(left)], refs[len(left) + 1 : -1], refs[-1]
    k_refs, refs = refs[: len(left)], refs[len(left) :]
    v_refs, refs = refs[: len(left)], refs[len(left) :]
    q_refs, g_refs = refs[:number], refs[number:]
    size = messages[0].shape[1]
    pairs = []
    for i, (first, many) in enumerate(left):
        wide = pl.ds(first * size, many * size)
        pairs += [(k_hbm.at[:, wide], k_refs[i]), (v_hbm.at[:, wide], v_refs[i])]
    for i, (first, many) in enumerate(chunks):
        wide = pl.ds(first * size, many * size)
        pairs += [(q_hbm.at[:, wide], q_refs[i]), (g_hbm.at[:, wide], g_refs[i])]
    copies = [pltpu.make_async_copy(*pair, sems.at[i]) for i, pair in enumerate(pairs)]
    for copy in copies:
        copy.start()
    make_mask(seg_ref, mask_ref)
    last = seg_ref[:, tokens - 1 :]
    for i, (first, many) in enumerate(left):
        copies[2 * i].wait()
        copies[2 * i + 1].wait()
        final = a_ref[first : first + many, tokens - 1 :]
        put_message(messages[i], first, many, size, w_ref, final, last, k_refs[i], v_refs[i])
    for copy in copies[2 * len(left) :]:
        copy.wait()


def rest_messages(seg, a, w, q, k, v, g, chunks, done):
    heads = a.shape[0]
    tokens, size = k.shape[0], k.shape[1] // heads
    near = [pltpu.VMEM((tokens, many * size), BF16) for _, many in chunks]
    shapes = [message_of(size, many) for _, many in chunks[done:]]
    shapes += [pltpu.VMEM((tokens, tokens), F32)] + near[done:] * 2 + near * 2
    left, number = len(chunks) - done, len(chunks)
    out = pl.pallas_call(
        functools.partial(rest_kernel, chunks, done),
        in_specs=[pl.BlockSpec(memory_space=pltpu.VMEM)] * 3
        + [pl.BlockSpec(memory_space=pltpu.HBM)] * 4,
        out_specs=[pl.BlockSpec(memory_space=pltpu.VMEM)] * len(shapes),
        out_shape=shapes,
        scratch_shapes=[pltpu.SemaphoreType.DMA((2 * (left + number),))],
        compiler_params=pltpu.CompilerParams(vmem_limit_bytes=8 * MIB),
        cost_estimate=SHORT,
        name="rest_messages",
    )(seg, a, w, q, k, v, g)
    messages, mask, out = out[:left], out[left], out[left + 1 :]
    k_near, v_near, out = out[:left], out[left : 2 * left], out[2 * left :]
    return messages, mask, k_near, v_near, out[:number], out[number:]


def join_kernel(heads, order_ref, mine_ref, other_ref, out_ref):
    size = mine_ref.shape[1]
    top = heads * size
    mine_later = (order_ref[0] & 1) == 1
    final_mine, final_other = mine_ref[top : top + heads, :], other_ref[top : top + heads, :]
    end_mine, end_other = mine_ref[top + heads :, :], other_ref[top + heads :, :]
    same = jnp.where(end_mine[:1] == end_other[:1], 1.0, 0.0)
    scale_mine = jnp.where(mine_later, 1.0, jnp.exp(final_other) * same)
    scale_other = jnp.where(mine_later, jnp.exp(final_mine) * same, 1.0)
    for head in range(heads):
        rows = slice(head * size, (head + 1) * size)
        out_ref[rows, :] = (
            scale_mine[head : head + 1] * mine_ref[rows, :]
            + scale_other[head : head + 1] * other_ref[rows, :]
        )
    out_ref[top : top + heads, :] = final_mine + final_other
    out_ref[top + heads :, :] = jnp.where(mine_later, end_mine, end_other)


def small_call(kernel, name, order, arrays, after):
    vmem = pl.BlockSpec(memory_space=pltpu.VMEM)
    return pl.pallas_call(
        lambda *refs: kernel(*refs[: 1 + len(arrays)], refs[-1]),
        in_specs=[pl.BlockSpec(memory_space=pltpu.SMEM)]
        + [vmem] * len(arrays)
        + [pl.BlockSpec(memory_space=pl.ANY)] * len(after),
        out_specs=vmem,
        out_shape=pltpu.VMEM(arrays[0].shape, F32),
        compiler_params=pltpu.CompilerParams(vmem_limit_bytes=8 * MIB),
        cost_estimate=SHORT,
        name=name,
    )(order, *arrays, *after)


def joined(order, mine, other, heads, after=()):
    return small_call(
        functools.partial(join_kernel, heads), "join_windows", order, (mine, other), after
    )


def picked(order, even, odd, after=(), through=()):
    vmem = pl.BlockSpec(memory_space=pltpu.VMEM)

    def kernel(order_ref, even_ref, odd_ref, *refs):
        outs = refs[len(through) + len(after) :]
        for source, target in zip(refs, outs[1:]):
            target[...] = source[...]
        odd = (order_ref[0] & 1) == 1

        @pl.when(odd)
        def _():
            outs[0][...] = odd_ref[...]

        @pl.when(jnp.logical_not(odd))
        def _():
            outs[0][...] = even_ref[...]

    return pl.pallas_call(
        kernel,
        in_specs=[pl.BlockSpec(memory_space=pltpu.SMEM)]
        + [vmem] * (2 + len(through))
        + [pl.BlockSpec(memory_space=pl.ANY)] * len(after),
        out_specs=[vmem] * (1 + len(through)),
        out_shape=[pltpu.VMEM(x.shape, F32) for x in (even, *through)],
        compiler_params=pltpu.CompilerParams(vmem_limit_bytes=8 * MIB),
        cost_estimate=SHORT,
        name="pick_message",
    )(order, even, odd, *through, *after)


def make_mask(seg_ref, mask_ref):
    tokens = seg_ref.shape[1]
    seg = seg_ref[...].astype(F32)
    column = as_column(seg, 128)
    for start in range(0, tokens, 128):
        across = lax.broadcasted_iota(jnp.int32, (tokens, 128), 1) + start
        down = lax.broadcasted_iota(jnp.int32, (tokens, 128), 0)
        seen = (column == seg[:, start : start + 128]) & (across <= down)
        mask_ref[:, start : start + 128] = jnp.where(seen, 0.0, -1e30)


def intra_kernel(
    first, heads, through, after, mask_ref, a_ref, gain_ref, q_ref, k_ref, v_ref, g_ref, *refs
):
    o_ref, gate_ref, decay_ref, *copied = refs[through + after :]
    for source, target in zip(refs[:through], copied):
        target[...] = source[...]
    tokens = mask_ref.shape[0]
    size = q_ref.shape[1] // heads
    block = min(tokens, 256)
    for j in range(heads):
        columns = slice(j * size, (j + 1) * size)
        a_row = a_ref[first + j : first + j + 1, :] * 1.4426950408889634
        a_column = as_column(a_row, 128)
        decay_ref[:, columns] = jnp.exp2(a_column)
        for start in range(0, tokens, block):
            here, upto = slice(start, start + block), slice(0, start + block)
            scores = lax.dot_general(
                q_ref[here, columns], k_ref[upto, columns], NT, preferred_element_type=F32
            )
            spread = jnp.concatenate([a_column[here]] * ((start + block) // 128), axis=1)
            weight = jnp.exp2(spread - a_row[:, upto] + mask_ref[here, upto])
            probs = (scores * weight).astype(BF16)
            o_ref[here, columns] = lax.dot_general(
                probs, v_ref[upto, columns], NN, preferred_element_type=F32
            )
        half = 0.5 * size**0.5 * gain_ref[:, (first + j) * size : (first + j + 1) * size]
        gate_ref[:, columns] = half + half * jnp.tanh(0.5 * g_ref[:, columns].astype(F32))


def intra(mask, a, gain, q, k, v, g, first, heads, through=(), after=()):
    tokens, size = mask.shape[0], gain.shape[1] // a.shape[0]
    vmem = pl.BlockSpec(memory_space=pltpu.VMEM)
    o, gate, decay, *copied = pl.pallas_call(
        functools.partial(intra_kernel, first, heads, len(through), len(after)),
        in_specs=[vmem] * (7 + len(through)) + [pl.BlockSpec(memory_space=pl.ANY)] * len(after),
        out_specs=[vmem] * (3 + len(through)),
        out_shape=[pltpu.VMEM((tokens, heads * size), F32)] * 3
        + [pltpu.VMEM(x.shape, x.dtype) for x in through],
        compiler_params=pltpu.CompilerParams(vmem_limit_bytes=8 * MIB),
        cost_estimate=SHORT,
        name="intra_span",
    )(mask, a, gain, q, k, v, g, *through, *after)
    return (o, gate, decay, q), copied


def final_kernel(groups, unread, order_ref, seg_ref, *rest):
    number = len(groups)
    inputs, rest = rest[: 7 * number], rest[7 * number + unread :]
    gated_hbm, snap_hbm, *scratch, inter_ref, sems = rest
    place = order_ref[0]
    seg = seg_ref[...].astype(F32)
    copies, work = [], []

    def send(source, target):
        copies.append(pltpu.make_async_copy(source, target, sems.at[len(copies)]))
        copies[-1].start()

    for i, (first, heads, kind) in enumerate(groups):
        own_ref, near_ref, past_ref = inputs[7 * i : 7 * i + 3]
        gated_ref, snap_ref = scratch[2 * i : 2 * i + 2]
        size = own_ref.shape[1]
        top = heads * size
        ends = slice(top + heads, top + heads + 1)
        finals = slice(top, top + heads)
        own_end, near_end, past_end = own_ref[ends, :], near_ref[ends, :], past_ref[ends, :]
        bridged = jnp.exp(near_ref[finals, :]) * jnp.where(near_end == past_end, 1.0, 0.0)
        if kind == "pair":
            odd = (place & 1) == 1
            previous = jnp.where(odd, near_end, past_end)
            scale_near = jnp.where(odd, 1.0, 0.0)
            scale_past = jnp.where(odd, bridged, 1.0)
        else:
            previous = near_end
            scale_near = jnp.where(place > 0, 1.0, 0.0)
            scale_past = bridged
        scale_past = jnp.where(place >= 2, scale_past, 0.0)
        own_decay = jnp.exp(own_ref[finals, :]) * jnp.where(own_end == previous, 1.0, 0.0)
        number_valid = jnp.sum(
            jnp.where(seg == previous[:, :1], 1.0, 0.0), axis=1, keepdims=True
        )
        for j in range(heads):
            rows = slice(j * size, (j + 1) * size)
            state = scale_past[j : j + 1] * past_ref[rows, :] + scale_near * near_ref[rows, :]
            snap_ref[j] = own_decay[j : j + 1] * state + own_ref[rows, :]
            high = state.astype(BF16)
            low = (state - high.astype(F32)).astype(BF16)
            both = jnp.concatenate([high, low], axis=0)
            work.append((i, j, first, heads, both, number_valid, inputs[7 * i + 3 : 7 * i + 7]))
        send(snap_ref, snap_hbm.at[0, pl.ds(first, heads)])

    rows = lax.broadcasted_iota(jnp.int32, (64, 128), 0).astype(F32)
    for number, (i, j, first, heads, both, number_valid, arrays) in enumerate(work):
        o_ref, gate_ref, decay_ref, q_ref = arrays
        gated_ref = scratch[2 * i]
        tokens, size = seg.shape[1], q_ref.shape[1] // heads
        columns = slice(j * size, (j + 1) * size)
        q = q_ref[:, columns]
        inter_ref[number % 4] = lax.dot_general(
            jnp.concatenate([q, q], axis=1), both, NN, preferred_element_type=F32
        )
        for start in range(0, tokens, 64):
            here = slice(start, start + 64)
            inter = inter_ref[number % 4, here, :]
            inter = jnp.where(rows < number_valid - start, inter * decay_ref[here, columns], 0.0)
            mixed = o_ref[here, columns] + inter
            square = jnp.sum(mixed * mixed, axis=1, keepdims=True)
            gated = mixed * gate_ref[here, columns] * lax.rsqrt(square + size * 1e-06)
            gated_ref[here, columns] = gated.astype(BF16)
            if number == len(work) - 1 and start % 128 == 64:
                block = pl.ds(start - 64, 128)
                there = pl.ds((first + j) * size, size)
                send(gated_ref.at[block, pl.ds(j * size, size)], gated_hbm.at[block, there])
        if number == len(work) - 1:
            continue
        alone = number + 2 == len(work) and j % 2 == 0
        if alone or j % 2 == 1 or j == heads - 1:
            begin = j if alone else j - j % 2
            width = (j + 1 - begin) * size
            there = pl.ds((first + begin) * size, width)
            send(gated_ref.at[:, pl.ds(begin * size, width)], gated_hbm.at[:, there])
    for copy in copies:
        copy.wait()


def finish(order, seg, total, groups, arrays, so_far, after):
    tokens, size = seg.shape[1], arrays[0].shape[1]
    vmem, anywhere = pl.BlockSpec(memory_space=pltpu.VMEM), pl.BlockSpec(memory_space=pl.ANY)
    unread = len(so_far) + len(after)
    scratch = []
    for _, many, _ in groups:
        scratch.append(pltpu.VMEM((tokens, many * size), BF16))
        scratch.append(pltpu.VMEM((many, size, size), F32))
    return pl.pallas_call(
        functools.partial(final_kernel, groups, unread),
        in_specs=[pl.BlockSpec(memory_space=pltpu.SMEM)]
        + [vmem] * (1 + len(arrays))
        + [anywhere] * unread,
        out_specs=[anywhere, anywhere],
        out_shape=[
            jax.ShapeDtypeStruct((tokens, total * size), BF16),
            jax.ShapeDtypeStruct((1, total, size, size), F32),
        ],
        scratch_shapes=scratch
        + [pltpu.VMEM((4, tokens, size), F32), pltpu.SemaphoreType.DMA((2 * total,))],
        input_output_aliases={2 + len(arrays) + i: i for i in range(len(so_far))},
        compiler_params=pltpu.CompilerParams(vmem_limit_bytes=12 * MIB),
        cost_estimate=SHORT,
        name="finish",
    )(order, seg, *arrays, *so_far, *after)


def shards(q, k, v, g, segment, decay_exponent, retention, norm_gain):
    heads = decay_exponent.shape[0]
    tokens = q.shape[0]
    count = lax.axis_size("seq")
    place = lax.axis_index("seq")
    reach = max(1, count // 4)
    far = lambda x: pltpu.with_memory_space_constraint(x, pltpu.HBM)
    q, k, v, g = far(q), far(k), far(v), far(g)
    gain = norm_gain.reshape(1, -1)
    order = jnp.where(place >= 2, 2 + (place & 1), place & 1).astype(jnp.int32).reshape(1)
    later = jnp.ones((1,), jnp.int32)
    swap = lambda x: lax.ppermute(x, "seq", [(c, c ^ 1) for c in range(count)])
    turn = lambda x: lax.ppermute(x, "seq", [(c, (c + 2) % count) for c in range(count)])
    ahead = lambda x: lax.ppermute(x, "seq", [(c, c + 2) for c in range(count - 2)])

    half = heads // 2
    even, odd = half // 2, half // 2
    chunks = [(0, half - even), (half, half - odd), (half - even, even), (heads - odd, odd)]

    def widened(x, many, shift, window):
        while window < reach:
            past = lax.ppermute(x, "seq", [(c, c + shift) for c in range(count - shift)])
            x = joined(later, x, past, many)
            shift, window = 2 * shift, 2 * window
        return x

    message, a, w, seg, k_near, v_near = first_message(
        order,
        far(segment.reshape(1, tokens)),
        far(decay_exponent.reshape(1, heads)),
        far(retention),
        k,
        v,
        heads,
        (chunks[1], chunks[0]),
    )
    k_near, v_near = k_near[::-1], v_near[::-1]
    near, past, inside = {}, {}, {}
    near[1] = swap(message)
    own = [second_message(seg, a, w, k_near[0], v_near[0], *chunks[0]), message]
    past[0] = turn(own[0])
    messages, mask, k_rest, v_rest, q_near, g_near = rest_messages(
        seg, a, w, q, k, v, g, chunks, 2
    )
    own, k_near, v_near = [*own, *messages], [*k_near, *k_rest], [*v_near, *v_rest]

    def look_inside(i, through=(), after=()):
        inside[i], copied = intra(
            mask, a, gain, q_near[i], k_near[i], v_near[i], g_near[i], *chunks[i], through, after
        )
        return copied

    def pair_last(i, after, through=()):
        message, *copied = picked(order, own[i], past[i], after, through)
        near[i] = swap(message)
        return message, *copied

    near[3] = swap(own[3])
    past[2] = turn(own[2])
    look_inside(0)
    both = joined(order, own[1], near[1], chunks[1][1], (inside[0][0],))
    message, both = pair_last(0, (), (both,))
    past[1] = turn(both)
    look_inside(1, (), (message,))
    look_inside(2, (), (inside[1][0],))
    both = joined(order, own[3], near[3], chunks[3][1], (inside[2][0],))
    message, both = pair_last(2, (), (both,))
    past[3] = ahead(both)
    look_inside(3, (), (message,))

    if reach > 2:
        for i, (_, many) in enumerate(chunks):
            past[i] = jnp.where(place >= 2, past[i], 0.0)
            if i % 2 == 0:
                near[i] = jnp.where(place >= 1, near[i], 0.0)
                near[i] = widened(joined(later, near[i], past[i], many), many, 2, 2)
                past[i] = jnp.zeros_like(near[i])
            else:
                past[i] = widened(past[i], many, 2, 2)

    result = ()
    for group in ((0, 1), (2, 3)):
        groups = [(*chunks[i], ("span", "pair")[i % 2]) for i in group]
        arrays = [x for i in group for x in (own[i], near[i], past[i], *inside[i])]
        result = finish(order, seg, heads, groups, arrays, result, (inside[3][0],))
    return tuple(result)


def solution(mesh):
    placed = (
        P(("groups", "seq"), "wt"),
        P(("groups", "seq"), "wt"),
        P(("groups", "seq"), "wt"),
        P(("groups", "seq"), "wt"),
        P(("groups", "seq")),
        P("wt"),
        P("wt", ("groups", "seq")),
        P("wt"),
    )
    return jax.shard_map(
        shards,
        mesh=mesh,
        in_specs=placed,
        out_specs=(P(("groups", "seq"), "wt"), P(("groups", "seq"), "wt", None, None)),
        check_vma=False,
    )
```

```python
import functools

import jax
import jax.numpy as jnp
from jax import lax
from jax.experimental import pallas as pl
from jax.experimental.pallas import tpu as pltpu
from jax.sharding import PartitionSpec as P

F32 = jnp.float32
BF16 = jnp.bfloat16
NN = (((1,), (0,)), ((), ()))
NT = (((1,), (1,)), ((), ()))
MIB = 1 << 20
SHORT = pl.CostEstimate(flops=1, bytes_accessed=1, transcendentals=0)


def vmem_spec(shape, index_map):
    return pl.BlockSpec(shape, index_map)


def as_column(row, lanes):
    return jnp.broadcast_to(row, (lanes, row.shape[1])).T


def meta_rows(heads):
    return -(-(heads + 1) // 8) * 8


def put_message(msg_ref, first, heads, size, w_ref, finals, end, k_ref, v_ref):
    top = heads * size
    for j in range(heads):
        columns = slice(j * size, (j + 1) * size)
        weight = w_ref[first + j : first + j + 1, :]
        keyed = (k_ref[:, columns].astype(F32).T * weight).astype(BF16)
        msg_ref[columns, :] = lax.dot_general(
            keyed, v_ref[:, columns], NN, preferred_element_type=F32
        )
    msg_ref[top : top + heads, :] = jnp.broadcast_to(finals, (heads, size))
    below = meta_rows(heads) - heads
    msg_ref[top + heads :, :] = jnp.broadcast_to(end.astype(F32), (below, size))


def first_kernel(heads, chunks, order_ref, seg_hbm, exponent_hbm, keep_hbm, k_hbm, v_hbm, *refs):
    number = len(chunks)
    (msg_ref, a_ref, w_ref, seg_ref), refs = refs[:4], refs[4:]
    k_refs, v_refs, refs = refs[:number], refs[number : 2 * number], refs[2 * number :]
    exponent_ref, keep_ref, sems = refs
    tokens = seg_ref.shape[1]
    size = msg_ref.shape[1]
    pairs = [(keep_hbm, keep_ref), (exponent_hbm, exponent_ref), (seg_hbm, seg_ref)]
    for i, (first, many) in enumerate(chunks):
        wide = pl.ds(first * size, many * size)
        pairs += [(k_hbm.at[:, wide], k_refs[i]), (v_hbm.at[:, wide], v_refs[i])]
    copies = [pltpu.make_async_copy(*pair, sems.at[i]) for i, pair in enumerate(pairs)]
    for copy in copies:
        copy.start()
    earlier = lax.broadcasted_iota(jnp.int32, (tokens, tokens), 0)
    later = lax.broadcasted_iota(jnp.int32, (tokens, tokens), 1)
    upper = jnp.where(earlier <= later, 1.0, 0.0).astype(BF16)
    across = lax.broadcasted_iota(jnp.int32, (heads, heads), 1)
    down = lax.broadcasted_iota(jnp.int32, (heads, heads), 0)
    for copy in copies[:3]:
        copy.wait()
    spread = jnp.broadcast_to(exponent_ref[...], (heads, heads))
    exponent = jnp.sum(jnp.where(across == down, spread, 0).astype(F32), axis=1, keepdims=True)
    a = -jnp.exp2(-exponent) + jnp.log(keep_ref[...])
    high = a.astype(BF16)
    rest = a - high.astype(F32)
    middle = rest.astype(BF16)
    low = (rest - middle.astype(F32)).astype(BF16)
    parts = jnp.concatenate([high, middle, low], axis=0)
    sums = lax.dot_general(parts, upper, NN, preferred_element_type=F32)
    cumulative = sums[:heads] + (sums[heads : 2 * heads] + sums[2 * heads :])
    a_ref[...] = cumulative
    final = cumulative[:, tokens - 1 :]
    seg = seg_ref[...]
    last = seg[:, tokens - 1 :]
    w_ref[...] = jnp.where(seg == last, jnp.exp(final - cumulative), 0.0)
    for copy in copies[3:5]:
        copy.wait()
    first, many = chunks[0]
    finals = final[first : first + many]
    put_message(msg_ref, first, many, size, w_ref, finals, last, k_refs[0], v_refs[0])
    for copy in copies[5:]:
        copy.wait()


def message_of(size, many):
    return pltpu.VMEM((many * size + meta_rows(many), size), F32)


def first_message(order, seg, exponent, keep, k, v, heads, chunks):
    tokens, size = k.shape[0], k.shape[1] // heads
    near = [pltpu.VMEM((tokens, many * size), BF16) for _, many in chunks]
    shapes = [message_of(size, chunks[0][1])]
    shapes += [pltpu.VMEM((heads, tokens), F32)] * 2 + [pltpu.VMEM((1, tokens), jnp.int32)]
    shapes += near + near
    number = len(chunks)
    out = pl.pallas_call(
        functools.partial(first_kernel, heads, chunks),
        in_specs=[pl.BlockSpec(memory_space=pltpu.SMEM)]
        + [pl.BlockSpec(memory_space=pltpu.HBM)] * 5,
        out_specs=[pl.BlockSpec(memory_space=pltpu.VMEM)] * len(shapes),
        out_shape=shapes,
        scratch_shapes=[
            pltpu.VMEM((1, heads), jnp.int32),
            pltpu.VMEM((heads, tokens), F32),
            pltpu.SemaphoreType.DMA((3 + 2 * number,)),
        ],
        compiler_params=pltpu.CompilerParams(vmem_limit_bytes=8 * MIB),
        cost_estimate=SHORT,
        name="first_message",
    )(order, seg, exponent, keep, k, v)
    (message, a, w, seg), out = out[:4], out[4:]
    return message, a, w, seg, out[:number], out[number:]


def second_message(seg, a, w, k, v, first, heads):
    tokens, size = k.shape[0], k.shape[1] // heads

    def kernel(seg_ref, a_ref, w_ref, k_ref, v_ref, msg_ref):
        final = a_ref[first : first + heads, tokens - 1 :]
        last = seg_ref[:, tokens - 1 :]
        put_message(msg_ref, first, heads, size, w_ref, final, last, k_ref, v_ref)

    return pl.pallas_call(
        kernel,
        in_specs=[pl.BlockSpec(memory_space=pltpu.VMEM)] * 5,
        out_specs=pl.BlockSpec(memory_space=pltpu.VMEM),
        out_shape=message_of(size, heads),
        compiler_params=pltpu.CompilerParams(vmem_limit_bytes=8 * MIB),
        cost_estimate=SHORT,
        name="second_message",
    )(seg, a, w, k, v)


def rest_kernel(chunks, done, seg_ref, a_ref, w_ref, q_hbm, k_hbm, v_hbm, g_hbm, *refs):
    tokens = seg_ref.shape[1]
    left, number = chunks[done:], len(chunks)
    messages, mask_ref, refs, sems = refs[: len(left)], refs[len(left)], refs[len(left) + 1 : -1], refs[-1]
    k_refs, refs = refs[: len(left)], refs[len(left) :]
    v_refs, refs = refs[: len(left)], refs[len(left) :]
    q_refs, g_refs = refs[:number], refs[number:]
    size = messages[0].shape[1]
    pairs = []
    for i, (first, many) in enumerate(left):
        wide = pl.ds(first * size, many * size)
        pairs += [(k_hbm.at[:, wide], k_refs[i]), (v_hbm.at[:, wide], v_refs[i])]
    for i, (first, many) in enumerate(chunks):
        wide = pl.ds(first * size, many * size)
        pairs += [(q_hbm.at[:, wide], q_refs[i]), (g_hbm.at[:, wide], g_refs[i])]
    copies = [pltpu.make_async_copy(*pair, sems.at[i]) for i, pair in enumerate(pairs)]
    for copy in copies:
        copy.start()
    make_mask(seg_ref, mask_ref)
    last = seg_ref[:, tokens - 1 :]
    for i, (first, many) in enumerate(left):
        copies[2 * i].wait()
        copies[2 * i + 1].wait()
        final = a_ref[first : first + many, tokens - 1 :]
        put_message(messages[i], first, many, size, w_ref, final, last, k_refs[i], v_refs[i])
    for copy in copies[2 * len(left) :]:
        copy.wait()


def rest_messages(seg, a, w, q, k, v, g, chunks, done):
    heads = a.shape[0]
    tokens, size = k.shape[0], k.shape[1] // heads
    near = [pltpu.VMEM((tokens, many * size), BF16) for _, many in chunks]
    shapes = [message_of(size, many) for _, many in chunks[done:]]
    shapes += [pltpu.VMEM((tokens, tokens), F32)] + near[done:] * 2 + near * 2
    left, number = len(chunks) - done, len(chunks)
    out = pl.pallas_call(
        functools.partial(rest_kernel, chunks, done),
        in_specs=[pl.BlockSpec(memory_space=pltpu.VMEM)] * 3
        + [pl.BlockSpec(memory_space=pltpu.HBM)] * 4,
        out_specs=[pl.BlockSpec(memory_space=pltpu.VMEM)] * len(shapes),
        out_shape=shapes,
        scratch_shapes=[pltpu.SemaphoreType.DMA((2 * (left + number),))],
        compiler_params=pltpu.CompilerParams(vmem_limit_bytes=8 * MIB),
        cost_estimate=SHORT,
        name="rest_messages",
    )(seg, a, w, q, k, v, g)
    messages, mask, out = out[:left], out[left], out[left + 1 :]
    k_near, v_near, out = out[:left], out[left : 2 * left], out[2 * left :]
    return messages, mask, k_near, v_near, out[:number], out[number:]


def join_kernel(heads, order_ref, mine_ref, other_ref, out_ref):
    size = mine_ref.shape[1]
    top = heads * size
    mine_later = (order_ref[0] & 1) == 1
    final_mine, final_other = mine_ref[top : top + heads, :], other_ref[top : top + heads, :]
    end_mine, end_other = mine_ref[top + heads :, :], other_ref[top + heads :, :]
    same = jnp.where(end_mine[:1] == end_other[:1], 1.0, 0.0)
    scale_mine = jnp.where(mine_later, 1.0, jnp.exp(final_other) * same)
    scale_other = jnp.where(mine_later, jnp.exp(final_mine) * same, 1.0)
    for head in range(heads):
        rows = slice(head * size, (head + 1) * size)
        out_ref[rows, :] = (
            scale_mine[head : head + 1] * mine_ref[rows, :]
            + scale_other[head : head + 1] * other_ref[rows, :]
        )
    out_ref[top : top + heads, :] = final_mine + final_other
    out_ref[top + heads :, :] = jnp.where(mine_later, end_mine, end_other)


def small_call(kernel, name, order, arrays, after):
    vmem = pl.BlockSpec(memory_space=pltpu.VMEM)
    return pl.pallas_call(
        lambda *refs: kernel(*refs[: 1 + len(arrays)], refs[-1]),
        in_specs=[pl.BlockSpec(memory_space=pltpu.SMEM)]
        + [vmem] * len(arrays)
        + [pl.BlockSpec(memory_space=pl.ANY)] * len(after),
        out_specs=vmem,
        out_shape=pltpu.VMEM(arrays[0].shape, F32),
        compiler_params=pltpu.CompilerParams(vmem_limit_bytes=8 * MIB),
        cost_estimate=SHORT,
        name=name,
    )(order, *arrays, *after)


def joined(order, mine, other, heads, after=()):
    return small_call(
        functools.partial(join_kernel, heads), "join_windows", order, (mine, other), after
    )


def picked(order, even, odd, after=(), through=()):
    vmem = pl.BlockSpec(memory_space=pltpu.VMEM)

    def kernel(order_ref, even_ref, odd_ref, *refs):
        outs = refs[len(through) + len(after) :]
        for source, target in zip(refs, outs[1:]):
            target[...] = source[...]
        odd = (order_ref[0] & 1) == 1

        @pl.when(odd)
        def _():
            outs[0][...] = odd_ref[...]

        @pl.when(jnp.logical_not(odd))
        def _():
            outs[0][...] = even_ref[...]

    return pl.pallas_call(
        kernel,
        in_specs=[pl.BlockSpec(memory_space=pltpu.SMEM)]
        + [vmem] * (2 + len(through))
        + [pl.BlockSpec(memory_space=pl.ANY)] * len(after),
        out_specs=[vmem] * (1 + len(through)),
        out_shape=[pltpu.VMEM(x.shape, F32) for x in (even, *through)],
        compiler_params=pltpu.CompilerParams(vmem_limit_bytes=8 * MIB),
        cost_estimate=SHORT,
        name="pick_message",
    )(order, even, odd, *through, *after)


def make_mask(seg_ref, mask_ref):
    tokens = seg_ref.shape[1]
    seg = seg_ref[...].astype(F32)
    column = as_column(seg, 128)
    for start in range(0, tokens, 128):
        across = lax.broadcasted_iota(jnp.int32, (tokens, 128), 1) + start
        down = lax.broadcasted_iota(jnp.int32, (tokens, 128), 0)
        seen = (column == seg[:, start : start + 128]) & (across <= down)
        mask_ref[:, start : start + 128] = jnp.where(seen, 0.0, -1e30)


def intra_kernel(
    first, heads, through, after, mask_ref, a_ref, gain_ref, q_ref, k_ref, v_ref, g_ref, *refs
):
    o_ref, gate_ref, decay_ref, *copied = refs[through + after :]
    for source, target in zip(refs[:through], copied):
        target[...] = source[...]
    tokens = mask_ref.shape[0]
    size = q_ref.shape[1] // heads
    block = min(tokens, 256)
    for j in range(heads):
        columns = slice(j * size, (j + 1) * size)
        a_row = a_ref[first + j : first + j + 1, :] * 1.4426950408889634
        a_column = as_column(a_row, 128)
        decay_ref[:, columns] = jnp.exp2(a_column)
        for start in range(0, tokens, block):
            here, upto = slice(start, start + block), slice(0, start + block)
            scores = lax.dot_general(
                q_ref[here, columns], k_ref[upto, columns], NT, preferred_element_type=F32
            )
            spread = jnp.concatenate([a_column[here]] * ((start + block) // 128), axis=1)
            weight = jnp.exp2(spread - a_row[:, upto] + mask_ref[here, upto])
            probs = (scores * weight).astype(BF16)
            o_ref[here, columns] = lax.dot_general(
                probs, v_ref[upto, columns], NN, preferred_element_type=F32
            )
        half = 0.5 * size**0.5 * gain_ref[:, (first + j) * size : (first + j + 1) * size]
        gate_ref[:, columns] = half + half * jnp.tanh(0.5 * g_ref[:, columns].astype(F32))


def intra(mask, a, gain, q, k, v, g, first, heads, through=(), after=()):
    tokens, size = mask.shape[0], gain.shape[1] // a.shape[0]
    vmem = pl.BlockSpec(memory_space=pltpu.VMEM)
    o, gate, decay, *copied = pl.pallas_call(
        functools.partial(intra_kernel, first, heads, len(through), len(after)),
        in_specs=[vmem] * (7 + len(through)) + [pl.BlockSpec(memory_space=pl.ANY)] * len(after),
        out_specs=[vmem] * (3 + len(through)),
        out_shape=[pltpu.VMEM((tokens, heads * size), F32)] * 3
        + [pltpu.VMEM(x.shape, x.dtype) for x in through],
        compiler_params=pltpu.CompilerParams(vmem_limit_bytes=8 * MIB),
        cost_estimate=SHORT,
        name="intra_span",
    )(mask, a, gain, q, k, v, g, *through, *after)
    return (o, gate, decay, q), copied


def final_kernel(groups, unread, order_ref, seg_ref, *rest):
    number = len(groups)
    inputs, rest = rest[: 7 * number], rest[7 * number + unread :]
    gated_hbm, snap_hbm, *scratch, inter_ref, sems = rest
    place = order_ref[0]
    seg = seg_ref[...].astype(F32)
    copies, work = [], []

    def send(source, target):
        copies.append(pltpu.make_async_copy(source, target, sems.at[len(copies)]))
        copies[-1].start(priority=len(copies) % 2)

    for i, (first, heads, kind) in enumerate(groups):
        own_ref, near_ref, past_ref = inputs[7 * i : 7 * i + 3]
        gated_ref, snap_ref = scratch[2 * i : 2 * i + 2]
        size = own_ref.shape[1]
        top = heads * size
        ends = slice(top + heads, top + heads + 1)
        finals = slice(top, top + heads)
        own_end, near_end, past_end = own_ref[ends, :], near_ref[ends, :], past_ref[ends, :]
        bridged = jnp.exp(near_ref[finals, :]) * jnp.where(near_end == past_end, 1.0, 0.0)
        if kind == "pair":
            odd = (place & 1) == 1
            previous = jnp.where(odd, near_end, past_end)
            scale_near = jnp.where(odd, 1.0, 0.0)
            scale_past = jnp.where(odd, bridged, 1.0)
        else:
            previous = near_end
            scale_near = jnp.where(place > 0, 1.0, 0.0)
            scale_past = bridged
        scale_past = jnp.where(place >= 2, scale_past, 0.0)
        own_decay = jnp.exp(own_ref[finals, :]) * jnp.where(own_end == previous, 1.0, 0.0)
        number_valid = jnp.sum(
            jnp.where(seg == previous[:, :1], 1.0, 0.0), axis=1, keepdims=True
        )
        for j in range(heads):
            rows = slice(j * size, (j + 1) * size)
            state = scale_past[j : j + 1] * past_ref[rows, :] + scale_near * near_ref[rows, :]
            snap_ref[j] = own_decay[j : j + 1] * state + own_ref[rows, :]
            high = state.astype(BF16)
            low = (state - high.astype(F32)).astype(BF16)
            both = jnp.concatenate([high, low], axis=0)
            work.append((i, j, first, heads, both, number_valid, inputs[7 * i + 3 : 7 * i + 7]))
        send(snap_ref, snap_hbm.at[0, pl.ds(first, heads)])

    rows = lax.broadcasted_iota(jnp.int32, (64, 128), 0).astype(F32)
    for number, (i, j, first, heads, both, number_valid, arrays) in enumerate(work):
        o_ref, gate_ref, decay_ref, q_ref = arrays
        gated_ref = scratch[2 * i]
        tokens, size = seg.shape[1], q_ref.shape[1] // heads
        columns = slice(j * size, (j + 1) * size)
        q = q_ref[:, columns]
        inter_ref[number % 4] = lax.dot_general(
            jnp.concatenate([q, q], axis=1), both, NN, preferred_element_type=F32
        )
        for start in range(0, tokens, 64):
            here = slice(start, start + 64)
            inter = inter_ref[number % 4, here, :]
            inter = jnp.where(rows < number_valid - start, inter * decay_ref[here, columns], 0.0)
            mixed = o_ref[here, columns] + inter
            square = jnp.sum(mixed * mixed, axis=1, keepdims=True)
            gated = mixed * gate_ref[here, columns] * lax.rsqrt(square + size * 1e-06)
            gated_ref[here, columns] = gated.astype(BF16)
            if number == len(work) - 1 and start % 128 == 64:
                block = pl.ds(start - 64, 128)
                there = pl.ds((first + j) * size, size)
                send(gated_ref.at[block, pl.ds(j * size, size)], gated_hbm.at[block, there])
        if number == len(work) - 1:
            continue
        alone = number + 2 == len(work) and j % 2 == 0
        if alone or j % 2 == 1 or j == heads - 1:
            begin = j if alone else j - j % 2
            width = (j + 1 - begin) * size
            there = pl.ds((first + begin) * size, width)
            send(gated_ref.at[:, pl.ds(begin * size, width)], gated_hbm.at[:, there])
    for copy in copies:
        copy.wait()


def finish(order, seg, total, groups, arrays, so_far, after):
    tokens, size = seg.shape[1], arrays[0].shape[1]
    vmem, anywhere = pl.BlockSpec(memory_space=pltpu.VMEM), pl.BlockSpec(memory_space=pl.ANY)
    unread = len(so_far) + len(after)
    scratch = []
    for _, many, _ in groups:
        scratch.append(pltpu.VMEM((tokens, many * size), BF16))
        scratch.append(pltpu.VMEM((many, size, size), F32))
    return pl.pallas_call(
        functools.partial(final_kernel, groups, unread),
        in_specs=[pl.BlockSpec(memory_space=pltpu.SMEM)]
        + [vmem] * (1 + len(arrays))
        + [anywhere] * unread,
        out_specs=[anywhere, anywhere],
        out_shape=[
            jax.ShapeDtypeStruct((tokens, total * size), BF16),
            jax.ShapeDtypeStruct((1, total, size, size), F32),
        ],
        scratch_shapes=scratch
        + [pltpu.VMEM((4, tokens, size), F32), pltpu.SemaphoreType.DMA((2 * total,))],
        input_output_aliases={2 + len(arrays) + i: i for i in range(len(so_far))},
        compiler_params=pltpu.CompilerParams(vmem_limit_bytes=12 * MIB),
        cost_estimate=SHORT,
        name="finish",
    )(order, seg, *arrays, *so_far, *after)


def shards(q, k, v, g, segment, decay_exponent, retention, norm_gain):
    heads = decay_exponent.shape[0]
    tokens = q.shape[0]
    count = lax.axis_size("seq")
    place = lax.axis_index("seq")
    reach = max(1, count // 4)
    far = lambda x: pltpu.with_memory_space_constraint(x, pltpu.HBM)
    q, k, v, g = far(q), far(k), far(v), far(g)
    gain = norm_gain.reshape(1, -1)
    order = jnp.where(place >= 2, 2 + (place & 1), place & 1).astype(jnp.int32).reshape(1)
    later = jnp.ones((1,), jnp.int32)
    swap = lambda x: lax.ppermute(x, "seq", [(c, c ^ 1) for c in range(count)])
    turn = lambda x: lax.ppermute(x, "seq", [(c, (c + 2) % count) for c in range(count)])
    ahead = lambda x: lax.ppermute(x, "seq", [(c, c + 2) for c in range(count - 2)])

    half = heads // 2
    even, odd = half // 2, half // 2
    chunks = [(0, half - even), (half, half - odd), (half - even, even), (heads - odd, odd)]

    def widened(x, many, shift, window):
        while window < reach:
            past = lax.ppermute(x, "seq", [(c, c + shift) for c in range(count - shift)])
            x = joined(later, x, past, many)
            shift, window = 2 * shift, 2 * window
        return x

    message, a, w, seg, k_near, v_near = first_message(
        order,
        far(segment.reshape(1, tokens)),
        far(decay_exponent.reshape(1, heads)),
        far(retention),
        k,
        v,
        heads,
        (chunks[1], chunks[0]),
    )
    k_near, v_near = k_near[::-1], v_near[::-1]
    near, past, inside = {}, {}, {}
    near[1] = swap(message)
    own = [second_message(seg, a, w, k_near[0], v_near[0], *chunks[0]), message]
    past[0] = turn(own[0])
    messages, mask, k_rest, v_rest, q_near, g_near = rest_messages(
        seg, a, w, q, k, v, g, chunks, 2
    )
    own, k_near, v_near = [*own, *messages], [*k_near, *k_rest], [*v_near, *v_rest]

    def look_inside(i, through=(), after=()):
        inside[i], copied = intra(
            mask, a, gain, q_near[i], k_near[i], v_near[i], g_near[i], *chunks[i], through, after
        )
        return copied

    def pair_last(i, after, through=()):
        message, *copied = picked(order, own[i], past[i], after, through)
        near[i] = swap(message)
        return message, *copied

    near[3] = swap(own[3])
    past[2] = turn(own[2])
    look_inside(0)
    both = joined(order, own[1], near[1], chunks[1][1], (inside[0][0],))
    message, both = pair_last(0, (), (both,))
    past[1] = turn(both)
    look_inside(1, (), (message,))
    look_inside(2, (), (inside[1][0],))
    both = joined(order, own[3], near[3], chunks[3][1], (inside[2][0],))
    message, both = pair_last(2, (), (both,))
    past[3] = ahead(both)
    look_inside(3, (), (message,))

    if reach > 2:
        for i, (_, many) in enumerate(chunks):
            past[i] = jnp.where(place >= 2, past[i], 0.0)
            if i % 2 == 0:
                near[i] = jnp.where(place >= 1, near[i], 0.0)
                near[i] = widened(joined(later, near[i], past[i], many), many, 2, 2)
                past[i] = jnp.zeros_like(near[i])
            else:
                past[i] = widened(past[i], many, 2, 2)

    result = ()
    for group in ((0, 1), (2, 3)):
        groups = [(*chunks[i], ("span", "pair")[i % 2]) for i in group]
        arrays = [x for i in group for x in (own[i], near[i], past[i], *inside[i])]
        result = finish(order, seg, heads, groups, arrays, result, (inside[3][0],))
    return tuple(result)


def solution(mesh):
    placed = (
        P(("groups", "seq"), "wt"),
        P(("groups", "seq"), "wt"),
        P(("groups", "seq"), "wt"),
        P(("groups", "seq"), "wt"),
        P(("groups", "seq")),
        P("wt"),
        P("wt", ("groups", "seq")),
        P("wt"),
    )
    return jax.shard_map(
        shards,
        mesh=mesh,
        in_specs=placed,
        out_specs=(P(("groups", "seq"), "wt"), P(("groups", "seq"), "wt", None, None)),
        check_vma=False,
    )
```

```python
import functools

import jax
import jax.numpy as jnp
from jax import lax
from jax.experimental import pallas as pl
from jax.experimental.pallas import tpu as pltpu
from jax.sharding import PartitionSpec as P

F32 = jnp.float32
BF16 = jnp.bfloat16
NN = (((1,), (0,)), ((), ()))
NT = (((1,), (1,)), ((), ()))
MIB = 1 << 20
SHORT = pl.CostEstimate(flops=1, bytes_accessed=1, transcendentals=0)


def vmem_spec(shape, index_map):
    return pl.BlockSpec(shape, index_map)


def as_column(row, lanes):
    return jnp.broadcast_to(row, (lanes, row.shape[1])).T


def meta_rows(heads):
    return -(-(heads + 1) // 8) * 8


def put_message(msg_ref, first, heads, size, w_ref, finals, end, k_ref, v_ref):
    top = heads * size
    for j in range(heads):
        columns = slice(j * size, (j + 1) * size)
        weight = w_ref[first + j : first + j + 1, :]
        keyed = (k_ref[:, columns].astype(F32).T * weight).astype(BF16)
        msg_ref[columns, :] = lax.dot_general(
            keyed, v_ref[:, columns], NN, preferred_element_type=F32
        )
    msg_ref[top : top + heads, :] = jnp.broadcast_to(finals, (heads, size))
    below = meta_rows(heads) - heads
    msg_ref[top + heads :, :] = jnp.broadcast_to(end.astype(F32), (below, size))


def first_kernel(heads, chunks, order_ref, seg_hbm, exponent_hbm, keep_hbm, k_hbm, v_hbm, *refs):
    number = len(chunks)
    (msg_ref, a_ref, w_ref, seg_ref), refs = refs[:4], refs[4:]
    k_refs, v_refs, refs = refs[:number], refs[number : 2 * number], refs[2 * number :]
    exponent_ref, keep_ref, sems = refs
    tokens = seg_ref.shape[1]
    size = msg_ref.shape[1]
    pairs = [(keep_hbm, keep_ref), (exponent_hbm, exponent_ref), (seg_hbm, seg_ref)]
    for i, (first, many) in enumerate(chunks):
        wide = pl.ds(first * size, many * size)
        pairs += [(k_hbm.at[:, wide], k_refs[i]), (v_hbm.at[:, wide], v_refs[i])]
    copies = [pltpu.make_async_copy(*pair, sems.at[i]) for i, pair in enumerate(pairs)]
    for copy in copies:
        copy.start()
    earlier = lax.broadcasted_iota(jnp.int32, (tokens, tokens), 0)
    later = lax.broadcasted_iota(jnp.int32, (tokens, tokens), 1)
    upper = jnp.where(earlier <= later, 1.0, 0.0).astype(BF16)
    across = lax.broadcasted_iota(jnp.int32, (heads, heads), 1)
    down = lax.broadcasted_iota(jnp.int32, (heads, heads), 0)
    for copy in copies[:3]:
        copy.wait()
    spread = jnp.broadcast_to(exponent_ref[...], (heads, heads))
    exponent = jnp.sum(jnp.where(across == down, spread, 0).astype(F32), axis=1, keepdims=True)
    a = -jnp.exp2(-exponent) + jnp.log(keep_ref[...])
    high = a.astype(BF16)
    rest = a - high.astype(F32)
    middle = rest.astype(BF16)
    low = (rest - middle.astype(F32)).astype(BF16)
    parts = jnp.concatenate([high, middle, low], axis=0)
    sums = lax.dot_general(parts, upper, NN, preferred_element_type=F32)
    cumulative = sums[:heads] + (sums[heads : 2 * heads] + sums[2 * heads :])
    a_ref[...] = cumulative
    final = cumulative[:, tokens - 1 :]
    seg = seg_ref[...]
    last = seg[:, tokens - 1 :]
    w_ref[...] = jnp.where(seg == last, jnp.exp(final - cumulative), 0.0)
    for copy in copies[3:5]:
        copy.wait()
    first, many = chunks[0]
    finals = final[first : first + many]
    put_message(msg_ref, first, many, size, w_ref, finals, last, k_refs[0], v_refs[0])
    for copy in copies[5:]:
        copy.wait()


def message_of(size, many):
    return pltpu.VMEM((many * size + meta_rows(many), size), F32)


def first_message(order, seg, exponent, keep, k, v, heads, chunks):
    tokens, size = k.shape[0], k.shape[1] // heads
    near = [pltpu.VMEM((tokens, many * size), BF16) for _, many in chunks]
    shapes = [message_of(size, chunks[0][1])]
    shapes += [pltpu.VMEM((heads, tokens), F32)] * 2 + [pltpu.VMEM((1, tokens), jnp.int32)]
    shapes += near + near
    number = len(chunks)
    out = pl.pallas_call(
        functools.partial(first_kernel, heads, chunks),
        in_specs=[pl.BlockSpec(memory_space=pltpu.SMEM)]
        + [pl.BlockSpec(memory_space=pltpu.HBM)] * 5,
        out_specs=[pl.BlockSpec(memory_space=pltpu.VMEM)] * len(shapes),
        out_shape=shapes,
        scratch_shapes=[
            pltpu.VMEM((1, heads), jnp.int32),
            pltpu.VMEM((heads, tokens), F32),
            pltpu.SemaphoreType.DMA((3 + 2 * number,)),
        ],
        compiler_params=pltpu.CompilerParams(vmem_limit_bytes=8 * MIB),
        cost_estimate=SHORT,
        name="first_message",
    )(order, seg, exponent, keep, k, v)
    (message, a, w, seg), out = out[:4], out[4:]
    return message, a, w, seg, out[:number], out[number:]


def second_message(seg, a, w, k, v, first, heads):
    tokens, size = k.shape[0], k.shape[1] // heads

    def kernel(seg_ref, a_ref, w_ref, k_ref, v_ref, msg_ref):
        final = a_ref[first : first + heads, tokens - 1 :]
        last = seg_ref[:, tokens - 1 :]
        put_message(msg_ref, first, heads, size, w_ref, final, last, k_ref, v_ref)

    return pl.pallas_call(
        kernel,
        in_specs=[pl.BlockSpec(memory_space=pltpu.VMEM)] * 5,
        out_specs=pl.BlockSpec(memory_space=pltpu.VMEM),
        out_shape=message_of(size, heads),
        compiler_params=pltpu.CompilerParams(vmem_limit_bytes=8 * MIB),
        cost_estimate=SHORT,
        name="second_message",
    )(seg, a, w, k, v)


def rest_kernel(chunks, done, seg_ref, a_ref, w_ref, q_hbm, k_hbm, v_hbm, g_hbm, *refs):
    tokens = seg_ref.shape[1]
    left, number = chunks[done:], len(chunks)
    messages, mask_ref, refs, sems = refs[: len(left)], refs[len(left)], refs[len(left) + 1 : -1], refs[-1]
    k_refs, refs = refs[: len(left)], refs[len(left) :]
    v_refs, refs = refs[: len(left)], refs[len(left) :]
    q_refs, g_refs = refs[:number], refs[number:]
    size = messages[0].shape[1]
    pairs = []
    for i, (first, many) in enumerate(left):
        wide = pl.ds(first * size, many * size)
        pairs += [(k_hbm.at[:, wide], k_refs[i]), (v_hbm.at[:, wide], v_refs[i])]
    for i, (first, many) in enumerate(chunks):
        wide = pl.ds(first * size, many * size)
        pairs += [(q_hbm.at[:, wide], q_refs[i]), (g_hbm.at[:, wide], g_refs[i])]
    copies = [pltpu.make_async_copy(*pair, sems.at[i]) for i, pair in enumerate(pairs)]
    for copy in copies:
        copy.start()
    make_mask(seg_ref, mask_ref)
    last = seg_ref[:, tokens - 1 :]
    for i, (first, many) in enumerate(left):
        copies[2 * i].wait()
        copies[2 * i + 1].wait()
        final = a_ref[first : first + many, tokens - 1 :]
        put_message(messages[i], first, many, size, w_ref, final, last, k_refs[i], v_refs[i])
    for copy in copies[2 * len(left) :]:
        copy.wait()


def rest_messages(seg, a, w, q, k, v, g, chunks, done):
    heads = a.shape[0]
    tokens, size = k.shape[0], k.shape[1] // heads
    near = [pltpu.VMEM((tokens, many * size), BF16) for _, many in chunks]
    shapes = [message_of(size, many) for _, many in chunks[done:]]
    shapes += [pltpu.VMEM((tokens, tokens), F32)] + near[done:] * 2 + near * 2
    left, number = len(chunks) - done, len(chunks)
    out = pl.pallas_call(
        functools.partial(rest_kernel, chunks, done),
        in_specs=[pl.BlockSpec(memory_space=pltpu.VMEM)] * 3
        + [pl.BlockSpec(memory_space=pltpu.HBM)] * 4,
        out_specs=[pl.BlockSpec(memory_space=pltpu.VMEM)] * len(shapes),
        out_shape=shapes,
        scratch_shapes=[pltpu.SemaphoreType.DMA((2 * (left + number),))],
        compiler_params=pltpu.CompilerParams(vmem_limit_bytes=8 * MIB),
        cost_estimate=SHORT,
        name="rest_messages",
    )(seg, a, w, q, k, v, g)
    messages, mask, out = out[:left], out[left], out[left + 1 :]
    k_near, v_near, out = out[:left], out[left : 2 * left], out[2 * left :]
    return messages, mask, k_near, v_near, out[:number], out[number:]


def join_kernel(heads, order_ref, mine_ref, other_ref, out_ref):
    size = mine_ref.shape[1]
    top = heads * size
    mine_later = (order_ref[0] & 1) == 1
    final_mine, final_other = mine_ref[top : top + heads, :], other_ref[top : top + heads, :]
    end_mine, end_other = mine_ref[top + heads :, :], other_ref[top + heads :, :]
    same = jnp.where(end_mine[:1] == end_other[:1], 1.0, 0.0)
    scale_mine = jnp.where(mine_later, 1.0, jnp.exp(final_other) * same)
    scale_other = jnp.where(mine_later, jnp.exp(final_mine) * same, 1.0)
    for head in range(heads):
        rows = slice(head * size, (head + 1) * size)
        out_ref[rows, :] = (
            scale_mine[head : head + 1] * mine_ref[rows, :]
            + scale_other[head : head + 1] * other_ref[rows, :]
        )
    out_ref[top : top + heads, :] = final_mine + final_other
    out_ref[top + heads :, :] = jnp.where(mine_later, end_mine, end_other)


def small_call(kernel, name, order, arrays, after):
    vmem = pl.BlockSpec(memory_space=pltpu.VMEM)
    return pl.pallas_call(
        lambda *refs: kernel(*refs[: 1 + len(arrays)], refs[-1]),
        in_specs=[pl.BlockSpec(memory_space=pltpu.SMEM)]
        + [vmem] * len(arrays)
        + [pl.BlockSpec(memory_space=pl.ANY)] * len(after),
        out_specs=vmem,
        out_shape=pltpu.VMEM(arrays[0].shape, F32),
        compiler_params=pltpu.CompilerParams(vmem_limit_bytes=8 * MIB),
        cost_estimate=SHORT,
        name=name,
    )(order, *arrays, *after)


def joined(order, mine, other, heads, after=()):
    return small_call(
        functools.partial(join_kernel, heads), "join_windows", order, (mine, other), after
    )


def picked(order, even, odd, after=(), through=()):
    vmem = pl.BlockSpec(memory_space=pltpu.VMEM)

    def kernel(order_ref, even_ref, odd_ref, *refs):
        outs = refs[len(through) + len(after) :]
        for source, target in zip(refs, outs[1:]):
            target[...] = source[...]
        odd = (order_ref[0] & 1) == 1

        @pl.when(odd)
        def _():
            outs[0][...] = odd_ref[...]

        @pl.when(jnp.logical_not(odd))
        def _():
            outs[0][...] = even_ref[...]

    return pl.pallas_call(
        kernel,
        in_specs=[pl.BlockSpec(memory_space=pltpu.SMEM)]
        + [vmem] * (2 + len(through))
        + [pl.BlockSpec(memory_space=pl.ANY)] * len(after),
        out_specs=[vmem] * (1 + len(through)),
        out_shape=[pltpu.VMEM(x.shape, F32) for x in (even, *through)],
        compiler_params=pltpu.CompilerParams(vmem_limit_bytes=8 * MIB),
        cost_estimate=SHORT,
        name="pick_message",
    )(order, even, odd, *through, *after)


def make_mask(seg_ref, mask_ref):
    tokens = seg_ref.shape[1]
    seg = seg_ref[...].astype(F32)
    column = as_column(seg, 128)
    for start in range(0, tokens, 128):
        across = lax.broadcasted_iota(jnp.int32, (tokens, 128), 1) + start
        down = lax.broadcasted_iota(jnp.int32, (tokens, 128), 0)
        seen = (column == seg[:, start : start + 128]) & (across <= down)
        mask_ref[:, start : start + 128] = jnp.where(seen, 0.0, -1e30)


def intra_kernel(
    first, heads, through, after, mask_ref, a_ref, gain_ref, q_ref, k_ref, v_ref, g_ref, *refs
):
    o_ref, gate_ref, decay_ref, *copied = refs[through + after :]
    for source, target in zip(refs[:through], copied):
        target[...] = source[...]
    tokens = mask_ref.shape[0]
    size = q_ref.shape[1] // heads
    block = min(tokens, 256)
    for j in range(heads):
        columns = slice(j * size, (j + 1) * size)
        a_row = a_ref[first + j : first + j + 1, :] * 1.4426950408889634
        a_column = as_column(a_row, 128)
        decay_ref[:, columns] = jnp.exp2(a_column)
        for start in range(0, tokens, block):
            here, upto = slice(start, start + block), slice(0, start + block)
            scores = lax.dot_general(
                q_ref[here, columns], k_ref[upto, columns], NT, preferred_element_type=F32
            )
            spread = jnp.concatenate([a_column[here]] * ((start + block) // 128), axis=1)
            weight = jnp.exp2(spread - a_row[:, upto] + mask_ref[here, upto])
            probs = (scores * weight).astype(BF16)
            o_ref[here, columns] = lax.dot_general(
                probs, v_ref[upto, columns], NN, preferred_element_type=F32
            )
        half = 0.5 * size**0.5 * gain_ref[:, (first + j) * size : (first + j + 1) * size]
        gate_ref[:, columns] = half + half * jnp.tanh(0.5 * g_ref[:, columns].astype(F32))


def intra(mask, a, gain, q, k, v, g, first, heads, through=(), after=()):
    tokens, size = mask.shape[0], gain.shape[1] // a.shape[0]
    vmem = pl.BlockSpec(memory_space=pltpu.VMEM)
    o, gate, decay, *copied = pl.pallas_call(
        functools.partial(intra_kernel, first, heads, len(through), len(after)),
        in_specs=[vmem] * (7 + len(through)) + [pl.BlockSpec(memory_space=pl.ANY)] * len(after),
        out_specs=[vmem] * (3 + len(through)),
        out_shape=[pltpu.VMEM((tokens, heads * size), F32)] * 3
        + [pltpu.VMEM(x.shape, x.dtype) for x in through],
        compiler_params=pltpu.CompilerParams(vmem_limit_bytes=8 * MIB),
        cost_estimate=SHORT,
        name="intra_span",
    )(mask, a, gain, q, k, v, g, *through, *after)
    return (o, gate, decay, q), copied


def final_kernel(groups, unread, order_ref, seg_ref, *rest):
    number = len(groups)
    inputs, rest = rest[: 7 * number], rest[7 * number + unread :]
    gated_hbm, snap_hbm, *scratch, inter_ref, sems = rest
    place = order_ref[0]
    seg = seg_ref[...].astype(F32)
    copies, work = [], []

    def send(source, target):
        copies.append(pltpu.make_async_copy(source, target, sems.at[len(copies)]))
        copies[-1].start()

    for i, (first, heads, kind) in enumerate(groups):
        own_ref, near_ref, past_ref = inputs[7 * i : 7 * i + 3]
        gated_ref, snap_ref = scratch[2 * i : 2 * i + 2]
        size = own_ref.shape[1]
        top = heads * size
        ends = slice(top + heads, top + heads + 1)
        finals = slice(top, top + heads)
        own_end, near_end, past_end = own_ref[ends, :], near_ref[ends, :], past_ref[ends, :]
        bridged = jnp.exp(near_ref[finals, :]) * jnp.where(near_end == past_end, 1.0, 0.0)
        if kind == "pair":
            odd = (place & 1) == 1
            previous = jnp.where(odd, near_end, past_end)
            scale_near = jnp.where(odd, 1.0, 0.0)
            scale_past = jnp.where(odd, bridged, 1.0)
        else:
            previous = near_end
            scale_near = jnp.where(place > 0, 1.0, 0.0)
            scale_past = bridged
        scale_past = jnp.where(place >= 2, scale_past, 0.0)
        own_decay = jnp.exp(own_ref[finals, :]) * jnp.where(own_end == previous, 1.0, 0.0)
        number_valid = jnp.sum(
            jnp.where(seg == previous[:, :1], 1.0, 0.0), axis=1, keepdims=True
        )
        for j in range(heads):
            rows = slice(j * size, (j + 1) * size)
            state = scale_past[j : j + 1] * past_ref[rows, :] + scale_near * near_ref[rows, :]
            snap_ref[j] = own_decay[j : j + 1] * state + own_ref[rows, :]
            high = state.astype(BF16)
            low = (state - high.astype(F32)).astype(BF16)
            both = jnp.concatenate([high, low], axis=0)
            work.append((i, j, first, heads, both, number_valid, inputs[7 * i + 3 : 7 * i + 7]))
        send(snap_ref, snap_hbm.at[0, pl.ds(first, heads)])

    rows = lax.broadcasted_iota(jnp.int32, (32, 128), 0).astype(F32)
    for number, (i, j, first, heads, both, number_valid, arrays) in enumerate(work):
        o_ref, gate_ref, decay_ref, q_ref = arrays
        gated_ref = scratch[2 * i]
        tokens, size = seg.shape[1], q_ref.shape[1] // heads
        columns = slice(j * size, (j + 1) * size)
        q = q_ref[:, columns]
        inter_ref[number % 4] = lax.dot_general(
            jnp.concatenate([q, q], axis=1), both, NN, preferred_element_type=F32
        )
        for start in range(0, tokens, 32):
            here = slice(start, start + 32)
            inter = inter_ref[number % 4, here, :]
            inter = jnp.where(rows < number_valid - start, inter * decay_ref[here, columns], 0.0)
            mixed = o_ref[here, columns] + inter
            square = jnp.sum(mixed * mixed, axis=1, keepdims=True)
            gated = mixed * gate_ref[here, columns] * lax.rsqrt(square + size * 1e-06)
            gated_ref[here, columns] = gated.astype(BF16)
            if number == len(work) - 1 and start % 128 == 96:
                block = pl.ds(start - 96, 128)
                there = pl.ds((first + j) * size, size)
                send(gated_ref.at[block, pl.ds(j * size, size)], gated_hbm.at[block, there])
        if number == len(work) - 1:
            continue
        alone = number + 2 == len(work) and j % 2 == 0
        if alone or j % 2 == 1 or j == heads - 1:
            begin = j if alone else j - j % 2
            width = (j + 1 - begin) * size
            there = pl.ds((first + begin) * size, width)
            send(gated_ref.at[:, pl.ds(begin * size, width)], gated_hbm.at[:, there])
    for copy in copies:
        copy.wait()


def finish(order, seg, total, groups, arrays, so_far, after):
    tokens, size = seg.shape[1], arrays[0].shape[1]
    vmem, anywhere = pl.BlockSpec(memory_space=pltpu.VMEM), pl.BlockSpec(memory_space=pl.ANY)
    unread = len(so_far) + len(after)
    scratch = []
    for _, many, _ in groups:
        scratch.append(pltpu.VMEM((tokens, many * size), BF16))
        scratch.append(pltpu.VMEM((many, size, size), F32))
    return pl.pallas_call(
        functools.partial(final_kernel, groups, unread),
        in_specs=[pl.BlockSpec(memory_space=pltpu.SMEM)]
        + [vmem] * (1 + len(arrays))
        + [anywhere] * unread,
        out_specs=[anywhere, anywhere],
        out_shape=[
            jax.ShapeDtypeStruct((tokens, total * size), BF16),
            jax.ShapeDtypeStruct((1, total, size, size), F32),
        ],
        scratch_shapes=scratch
        + [pltpu.VMEM((4, tokens, size), F32), pltpu.SemaphoreType.DMA((2 * total,))],
        input_output_aliases={2 + len(arrays) + i: i for i in range(len(so_far))},
        compiler_params=pltpu.CompilerParams(vmem_limit_bytes=12 * MIB),
        cost_estimate=SHORT,
        name="finish",
    )(order, seg, *arrays, *so_far, *after)


def shards(q, k, v, g, segment, decay_exponent, retention, norm_gain):
    heads = decay_exponent.shape[0]
    tokens = q.shape[0]
    count = lax.axis_size("seq")
    place = lax.axis_index("seq")
    reach = max(1, count // 4)
    far = lambda x: pltpu.with_memory_space_constraint(x, pltpu.HBM)
    q, k, v, g = far(q), far(k), far(v), far(g)
    gain = norm_gain.reshape(1, -1)
    order = jnp.where(place >= 2, 2 + (place & 1), place & 1).astype(jnp.int32).reshape(1)
    later = jnp.ones((1,), jnp.int32)
    swap = lambda x: lax.ppermute(x, "seq", [(c, c ^ 1) for c in range(count)])
    turn = lambda x: lax.ppermute(x, "seq", [(c, (c + 2) % count) for c in range(count)])
    ahead = lambda x: lax.ppermute(x, "seq", [(c, c + 2) for c in range(count - 2)])

    half = heads // 2
    even, odd = half // 2, half // 2
    chunks = [(0, half - even), (half, half - odd), (half - even, even), (heads - odd, odd)]

    def widened(x, many, shift, window):
        while window < reach:
            past = lax.ppermute(x, "seq", [(c, c + shift) for c in range(count - shift)])
            x = joined(later, x, past, many)
            shift, window = 2 * shift, 2 * window
        return x

    message, a, w, seg, k_near, v_near = first_message(
        order,
        far(segment.reshape(1, tokens)),
        far(decay_exponent.reshape(1, heads)),
        far(retention),
        k,
        v,
        heads,
        (chunks[1], chunks[0]),
    )
    k_near, v_near = k_near[::-1], v_near[::-1]
    near, past, inside = {}, {}, {}
    near[1] = swap(message)
    own = [second_message(seg, a, w, k_near[0], v_near[0], *chunks[0]), message]
    past[0] = turn(own[0])
    messages, mask, k_rest, v_rest, q_near, g_near = rest_messages(
        seg, a, w, q, k, v, g, chunks, 2
    )
    own, k_near, v_near = [*own, *messages], [*k_near, *k_rest], [*v_near, *v_rest]

    def look_inside(i, through=(), after=()):
        inside[i], copied = intra(
            mask, a, gain, q_near[i], k_near[i], v_near[i], g_near[i], *chunks[i], through, after
        )
        return copied

    def pair_last(i, after, through=()):
        message, *copied = picked(order, own[i], past[i], after, through)
        near[i] = swap(message)
        return message, *copied

    near[3] = swap(own[3])
    past[2] = turn(own[2])
    look_inside(0)
    both = joined(order, own[1], near[1], chunks[1][1], (inside[0][0],))
    message, both = pair_last(0, (), (both,))
    past[1] = turn(both)
    look_inside(1, (), (message,))
    look_inside(2, (), (inside[1][0],))
    both = joined(order, own[3], near[3], chunks[3][1], (inside[2][0],))
    message, both = pair_last(2, (), (both,))
    past[3] = ahead(both)
    look_inside(3, (), (message,))

    if reach > 2:
        for i, (_, many) in enumerate(chunks):
            past[i] = jnp.where(place >= 2, past[i], 0.0)
            if i % 2 == 0:
                near[i] = jnp.where(place >= 1, near[i], 0.0)
                near[i] = widened(joined(later, near[i], past[i], many), many, 2, 2)
                past[i] = jnp.zeros_like(near[i])
            else:
                past[i] = widened(past[i], many, 2, 2)

    result = ()
    for group in ((0, 1), (2, 3)):
        groups = [(*chunks[i], ("span", "pair")[i % 2]) for i in group]
        arrays = [x for i in group for x in (own[i], near[i], past[i], *inside[i])]
        result = finish(order, seg, heads, groups, arrays, result, (inside[3][0],))
    return tuple(result)


def solution(mesh):
    placed = (
        P(("groups", "seq"), "wt"),
        P(("groups", "seq"), "wt"),
        P(("groups", "seq"), "wt"),
        P(("groups", "seq"), "wt"),
        P(("groups", "seq")),
        P("wt"),
        P("wt", ("groups", "seq")),
        P("wt"),
    )
    return jax.shard_map(
        shards,
        mesh=mesh,
        in_specs=placed,
        out_specs=(P(("groups", "seq"), "wt"), P(("groups", "seq"), "wt", None, None)),
        check_vma=False,
    )
```

```python
import functools

import jax
import jax.numpy as jnp
from jax import lax
from jax.experimental import pallas as pl
from jax.experimental.pallas import tpu as pltpu
from jax.sharding import PartitionSpec as P

F32 = jnp.float32
BF16 = jnp.bfloat16
NN = (((1,), (0,)), ((), ()))
NT = (((1,), (1,)), ((), ()))
MIB = 1 << 20
SHORT = pl.CostEstimate(flops=1, bytes_accessed=1, transcendentals=0)


def vmem_spec(shape, index_map):
    return pl.BlockSpec(shape, index_map)


def as_column(row, lanes):
    return jnp.broadcast_to(row, (lanes, row.shape[1])).T


def meta_rows(heads):
    return -(-(heads + 1) // 8) * 8


def put_message(msg_ref, first, heads, size, w_ref, finals, end, k_ref, v_ref):
    top = heads * size
    for j in range(heads):
        columns = slice(j * size, (j + 1) * size)
        weight = w_ref[first + j : first + j + 1, :]
        keyed = (k_ref[:, columns].astype(F32).T * weight).astype(BF16)
        msg_ref[columns, :] = lax.dot_general(
            keyed, v_ref[:, columns], NN, preferred_element_type=F32
        )
    msg_ref[top : top + heads, :] = jnp.broadcast_to(finals, (heads, size))
    below = meta_rows(heads) - heads
    msg_ref[top + heads :, :] = jnp.broadcast_to(end.astype(F32), (below, size))


def first_kernel(heads, chunks, order_ref, seg_hbm, exponent_hbm, keep_hbm, k_hbm, v_hbm, *refs):
    number = len(chunks)
    (msg_ref, a_ref, w_ref, seg_ref), refs = refs[:4], refs[4:]
    k_refs, v_refs, refs = refs[:number], refs[number : 2 * number], refs[2 * number :]
    exponent_ref, keep_ref, sems = refs
    tokens = seg_ref.shape[1]
    size = msg_ref.shape[1]
    pairs = [(keep_hbm, keep_ref), (exponent_hbm, exponent_ref), (seg_hbm, seg_ref)]
    for i, (first, many) in enumerate(chunks):
        wide = pl.ds(first * size, many * size)
        pairs += [(k_hbm.at[:, wide], k_refs[i]), (v_hbm.at[:, wide], v_refs[i])]
    copies = [pltpu.make_async_copy(*pair, sems.at[i]) for i, pair in enumerate(pairs)]
    for copy in copies:
        copy.start()
    earlier = lax.broadcasted_iota(jnp.int32, (tokens, tokens), 0)
    later = lax.broadcasted_iota(jnp.int32, (tokens, tokens), 1)
    upper = jnp.where(earlier <= later, 1.0, 0.0).astype(BF16)
    across = lax.broadcasted_iota(jnp.int32, (heads, heads), 1)
    down = lax.broadcasted_iota(jnp.int32, (heads, heads), 0)
    for copy in copies[:3]:
        copy.wait()
    spread = jnp.broadcast_to(exponent_ref[...], (heads, heads))
    exponent = jnp.sum(jnp.where(across == down, spread, 0).astype(F32), axis=1, keepdims=True)
    a = -jnp.exp2(-exponent) + jnp.log(keep_ref[...])
    high = a.astype(BF16)
    rest = a - high.astype(F32)
    middle = rest.astype(BF16)
    low = (rest - middle.astype(F32)).astype(BF16)
    parts = jnp.concatenate([high, middle, low], axis=0)
    sums = lax.dot_general(parts, upper, NN, preferred_element_type=F32)
    cumulative = sums[:heads] + (sums[heads : 2 * heads] + sums[2 * heads :])
    a_ref[...] = cumulative
    final = cumulative[:, tokens - 1 :]
    seg = seg_ref[...]
    last = seg[:, tokens - 1 :]
    w_ref[...] = jnp.where(seg == last, jnp.exp(final - cumulative), 0.0)
    for copy in copies[3:5]:
        copy.wait()
    first, many = chunks[0]
    finals = final[first : first + many]
    put_message(msg_ref, first, many, size, w_ref, finals, last, k_refs[0], v_refs[0])
    for copy in copies[5:]:
        copy.wait()


def message_of(size, many):
    return pltpu.VMEM((many * size + meta_rows(many), size), F32)


def first_message(order, seg, exponent, keep, k, v, heads, chunks):
    tokens, size = k.shape[0], k.shape[1] // heads
    near = [pltpu.VMEM((tokens, many * size), BF16) for _, many in chunks]
    shapes = [message_of(size, chunks[0][1])]
    shapes += [pltpu.VMEM((heads, tokens), F32)] * 2 + [pltpu.VMEM((1, tokens), jnp.int32)]
    shapes += near + near
    number = len(chunks)
    out = pl.pallas_call(
        functools.partial(first_kernel, heads, chunks),
        in_specs=[pl.BlockSpec(memory_space=pltpu.SMEM)]
        + [pl.BlockSpec(memory_space=pltpu.HBM)] * 5,
        out_specs=[pl.BlockSpec(memory_space=pltpu.VMEM)] * len(shapes),
        out_shape=shapes,
        scratch_shapes=[
            pltpu.VMEM((1, heads), jnp.int32),
            pltpu.VMEM((heads, tokens), F32),
            pltpu.SemaphoreType.DMA((3 + 2 * number,)),
        ],
        compiler_params=pltpu.CompilerParams(vmem_limit_bytes=8 * MIB),
        cost_estimate=SHORT,
        name="first_message",
    )(order, seg, exponent, keep, k, v)
    (message, a, w, seg), out = out[:4], out[4:]
    return message, a, w, seg, out[:number], out[number:]


def second_message(seg, a, w, k, v, first, heads):
    tokens, size = k.shape[0], k.shape[1] // heads

    def kernel(seg_ref, a_ref, w_ref, k_ref, v_ref, msg_ref):
        final = a_ref[first : first + heads, tokens - 1 :]
        last = seg_ref[:, tokens - 1 :]
        put_message(msg_ref, first, heads, size, w_ref, final, last, k_ref, v_ref)

    return pl.pallas_call(
        kernel,
        in_specs=[pl.BlockSpec(memory_space=pltpu.VMEM)] * 5,
        out_specs=pl.BlockSpec(memory_space=pltpu.VMEM),
        out_shape=message_of(size, heads),
        compiler_params=pltpu.CompilerParams(vmem_limit_bytes=8 * MIB),
        cost_estimate=SHORT,
        name="second_message",
    )(seg, a, w, k, v)


def rest_kernel(chunks, done, seg_ref, a_ref, w_ref, q_hbm, k_hbm, v_hbm, g_hbm, *refs):
    tokens = seg_ref.shape[1]
    left, number = chunks[done:], len(chunks)
    messages, mask_ref, refs, sems = refs[: len(left)], refs[len(left)], refs[len(left) + 1 : -1], refs[-1]
    k_refs, refs = refs[: len(left)], refs[len(left) :]
    v_refs, refs = refs[: len(left)], refs[len(left) :]
    q_refs, g_refs = refs[:number], refs[number:]
    size = messages[0].shape[1]
    pairs = []
    for i, (first, many) in enumerate(left):
        wide = pl.ds(first * size, many * size)
        pairs += [(k_hbm.at[:, wide], k_refs[i]), (v_hbm.at[:, wide], v_refs[i])]
    for i, (first, many) in enumerate(chunks):
        wide = pl.ds(first * size, many * size)
        pairs += [(q_hbm.at[:, wide], q_refs[i]), (g_hbm.at[:, wide], g_refs[i])]
    copies = [pltpu.make_async_copy(*pair, sems.at[i]) for i, pair in enumerate(pairs)]
    for copy in copies:
        copy.start()
    make_mask(seg_ref, mask_ref)
    last = seg_ref[:, tokens - 1 :]
    for i, (first, many) in enumerate(left):
        copies[2 * i].wait()
        copies[2 * i + 1].wait()
        final = a_ref[first : first + many, tokens - 1 :]
        put_message(messages[i], first, many, size, w_ref, final, last, k_refs[i], v_refs[i])
    for copy in copies[2 * len(left) :]:
        copy.wait()


def rest_messages(seg, a, w, q, k, v, g, chunks, done):
    heads = a.shape[0]
    tokens, size = k.shape[0], k.shape[1] // heads
    near = [pltpu.VMEM((tokens, many * size), BF16) for _, many in chunks]
    shapes = [message_of(size, many) for _, many in chunks[done:]]
    shapes += [pltpu.VMEM((tokens, tokens), F32)] + near[done:] * 2 + near * 2
    left, number = len(chunks) - done, len(chunks)
    out = pl.pallas_call(
        functools.partial(rest_kernel, chunks, done),
        in_specs=[pl.BlockSpec(memory_space=pltpu.VMEM)] * 3
        + [pl.BlockSpec(memory_space=pltpu.HBM)] * 4,
        out_specs=[pl.BlockSpec(memory_space=pltpu.VMEM)] * len(shapes),
        out_shape=shapes,
        scratch_shapes=[pltpu.SemaphoreType.DMA((2 * (left + number),))],
        compiler_params=pltpu.CompilerParams(vmem_limit_bytes=8 * MIB),
        cost_estimate=SHORT,
        name="rest_messages",
    )(seg, a, w, q, k, v, g)
    messages, mask, out = out[:left], out[left], out[left + 1 :]
    k_near, v_near, out = out[:left], out[left : 2 * left], out[2 * left :]
    return messages, mask, k_near, v_near, out[:number], out[number:]


def join_kernel(heads, order_ref, mine_ref, other_ref, out_ref):
    size = mine_ref.shape[1]
    top = heads * size
    mine_later = (order_ref[0] & 1) == 1
    final_mine, final_other = mine_ref[top : top + heads, :], other_ref[top : top + heads, :]
    end_mine, end_other = mine_ref[top + heads :, :], other_ref[top + heads :, :]
    same = jnp.where(end_mine[:1] == end_other[:1], 1.0, 0.0)
    scale_mine = jnp.where(mine_later, 1.0, jnp.exp(final_other) * same)
    scale_other = jnp.where(mine_later, jnp.exp(final_mine) * same, 1.0)
    for head in range(heads):
        rows = slice(head * size, (head + 1) * size)
        out_ref[rows, :] = (
            scale_mine[head : head + 1] * mine_ref[rows, :]
            + scale_other[head : head + 1] * other_ref[rows, :]
        )
    out_ref[top : top + heads, :] = final_mine + final_other
    out_ref[top + heads :, :] = jnp.where(mine_later, end_mine, end_other)


def small_call(kernel, name, order, arrays, after):
    vmem = pl.BlockSpec(memory_space=pltpu.VMEM)
    return pl.pallas_call(
        lambda *refs: kernel(*refs[: 1 + len(arrays)], refs[-1]),
        in_specs=[pl.BlockSpec(memory_space=pltpu.SMEM)]
        + [vmem] * len(arrays)
        + [pl.BlockSpec(memory_space=pl.ANY)] * len(after),
        out_specs=vmem,
        out_shape=pltpu.VMEM(arrays[0].shape, F32),
        compiler_params=pltpu.CompilerParams(vmem_limit_bytes=8 * MIB),
        cost_estimate=SHORT,
        name=name,
    )(order, *arrays, *after)


def joined(order, mine, other, heads, after=()):
    return small_call(
        functools.partial(join_kernel, heads), "join_windows", order, (mine, other), after
    )


def picked(order, even, odd, after=(), through=()):
    vmem = pl.BlockSpec(memory_space=pltpu.VMEM)

    def kernel(order_ref, even_ref, odd_ref, *refs):
        outs = refs[len(through) + len(after) :]
        for source, target in zip(refs, outs[1:]):
            target[...] = source[...]
        odd = (order_ref[0] & 1) == 1

        @pl.when(odd)
        def _():
            outs[0][...] = odd_ref[...]

        @pl.when(jnp.logical_not(odd))
        def _():
            outs[0][...] = even_ref[...]

    return pl.pallas_call(
        kernel,
        in_specs=[pl.BlockSpec(memory_space=pltpu.SMEM)]
        + [vmem] * (2 + len(through))
        + [pl.BlockSpec(memory_space=pl.ANY)] * len(after),
        out_specs=[vmem] * (1 + len(through)),
        out_shape=[pltpu.VMEM(x.shape, F32) for x in (even, *through)],
        compiler_params=pltpu.CompilerParams(vmem_limit_bytes=8 * MIB),
        cost_estimate=SHORT,
        name="pick_message",
    )(order, even, odd, *through, *after)


def make_mask(seg_ref, mask_ref):
    tokens = seg_ref.shape[1]
    seg = seg_ref[...].astype(F32)
    column = as_column(seg, 128)
    for start in range(0, tokens, 128):
        across = lax.broadcasted_iota(jnp.int32, (tokens, 128), 1) + start
        down = lax.broadcasted_iota(jnp.int32, (tokens, 128), 0)
        seen = (column == seg[:, start : start + 128]) & (across <= down)
        mask_ref[:, start : start + 128] = jnp.where(seen, 0.0, -1e30)


def intra_kernel(
    first, heads, through, after, mask_ref, a_ref, gain_ref, q_ref, k_ref, v_ref, g_ref, *refs
):
    o_ref, gate_ref, decay_ref, *copied = refs[through + after :]
    for source, target in zip(refs[:through], copied):
        target[...] = source[...]
    tokens = mask_ref.shape[0]
    size = q_ref.shape[1] // heads
    block = min(tokens, 256)
    for j in range(heads):
        columns = slice(j * size, (j + 1) * size)
        a_row = a_ref[first + j : first + j + 1, :] * 1.4426950408889634
        a_column = as_column(a_row, 128)
        decay_ref[:, columns] = jnp.exp2(a_column)
        for start in range(0, tokens, block):
            here, upto = slice(start, start + block), slice(0, start + block)
            scores = lax.dot_general(
                q_ref[here, columns], k_ref[upto, columns], NT, preferred_element_type=F32
            )
            spread = jnp.concatenate([a_column[here]] * ((start + block) // 128), axis=1)
            weight = jnp.exp2(spread - a_row[:, upto] + mask_ref[here, upto])
            probs = (scores * weight).astype(BF16)
            o_ref[here, columns] = lax.dot_general(
                probs, v_ref[upto, columns], NN, preferred_element_type=F32
            )
        half = 0.5 * size**0.5 * gain_ref[:, (first + j) * size : (first + j + 1) * size]
        gate_ref[:, columns] = half + half * jnp.tanh(0.5 * g_ref[:, columns].astype(F32))


def intra(mask, a, gain, q, k, v, g, first, heads, through=(), after=()):
    tokens, size = mask.shape[0], gain.shape[1] // a.shape[0]
    vmem = pl.BlockSpec(memory_space=pltpu.VMEM)
    o, gate, decay, *copied = pl.pallas_call(
        functools.partial(intra_kernel, first, heads, len(through), len(after)),
        in_specs=[vmem] * (7 + len(through)) + [pl.BlockSpec(memory_space=pl.ANY)] * len(after),
        out_specs=[vmem] * (3 + len(through)),
        out_shape=[pltpu.VMEM((tokens, heads * size), F32)] * 3
        + [pltpu.VMEM(x.shape, x.dtype) for x in through],
        compiler_params=pltpu.CompilerParams(vmem_limit_bytes=8 * MIB),
        cost_estimate=SHORT,
        name="intra_span",
    )(mask, a, gain, q, k, v, g, *through, *after)
    return (o, gate, decay, q), copied


def final_kernel(groups, unread, order_ref, seg_ref, *rest):
    number = len(groups)
    inputs, rest = rest[: 7 * number], rest[7 * number + unread :]
    gated_hbm, snap_hbm, *scratch, inter_ref, sems = rest
    place = order_ref[0]
    seg = seg_ref[...].astype(F32)
    copies, work = [], []

    def send(source, target):
        copies.append(pltpu.make_async_copy(source, target, sems.at[len(copies)]))
        copies[-1].start()

    for i, (first, heads, kind) in enumerate(groups):
        own_ref, near_ref, past_ref = inputs[7 * i : 7 * i + 3]
        gated_ref, snap_ref = scratch[2 * i : 2 * i + 2]
        size = own_ref.shape[1]
        top = heads * size
        ends = slice(top + heads, top + heads + 1)
        finals = slice(top, top + heads)
        own_end, near_end, past_end = own_ref[ends, :], near_ref[ends, :], past_ref[ends, :]
        bridged = jnp.exp(near_ref[finals, :]) * jnp.where(near_end == past_end, 1.0, 0.0)
        if kind == "pair":
            odd = (place & 1) == 1
            previous = jnp.where(odd, near_end, past_end)
            scale_near = jnp.where(odd, 1.0, 0.0)
            scale_past = jnp.where(odd, bridged, 1.0)
        else:
            previous = near_end
            scale_near = jnp.where(place > 0, 1.0, 0.0)
            scale_past = bridged
        scale_past = jnp.where(place >= 2, scale_past, 0.0)
        own_decay = jnp.exp(own_ref[finals, :]) * jnp.where(own_end == previous, 1.0, 0.0)
        number_valid = jnp.sum(
            jnp.where(seg == previous[:, :1], 1.0, 0.0), axis=1, keepdims=True
        )
        for j in range(heads):
            rows = slice(j * size, (j + 1) * size)
            state = scale_past[j : j + 1] * past_ref[rows, :] + scale_near * near_ref[rows, :]
            snap_ref[j] = own_decay[j : j + 1] * state + own_ref[rows, :]
            high = state.astype(BF16)
            low = (state - high.astype(F32)).astype(BF16)
            both = jnp.concatenate([high, low], axis=0)
            work.append((i, j, first, heads, both, number_valid, inputs[7 * i + 3 : 7 * i + 7]))
        send(snap_ref, snap_hbm.at[0, pl.ds(first, heads)])

    rows = lax.broadcasted_iota(jnp.int32, (64, 128), 0).astype(F32)
    tokens, size = seg.shape[1], inter_ref.shape[2]
    for number, (i, j, first, heads, both, number_valid, arrays) in enumerate(work):
        q = arrays[3][:, j * size : (j + 1) * size]
        inter_ref[number] = lax.dot_general(
            jnp.concatenate([q, q], axis=1), both, NN, preferred_element_type=F32
        )
    for i, (first, heads, _) in enumerate(groups):
        gated_ref = scratch[2 * i]
        for start in range(0, tokens, 64):
            here = slice(start, start + 64)
            for number, (i_of, j, _, _, _, number_valid, arrays) in enumerate(work):
                if i_of != i:
                    continue
                o_ref, gate_ref, decay_ref, _ = arrays
                columns = slice(j * size, (j + 1) * size)
                inter = inter_ref[number, here, :] * decay_ref[here, columns]
                inter = jnp.where(rows < number_valid - start, inter, 0.0)
                mixed = o_ref[here, columns] + inter
                square = jnp.sum(mixed * mixed, axis=1, keepdims=True)
                gated = mixed * gate_ref[here, columns] * lax.rsqrt(square + size * 1e-06)
                gated_ref[here, columns] = gated.astype(BF16)
            if start % 128 == 64:
                block, there = pl.ds(start - 64, 128), pl.ds(first * size, heads * size)
                send(gated_ref.at[block, :], gated_hbm.at[block, there])
    for copy in copies:
        copy.wait()


def finish(order, seg, total, groups, arrays, so_far, after):
    tokens, size = seg.shape[1], arrays[0].shape[1]
    vmem, anywhere = pl.BlockSpec(memory_space=pltpu.VMEM), pl.BlockSpec(memory_space=pl.ANY)
    unread = len(so_far) + len(after)
    scratch = []
    for _, many, _ in groups:
        scratch.append(pltpu.VMEM((tokens, many * size), BF16))
        scratch.append(pltpu.VMEM((many, size, size), F32))
    return pl.pallas_call(
        functools.partial(final_kernel, groups, unread),
        in_specs=[pl.BlockSpec(memory_space=pltpu.SMEM)]
        + [vmem] * (1 + len(arrays))
        + [anywhere] * unread,
        out_specs=[anywhere, anywhere],
        out_shape=[
            jax.ShapeDtypeStruct((tokens, total * size), BF16),
            jax.ShapeDtypeStruct((1, total, size, size), F32),
        ],
        scratch_shapes=scratch
        + [
            pltpu.VMEM((sum(many for _, many, _ in groups), tokens, size), F32),
            pltpu.SemaphoreType.DMA((2 * total,)),
        ],
        input_output_aliases={2 + len(arrays) + i: i for i in range(len(so_far))},
        compiler_params=pltpu.CompilerParams(vmem_limit_bytes=12 * MIB),
        cost_estimate=SHORT,
        name="finish",
    )(order, seg, *arrays, *so_far, *after)


def shards(q, k, v, g, segment, decay_exponent, retention, norm_gain):
    heads = decay_exponent.shape[0]
    tokens = q.shape[0]
    count = lax.axis_size("seq")
    place = lax.axis_index("seq")
    reach = max(1, count // 4)
    far = lambda x: pltpu.with_memory_space_constraint(x, pltpu.HBM)
    q, k, v, g = far(q), far(k), far(v), far(g)
    gain = norm_gain.reshape(1, -1)
    order = jnp.where(place >= 2, 2 + (place & 1), place & 1).astype(jnp.int32).reshape(1)
    later = jnp.ones((1,), jnp.int32)
    swap = lambda x: lax.ppermute(x, "seq", [(c, c ^ 1) for c in range(count)])
    turn = lambda x: lax.ppermute(x, "seq", [(c, (c + 2) % count) for c in range(count)])
    ahead = lambda x: lax.ppermute(x, "seq", [(c, c + 2) for c in range(count - 2)])

    half = heads // 2
    even, odd = half // 2, half // 2
    chunks = [(0, half - even), (half, half - odd), (half - even, even), (heads - odd, odd)]

    def widened(x, many, shift, window):
        while window < reach:
            past = lax.ppermute(x, "seq", [(c, c + shift) for c in range(count - shift)])
            x = joined(later, x, past, many)
            shift, window = 2 * shift, 2 * window
        return x

    message, a, w, seg, k_near, v_near = first_message(
        order,
        far(segment.reshape(1, tokens)),
        far(decay_exponent.reshape(1, heads)),
        far(retention),
        k,
        v,
        heads,
        (chunks[1], chunks[0]),
    )
    k_near, v_near = k_near[::-1], v_near[::-1]
    near, past, inside = {}, {}, {}
    near[1] = swap(message)
    own = [second_message(seg, a, w, k_near[0], v_near[0], *chunks[0]), message]
    past[0] = turn(own[0])
    messages, mask, k_rest, v_rest, q_near, g_near = rest_messages(
        seg, a, w, q, k, v, g, chunks, 2
    )
    own, k_near, v_near = [*own, *messages], [*k_near, *k_rest], [*v_near, *v_rest]

    def look_inside(i, through=(), after=()):
        inside[i], copied = intra(
            mask, a, gain, q_near[i], k_near[i], v_near[i], g_near[i], *chunks[i], through, after
        )
        return copied

    def pair_last(i, after, through=()):
        message, *copied = picked(order, own[i], past[i], after, through)
        near[i] = swap(message)
        return message, *copied

    near[3] = swap(own[3])
    past[2] = turn(own[2])
    look_inside(0)
    both = joined(order, own[1], near[1], chunks[1][1], (inside[0][0],))
    message, both = pair_last(0, (), (both,))
    past[1] = turn(both)
    look_inside(1, (), (message,))
    look_inside(2, (), (inside[1][0],))
    both = joined(order, own[3], near[3], chunks[3][1], (inside[2][0],))
    message, both = pair_last(2, (), (both,))
    past[3] = ahead(both)
    look_inside(3, (), (message,))

    if reach > 2:
        for i, (_, many) in enumerate(chunks):
            past[i] = jnp.where(place >= 2, past[i], 0.0)
            if i % 2 == 0:
                near[i] = jnp.where(place >= 1, near[i], 0.0)
                near[i] = widened(joined(later, near[i], past[i], many), many, 2, 2)
                past[i] = jnp.zeros_like(near[i])
            else:
                past[i] = widened(past[i], many, 2, 2)

    result = ()
    for group in ((0, 1), (2, 3)):
        groups = [(*chunks[i], ("span", "pair")[i % 2]) for i in group]
        arrays = [x for i in group for x in (own[i], near[i], past[i], *inside[i])]
        result = finish(order, seg, heads, groups, arrays, result, (inside[3][0],))
    return tuple(result)


def solution(mesh):
    placed = (
        P(("groups", "seq"), "wt"),
        P(("groups", "seq"), "wt"),
        P(("groups", "seq"), "wt"),
        P(("groups", "seq"), "wt"),
        P(("groups", "seq")),
        P("wt"),
        P("wt", ("groups", "seq")),
        P("wt"),
    )
    return jax.shard_map(
        shards,
        mesh=mesh,
        in_specs=placed,
        out_specs=(P(("groups", "seq"), "wt"), P(("groups", "seq"), "wt", None, None)),
        check_vma=False,
    )
```

```python
import functools

import jax
import jax.numpy as jnp
from jax import lax
from jax.experimental import pallas as pl
from jax.experimental.pallas import tpu as pltpu
from jax.sharding import PartitionSpec as P

F32 = jnp.float32
BF16 = jnp.bfloat16
NN = (((1,), (0,)), ((), ()))
NT = (((1,), (1,)), ((), ()))
MIB = 1 << 20
SHORT = pl.CostEstimate(flops=1, bytes_accessed=1, transcendentals=0)


def vmem_spec(shape, index_map):
    return pl.BlockSpec(shape, index_map)


def as_column(row, lanes):
    return jnp.broadcast_to(row, (lanes, row.shape[1])).T


def meta_rows(heads):
    return -(-(heads + 1) // 8) * 8


def put_message(msg_ref, first, heads, size, w_ref, finals, end, k_ref, v_ref):
    top = heads * size
    for j in range(heads):
        columns = slice(j * size, (j + 1) * size)
        weight = w_ref[first + j : first + j + 1, :]
        keyed = (k_ref[:, columns].astype(F32).T * weight).astype(BF16)
        msg_ref[columns, :] = lax.dot_general(
            keyed, v_ref[:, columns], NN, preferred_element_type=F32
        )
    msg_ref[top : top + heads, :] = jnp.broadcast_to(finals, (heads, size))
    below = meta_rows(heads) - heads
    msg_ref[top + heads :, :] = jnp.broadcast_to(end.astype(F32), (below, size))


def first_kernel(heads, chunks, order_ref, seg_hbm, exponent_hbm, keep_hbm, k_hbm, v_hbm, *refs):
    number = len(chunks)
    (msg_ref, a_ref, w_ref, seg_ref), refs = refs[:4], refs[4:]
    k_refs, v_refs, refs = refs[:number], refs[number : 2 * number], refs[2 * number :]
    exponent_ref, keep_ref, sems = refs
    tokens = seg_ref.shape[1]
    size = msg_ref.shape[1]
    pairs = [(keep_hbm, keep_ref), (exponent_hbm, exponent_ref), (seg_hbm, seg_ref)]
    for i, (first, many) in enumerate(chunks):
        wide = pl.ds(first * size, many * size)
        pairs += [(k_hbm.at[:, wide], k_refs[i]), (v_hbm.at[:, wide], v_refs[i])]
    copies = [pltpu.make_async_copy(*pair, sems.at[i]) for i, pair in enumerate(pairs)]
    for copy in copies:
        copy.start()
    earlier = lax.broadcasted_iota(jnp.int32, (tokens, tokens), 0)
    later = lax.broadcasted_iota(jnp.int32, (tokens, tokens), 1)
    upper = jnp.where(earlier <= later, 1.0, 0.0).astype(BF16)
    across = lax.broadcasted_iota(jnp.int32, (heads, heads), 1)
    down = lax.broadcasted_iota(jnp.int32, (heads, heads), 0)
    for copy in copies[:3]:
        copy.wait()
    spread = jnp.broadcast_to(exponent_ref[...], (heads, heads))
    exponent = jnp.sum(jnp.where(across == down, spread, 0).astype(F32), axis=1, keepdims=True)
    a = -jnp.exp2(-exponent) + jnp.log(keep_ref[...])
    high = a.astype(BF16)
    rest = a - high.astype(F32)
    middle = rest.astype(BF16)
    low = (rest - middle.astype(F32)).astype(BF16)
    parts = jnp.concatenate([high, middle, low], axis=0)
    sums = lax.dot_general(parts, upper, NN, preferred_element_type=F32)
    cumulative = sums[:heads] + (sums[heads : 2 * heads] + sums[2 * heads :])
    a_ref[...] = cumulative
    final = cumulative[:, tokens - 1 :]
    seg = seg_ref[...]
    last = seg[:, tokens - 1 :]
    w_ref[...] = jnp.where(seg == last, jnp.exp(final - cumulative), 0.0)
    for copy in copies[3:5]:
        copy.wait()
    first, many = chunks[0]
    finals = final[first : first + many]
    put_message(msg_ref, first, many, size, w_ref, finals, last, k_refs[0], v_refs[0])
    for copy in copies[5:]:
        copy.wait()


def message_of(size, many):
    return pltpu.VMEM((many * size + meta_rows(many), size), F32)


def first_message(order, seg, exponent, keep, k, v, heads, chunks):
    tokens, size = k.shape[0], k.shape[1] // heads
    near = [pltpu.VMEM((tokens, many * size), BF16) for _, many in chunks]
    shapes = [message_of(size, chunks[0][1])]
    shapes += [pltpu.VMEM((heads, tokens), F32)] * 2 + [pltpu.VMEM((1, tokens), jnp.int32)]
    shapes += near + near
    number = len(chunks)
    out = pl.pallas_call(
        functools.partial(first_kernel, heads, chunks),
        in_specs=[pl.BlockSpec(memory_space=pltpu.SMEM)]
        + [pl.BlockSpec(memory_space=pltpu.HBM)] * 5,
        out_specs=[pl.BlockSpec(memory_space=pltpu.VMEM)] * len(shapes),
        out_shape=shapes,
        scratch_shapes=[
            pltpu.VMEM((1, heads), jnp.int32),
            pltpu.VMEM((heads, tokens), F32),
            pltpu.SemaphoreType.DMA((3 + 2 * number,)),
        ],
        compiler_params=pltpu.CompilerParams(vmem_limit_bytes=8 * MIB),
        cost_estimate=SHORT,
        name="first_message",
    )(order, seg, exponent, keep, k, v)
    (message, a, w, seg), out = out[:4], out[4:]
    return message, a, w, seg, out[:number], out[number:]


def second_message(seg, a, w, k, v, first, heads):
    tokens, size = k.shape[0], k.shape[1] // heads

    def kernel(seg_ref, a_ref, w_ref, k_ref, v_ref, msg_ref):
        final = a_ref[first : first + heads, tokens - 1 :]
        last = seg_ref[:, tokens - 1 :]
        put_message(msg_ref, first, heads, size, w_ref, final, last, k_ref, v_ref)

    return pl.pallas_call(
        kernel,
        in_specs=[pl.BlockSpec(memory_space=pltpu.VMEM)] * 5,
        out_specs=pl.BlockSpec(memory_space=pltpu.VMEM),
        out_shape=message_of(size, heads),
        compiler_params=pltpu.CompilerParams(vmem_limit_bytes=8 * MIB),
        cost_estimate=SHORT,
        name="second_message",
    )(seg, a, w, k, v)


def rest_kernel(chunks, done, seg_ref, a_ref, w_ref, q_hbm, k_hbm, v_hbm, g_hbm, *refs):
    tokens = seg_ref.shape[1]
    left, number = chunks[done:], len(chunks)
    messages, mask_ref, refs, sems = refs[: len(left)], refs[len(left)], refs[len(left) + 1 : -1], refs[-1]
    k_refs, refs = refs[: len(left)], refs[len(left) :]
    v_refs, refs = refs[: len(left)], refs[len(left) :]
    q_refs, g_refs = refs[:number], refs[number:]
    size = messages[0].shape[1]
    pairs = []
    for i, (first, many) in enumerate(left):
        wide = pl.ds(first * size, many * size)
        pairs += [(k_hbm.at[:, wide], k_refs[i]), (v_hbm.at[:, wide], v_refs[i])]
    for i, (first, many) in enumerate(chunks):
        wide = pl.ds(first * size, many * size)
        pairs += [(q_hbm.at[:, wide], q_refs[i]), (g_hbm.at[:, wide], g_refs[i])]
    copies = [pltpu.make_async_copy(*pair, sems.at[i]) for i, pair in enumerate(pairs)]
    for copy in copies:
        copy.start()
    make_mask(seg_ref, mask_ref)
    last = seg_ref[:, tokens - 1 :]
    for i, (first, many) in enumerate(left):
        copies[2 * i].wait()
        copies[2 * i + 1].wait()
        final = a_ref[first : first + many, tokens - 1 :]
        put_message(messages[i], first, many, size, w_ref, final, last, k_refs[i], v_refs[i])
    for copy in copies[2 * len(left) :]:
        copy.wait()


def rest_messages(seg, a, w, q, k, v, g, chunks, done):
    heads = a.shape[0]
    tokens, size = k.shape[0], k.shape[1] // heads
    near = [pltpu.VMEM((tokens, many * size), BF16) for _, many in chunks]
    shapes = [message_of(size, many) for _, many in chunks[done:]]
    shapes += [pltpu.VMEM((tokens, tokens), F32)] + near[done:] * 2 + near * 2
    left, number = len(chunks) - done, len(chunks)
    out = pl.pallas_call(
        functools.partial(rest_kernel, chunks, done),
        in_specs=[pl.BlockSpec(memory_space=pltpu.VMEM)] * 3
        + [pl.BlockSpec(memory_space=pltpu.HBM)] * 4,
        out_specs=[pl.BlockSpec(memory_space=pltpu.VMEM)] * len(shapes),
        out_shape=shapes,
        scratch_shapes=[pltpu.SemaphoreType.DMA((2 * (left + number),))],
        compiler_params=pltpu.CompilerParams(vmem_limit_bytes=8 * MIB),
        cost_estimate=SHORT,
        name="rest_messages",
    )(seg, a, w, q, k, v, g)
    messages, mask, out = out[:left], out[left], out[left + 1 :]
    k_near, v_near, out = out[:left], out[left : 2 * left], out[2 * left :]
    return messages, mask, k_near, v_near, out[:number], out[number:]


def join_kernel(heads, order_ref, mine_ref, other_ref, out_ref):
    size = mine_ref.shape[1]
    top = heads * size
    mine_later = (order_ref[0] & 1) == 1
    final_mine, final_other = mine_ref[top : top + heads, :], other_ref[top : top + heads, :]
    end_mine, end_other = mine_ref[top + heads :, :], other_ref[top + heads :, :]
    same = jnp.where(end_mine[:1] == end_other[:1], 1.0, 0.0)
    scale_mine = jnp.where(mine_later, 1.0, jnp.exp(final_other) * same)
    scale_other = jnp.where(mine_later, jnp.exp(final_mine) * same, 1.0)
    for head in range(heads):
        rows = slice(head * size, (head + 1) * size)
        out_ref[rows, :] = (
            scale_mine[head : head + 1] * mine_ref[rows, :]
            + scale_other[head : head + 1] * other_ref[rows, :]
        )
    out_ref[top : top + heads, :] = final_mine + final_other
    out_ref[top + heads :, :] = jnp.where(mine_later, end_mine, end_other)


def small_call(kernel, name, order, arrays, after):
    vmem = pl.BlockSpec(memory_space=pltpu.VMEM)
    return pl.pallas_call(
        lambda *refs: kernel(*refs[: 1 + len(arrays)], refs[-1]),
        in_specs=[pl.BlockSpec(memory_space=pltpu.SMEM)]
        + [vmem] * len(arrays)
        + [pl.BlockSpec(memory_space=pl.ANY)] * len(after),
        out_specs=vmem,
        out_shape=pltpu.VMEM(arrays[0].shape, F32),
        compiler_params=pltpu.CompilerParams(vmem_limit_bytes=8 * MIB),
        cost_estimate=SHORT,
        name=name,
    )(order, *arrays, *after)


def joined(order, mine, other, heads, after=()):
    return small_call(
        functools.partial(join_kernel, heads), "join_windows", order, (mine, other), after
    )


def picked(order, even, odd, after=(), through=()):
    vmem = pl.BlockSpec(memory_space=pltpu.VMEM)

    def kernel(order_ref, even_ref, odd_ref, *refs):
        outs = refs[len(through) + len(after) :]
        for source, target in zip(refs, outs[1:]):
            target[...] = source[...]
        odd = (order_ref[0] & 1) == 1

        @pl.when(odd)
        def _():
            outs[0][...] = odd_ref[...]

        @pl.when(jnp.logical_not(odd))
        def _():
            outs[0][...] = even_ref[...]

    return pl.pallas_call(
        kernel,
        in_specs=[pl.BlockSpec(memory_space=pltpu.SMEM)]
        + [vmem] * (2 + len(through))
        + [pl.BlockSpec(memory_space=pl.ANY)] * len(after),
        out_specs=[vmem] * (1 + len(through)),
        out_shape=[pltpu.VMEM(x.shape, F32) for x in (even, *through)],
        compiler_params=pltpu.CompilerParams(vmem_limit_bytes=8 * MIB),
        cost_estimate=SHORT,
        name="pick_message",
    )(order, even, odd, *through, *after)


def make_mask(seg_ref, mask_ref):
    tokens = seg_ref.shape[1]
    seg = seg_ref[...].astype(F32)
    column = as_column(seg, 128)
    for start in range(0, tokens, 128):
        across = lax.broadcasted_iota(jnp.int32, (tokens, 128), 1) + start
        down = lax.broadcasted_iota(jnp.int32, (tokens, 128), 0)
        seen = (column == seg[:, start : start + 128]) & (across <= down)
        mask_ref[:, start : start + 128] = jnp.where(seen, 0.0, -1e30)


def intra_kernel(
    first, heads, through, after, mask_ref, a_ref, gain_ref, q_ref, k_ref, v_ref, g_ref, *refs
):
    o_ref, gate_ref, decay_ref, *copied = refs[through + after :]
    for source, target in zip(refs[:through], copied):
        target[...] = source[...]
    tokens = mask_ref.shape[0]
    size = q_ref.shape[1] // heads
    block = min(tokens, 256)
    for j in range(heads):
        columns = slice(j * size, (j + 1) * size)
        a_row = a_ref[first + j : first + j + 1, :] * 1.4426950408889634
        a_column = as_column(a_row, 128)
        decay_ref[:, columns] = jnp.exp2(a_column)
        for start in range(0, tokens, block):
            here, upto = slice(start, start + block), slice(0, start + block)
            scores = lax.dot_general(
                q_ref[here, columns], k_ref[upto, columns], NT, preferred_element_type=F32
            )
            spread = jnp.concatenate([a_column[here]] * ((start + block) // 128), axis=1)
            weight = jnp.exp2(spread - a_row[:, upto] + mask_ref[here, upto])
            probs = (scores * weight).astype(BF16)
            o_ref[here, columns] = lax.dot_general(
                probs, v_ref[upto, columns], NN, preferred_element_type=F32
            )
        half = 0.5 * size**0.5 * gain_ref[:, (first + j) * size : (first + j + 1) * size]
        gate_ref[:, columns] = half + half * jnp.tanh(0.5 * g_ref[:, columns].astype(F32))


def intra(mask, a, gain, q, k, v, g, first, heads, through=(), after=()):
    tokens, size = mask.shape[0], gain.shape[1] // a.shape[0]
    vmem = pl.BlockSpec(memory_space=pltpu.VMEM)
    o, gate, decay, *copied = pl.pallas_call(
        functools.partial(intra_kernel, first, heads, len(through), len(after)),
        in_specs=[vmem] * (7 + len(through)) + [pl.BlockSpec(memory_space=pl.ANY)] * len(after),
        out_specs=[vmem] * (3 + len(through)),
        out_shape=[pltpu.VMEM((tokens, heads * size), F32)] * 3
        + [pltpu.VMEM(x.shape, x.dtype) for x in through],
        compiler_params=pltpu.CompilerParams(vmem_limit_bytes=8 * MIB),
        cost_estimate=SHORT,
        name="intra_span",
    )(mask, a, gain, q, k, v, g, *through, *after)
    return (o, gate, decay, q), copied


def final_kernel(groups, unread, order_ref, seg_ref, *rest):
    number = len(groups)
    inputs, rest = rest[: 7 * number], rest[7 * number + unread :]
    gated_hbm, snap_hbm, *scratch, inter_ref, sems = rest
    place = order_ref[0]
    seg = seg_ref[...].astype(F32)
    copies, work = [], []

    def send(source, target):
        copies.append(pltpu.make_async_copy(source, target, sems.at[len(copies)]))
        copies[-1].start()

    for i, (first, heads, kind) in enumerate(groups):
        own_ref, near_ref, past_ref = inputs[7 * i : 7 * i + 3]
        gated_ref, snap_ref = scratch[2 * i : 2 * i + 2]
        size = own_ref.shape[1]
        top = heads * size
        ends = slice(top + heads, top + heads + 1)
        finals = slice(top, top + heads)
        own_end, near_end, past_end = own_ref[ends, :], near_ref[ends, :], past_ref[ends, :]
        bridged = jnp.exp(near_ref[finals, :]) * jnp.where(near_end == past_end, 1.0, 0.0)
        if kind == "pair":
            odd = (place & 1) == 1
            previous = jnp.where(odd, near_end, past_end)
            scale_near = jnp.where(odd, 1.0, 0.0)
            scale_past = jnp.where(odd, bridged, 1.0)
        else:
            previous = near_end
            scale_near = jnp.where(place > 0, 1.0, 0.0)
            scale_past = bridged
        scale_past = jnp.where(place >= 2, scale_past, 0.0)
        own_decay = jnp.exp(own_ref[finals, :]) * jnp.where(own_end == previous, 1.0, 0.0)
        number_valid = jnp.sum(
            jnp.where(seg == previous[:, :1], 1.0, 0.0), axis=1, keepdims=True
        )
        for j in range(heads):
            rows = slice(j * size, (j + 1) * size)
            state = scale_past[j : j + 1] * past_ref[rows, :] + scale_near * near_ref[rows, :]
            snap_ref[j] = own_decay[j : j + 1] * state + own_ref[rows, :]
            high = state.astype(BF16)
            low = (state - high.astype(F32)).astype(BF16)
            both = jnp.concatenate([high, low], axis=0)
            work.append((i, j, first, heads, both, number_valid, inputs[7 * i + 3 : 7 * i + 7]))
        send(snap_ref, snap_hbm.at[0, pl.ds(first, heads)])

    rows = lax.broadcasted_iota(jnp.int32, (64, 128), 0).astype(F32)
    for number, (i, j, first, heads, both, number_valid, arrays) in enumerate(work):
        o_ref, gate_ref, decay_ref, q_ref = arrays
        gated_ref = scratch[2 * i]
        tokens, size = seg.shape[1], q_ref.shape[1] // heads
        columns = slice(j * size, (j + 1) * size)
        q = q_ref[:, columns]
        inter_ref[number % 4] = lax.dot_general(
            jnp.concatenate([q, q], axis=1), both, NN, preferred_element_type=F32
        )
        for start in range(0, tokens, 64):
            here = slice(start, start + 64)
            inter = inter_ref[number % 4, here, :]
            inter = jnp.where(rows < number_valid - start, inter * decay_ref[here, columns], 0.0)
            mixed = o_ref[here, columns] + inter
            square = jnp.sum(mixed * mixed, axis=1, keepdims=True)
            gated = mixed * gate_ref[here, columns] * lax.rsqrt(square + size * 1e-06)
            gated_ref[here, columns] = gated.astype(BF16)
            if number == len(work) - 1 and start % 128 == 64:
                block = pl.ds(start - 64, 128)
                there = pl.ds((first + j) * size, size)
                send(gated_ref.at[block, pl.ds(j * size, size)], gated_hbm.at[block, there])
        if number == len(work) - 1:
            continue
        alone = number + 2 == len(work) and j % 2 == 0
        if alone or j % 2 == 1 or j == heads - 1:
            begin = j if alone else j - j % 2
            width = (j + 1 - begin) * size
            there = pl.ds((first + begin) * size, width)
            send(gated_ref.at[:, pl.ds(begin * size, width)], gated_hbm.at[:, there])
    for copy in copies:
        copy.wait()


def finish(order, seg, total, groups, arrays, so_far, after):
    tokens, size = seg.shape[1], arrays[0].shape[1]
    vmem, anywhere = pl.BlockSpec(memory_space=pltpu.VMEM), pl.BlockSpec(memory_space=pl.ANY)
    unread = len(so_far) + len(after)
    scratch = []
    for _, many, _ in groups:
        scratch.append(pltpu.VMEM((tokens, many * size), BF16))
        scratch.append(pltpu.VMEM((many, size, size), F32))
    return pl.pallas_call(
        functools.partial(final_kernel, groups, unread),
        in_specs=[pl.BlockSpec(memory_space=pltpu.SMEM)]
        + [vmem] * (1 + len(arrays))
        + [anywhere] * unread,
        out_specs=[anywhere, anywhere],
        out_shape=[
            jax.ShapeDtypeStruct((tokens, total * size), BF16),
            jax.ShapeDtypeStruct((1, total, size, size), F32),
        ],
        scratch_shapes=scratch
        + [pltpu.VMEM((4, tokens, size), F32), pltpu.SemaphoreType.DMA((2 * total,))],
        input_output_aliases={2 + len(arrays) + i: i for i in range(len(so_far))},
        compiler_params=pltpu.CompilerParams(vmem_limit_bytes=12 * MIB),
        cost_estimate=SHORT,
        name="finish",
    )(order, seg, *arrays, *so_far, *after)


def shards(q, k, v, g, segment, decay_exponent, retention, norm_gain):
    heads = decay_exponent.shape[0]
    tokens = q.shape[0]
    count = lax.axis_size("seq")
    place = lax.axis_index("seq")
    reach = max(1, count // 4)
    far = lambda x: pltpu.with_memory_space_constraint(x, pltpu.HBM)
    q, k, v, g = far(q), far(k), far(v), far(g)
    gain = norm_gain.reshape(1, -1)
    order = jnp.where(place >= 2, 2 + (place & 1), place & 1).astype(jnp.int32).reshape(1)
    later = jnp.ones((1,), jnp.int32)
    swap = lambda x: lax.ppermute(x, "seq", [(c, c ^ 1) for c in range(count)])
    turn = lambda x: lax.ppermute(x, "seq", [(c, (c + 2) % count) for c in range(count)])
    ahead = lambda x: lax.ppermute(x, "seq", [(c, c + 2) for c in range(count - 2)])

    half = heads // 2
    even = odd = half - half * 3 // 8
    chunks = [(0, half - even), (half, half - odd), (half - even, even), (heads - odd, odd)]

    def widened(x, many, shift, window):
        while window < reach:
            past = lax.ppermute(x, "seq", [(c, c + shift) for c in range(count - shift)])
            x = joined(later, x, past, many)
            shift, window = 2 * shift, 2 * window
        return x

    message, a, w, seg, k_near, v_near = first_message(
        order,
        far(segment.reshape(1, tokens)),
        far(decay_exponent.reshape(1, heads)),
        far(retention),
        k,
        v,
        heads,
        (chunks[1], chunks[0]),
    )
    k_near, v_near = k_near[::-1], v_near[::-1]
    near, past, inside = {}, {}, {}
    near[1] = swap(message)
    own = [second_message(seg, a, w, k_near[0], v_near[0], *chunks[0]), message]
    past[0] = turn(own[0])
    messages, mask, k_rest, v_rest, q_near, g_near = rest_messages(
        seg, a, w, q, k, v, g, chunks, 2
    )
    own, k_near, v_near = [*own, *messages], [*k_near, *k_rest], [*v_near, *v_rest]

    def look_inside(i, through=(), after=()):
        inside[i], copied = intra(
            mask, a, gain, q_near[i], k_near[i], v_near[i], g_near[i], *chunks[i], through, after
        )
        return copied

    def pair_last(i, after, through=()):
        message, *copied = picked(order, own[i], past[i], after, through)
        near[i] = swap(message)
        return message, *copied

    near[3] = swap(own[3])
    past[2] = turn(own[2])
    look_inside(0)
    both = joined(order, own[1], near[1], chunks[1][1], (inside[0][0],))
    message, both = pair_last(0, (), (both,))
    past[1] = turn(both)
    look_inside(1, (), (message,))
    look_inside(2, (), (inside[1][0],))
    both = joined(order, own[3], near[3], chunks[3][1], (inside[2][0],))
    message, both = pair_last(2, (), (both,))
    past[3] = ahead(both)
    look_inside(3, (), (message,))

    if reach > 2:
        for i, (_, many) in enumerate(chunks):
            past[i] = jnp.where(place >= 2, past[i], 0.0)
            if i % 2 == 0:
                near[i] = jnp.where(place >= 1, near[i], 0.0)
                near[i] = widened(joined(later, near[i], past[i], many), many, 2, 2)
                past[i] = jnp.zeros_like(near[i])
            else:
                past[i] = widened(past[i], many, 2, 2)

    result = ()
    for group in ((0, 1), (2, 3)):
        groups = [(*chunks[i], ("span", "pair")[i % 2]) for i in group]
        arrays = [x for i in group for x in (own[i], near[i], past[i], *inside[i])]
        result = finish(order, seg, heads, groups, arrays, result, (inside[3][0],))
    return tuple(result)


def solution(mesh):
    placed = (
        P(("groups", "seq"), "wt"),
        P(("groups", "seq"), "wt"),
        P(("groups", "seq"), "wt"),
        P(("groups", "seq"), "wt"),
        P(("groups", "seq")),
        P("wt"),
        P("wt", ("groups", "seq")),
        P("wt"),
    )
    return jax.shard_map(
        shards,
        mesh=mesh,
        in_specs=placed,
        out_specs=(P(("groups", "seq"), "wt"), P(("groups", "seq"), "wt", None, None)),
        check_vma=False,
    )
```

```python
import functools

import jax
import jax.numpy as jnp
from jax import lax
from jax.experimental import pallas as pl
from jax.experimental.pallas import tpu as pltpu
from jax.sharding import PartitionSpec as P

F32 = jnp.float32
BF16 = jnp.bfloat16
NN = (((1,), (0,)), ((), ()))
NT = (((1,), (1,)), ((), ()))
MIB = 1 << 20
SHORT = pl.CostEstimate(flops=1, bytes_accessed=1, transcendentals=0)


def vmem_spec(shape, index_map):
    return pl.BlockSpec(shape, index_map)


def as_column(row, lanes):
    return jnp.broadcast_to(row, (lanes, row.shape[1])).T


def meta_rows(heads):
    return -(-(heads + 1) // 8) * 8


def put_message(msg_ref, first, heads, size, w_ref, finals, end, k_ref, v_ref):
    top = heads * size
    for j in range(heads):
        columns = slice(j * size, (j + 1) * size)
        weight = w_ref[first + j : first + j + 1, :]
        keyed = (k_ref[:, columns].astype(F32).T * weight).astype(BF16)
        msg_ref[columns, :] = lax.dot_general(
            keyed, v_ref[:, columns], NN, preferred_element_type=F32
        )
    msg_ref[top : top + heads, :] = jnp.broadcast_to(finals, (heads, size))
    below = meta_rows(heads) - heads
    msg_ref[top + heads :, :] = jnp.broadcast_to(end.astype(F32), (below, size))


def first_kernel(heads, chunks, order_ref, seg_hbm, exponent_hbm, keep_hbm, k_hbm, v_hbm, *refs):
    number = len(chunks)
    (msg_ref, a_ref, w_ref, seg_ref), refs = refs[:4], refs[4:]
    k_refs, v_refs, refs = refs[:number], refs[number : 2 * number], refs[2 * number :]
    exponent_ref, keep_ref, sems = refs
    tokens = seg_ref.shape[1]
    size = msg_ref.shape[1]
    pairs = [(keep_hbm, keep_ref), (exponent_hbm, exponent_ref), (seg_hbm, seg_ref)]
    for i, (first, many) in enumerate(chunks):
        wide = pl.ds(first * size, many * size)
        pairs += [(k_hbm.at[:, wide], k_refs[i]), (v_hbm.at[:, wide], v_refs[i])]
    copies = [pltpu.make_async_copy(*pair, sems.at[i]) for i, pair in enumerate(pairs)]
    for copy in copies[:5]:
        copy.start()
    earlier = lax.broadcasted_iota(jnp.int32, (tokens, tokens), 0)
    later = lax.broadcasted_iota(jnp.int32, (tokens, tokens), 1)
    upper = jnp.where(earlier <= later, 1.0, 0.0).astype(BF16)
    across = lax.broadcasted_iota(jnp.int32, (heads, heads), 1)
    down = lax.broadcasted_iota(jnp.int32, (heads, heads), 0)
    for copy in copies[:3]:
        copy.wait()
    for copy in copies[5:]:
        copy.start()
    spread = jnp.broadcast_to(exponent_ref[...], (heads, heads))
    exponent = jnp.sum(jnp.where(across == down, spread, 0).astype(F32), axis=1, keepdims=True)
    a = -jnp.exp2(-exponent) + jnp.log(keep_ref[...])
    high = a.astype(BF16)
    rest = a - high.astype(F32)
    middle = rest.astype(BF16)
    low = (rest - middle.astype(F32)).astype(BF16)
    parts = jnp.concatenate([high, middle, low], axis=0)
    sums = lax.dot_general(parts, upper, NN, preferred_element_type=F32)
    cumulative = sums[:heads] + (sums[heads : 2 * heads] + sums[2 * heads :])
    a_ref[...] = cumulative
    final = cumulative[:, tokens - 1 :]
    seg = seg_ref[...]
    last = seg[:, tokens - 1 :]
    w_ref[...] = jnp.where(seg == last, jnp.exp(final - cumulative), 0.0)
    for copy in copies[3:5]:
        copy.wait()
    first, many = chunks[0]
    finals = final[first : first + many]
    put_message(msg_ref, first, many, size, w_ref, finals, last, k_refs[0], v_refs[0])
    for copy in copies[5:]:
        copy.wait()


def message_of(size, many):
    return pltpu.VMEM((many * size + meta_rows(many), size), F32)


def first_message(order, seg, exponent, keep, k, v, heads, chunks):
    tokens, size = k.shape[0], k.shape[1] // heads
    near = [pltpu.VMEM((tokens, many * size), BF16) for _, many in chunks]
    shapes = [message_of(size, chunks[0][1])]
    shapes += [pltpu.VMEM((heads, tokens), F32)] * 2 + [pltpu.VMEM((1, tokens), jnp.int32)]
    shapes += near + near
    number = len(chunks)
    out = pl.pallas_call(
        functools.partial(first_kernel, heads, chunks),
        in_specs=[pl.BlockSpec(memory_space=pltpu.SMEM)]
        + [pl.BlockSpec(memory_space=pltpu.HBM)] * 5,
        out_specs=[pl.BlockSpec(memory_space=pltpu.VMEM)] * len(shapes),
        out_shape=shapes,
        scratch_shapes=[
            pltpu.VMEM((1, heads), jnp.int32),
            pltpu.VMEM((heads, tokens), F32),
            pltpu.SemaphoreType.DMA((3 + 2 * number,)),
        ],
        compiler_params=pltpu.CompilerParams(vmem_limit_bytes=8 * MIB),
        cost_estimate=SHORT,
        name="first_message",
    )(order, seg, exponent, keep, k, v)
    (message, a, w, seg), out = out[:4], out[4:]
    return message, a, w, seg, out[:number], out[number:]


def second_message(seg, a, w, k, v, first, heads):
    tokens, size = k.shape[0], k.shape[1] // heads

    def kernel(seg_ref, a_ref, w_ref, k_ref, v_ref, msg_ref):
        final = a_ref[first : first + heads, tokens - 1 :]
        last = seg_ref[:, tokens - 1 :]
        put_message(msg_ref, first, heads, size, w_ref, final, last, k_ref, v_ref)

    return pl.pallas_call(
        kernel,
        in_specs=[pl.BlockSpec(memory_space=pltpu.VMEM)] * 5,
        out_specs=pl.BlockSpec(memory_space=pltpu.VMEM),
        out_shape=message_of(size, heads),
        compiler_params=pltpu.CompilerParams(vmem_limit_bytes=8 * MIB),
        cost_estimate=SHORT,
        name="second_message",
    )(seg, a, w, k, v)


def rest_kernel(chunks, done, seg_ref, a_ref, w_ref, q_hbm, k_hbm, v_hbm, g_hbm, *refs):
    tokens = seg_ref.shape[1]
    left, number = chunks[done:], len(chunks)
    messages, mask_ref, refs, sems = refs[: len(left)], refs[len(left)], refs[len(left) + 1 : -1], refs[-1]
    k_refs, refs = refs[: len(left)], refs[len(left) :]
    v_refs, refs = refs[: len(left)], refs[len(left) :]
    q_refs, g_refs = refs[:number], refs[number:]
    size = messages[0].shape[1]
    pairs = []
    for i, (first, many) in enumerate(left):
        wide = pl.ds(first * size, many * size)
        pairs += [(k_hbm.at[:, wide], k_refs[i]), (v_hbm.at[:, wide], v_refs[i])]
    for i, (first, many) in enumerate(chunks):
        wide = pl.ds(first * size, many * size)
        pairs += [(q_hbm.at[:, wide], q_refs[i]), (g_hbm.at[:, wide], g_refs[i])]
    copies = [pltpu.make_async_copy(*pair, sems.at[i]) for i, pair in enumerate(pairs)]
    for copy in copies:
        copy.start()
    make_mask(seg_ref, mask_ref)
    last = seg_ref[:, tokens - 1 :]
    for i, (first, many) in enumerate(left):
        copies[2 * i].wait()
        copies[2 * i + 1].wait()
        final = a_ref[first : first + many, tokens - 1 :]
        put_message(messages[i], first, many, size, w_ref, final, last, k_refs[i], v_refs[i])
    for copy in copies[2 * len(left) :]:
        copy.wait()


def rest_messages(seg, a, w, q, k, v, g, chunks, done):
    heads = a.shape[0]
    tokens, size = k.shape[0], k.shape[1] // heads
    near = [pltpu.VMEM((tokens, many * size), BF16) for _, many in chunks]
    shapes = [message_of(size, many) for _, many in chunks[done:]]
    shapes += [pltpu.VMEM((tokens, tokens), F32)] + near[done:] * 2 + near * 2
    left, number = len(chunks) - done, len(chunks)
    out = pl.pallas_call(
        functools.partial(rest_kernel, chunks, done),
        in_specs=[pl.BlockSpec(memory_space=pltpu.VMEM)] * 3
        + [pl.BlockSpec(memory_space=pltpu.HBM)] * 4,
        out_specs=[pl.BlockSpec(memory_space=pltpu.VMEM)] * len(shapes),
        out_shape=shapes,
        scratch_shapes=[pltpu.SemaphoreType.DMA((2 * (left + number),))],
        compiler_params=pltpu.CompilerParams(vmem_limit_bytes=8 * MIB),
        cost_estimate=SHORT,
        name="rest_messages",
    )(seg, a, w, q, k, v, g)
    messages, mask, out = out[:left], out[left], out[left + 1 :]
    k_near, v_near, out = out[:left], out[left : 2 * left], out[2 * left :]
    return messages, mask, k_near, v_near, out[:number], out[number:]


def join_kernel(heads, order_ref, mine_ref, other_ref, out_ref):
    size = mine_ref.shape[1]
    top = heads * size
    mine_later = (order_ref[0] & 1) == 1
    final_mine, final_other = mine_ref[top : top + heads, :], other_ref[top : top + heads, :]
    end_mine, end_other = mine_ref[top + heads :, :], other_ref[top + heads :, :]
    same = jnp.where(end_mine[:1] == end_other[:1], 1.0, 0.0)
    scale_mine = jnp.where(mine_later, 1.0, jnp.exp(final_other) * same)
    scale_other = jnp.where(mine_later, jnp.exp(final_mine) * same, 1.0)
    for head in range(heads):
        rows = slice(head * size, (head + 1) * size)
        out_ref[rows, :] = (
            scale_mine[head : head + 1] * mine_ref[rows, :]
            + scale_other[head : head + 1] * other_ref[rows, :]
        )
    out_ref[top : top + heads, :] = final_mine + final_other
    out_ref[top + heads :, :] = jnp.where(mine_later, end_mine, end_other)


def small_call(kernel, name, order, arrays, after):
    vmem = pl.BlockSpec(memory_space=pltpu.VMEM)
    return pl.pallas_call(
        lambda *refs: kernel(*refs[: 1 + len(arrays)], refs[-1]),
        in_specs=[pl.BlockSpec(memory_space=pltpu.SMEM)]
        + [vmem] * len(arrays)
        + [pl.BlockSpec(memory_space=pl.ANY)] * len(after),
        out_specs=vmem,
        out_shape=pltpu.VMEM(arrays[0].shape, F32),
        compiler_params=pltpu.CompilerParams(vmem_limit_bytes=8 * MIB),
        cost_estimate=SHORT,
        name=name,
    )(order, *arrays, *after)


def joined(order, mine, other, heads, after=()):
    return small_call(
        functools.partial(join_kernel, heads), "join_windows", order, (mine, other), after
    )


def picked(order, even, odd, after=(), through=()):
    vmem = pl.BlockSpec(memory_space=pltpu.VMEM)

    def kernel(order_ref, even_ref, odd_ref, *refs):
        outs = refs[len(through) + len(after) :]
        for source, target in zip(refs, outs[1:]):
            target[...] = source[...]
        odd = (order_ref[0] & 1) == 1

        @pl.when(odd)
        def _():
            outs[0][...] = odd_ref[...]

        @pl.when(jnp.logical_not(odd))
        def _():
            outs[0][...] = even_ref[...]

    return pl.pallas_call(
        kernel,
        in_specs=[pl.BlockSpec(memory_space=pltpu.SMEM)]
        + [vmem] * (2 + len(through))
        + [pl.BlockSpec(memory_space=pl.ANY)] * len(after),
        out_specs=[vmem] * (1 + len(through)),
        out_shape=[pltpu.VMEM(x.shape, F32) for x in (even, *through)],
        compiler_params=pltpu.CompilerParams(vmem_limit_bytes=8 * MIB),
        cost_estimate=SHORT,
        name="pick_message",
    )(order, even, odd, *through, *after)


def make_mask(seg_ref, mask_ref):
    tokens = seg_ref.shape[1]
    seg = seg_ref[...].astype(F32)
    column = as_column(seg, 128)
    for start in range(0, tokens, 128):
        across = lax.broadcasted_iota(jnp.int32, (tokens, 128), 1) + start
        down = lax.broadcasted_iota(jnp.int32, (tokens, 128), 0)
        seen = (column == seg[:, start : start + 128]) & (across <= down)
        mask_ref[:, start : start + 128] = jnp.where(seen, 0.0, -1e30)


def intra_kernel(
    first, heads, through, after, mask_ref, a_ref, gain_ref, q_ref, k_ref, v_ref, g_ref, *refs
):
    o_ref, gate_ref, decay_ref, *copied = refs[through + after :]
    for source, target in zip(refs[:through], copied):
        target[...] = source[...]
    tokens = mask_ref.shape[0]
    size = q_ref.shape[1] // heads
    block = min(tokens, 256)
    for j in range(heads):
        columns = slice(j * size, (j + 1) * size)
        a_row = a_ref[first + j : first + j + 1, :] * 1.4426950408889634
        a_column = as_column(a_row, 128)
        decay_ref[:, columns] = jnp.exp2(a_column)
        for start in range(0, tokens, block):
            here, upto = slice(start, start + block), slice(0, start + block)
            scores = lax.dot_general(
                q_ref[here, columns], k_ref[upto, columns], NT, preferred_element_type=F32
            )
            spread = jnp.concatenate([a_column[here]] * ((start + block) // 128), axis=1)
            weight = jnp.exp2(spread - a_row[:, upto] + mask_ref[here, upto])
            probs = (scores * weight).astype(BF16)
            o_ref[here, columns] = lax.dot_general(
                probs, v_ref[upto, columns], NN, preferred_element_type=F32
            )
        half = 0.5 * size**0.5 * gain_ref[:, (first + j) * size : (first + j + 1) * size]
        gate_ref[:, columns] = half + half * jnp.tanh(0.5 * g_ref[:, columns].astype(F32))


def intra(mask, a, gain, q, k, v, g, first, heads, through=(), after=()):
    tokens, size = mask.shape[0], gain.shape[1] // a.shape[0]
    vmem = pl.BlockSpec(memory_space=pltpu.VMEM)
    o, gate, decay, *copied = pl.pallas_call(
        functools.partial(intra_kernel, first, heads, len(through), len(after)),
        in_specs=[vmem] * (7 + len(through)) + [pl.BlockSpec(memory_space=pl.ANY)] * len(after),
        out_specs=[vmem] * (3 + len(through)),
        out_shape=[pltpu.VMEM((tokens, heads * size), F32)] * 3
        + [pltpu.VMEM(x.shape, x.dtype) for x in through],
        compiler_params=pltpu.CompilerParams(vmem_limit_bytes=8 * MIB),
        cost_estimate=SHORT,
        name="intra_span",
    )(mask, a, gain, q, k, v, g, *through, *after)
    return (o, gate, decay, q), copied


def final_kernel(groups, unread, order_ref, seg_ref, *rest):
    number = len(groups)
    inputs, rest = rest[: 7 * number], rest[7 * number + unread :]
    gated_hbm, snap_hbm, *scratch, inter_ref, sems = rest
    place = order_ref[0]
    seg = seg_ref[...].astype(F32)
    copies, work = [], []

    def send(source, target):
        copies.append(pltpu.make_async_copy(source, target, sems.at[len(copies)]))
        copies[-1].start()

    for i, (first, heads, kind) in enumerate(groups):
        own_ref, near_ref, past_ref = inputs[7 * i : 7 * i + 3]
        gated_ref, snap_ref = scratch[2 * i : 2 * i + 2]
        size = own_ref.shape[1]
        top = heads * size
        ends = slice(top + heads, top + heads + 1)
        finals = slice(top, top + heads)
        own_end, near_end, past_end = own_ref[ends, :], near_ref[ends, :], past_ref[ends, :]
        bridged = jnp.exp(near_ref[finals, :]) * jnp.where(near_end == past_end, 1.0, 0.0)
        if kind == "pair":
            odd = (place & 1) == 1
            previous = jnp.where(odd, near_end, past_end)
            scale_near = jnp.where(odd, 1.0, 0.0)
            scale_past = jnp.where(odd, bridged, 1.0)
        else:
            previous = near_end
            scale_near = jnp.where(place > 0, 1.0, 0.0)
            scale_past = bridged
        scale_past = jnp.where(place >= 2, scale_past, 0.0)
        own_decay = jnp.exp(own_ref[finals, :]) * jnp.where(own_end == previous, 1.0, 0.0)
        number_valid = jnp.sum(
            jnp.where(seg == previous[:, :1], 1.0, 0.0), axis=1, keepdims=True
        )
        for j in range(heads):
            rows = slice(j * size, (j + 1) * size)
            state = scale_past[j : j + 1] * past_ref[rows, :] + scale_near * near_ref[rows, :]
            snap_ref[j] = own_decay[j : j + 1] * state + own_ref[rows, :]
            high = state.astype(BF16)
            low = (state - high.astype(F32)).astype(BF16)
            both = jnp.concatenate([high, low], axis=0)
            work.append((i, j, first, heads, both, number_valid, inputs[7 * i + 3 : 7 * i + 7]))
        send(snap_ref, snap_hbm.at[0, pl.ds(first, heads)])

    rows = lax.broadcasted_iota(jnp.int32, (64, 128), 0).astype(F32)
    for number, (i, j, first, heads, both, number_valid, arrays) in enumerate(work):
        o_ref, gate_ref, decay_ref, q_ref = arrays
        gated_ref = scratch[2 * i]
        tokens, size = seg.shape[1], q_ref.shape[1] // heads
        columns = slice(j * size, (j + 1) * size)
        q = q_ref[:, columns]
        inter_ref[number % 4] = lax.dot_general(
            jnp.concatenate([q, q], axis=1), both, NN, preferred_element_type=F32
        )
        for start in range(0, tokens, 64):
            here = slice(start, start + 64)
            inter = inter_ref[number % 4, here, :]
            inter = jnp.where(rows < number_valid - start, inter * decay_ref[here, columns], 0.0)
            mixed = o_ref[here, columns] + inter
            square = jnp.sum(mixed * mixed, axis=1, keepdims=True)
            gated = mixed * gate_ref[here, columns] * lax.rsqrt(square + size * 1e-06)
            gated_ref[here, columns] = gated.astype(BF16)
            if number == len(work) - 1 and start % 128 == 64:
                block = pl.ds(start - 64, 128)
                there = pl.ds((first + j) * size, size)
                send(gated_ref.at[block, pl.ds(j * size, size)], gated_hbm.at[block, there])
        if number == len(work) - 1:
            continue
        alone = number + 2 == len(work) and j % 2 == 0
        if alone or j % 2 == 1 or j == heads - 1:
            begin = j if alone else j - j % 2
            width = (j + 1 - begin) * size
            there = pl.ds((first + begin) * size, width)
            send(gated_ref.at[:, pl.ds(begin * size, width)], gated_hbm.at[:, there])
    for copy in copies:
        copy.wait()


def finish(order, seg, total, groups, arrays, so_far, after):
    tokens, size = seg.shape[1], arrays[0].shape[1]
    vmem, anywhere = pl.BlockSpec(memory_space=pltpu.VMEM), pl.BlockSpec(memory_space=pl.ANY)
    unread = len(so_far) + len(after)
    scratch = []
    for _, many, _ in groups:
        scratch.append(pltpu.VMEM((tokens, many * size), BF16))
        scratch.append(pltpu.VMEM((many, size, size), F32))
    return pl.pallas_call(
        functools.partial(final_kernel, groups, unread),
        in_specs=[pl.BlockSpec(memory_space=pltpu.SMEM)]
        + [vmem] * (1 + len(arrays))
        + [anywhere] * unread,
        out_specs=[anywhere, anywhere],
        out_shape=[
            jax.ShapeDtypeStruct((tokens, total * size), BF16),
            jax.ShapeDtypeStruct((1, total, size, size), F32),
        ],
        scratch_shapes=scratch
        + [pltpu.VMEM((4, tokens, size), F32), pltpu.SemaphoreType.DMA((2 * total,))],
        input_output_aliases={2 + len(arrays) + i: i for i in range(len(so_far))},
        compiler_params=pltpu.CompilerParams(vmem_limit_bytes=12 * MIB),
        cost_estimate=SHORT,
        name="finish",
    )(order, seg, *arrays, *so_far, *after)


def shards(q, k, v, g, segment, decay_exponent, retention, norm_gain):
    heads = decay_exponent.shape[0]
    tokens = q.shape[0]
    count = lax.axis_size("seq")
    place = lax.axis_index("seq")
    reach = max(1, count // 4)
    far = lambda x: pltpu.with_memory_space_constraint(x, pltpu.HBM)
    q, k, v, g = far(q), far(k), far(v), far(g)
    gain = norm_gain.reshape(1, -1)
    order = jnp.where(place >= 2, 2 + (place & 1), place & 1).astype(jnp.int32).reshape(1)
    later = jnp.ones((1,), jnp.int32)
    swap = lambda x: lax.ppermute(x, "seq", [(c, c ^ 1) for c in range(count)])
    turn = lambda x: lax.ppermute(x, "seq", [(c, (c + 2) % count) for c in range(count)])
    ahead = lambda x: lax.ppermute(x, "seq", [(c, c + 2) for c in range(count - 2)])

    half = heads // 2
    even, odd = half // 2, half // 2
    chunks = [(0, half - even), (half, half - odd), (half - even, even), (heads - odd, odd)]

    def widened(x, many, shift, window):
        while window < reach:
            past = lax.ppermute(x, "seq", [(c, c + shift) for c in range(count - shift)])
            x = joined(later, x, past, many)
            shift, window = 2 * shift, 2 * window
        return x

    message, a, w, seg, k_near, v_near = first_message(
        order,
        far(segment.reshape(1, tokens)),
        far(decay_exponent.reshape(1, heads)),
        far(retention),
        k,
        v,
        heads,
        (chunks[1], chunks[0]),
    )
    k_near, v_near = k_near[::-1], v_near[::-1]
    near, past, inside = {}, {}, {}
    near[1] = swap(message)
    own = [second_message(seg, a, w, k_near[0], v_near[0], *chunks[0]), message]
    past[0] = turn(own[0])
    messages, mask, k_rest, v_rest, q_near, g_near = rest_messages(
        seg, a, w, q, k, v, g, chunks, 2
    )
    own, k_near, v_near = [*own, *messages], [*k_near, *k_rest], [*v_near, *v_rest]

    def look_inside(i, through=(), after=()):
        inside[i], copied = intra(
            mask, a, gain, q_near[i], k_near[i], v_near[i], g_near[i], *chunks[i], through, after
        )
        return copied

    def pair_last(i, after, through=()):
        message, *copied = picked(order, own[i], past[i], after, through)
        near[i] = swap(message)
        return message, *copied

    near[3] = swap(own[3])
    past[2] = turn(own[2])
    look_inside(0)
    both = joined(order, own[1], near[1], chunks[1][1], (inside[0][0],))
    message, both = pair_last(0, (), (both,))
    past[1] = turn(both)
    look_inside(1, (), (message,))
    look_inside(2, (), (inside[1][0],))
    both = joined(order, own[3], near[3], chunks[3][1], (inside[2][0],))
    message, both = pair_last(2, (), (both,))
    past[3] = ahead(both)
    look_inside(3, (), (message,))

    if reach > 2:
        for i, (_, many) in enumerate(chunks):
            past[i] = jnp.where(place >= 2, past[i], 0.0)
            if i % 2 == 0:
                near[i] = jnp.where(place >= 1, near[i], 0.0)
                near[i] = widened(joined(later, near[i], past[i], many), many, 2, 2)
                past[i] = jnp.zeros_like(near[i])
            else:
                past[i] = widened(past[i], many, 2, 2)

    result = ()
    for group in ((0, 1), (2, 3)):
        groups = [(*chunks[i], ("span", "pair")[i % 2]) for i in group]
        arrays = [x for i in group for x in (own[i], near[i], past[i], *inside[i])]
        result = finish(order, seg, heads, groups, arrays, result, (inside[3][0],))
    return tuple(result)


def solution(mesh):
    placed = (
        P(("groups", "seq"), "wt"),
        P(("groups", "seq"), "wt"),
        P(("groups", "seq"), "wt"),
        P(("groups", "seq"), "wt"),
        P(("groups", "seq")),
        P("wt"),
        P("wt", ("groups", "seq")),
        P("wt"),
    )
    return jax.shard_map(
        shards,
        mesh=mesh,
        in_specs=placed,
        out_specs=(P(("groups", "seq"), "wt"), P(("groups", "seq"), "wt", None, None)),
        check_vma=False,
    )
```
